32 devices in a mesh: tm: 8 (over z, x), space: 4 (over y, core).
Axes of the slice: x: 2, y: 2, z: 4, core: 2. Of those that a mesh axis runs over, the one named last changes fastest.
Arguments:
- ensembles: bfloat16 [128, 80, 8192], P('tm', None, 'space'), may hold values from -6 to 6
- cotangents: bfloat16 [128, 80, 8192], P('tm', None, 'space'), may hold values from -6 to 6
- transforms: float32 [128, 80, 80], P('tm'), may hold values from -1.5 to 1.5
Outputs:
- smoothed: bfloat16 [128, 80, 8192], P('tm', None, 'space')
- ensemble_grad: bfloat16 [128, 80, 8192], P('tm', None, 'space')
- transform_grad: float32 [128, 80, 80], P('tm')
The draws below stay inside these ranges and needn't reach their ends.
All inputs are finite; a program needn't handle non-finite values.
Results may differ from the reference program's by a relative error of at most 0.0049.
Values sent between devices are 32-bit elements; how exact they have to be, the bound alone decides.
No kernel may reach another device: no remote copies, remote signals or barrier semaphores. Data moves between devices by JAX's collectives and lax.ppermute only.
A program may use at most 64 MiB of HBM per device.

```python
import jax
import jax.numpy as jnp
from jax import lax

MEMBERS = 80
TIMES = 128
CELLS = 8192


def draw_transforms(key, part):
    first_key, second_key = jax.random.split(jax.random.fold_in(key, 11))
    noise = jax.random.normal(first_key, (TIMES, MEMBERS, MEMBERS), jnp.float32)
    gains = jnp.exp(0.05 * jnp.clip(jax.random.normal(second_key, (TIMES, MEMBERS, 1), jnp.float32), -3.0, 3.0))
    skewed = (noise - jnp.swapaxes(noise, 1, 2)) * (0.4 / jnp.sqrt(2.0 * MEMBERS))
    squared = jnp.einsum('tij,tjk->tik', skewed, skewed, precision=lax.Precision.HIGHEST)
    rotation = jnp.eye(MEMBERS, dtype=jnp.float32)[None] + skewed + 0.5 * squared
    return (rotation * gains).astype(jnp.float32)


def level_of(stream_key, shape, pieces, low, largest):
    gain = 1.0
    for axis_at, parts in pieces:
        draws = jax.random.uniform(jax.random.fold_in(jax.random.fold_in(stream_key, 6), axis_at), (parts,), jnp.float32, low / len(pieces), largest / len(pieces))
        gain = gain * jnp.repeat(jnp.exp(draws), shape[axis_at] // parts).reshape((-1,) + (1,) * (len(shape) - 1 - axis_at))
    return gain


def scatter_about(rng, dims, width, limit, pieces=(), kind=jnp.bfloat16):
    loudness = level_of(rng, dims, pieces, -0.22, 0.18) if pieces else 1.0
    result = jax.random.normal(rng, dims, jnp.float32) * width * loudness
    return jnp.minimum(jnp.maximum(result, -limit), limit).astype(kind)


def setup_inputs(seed: int = 0) -> dict:
    key_of = jax.random.split(jax.random.key(seed), 4)
    ensembles = scatter_about(key_of[0], (TIMES, MEMBERS, CELLS), 1.0, 6.0, ((0, 8), (2, 4)))
    cotangents = scatter_about(key_of[1], (TIMES, MEMBERS, CELLS), 1.0, 6.0, ((0, 8), (2, 4)))
    transforms = draw_transforms(jax.random.fold_in(key_of[3], 71), 0)
    return {"ensembles": ensembles, "cotangents": cotangents, "transforms": transforms}


def reference(ensembles, cotangents, transforms):
    exact_mode = lax.Precision.HIGHEST
    identity = jnp.eye(MEMBERS, dtype=jnp.float32)

    def backward(following_prod, weight):
        current = jnp.dot(weight, following_prod, precision=exact_mode)
        return (current, (current, following_prod))
    _, (products, following) = lax.scan(backward, identity, transforms, reverse=True)
    rounded = products.astype(jnp.bfloat16)

    def smooth_one(index):
        block = ensembles[index].astype(jnp.float32)
        weights = cotangents[index].astype(jnp.float32)
        factor = rounded[index].astype(jnp.float32)
        smoothed_one = jnp.dot(factor.T, block, precision=exact_mode).astype(jnp.bfloat16)
        grad_one = jnp.dot(factor, weights, precision=exact_mode).astype(jnp.bfloat16)
        gram_one = jnp.dot(block, weights.T, precision=exact_mode)
        return (smoothed_one, grad_one, gram_one)
    smoothed, ensemble_grad, gram = lax.map(smooth_one, jnp.arange(TIMES, dtype=jnp.int32))

    def forward(message, inputs):
        weight, gram_one = inputs
        total = gram_one + message
        return (jnp.dot(weight.T, total, precision=exact_mode), total)
    _, totals = lax.scan(forward, jnp.zeros((MEMBERS, MEMBERS), jnp.float32), (transforms, gram))
    scale = 1.0 / jnp.sqrt(jnp.float32(CELLS) * jnp.float32(TIMES))
    transform_grad = jnp.einsum('tkm,tjm->tkj', totals, following, precision=exact_mode) * scale
    return (smoothed, ensemble_grad, transform_grad)
```

```python
import functools
import math

import jax
import jax.numpy as jnp
from jax import lax
from jax.experimental import pallas as pl
from jax.experimental.pallas import tpu as pltpu
from jax.sharding import PartitionSpec as P

F32 = jnp.float32
BF16 = jnp.bfloat16
VMEM = pl.BlockSpec(memory_space=pltpu.VMEM)
HBM = pl.BlockSpec(memory_space=pl.ANY)


def split(value):
    high = value.astype(BF16)
    return high, (value - high.astype(F32)).astype(BF16)


def mul(left, right, dims=(((1,), (0,)), ((), ()))):
    return lax.dot_general(left, right, dims, preferred_element_type=F32)


def mul_pairs(left, right):
    return mul(left[0], right[0]) + (mul(left[0], right[1]) + mul(left[1], right[0]))


def mul_exact(left, right):
    return mul_pairs(split(left), split(right))


def product_of(factors):
    while len(factors) > 1:
        joined = [mul_exact(*factors[at : at + 2]) for at in range(0, len(factors) - 1, 2)]
        factors = joined + factors[len(joined) * 2 :]
    return factors[0]


def suffix_scan(ref, count, members, stop):
    width = 1
    while width < stop:
        for start in range(0, count, 2 * width):
            middle = start + width
            if middle < count:
                rows = slice(start * members, middle * members)
                ref[rows] = mul_exact(ref[rows], ref[middle * members : (middle + 1) * members])
        width *= 2


def eye(members):
    rows = lax.broadcasted_iota(jnp.int32, (members, members), 0)
    columns = lax.broadcasted_iota(jnp.int32, (members, members), 1)
    return (rows == columns).astype(F32)


def chain_kernel(count, members, transforms, halves, suffixes, total):
    half = count // 2 * members
    halves[...] = transforms[...]
    suffix_scan(halves, count, members, count // 2)
    suffixes[half:] = halves[half:]
    suffixes[:half] = mul_exact(halves[:half], halves[half : half + members])
    total[...] = suffixes[:members]


def gram_kernel(
    count, members, ensembles, cotangents, halves, sent, kept, offsets,
    ens_buf, cot_buf, gram_buf, ens_sem, cot_sem,
):
    copies = []
    for at in range(count):
        pair = (
            pltpu.make_async_copy(ensembles.at[at], ens_buf.at[at], ens_sem.at[at]),
            pltpu.make_async_copy(cotangents.at[at], cot_buf.at[at], cot_sem.at[at]),
        )
        for copy in pair:
            copy.start()
        copies.append(pair)
    half = count // 2
    sums = []
    for group in range(2):
        total = jnp.zeros((members, members), F32)
        for at in range(group * half, (group + 1) * half):
            for copy in copies[at]:
                copy.wait()
            gram = mul(cot_buf[at], ens_buf[at], (((1,), (1,)), ((), ())))
            gram_buf[at] = gram
            total += mul_exact(gram, halves[at * members : (at + 1) * members])
        sums.append(total)
    offsets[0] = sums[0]
    offsets[1] = sums[1] + mul_exact(sums[0], halves[half * members : (half + 1) * members])
    core = lax.rem(lax.axis_index("space"), 2)
    kept[...] = gram_buf[pl.ds(core * half, half)]
    sent[...] = gram_buf[pl.ds((1 - core) * half, half)]


def carry_kernel(count, members, blocks, *refs):
    transforms, suffixes = refs[:2]
    others = refs[2 : 1 + blocks]
    rounded, rounded_t, follow_high, follow_low, step_high, step_low, windows, products = refs[1 + blocks :]
    mine = lax.axis_index("tm")
    core = lax.rem(lax.axis_index("space"), 2)
    unit = eye(members)
    later = [jnp.where(mine + d < blocks, others[d - 1][...], unit) for d in range(1, blocks)]
    entering = product_of(later)
    products[: count * members] = mul_exact(suffixes[...], entering)
    products[count * members :] = entering
    for at in range(count):
        rows = slice(at * members, (at + 1) * members)
        rounded[at] = products[rows].astype(BF16)
        rounded_t[at] = products[rows].T.astype(BF16)
    for e in range(1, blocks - 1):
        rows = slice((blocks - 2 - e) * members, (blocks - 1 - e) * members)
        windows[rows] = jnp.where(mine >= e, others[blocks - e - 1][...], unit)
    suffix_scan(windows, blocks - 2, members, blocks - 2)
    half = count // 2
    following = products[pl.ds((core * half + 1) * members, half * members)]
    high, low = split(following)
    follow_high[...] = high
    follow_low[...] = low
    for at, (first, last) in enumerate(scan_steps(half)):
        factors = [transforms[core * half + i] for i in range(first, last)]
        high, low = split(product_of(factors))
        step_high[at] = high
        step_low[at] = low


def scan_steps(count):
    steps = []
    width = 1
    while width < count:
        for middle in range(width, count, 2 * width):
            for at in range(middle, min(middle + width, count)):
                steps.append((middle - 1, at))
        width *= 2
    return steps


def final_kernel(count, members, blocks, chips, scale, *refs):
    gram_refs = refs[:chips]
    offset_refs = refs[chips : chips + blocks - 1]
    own, halves, windows, follow_high, follow_low, step_high, step_low, out = refs[chips + blocks - 1 :]
    half = count // 2
    core = lax.rem(lax.axis_index("space"), 2)
    carry = offset_refs[0][...]
    for e in range(2, blocks):
        rows = slice((blocks - 1 - e) * members, (blocks - e) * members)
        carry += mul_exact(offset_refs[e - 1][...], windows[rows])
    middle = mul_exact(carry, halves[:members]) + own[0]
    carry = jnp.where(core == 0, carry, middle)
    totals = []
    for at in range(half):
        total = gram_refs[0][at]
        for ref in gram_refs[1:]:
            total = total + ref[at]
        totals.append(total)
    totals[0] += carry
    number = 0
    width = 1
    while width < half:
        for start in range(width, half, 2 * width):
            left = split(totals[start - 1])
            for at in range(start, min(start + width, half)):
                totals[at] += mul_pairs(left, (step_high[number], step_low[number]))
                number += 1
        width *= 2
    for at in range(half):
        rows = slice(at * members, (at + 1) * members)
        grad = mul_pairs((follow_high[rows], follow_low[rows]), split(totals[at]))
        out[at] = (grad * scale).T


def apply_kernel(count, factors, values, out, in_buf, out_buf, in_sem, out_sem):
    reads, writes = [], []
    for at in range(count):
        copy = pltpu.make_async_copy(values.at[at], in_buf.at[at], in_sem.at[at])
        copy.start()
        reads.append(copy)
    for at in range(count):
        reads[at].wait()
        out_buf[at] = mul(factors[at], in_buf[at]).astype(BF16)
        copy = pltpu.make_async_copy(out_buf.at[at], out.at[at], out_sem.at[at])
        copy.start()
        writes.append(copy)
    for copy in writes:
        copy.wait()


def call(kernel, outs, in_specs, out_specs, scratch, micros, name, limit=16):
    return pl.pallas_call(
        kernel,
        out_shape=outs,
        in_specs=in_specs,
        out_specs=out_specs,
        scratch_shapes=scratch,
        compiler_params=pltpu.CompilerParams(vmem_limit_bytes=limit << 20),
        cost_estimate=pl.CostEstimate(
            flops=0, bytes_accessed=int(micros * 3.6e6), transcendentals=0
        ),
        name=name,
    )


def shape(*dims, kind=F32):
    return jax.ShapeDtypeStruct(dims, kind)


def shards(ensembles, cotangents, transforms):
    count, members, cells = ensembles.shape
    blocks, lanes = lax.axis_size("tm"), lax.axis_size("space")
    chips, half = lanes // 2, count // 2
    scale = 1.0 / math.sqrt(cells * lanes * count * blocks)

    def shift(value, axis, size, distance, wrap=True):
        pairs = [(at, (at + distance) % size) for at in range(size) if wrap or 0 <= at + distance < size]
        return lax.ppermute(value, axis, pairs)

    halves, suffixes, total = call(
        functools.partial(chain_kernel, count, members),
        [shape(count * members, members)] * 2 + [shape(members, members)],
        [VMEM], [VMEM] * 3, [], 2, "transform_chain",
    )(transforms.reshape(count * members, members))
    others = [shift(total, "tm", blocks, -d) for d in range(1, blocks)]

    buffer = pltpu.VMEM((count, members, cells), BF16)
    sent, kept, offsets = call(
        functools.partial(gram_kernel, count, members),
        [shape(half, members, members)] * 2 + [shape(2, members, members)],
        [HBM, HBM, VMEM], [VMEM] * 3,
        [buffer, buffer, pltpu.VMEM((count, members, members), F32)]
        + [pltpu.SemaphoreType.DMA((count,))] * 2,
        4, "gram", 32,
    )(ensembles, cotangents, halves)
    pair = [(at, at ^ 1) for at in range(lanes)]
    own = offsets
    for d in range(1, lanes):
        own = own + shift(offsets, "space", lanes, d)
    chip_gram = kept + lax.ppermute(sent, "space", pair)
    grams = [chip_gram] + [shift(chip_gram, "space", lanes, 2 * d) for d in range(1, chips)]
    entering = [shift(own[1], "tm", blocks, d, wrap=False) for d in range(1, blocks)]

    steps = len(scan_steps(half))
    rounded, rounded_t, follow_high, follow_low, step_high, step_low, windows = call(
        functools.partial(carry_kernel, count, members, blocks),
        [shape(count, members, members, kind=BF16)] * 2
        + [shape(half * members, members, kind=BF16)] * 2
        + [shape(steps, members, members, kind=BF16)] * 2
        + [shape((blocks - 2) * members, members)],
        [VMEM] * (blocks + 1), [VMEM] * 7,
        [pltpu.VMEM(((count + 1) * members, members), F32)],
        2, "carries",
    )(transforms, suffixes, *others)

    def apply(factors, values, name):
        return call(
            functools.partial(apply_kernel, count),
            shape(count, members, cells, kind=BF16),
            [VMEM, HBM], HBM, [buffer, buffer] + [pltpu.SemaphoreType.DMA((count,))] * 2,
            3.5, name, 32,
        )(factors, values)

    smoothed = apply(rounded_t, ensembles, "smoothed")
    ensemble_grad = apply(rounded, cotangents, "ensemble_grad")

    mine = call(
        functools.partial(final_kernel, count, members, blocks, chips, scale),
        shape(half, members, members),
        [VMEM] * (chips + blocks - 1 + 7), VMEM, [], 2, "transform_grad",
    )(*grams, *entering, own, halves, windows, follow_high, follow_low, step_high, step_low)
    other = lax.ppermute(mine, "space", pair)
    first = lax.rem(lax.axis_index("space"), 2) == 0
    transform_grad = jnp.concatenate([jnp.where(first, mine, other), jnp.where(first, other, mine)])
    return (smoothed, ensemble_grad, transform_grad)


def solution(mesh):
    return jax.shard_map(
        shards,
        mesh=mesh,
        in_specs=(P("tm", None, "space"), P("tm", None, "space"), P("tm", None, None)),
        out_specs=(P("tm", None, "space"), P("tm", None, "space"), P("tm", None, None)),
        check_vma=False,
    )
```

```python
import functools
import math

import jax
import jax.numpy as jnp
from jax import lax
from jax.experimental import pallas as pl
from jax.experimental.pallas import tpu as pltpu
from jax.sharding import PartitionSpec as P

F32 = jnp.float32
BF16 = jnp.bfloat16
VMEM = pl.BlockSpec(memory_space=pltpu.VMEM)
HBM = pl.BlockSpec(memory_space=pltpu.HBM)
DEPTH = 256
PIECES = 3
NORMAL = (((1,), (0,)), ((), ()))
ROWS = (((1,), (1,)), ((), ()))


def split(value):
    high = value.astype(BF16)
    return high, (value - high.astype(F32)).astype(BF16)


def mul(left, right, dims=NORMAL):
    return lax.dot_general(left, right, dims, preferred_element_type=F32)


def mul_pairs(left, right, dims=NORMAL):
    return mul(left[0], right[0], dims) + (
        mul(left[0], right[1], dims) + mul(left[1], right[0], dims)
    )


def mul_exact(left, right, dims=NORMAL):
    return mul_pairs(split(left), split(right), dims)


def product_of(factors):
    while len(factors) > 1:
        joined = [mul_exact(*factors[at : at + 2]) for at in range(0, len(factors) - 1, 2)]
        factors = joined + factors[len(joined) * 2 :]
    return factors[0]


def suffix_scan(ref, count, members, stop):
    width = 1
    while width < stop:
        for start in range(0, count, 2 * width):
            middle = start + width
            if middle < count:
                rows = slice(start * members, middle * members)
                ref[rows] = mul_exact(ref[rows], ref[middle * members : (middle + 1) * members])
        width *= 2


def scan_steps(count):
    steps = []
    width = 1
    while width < count:
        for middle in range(width, count, 2 * width):
            for at in range(middle, min(middle + width, count)):
                steps.append((middle - 1, at))
        width *= 2
    return steps


class Plan:
    def __init__(self, count, members):
        self.count, self.members, self.half = count, members, count // 2
        self.stack = DEPTH // members
        self.groups = [
            (start, min(start + self.stack, base + self.half))
            for base in (0, self.half)
            for start in range(base, base + self.half, self.stack)
        ]
        bounds = [len(self.groups) * at // PIECES for at in range(PIECES + 1)]
        self.piece_groups = [self.groups[a:b] for a, b in zip(bounds, bounds[1:])]
        self.pieces = [(part[0][0], part[-1][1]) for part in self.piece_groups]
        self.first_group = bounds[:-1]
        self.width = -(-self.slot(self.half + 1).stop // 128) * 128

    def slot(self, at):
        start = at // self.stack * DEPTH + at % self.stack * self.members
        return slice(start, start + self.members)

    def rows(self, first, last):
        return slice(first * self.members, last * self.members)


def on_blocks(members, size):
    rows = lax.broadcasted_iota(jnp.int32, (size, size), 0) // members
    columns = lax.broadcasted_iota(jnp.int32, (size, size), 1) // members
    return rows == columns


def loads(values, buffer, sems, first, last):
    copies = [
        pltpu.make_async_copy(values.at[at], buffer.at[at - first], sems.at[at - first])
        for at in range(first, last)
    ]
    for copy in copies:
        copy.start()
    return copies


def chain_kernel(plan, transforms, ensembles, cotangents, kept, halves, total, ens, cot, sems, ens_sem, cot_sem):
    count, members = plan.count, plan.members
    reads = loads(transforms, kept, sems, 0, count)
    more = loads(ensembles, ens, ens_sem, *plan.pieces[0])
    more += loads(cotangents, cot, cot_sem, *plan.pieces[0])
    for at, copy in enumerate(reads):
        copy.wait()
        halves[plan.rows(at, at + 1)] = kept[at]
    suffix_scan(halves, count, members, plan.half)
    total[...] = mul_exact(halves[plan.rows(0, 1)], halves[plan.rows(plan.half, plan.half + 1)])
    for copy in more:
        copy.wait()


def gram_kernel(plan, piece, *refs):
    members, half = plan.members, plan.half
    ens, cot, halves = refs[:3]
    refs = refs[3:]
    last = piece == PIECES - 1
    copies = []
    if last:
        earlier, refs = refs[: 2 * piece], refs[2 * piece :]
        sent, kept = refs
    else:
        ensembles, cotangents, grams, offsets, next_ens, next_cot, ens_sem, cot_sem = refs
        copies = loads(ensembles, next_ens, ens_sem, *plan.pieces[piece + 1])
        copies += loads(cotangents, next_cot, cot_sem, *plan.pieces[piece + 1])
    base = plan.pieces[piece][0]
    sums = [jnp.zeros((members, members), F32)] * 2
    packed = []
    for start, stop in plan.piece_groups[piece]:
        size = (stop - start) * members
        stacked = [ref[start - base : stop - base].reshape(size, ref.shape[2]) for ref in (cot, ens)]
        wide = jnp.where(on_blocks(members, size), mul(*stacked, ROWS), 0.0)
        gram = wide[:members]
        for at in range(1, stop - start):
            gram = gram + wide[at * members : (at + 1) * members]
        side = start // half
        sums[side] = sums[side] + mul_exact(gram, halves[plan.rows(start, stop)])
        packed.append(jnp.pad(gram, ((0, 0), (0, DEPTH - size))))
    if not last:
        for at, gram in enumerate(packed):
            grams[at] = gram
        for side in range(2):
            offsets[side] = sums[side]
    else:
        groups = []
        for at in range(piece):
            groups += [earlier[2 * at][i] for i in range(len(plan.piece_groups[at]))]
            sums = [sums[side] + earlier[2 * at + 1][side] for side in range(2)]
        groups += packed
        whole = sums[1] + mul_exact(sums[0], halves[plan.rows(half, half + 1)])
        core = lax.rem(lax.axis_index("space"), 2)
        side_groups = len(groups) // 2
        for ref, side in ((kept, core), (sent, 1 - core)):
            for at in range(side_groups):
                lanes = slice(at * DEPTH, min((at + 1) * DEPTH, plan.width))
                chosen = jnp.where(side == 0, groups[at], groups[side_groups + at])
                ref[:, lanes] = chosen[:, : lanes.stop - lanes.start]
            if plan.width > side_groups * DEPTH:
                ref[:, side_groups * DEPTH :] = jnp.zeros(
                    (members, plan.width - side_groups * DEPTH), F32
                )
            ref[:, plan.slot(half)] = whole
            ref[:, plan.slot(half + 1)] = sums[0]
    for copy in copies:
        copy.wait()


def upper_half(level):
    return lax.rem(lax.axis_index("tm") // (1 << level), 2) == 1


def join_kernel(level, total, other, later, before, new_total, new_later, new_before, upper_total):
    upper = upper_half(level)
    left = jnp.where(upper, other[...], total[...])
    right = jnp.where(upper, total[...], other[...])
    new_total[...] = mul_exact(left, right)
    upper_total[...] = right
    new_later[...] = jnp.where(upper, later[...], mul_exact(later[...], other[...]))
    new_before[...] = jnp.where(upper, mul_exact(other[...], before[...]), before[...])


def pass_kernel(level, own, other, carry, upper_total, before, new_own, new_carry):
    upper = upper_half(level)
    left = jnp.where(upper, other[...], own[...])
    right = jnp.where(upper, own[...], other[...])
    new_own[...] = mul_exact(left, upper_total[...]) + right
    new_carry[...] = carry[...] + jnp.where(upper, mul_exact(left, before[...]), 0.0)


def carry_kernel(plan, level, transforms, halves, later, other, ens_factors, cot_factors, follow, steps):
    count, members, half = plan.count, plan.members, plan.half
    core = lax.rem(lax.axis_index("space"), 2)
    entering = later[...]
    entering = jnp.where(upper_half(level), entering, mul_exact(entering, other[...]))
    middle = mul_exact(halves[plan.rows(half, half + 1)], entering)
    mask = on_blocks(members, plan.stack * members)
    follows = [[], []]
    for side, end in ((0, middle), (1, entering)):
        rows = plan.rows(side * half, (side + 1) * half)
        wide = mul_exact(halves[rows], jnp.concatenate([end] * plan.stack, axis=1))
        follows[side] = jnp.concatenate([wide[members:, :members], end], axis=0)
        for at, (start, stop) in enumerate(plan.groups):
            if start // half == side:
                size = (stop - start) * members
                offset = (start - side * half) * members
                part = jnp.where(mask[:size, :size], wide[offset : offset + size, :size], 0.0)
                cot_factors[at, :size, :size] = part.astype(BF16)
                ens_factors[at, :size, :size] = part.T.astype(BF16)
    for at, part in enumerate(split(jnp.where(core == 0, follows[0], follows[1]))):
        follow[at] = part
    for at, (first, last) in enumerate(scan_steps(half)):
        factors = [transforms[core * half + i] for i in range(first, last)]
        for side, part in enumerate(split(product_of(factors).T)):
            steps[side, plan.rows(at, at + 1)] = part


def apply_kernel(plan, piece, factors, values, *refs):
    out, out_buf, out_sem = refs[-3:]
    members = plan.members
    base = plan.pieces[piece][0]
    writes = []
    for at, (start, stop) in enumerate(plan.piece_groups[piece]):
        size = (stop - start) * members
        part = slice(start - base, stop - base)
        stacked = values[part].reshape(size, values.shape[2])
        result = mul(factors[plan.first_group[piece] + at, :size, :size], stacked)
        out_buf[part] = result.astype(BF16).reshape(stop - start, members, values.shape[2])
        copy = pltpu.make_async_copy(out_buf.at[part], out.at[start:stop], out_sem.at[at])
        copy.start()
        writes.append(copy)
    for copy in writes:
        copy.wait()


def final_kernel(plan, level, scale, message, own, other, carry, before, halves, follow, steps, out):
    members, half = plan.members, plan.half
    core = lax.rem(lax.axis_index("space"), 2)
    entering = carry[...] + jnp.where(
        upper_half(level), mul_exact(other[...], before[...]), 0.0
    )
    middle = mul_exact(entering, halves[plan.rows(0, 1)]) + message[:, plan.slot(half + 1)]
    entering = jnp.where(core == 0, entering, middle)
    totals = []
    for start in range(0, half, plan.stack):
        at = start // plan.stack
        tall = message[:, at * DEPTH : (at + 1) * DEPTH].T
        for i in range(min(plan.stack, half - start)):
            totals.append(tall[i * members : (i + 1) * members])
    totals[0] = totals[0] + entering.T
    number = 0
    width = 1
    while width < half:
        for start in range(width, half, 2 * width):
            size = min(width, half - start)
            rows = plan.rows(number, number + size)
            added = mul_pairs((steps[0, rows], steps[1, rows]), split(totals[start - 1]))
            for at in range(size):
                totals[start + at] = totals[start + at] + added[at * members : (at + 1) * members]
            number += size
        width *= 2
    for at in range(half):
        rows = plan.rows(at, at + 1)
        out[at] = mul_pairs(split(totals[at]), (follow[0, rows], follow[1, rows]), ROWS) * scale


def place_kernel(half, mine, other, out, sems):
    core = lax.rem(lax.axis_index("space"), 2)
    copies = [
        pltpu.make_async_copy(mine, out.at[pl.ds(core * half, half)], sems.at[0]),
        pltpu.make_async_copy(other, out.at[pl.ds((1 - core) * half, half)], sems.at[1]),
    ]
    for copy in copies:
        copy.start()
    for copy in copies:
        copy.wait()


def call(kernel, outs, ins, out_specs, scratch, micros, name, limit=16, aliases=None):
    return pl.pallas_call(
        kernel,
        out_shape=outs,
        in_specs=ins,
        out_specs=out_specs,
        scratch_shapes=scratch,
        input_output_aliases=aliases or {},
        compiler_params=pltpu.CompilerParams(vmem_limit_bytes=limit << 20),
        cost_estimate=pl.CostEstimate(
            flops=0, bytes_accessed=int(micros * 3.6e6), transcendentals=0
        ),
        name=name,
    )


def shape(*dims, kind=F32):
    return jax.ShapeDtypeStruct(dims, kind)


def shards(ensembles, cotangents, transforms):
    count, members, cells = ensembles.shape
    blocks, lanes = lax.axis_size("tm"), lax.axis_size("space")
    chips, half = lanes // 2, count // 2
    scale = 1.0 / math.sqrt(cells * lanes * count * blocks)
    plan = Plan(count, members)
    levels = blocks.bit_length() - 1
    square = shape(members, members)

    def exchange(value, axis, size, bit):
        return lax.ppermute(value, axis, [(at, at ^ bit) for at in range(size)])

    def loaded(piece):
        first, last = plan.pieces[piece]
        return [shape(last - first, members, cells, kind=BF16)] * 2

    def sems(piece):
        first, last = plan.pieces[piece]
        return [pltpu.SemaphoreType.DMA((last - first,))] * 2

    kept, halves, total, *first_part = call(
        functools.partial(chain_kernel, plan),
        [shape(count, members, members), shape(count * members, members), square] + loaded(0),
        [HBM] * 3, [VMEM] * 5,
        [pltpu.SemaphoreType.DMA((count,))] + sems(0), 2, "transform_chain",
    )(transforms, ensembles, cotangents)

    later = before = jnp.eye(members, dtype=F32)
    parts, grams, uppers, befores = [first_part], [], [], []
    for level in range(levels):
        other = exchange(total, "tm", blocks, 1 << level)
        if level < PIECES - 1:
            *sums, ens, cot = call(
                functools.partial(gram_kernel, plan, level),
                [shape(len(plan.piece_groups[level]), members, DEPTH), shape(2, members, members)]
                + loaded(level + 1),
                [VMEM] * 3 + [HBM] * 2, [VMEM] * 4, sems(level + 1), 1.5, f"gram_{level}",
            )(*parts[-1], halves, ensembles, cotangents)
            parts.append((ens, cot))
            grams += sums
        befores.append(before)
        if level < levels - 1:
            total, later, before, upper = call(
                functools.partial(join_kernel, level),
                [square] * 4, [VMEM] * 4, [VMEM] * 4, [], 0.4, f"join_{level}",
            )(total, other, later, before)
            uppers.append(upper)
    sent, mine = call(
        functools.partial(gram_kernel, plan, PIECES - 1),
        [shape(members, plan.width)] * 2,
        [VMEM] * (3 + len(grams)), [VMEM] * 2, [], 1.5, "gram_last",
    )(*parts[-1], halves, *grams)
    message = mine + exchange(sent, "space", lanes, 1)

    size = plan.stack * members
    steps = len(scan_steps(half))
    ens_factors, cot_factors, follow, steps = call(
        functools.partial(carry_kernel, plan, levels - 1),
        [shape(len(plan.groups), size, size, kind=BF16)] * 2
        + [shape(2, half * members, members, kind=BF16), shape(2, steps * members, members, kind=BF16)],
        [VMEM] * 4, [VMEM] * 4, [], 1.5, "carries",
    )(kept, halves, later, other)

    whole = message
    for d in range(1, chips):
        whole = whole + lax.ppermute(
            message, "space", [(at, (at + 2 * d) % lanes) for at in range(lanes)]
        )
    own = whole[:, plan.slot(half)]

    def apply(factors, which, name):
        out = []
        for piece in range(PIECES):
            first, last = plan.pieces[piece]
            out = [call(
                functools.partial(apply_kernel, plan, piece),
                shape(count, members, cells, kind=BF16),
                [VMEM] * 2 + [HBM] * len(out), HBM,
                [pltpu.VMEM((last - first, members, cells), BF16),
                 pltpu.SemaphoreType.DMA((len(plan.piece_groups[piece]),))],
                1.2, f"{name}_{piece}", aliases={2: 0} if out else None,
            )(factors, parts[piece][which], *out)]
        return out[0]

    smoothed = apply(ens_factors, 0, "smoothed")
    ensemble_grad = apply(cot_factors, 1, "ensemble_grad")

    carry = jnp.zeros((members, members), F32)
    for level in range(levels):
        other = exchange(own, "tm", blocks, 1 << level)
        if level < levels - 1:
            own, carry = call(
                functools.partial(pass_kernel, level),
                [square] * 2, [VMEM] * 5, [VMEM] * 2, [], 0.4, f"pass_{level}",
            )(own, other, carry, uppers[level], befores[level])
    mine = call(
        functools.partial(final_kernel, plan, levels - 1, scale),
        shape(half, members, members),
        [VMEM] * 8, VMEM, [], 1.5, "transform_grad",
    )(whole, own, other, carry, befores[-1], halves, follow, steps)
    transform_grad = call(
        functools.partial(place_kernel, half),
        shape(count, members, members),
        [VMEM] * 2, HBM, [pltpu.SemaphoreType.DMA((2,))], 0.5, "place",
    )(mine, exchange(mine, "space", lanes, 1))
    return (smoothed, ensemble_grad, transform_grad)


def solution(mesh):
    return jax.shard_map(
        shards,
        mesh=mesh,
        in_specs=(P("tm", None, "space"), P("tm", None, "space"), P("tm", None, None)),
        out_specs=(P("tm", None, "space"), P("tm", None, "space"), P("tm", None, None)),
        check_vma=False,
    )
```

```python
import functools
import math

import jax
import jax.numpy as jnp
from jax import lax
from jax.experimental import pallas as pl
from jax.experimental.pallas import tpu as pltpu
from jax.sharding import PartitionSpec as P

F32 = jnp.float32
BF16 = jnp.bfloat16
VMEM = pl.BlockSpec(memory_space=pltpu.VMEM)
HBM = pl.BlockSpec(memory_space=pltpu.HBM)
ANY = pl.BlockSpec(memory_space=pl.ANY)
DEPTH = 256
PIECES = 3
NORMAL = (((1,), (0,)), ((), ()))
ROWS = (((1,), (1,)), ((), ()))


def split(value):
    high = value.astype(BF16)
    return high, (value - high.astype(F32)).astype(BF16)


def mul(left, right, dims=NORMAL):
    return lax.dot_general(left, right, dims, preferred_element_type=F32)


def mul_pairs(left, right, dims=NORMAL):
    return mul(left[0], right[0], dims) + (
        mul(left[0], right[1], dims) + mul(left[1], right[0], dims)
    )


def mul_exact(left, right, dims=NORMAL):
    return mul_pairs(split(left), split(right), dims)


def product_of(factors):
    while len(factors) > 1:
        joined = [mul_exact(*factors[at : at + 2]) for at in range(0, len(factors) - 1, 2)]
        factors = joined + factors[len(joined) * 2 :]
    return factors[0]


def suffix_scan(ref, count, members, stop):
    width = 1
    while width < stop:
        for start in range(0, count, 2 * width):
            middle = start + width
            if middle < count:
                rows = slice(start * members, middle * members)
                ref[rows] = mul_exact(ref[rows], ref[middle * members : (middle + 1) * members])
        width *= 2


class Plan:
    def __init__(self, count, members):
        self.count, self.members = count, members
        self.stack = DEPTH // members
        self.groups = [
            (start, min(start + self.stack, count)) for start in range(0, count, self.stack)
        ]
        bounds = [-(-len(self.groups) * at // PIECES) for at in range(PIECES + 1)]
        self.piece_groups = [self.groups[a:b] for a, b in zip(bounds, bounds[1:])]
        self.pieces = [(part[0][0], part[-1][1]) for part in self.piece_groups]
        self.first_group = bounds[:-1]
        self.widths = [-(-(stop - start) * members // 128) * 128 for start, stop in self.groups]
        self.width = sum(self.widths)

    def lanes(self, at):
        start = sum(self.widths[:at])
        return slice(start, start + self.widths[at])

    def rows(self, first, last):
        return slice(first * self.members, last * self.members)


def on_blocks(members, size):
    rows = lax.broadcasted_iota(jnp.int32, (size, size), 0) // members
    columns = lax.broadcasted_iota(jnp.int32, (size, size), 1) // members
    return rows == columns


def loads(values, buffer, sems, first, last):
    copies = [
        pltpu.make_async_copy(values.at[at], buffer.at[at - first], sems.at[at - first])
        for at in range(first, last)
    ]
    for copy in copies:
        copy.start()
    return copies


def chain_kernel(plan, transforms, ensembles, cotangents, suffixes, total, steps, ens, cot, kept, runs, sems, ens_sem, cot_sem):
    count, members = plan.count, plan.members
    reads = loads(transforms, kept, sems, 0, count)
    more = loads(ensembles, ens, ens_sem, *plan.pieces[0])
    more += loads(cotangents, cot, cot_sem, *plan.pieces[0])
    for at, copy in enumerate(reads):
        copy.wait()
        suffixes[plan.rows(at, at + 1)] = kept[at]
        if at + 1 < count:
            runs[plan.rows(at + 1, at + 2)] = kept[at].T
    suffix_scan(suffixes, count, members, count)
    total[...] = suffixes[plan.rows(0, 1)]
    number = 0
    width = 1
    while width < count:
        for middle in range(width, count, 2 * width):
            size = min(width, count - middle)
            for side, part in enumerate(split(runs[plan.rows(middle, middle + size)])):
                steps[side, plan.rows(number, number + size)] = part
            number += size
        for start in range(2 * width, count, 2 * width):
            if start + width < count:
                rows = plan.rows(start + width, min(start + 2 * width, count))
                runs[rows] = mul_exact(runs[rows], runs[plan.rows(start + width - 1, start + width)])
        width *= 2
    for copy in more:
        copy.wait()


def count_steps(count):
    total = 0
    width = 1
    while width < count:
        total += sum(min(width, count - middle) for middle in range(width, count, 2 * width))
        width *= 2
    return total


def gram_kernel(plan, piece, *refs):
    members = plan.members
    ens, cot, suffixes = refs[:3]
    refs = refs[3:]
    last = piece == PIECES - 1
    copies = []
    if last:
        earlier, refs = refs[: 2 * piece], refs[2 * piece :]
        _, grams, offsets = refs
    else:
        ensembles, cotangents, _, grams, offsets, next_ens, next_cot, ens_sem, cot_sem = refs
        copies = loads(ensembles, next_ens, ens_sem, *plan.pieces[piece + 1])
        copies += loads(cotangents, next_cot, cot_sem, *plan.pieces[piece + 1])
    base = plan.pieces[piece][0]
    offset = jnp.zeros((members, members), F32)
    first = plan.first_group[piece]
    if last:
        for at in range(piece):
            group = plan.first_group[at]
            lanes = slice(plan.lanes(group).start, plan.lanes(plan.first_group[at + 1]).start)
            grams[:, lanes] = earlier[2 * at][...]
            offset = offset + earlier[2 * at + 1][...]
        origin = 0
    else:
        origin = plan.lanes(first).start
    for at, (start, stop) in enumerate(plan.piece_groups[piece]):
        size = (stop - start) * members
        stacked = [ref[start - base : stop - base].reshape(size, ref.shape[2]) for ref in (cot, ens)]
        wide = jnp.where(on_blocks(members, size), mul(*stacked, ROWS), 0.0)
        gram = wide[:members]
        for i in range(1, stop - start):
            gram = gram + wide[i * members : (i + 1) * members]
        offset = offset + mul_exact(gram, suffixes[plan.rows(start, stop)])
        lanes = plan.lanes(first + at)
        width = lanes.stop - lanes.start
        grams[:, lanes.start - origin : lanes.stop - origin] = jnp.pad(gram, ((0, 0), (0, width - size)))
    offsets[...] = offset
    for copy in copies:
        copy.wait()


def upper_half(level):
    return lax.rem(lax.axis_index("tm") // (1 << level), 2) == 1


def join_kernel(level, total, other, later, before, _, new_total, new_later, new_before, upper_total):
    upper = upper_half(level)
    left = jnp.where(upper, other[...], total[...])
    right = jnp.where(upper, total[...], other[...])
    new_total[...] = mul_exact(left, right)
    upper_total[...] = right
    new_later[...] = jnp.where(upper, later[...], mul_exact(later[...], other[...]))
    new_before[...] = jnp.where(upper, mul_exact(other[...], before[...]), before[...])


def sum_kernel(number, *refs):
    out = refs[-1]
    total = refs[0][...]
    for ref in refs[1:number]:
        total = total + ref[...]
    out[...] = total


def pass_kernel(level, own, other, carry, upper_total, before, _, new_own, new_carry):
    upper = upper_half(level)
    left = jnp.where(upper, other[...], own[...])
    right = jnp.where(upper, own[...], other[...])
    new_own[...] = mul_exact(left, upper_total[...]) + right
    new_carry[...] = carry[...] + jnp.where(upper, mul_exact(left, before[...]), 0.0)


def carry_kernel(plan, level, suffixes, later, other, _, ens_factors, cot_factors, follow, __):
    count, members = plan.count, plan.members
    entering = later[...]
    entering = jnp.where(upper_half(level), entering, mul_exact(entering, other[...]))
    mask = on_blocks(members, plan.stack * members)
    repeated = split(jnp.concatenate([entering] * plan.stack, axis=1))
    for at, (start, stop) in enumerate(plan.groups):
        size = (stop - start) * members
        wide = mul_pairs(split(suffixes[plan.rows(start, stop)]), repeated)
        part = jnp.where(mask[:size, :size], wide[:, :size], 0.0)
        cot_factors[at, :size, :size] = part.astype(BF16)
        ens_factors[at, :size, :size] = part.T.astype(BF16)
        first = max(start - 1, 0)
        kept = wide[(first + 1 - start) * members :, :members]
        for side, value in enumerate(split(kept)):
            follow[side, plan.rows(first, stop - 1)] = value
    for side, value in enumerate(split(entering)):
        follow[side, plan.rows(count - 1, count)] = value


def apply_kernel(plan, pieces, factors, *refs):
    out, marker, out_buf, out_sem = refs[-4:]
    members = plan.members
    marker[...] = jnp.zeros_like(marker)
    base = plan.pieces[pieces[0]][0]
    chunk = out_buf.shape[2] // 2
    writes = []
    for values, piece in zip(refs, pieces):
        for at, (start, stop) in enumerate(plan.piece_groups[piece]):
            size = (stop - start) * members
            first = plan.pieces[piece][0]
            for side in range(2):
                columns = slice(side * chunk, (side + 1) * chunk)
                stacked = values[start - first : stop - first, :, columns].reshape(size, chunk)
                result = mul(factors[plan.first_group[piece] + at, :size, :size], stacked)
                out_buf[start - base : stop - base, :, columns] = result.astype(BF16).reshape(
                    stop - start, members, chunk
                )
                copy = pltpu.make_async_copy(
                    out_buf.at[start - base : stop - base, :, columns],
                    out.at[start:stop, :, columns],
                    out_sem.at[len(writes)],
                )
                copy.start()
                writes.append(copy)
    for copy in writes:
        copy.wait()


def final_kernel(plan, level, scale, number, *refs):
    messages = refs[:number]
    other, carry, before, follow, steps, _, out, buffer, sems = refs[number:]
    count, members = plan.count, plan.members
    entering = carry[...] + jnp.where(
        upper_half(level), mul_exact(other[...], before[...]), 0.0
    )
    totals = []
    for at, (start, stop) in enumerate(plan.groups):
        wide = messages[0][:, plan.lanes(at)]
        for ref in messages[1:]:
            wide = wide + ref[:, plan.lanes(at)]
        tall = wide.T
        for i in range(stop - start):
            totals.append(tall[i * members : (i + 1) * members])
    totals[0] = totals[0] + entering.T
    number = 0
    width = 1
    while width < count:
        for start in range(width, count, 2 * width):
            size = min(width, count - start)
            rows = plan.rows(number, number + size)
            added = mul_pairs((steps[0, rows], steps[1, rows]), split(totals[start - 1]))
            for at in range(size):
                totals[start + at] = totals[start + at] + added[at * members : (at + 1) * members]
            number += size
        width *= 2
    copies = []
    for at in range(count):
        rows = plan.rows(at, at + 1)
        buffer[at] = mul_pairs(split(totals[at]), (follow[0, rows], follow[1, rows]), ROWS) * scale
        copy = pltpu.make_async_copy(buffer.at[at], out.at[at], sems.at[at])
        copy.start()
        copies.append(copy)
    for copy in copies:
        copy.wait()


def call(kernel, outs, ins, out_specs, scratch, micros, name, limit=16, aliases=None):
    return pl.pallas_call(
        kernel,
        out_shape=outs,
        in_specs=ins,
        out_specs=out_specs,
        scratch_shapes=scratch,
        input_output_aliases=aliases or {},
        compiler_params=pltpu.CompilerParams(vmem_limit_bytes=limit << 20),
        cost_estimate=pl.CostEstimate(
            flops=0, bytes_accessed=int(micros * 3.6e6), transcendentals=0
        ),
        name=name,
    )


def shape(*dims, kind=F32):
    return jax.ShapeDtypeStruct(dims, kind)


def shards(ensembles, cotangents, transforms):
    count, members, cells = ensembles.shape
    blocks, lanes = lax.axis_size("tm"), lax.axis_size("space")
    chips = lanes // 2
    scale = 1.0 / math.sqrt(cells * lanes * count * blocks)
    plan = Plan(count, members)
    levels = blocks.bit_length() - 1
    square = shape(members, members)
    ensembles, cotangents, transforms = (
        pltpu.with_memory_space_constraint(value, pltpu.HBM)
        for value in (ensembles, cotangents, transforms)
    )

    def exchange(value, axis, size, bit):
        return lax.ppermute(value, axis, [(at, at ^ bit) for at in range(size)])

    def around(value):
        return [
            lax.ppermute(value, "space", [(at, (at + 2 * d) % lanes) for at in range(lanes)])
            for d in range(1, chips)
        ]

    def loaded(piece):
        first, last = plan.pieces[piece]
        return [shape(last - first, members, cells, kind=BF16)] * 2

    def sems(piece):
        first, last = plan.pieces[piece]
        return [pltpu.SemaphoreType.DMA((last - first,))] * 2

    steps_shape = shape(2, count_steps(count) * members, members, kind=BF16)
    suffixes, total, steps, *first_part = call(
        functools.partial(chain_kernel, plan),
        [shape(count * members, members), square, steps_shape] + loaded(0),
        [HBM] * 3, [VMEM] * 5,
        [pltpu.VMEM((count, members, members), F32), pltpu.VMEM((count * members, members), F32),
         pltpu.SemaphoreType.DMA((count,))] + sems(0), 2, "transform_chain",
    )(transforms, ensembles, cotangents)

    later = before = jnp.eye(members, dtype=F32)
    parts, grams, uppers, befores = [first_part], [], [], []
    done = suffixes
    for level in range(levels):
        other = exchange(total, "tm", blocks, 1 << level)
        if level < PIECES - 1:
            first, last = plan.first_group[level : level + 2]
            width = plan.lanes(last).start - plan.lanes(first).start
            *sums, ens, cot = call(
                functools.partial(gram_kernel, plan, level),
                [shape(members, width), square] + loaded(level + 1),
                [VMEM] * 3 + [HBM] * 2 + [ANY], [VMEM] * 4, sems(level + 1), 1.5, f"gram_{level}",
            )(*parts[-1], suffixes, ensembles, cotangents, done)
            parts.append((ens, cot))
            grams += sums
            done = sums[1]
        befores.append(before)
        if level < levels - 1:
            total, later, before, upper = call(
                functools.partial(join_kernel, level),
                [square] * 4, [VMEM] * 4 + [ANY], [VMEM] * 4, [], 0.3, f"join_{level}",
            )(total, other, later, before, done)
            uppers.append(upper)
            done = later
    gram, offset = call(
        functools.partial(gram_kernel, plan, PIECES - 1),
        [shape(members, plan.width), square],
        [VMEM] * (3 + len(grams)) + [ANY], [VMEM] * 2, [], 1.5, "gram_last",
    )(*parts[-1], suffixes, *grams, done)
    offset_core = exchange(offset, "space", lanes, 1)

    size = plan.stack * members
    ens_factors, cot_factors, follow, gram = call(
        functools.partial(carry_kernel, plan, levels - 1),
        [shape(len(plan.groups), size, size, kind=BF16)] * 2
        + [shape(2, count * members, members, kind=BF16), shape(members, plan.width)],
        [VMEM] * 3 + [ANY], [VMEM] * 3 + [ANY], [], 1.5, "carries", aliases={3: 3},
    )(suffixes, later, other, gram)
    gram_core = exchange(gram, "space", lanes, 1)

    def add(values, after, name):
        return call(
            functools.partial(sum_kernel, len(values)), shape(*values[0].shape),
            [VMEM] * len(values) + [ANY], VMEM, [], 0.1, name,
        )(*values, after)

    offset = add([offset, offset_core], follow, "chip_offset")
    offsets = [offset] + around(offset)

    def apply(factors, which, pieces, out, after, name):
        first, last = plan.pieces[pieces[0]][0], plan.pieces[pieces[-1]][1]
        number = 2 * sum(len(plan.piece_groups[piece]) for piece in pieces)
        return call(
            functools.partial(apply_kernel, plan, pieces),
            [shape(count, members, cells, kind=BF16), shape(8, 128)],
            [VMEM] * (1 + len(pieces)) + [ANY] + [HBM] * len(out), [HBM, VMEM],
            [pltpu.VMEM((last - first, members, cells), BF16),
             pltpu.SemaphoreType.DMA((number,))],
            1.5, name, aliases={2 + len(pieces): 0} if out else None,
        )(factors, *(parts[piece][which] for piece in pieces), after, *out)

    later_pieces = tuple(range(1, PIECES))
    smoothed, done = apply(ens_factors, 0, (0,), (), offset, "smoothed_0")
    own = add(offsets, done, "own_offset")
    gram = add([gram, gram_core], done, "chip_gram")
    grams = [gram] + around(gram)
    carry = jnp.zeros((members, members), F32)
    for level in range(levels):
        other = exchange(own, "tm", blocks, 1 << level)
        if level == 0:
            smoothed, done = apply(ens_factors, 0, later_pieces, (smoothed,), own, "smoothed_1")
        if level == 1:
            ensemble_grad, done = apply(cot_factors, 1, (0,), (), own, "ensemble_grad_0")
        if level == 2:
            ensemble_grad, done = apply(
                cot_factors, 1, later_pieces, (ensemble_grad,), own, "ensemble_grad_1"
            )
        if level < levels - 1:
            own, carry = call(
                functools.partial(pass_kernel, level),
                [square] * 2, [VMEM] * 5 + [ANY], [VMEM] * 2, [], 0.3, f"pass_{level}",
            )(own, other, carry, uppers[level], befores[level], done)
    transform_grad = call(
        functools.partial(final_kernel, plan, levels - 1, scale, chips),
        shape(count, members, members),
        [VMEM] * (chips + 5) + [ANY], HBM,
        [pltpu.VMEM((count, members, members), F32), pltpu.SemaphoreType.DMA((count,))],
        2, "transform_grad",
    )(*grams, other, carry, befores[-1], follow, steps, done)
    return (smoothed, ensemble_grad, transform_grad)


def solution(mesh):
    return jax.shard_map(
        shards,
        mesh=mesh,
        in_specs=(P("tm", None, "space"), P("tm", None, "space"), P("tm", None, None)),
        out_specs=(P("tm", None, "space"), P("tm", None, "space"), P("tm", None, None)),
        check_vma=False,
    )
```

```python
import functools
import math

import jax
import jax.numpy as jnp
from jax import lax
from jax.experimental import pallas as pl
from jax.experimental.pallas import tpu as pltpu
from jax.sharding import PartitionSpec as P

F32 = jnp.float32
BF16 = jnp.bfloat16
VMEM = pl.BlockSpec(memory_space=pltpu.VMEM)
HBM = pl.BlockSpec(memory_space=pltpu.HBM)
ANY = pl.BlockSpec(memory_space=pl.ANY)
DEPTH = 256
PIECES = 3
NORMAL = (((1,), (0,)), ((), ()))
ROWS = (((1,), (1,)), ((), ()))


def split(value):
    high = value.astype(BF16)
    return high, (value - high.astype(F32)).astype(BF16)


def mul(left, right, dims=NORMAL):
    return lax.dot_general(left, right, dims, preferred_element_type=F32)


def mul_pairs(left, right, dims=NORMAL):
    return mul(left[0], right[0], dims) + (
        mul(left[0], right[1], dims) + mul(left[1], right[0], dims)
    )


def mul_exact(left, right, dims=NORMAL):
    return mul_pairs(split(left), split(right), dims)


def product_of(factors):
    while len(factors) > 1:
        joined = [mul_exact(*factors[at : at + 2]) for at in range(0, len(factors) - 1, 2)]
        factors = joined + factors[len(joined) * 2 :]
    return factors[0]


def suffix_scan(ref, count, members, stop):
    width = 1
    while width < stop:
        for start in range(0, count, 2 * width):
            middle = start + width
            if middle < count:
                rows = slice(start * members, middle * members)
                ref[rows] = mul_exact(ref[rows], ref[middle * members : (middle + 1) * members])
        width *= 2


class Plan:
    def __init__(self, count, members):
        self.count, self.members = count, members
        self.stack = DEPTH // members
        self.groups = [
            (start, min(start + self.stack, count)) for start in range(0, count, self.stack)
        ]
        bounds = [-(-len(self.groups) * at // PIECES) for at in range(PIECES + 1)]
        self.piece_groups = [self.groups[a:b] for a, b in zip(bounds, bounds[1:])]
        self.pieces = [(part[0][0], part[-1][1]) for part in self.piece_groups]
        self.first_group = bounds[:-1]
        self.widths = [-(-(stop - start) * members // 128) * 128 for start, stop in self.groups]
        self.width = sum(self.widths)

    def lanes(self, at):
        start = sum(self.widths[:at])
        return slice(start, start + self.widths[at])

    def rows(self, first, last):
        return slice(first * self.members, last * self.members)


def on_blocks(members, size):
    rows = lax.broadcasted_iota(jnp.int32, (size, size), 0) // members
    columns = lax.broadcasted_iota(jnp.int32, (size, size), 1) // members
    return rows == columns


def loads(values, buffers, sems, plan):
    copies = []
    for (base, _), buffer, groups in zip(plan.pieces, buffers, plan.piece_groups):
        for start, stop in groups:
            part = buffer.at[start - base : stop - base]
            copies.append(pltpu.make_async_copy(values.at[start:stop], part, sems.at[len(copies)]))
    for copy in copies:
        copy.start()
    return copies


def chain_kernel(plan, transforms, ensembles, cotangents, suffixes, total, steps, *refs):
    count, members = plan.count, plan.members
    kept, runs, sem, ens_sem, cot_sem = refs[2 * PIECES :]
    read = pltpu.make_async_copy(transforms, kept, sem)
    read.start()
    more = loads(ensembles, refs[:PIECES], ens_sem, plan)
    more += loads(cotangents, refs[PIECES : 2 * PIECES], cot_sem, plan)
    read.wait()
    for at in range(count):
        suffixes[plan.rows(at, at + 1)] = kept[at]
        if at + 1 < count:
            runs[plan.rows(at + 1, at + 2)] = kept[at].T
    suffix_scan(suffixes, count, members, count)
    total[...] = suffixes[plan.rows(0, 1)]
    number = 0
    width = 1
    while width < count:
        for middle in range(width, count, 2 * width):
            size = min(width, count - middle)
            for side, part in enumerate(split(runs[plan.rows(middle, middle + size)])):
                steps[side, plan.rows(number, number + size)] = part
            number += size
        for start in range(2 * width, count, 2 * width):
            if start + width < count:
                rows = plan.rows(start + width, min(start + 2 * width, count))
                runs[rows] = mul_exact(runs[rows], runs[plan.rows(start + width - 1, start + width)])
        width *= 2
    for copy in more:
        copy.wait()


def count_steps(count):
    total = 0
    width = 1
    while width < count:
        total += sum(min(width, count - middle) for middle in range(width, count, 2 * width))
        width *= 2
    return total


def gram_kernel(plan, piece, *refs):
    members = plan.members
    ens, cot, suffixes = refs[:3]
    refs = refs[3:]
    last = piece == PIECES - 1
    if last:
        earlier, refs = refs[: 2 * piece], refs[2 * piece :]
    _, grams, offsets = refs
    base = plan.pieces[piece][0]
    offset = jnp.zeros((members, members), F32)
    first = plan.first_group[piece]
    if last:
        for at in range(piece):
            group = plan.first_group[at]
            lanes = slice(plan.lanes(group).start, plan.lanes(plan.first_group[at + 1]).start)
            grams[:, lanes] = earlier[2 * at][...]
            offset = offset + earlier[2 * at + 1][...]
        origin = 0
    else:
        origin = plan.lanes(first).start
    for at, (start, stop) in enumerate(plan.piece_groups[piece]):
        size = (stop - start) * members
        stacked = [ref[start - base : stop - base].reshape(size, ref.shape[2]) for ref in (cot, ens)]
        wide = jnp.where(on_blocks(members, size), mul(*stacked, ROWS), 0.0)
        gram = wide[:members]
        for i in range(1, stop - start):
            gram = gram + wide[i * members : (i + 1) * members]
        offset = offset + mul_exact(gram, suffixes[plan.rows(start, stop)])
        lanes = plan.lanes(first + at)
        width = lanes.stop - lanes.start
        grams[:, lanes.start - origin : lanes.stop - origin] = jnp.pad(gram, ((0, 0), (0, width - size)))
    offsets[...] = offset


def upper_half(level):
    return lax.rem(lax.axis_index("tm") // (1 << level), 2) == 1


def join_kernel(level, total, other, later, before, _, new_total, new_later, new_before, upper_total):
    upper = upper_half(level)
    left = jnp.where(upper, other[...], total[...])
    right = jnp.where(upper, total[...], other[...])
    new_total[...] = mul_exact(left, right)
    upper_total[...] = right
    new_later[...] = jnp.where(upper, later[...], mul_exact(later[...], other[...]))
    new_before[...] = jnp.where(upper, mul_exact(other[...], before[...]), before[...])


def sum_kernel(number, *refs):
    out = refs[-2]
    total = refs[0][...]
    for ref in refs[1:number]:
        total = total + ref[...]
    out[...] = total


def pass_kernel(level, own, other, carry, upper_total, before, _, new_own, new_carry):
    upper = upper_half(level)
    left = jnp.where(upper, other[...], own[...])
    right = jnp.where(upper, own[...], other[...])
    new_own[...] = mul_exact(left, upper_total[...]) + right
    new_carry[...] = carry[...] + jnp.where(upper, mul_exact(left, before[...]), 0.0)


def carry_kernel(plan, level, suffixes, later, other, _, ens_factors, cot_factors, follow):
    count, members = plan.count, plan.members
    entering = later[...]
    entering = jnp.where(upper_half(level), entering, mul_exact(entering, other[...]))
    mask = on_blocks(members, plan.stack * members)
    repeated = split(jnp.concatenate([entering] * plan.stack, axis=1))
    for at, (start, stop) in enumerate(plan.groups):
        size = (stop - start) * members
        wide = mul_pairs(split(suffixes[plan.rows(start, stop)]), repeated)
        part = jnp.where(mask[:size, :size], wide[:, :size], 0.0)
        cot_factors[at, :size, :size] = part.astype(BF16)
        ens_factors[at, :size, :size] = part.T.astype(BF16)
        first = max(start - 1, 0)
        kept = wide[(first + 1 - start) * members :, :members]
        for side, value in enumerate(split(kept)):
            follow[side, plan.rows(first, stop - 1)] = value
    for side, value in enumerate(split(entering)):
        follow[side, plan.rows(count - 1, count)] = value


def apply_kernel(plan, pieces, factors, *refs):
    out, marker, out_buf, out_sem = refs[-4:]
    members = plan.members
    marker[...] = jnp.zeros_like(marker)
    base = plan.pieces[pieces[0]][0]
    chunk = out_buf.shape[2] // 2
    writes = []
    for values, piece in zip(refs, pieces):
        for at, (start, stop) in enumerate(plan.piece_groups[piece]):
            size = (stop - start) * members
            first = plan.pieces[piece][0]
            for side in range(2):
                columns = slice(side * chunk, (side + 1) * chunk)
                stacked = values[start - first : stop - first, :, columns].reshape(size, chunk)
                result = mul(factors[plan.first_group[piece] + at, :size, :size], stacked)
                out_buf[start - base : stop - base, :, columns] = result.astype(BF16).reshape(
                    stop - start, members, chunk
                )
                copy = pltpu.make_async_copy(
                    out_buf.at[start - base : stop - base, :, columns],
                    out.at[start:stop, :, columns],
                    out_sem.at[len(writes)],
                )
                copy.start()
                writes.append(copy)
    for copy in writes:
        copy.wait()


def final_kernel(plan, level, scale, number, *refs):
    messages = refs[:number]
    other, carry, before, follow, steps, _, out, buffer, sems = refs[number:]
    count, members = plan.count, plan.members
    entering = carry[...] + jnp.where(
        upper_half(level), mul_exact(other[...], before[...]), 0.0
    )
    totals = []
    for at, (start, stop) in enumerate(plan.groups):
        wide = messages[0][:, plan.lanes(at)]
        for ref in messages[1:]:
            wide = wide + ref[:, plan.lanes(at)]
        tall = wide.T
        for i in range(stop - start):
            totals.append(tall[i * members : (i + 1) * members])
    totals[0] = totals[0] + entering.T
    number = 0
    width = 1
    while width < count:
        for start in range(width, count, 2 * width):
            size = min(width, count - start)
            rows = plan.rows(number, number + size)
            added = mul_pairs((steps[0, rows], steps[1, rows]), split(totals[start - 1]))
            for at in range(size):
                totals[start + at] = totals[start + at] + added[at * members : (at + 1) * members]
            number += size
        width *= 2
    copies = []
    for at in range(count):
        rows = plan.rows(at, at + 1)
        buffer[at] = mul_pairs(split(totals[at]), (follow[0, rows], follow[1, rows]), ROWS) * scale
        copy = pltpu.make_async_copy(buffer.at[at], out.at[at], sems.at[at])
        copy.start()
        copies.append(copy)
    for copy in copies:
        copy.wait()


def call(kernel, outs, ins, out_specs, scratch, micros, name, limit=16, aliases=None):
    return pl.pallas_call(
        kernel,
        out_shape=outs,
        in_specs=ins,
        out_specs=out_specs,
        scratch_shapes=scratch,
        input_output_aliases=aliases or {},
        compiler_params=pltpu.CompilerParams(vmem_limit_bytes=limit << 20),
        cost_estimate=pl.CostEstimate(
            flops=0, bytes_accessed=int(micros * 3.6e6), transcendentals=0
        ),
        name=name,
    )


def shape(*dims, kind=F32):
    return jax.ShapeDtypeStruct(dims, kind)


def shards(ensembles, cotangents, transforms):
    count, members, cells = ensembles.shape
    blocks, lanes = lax.axis_size("tm"), lax.axis_size("space")
    chips = lanes // 2
    scale = 1.0 / math.sqrt(cells * lanes * count * blocks)
    plan = Plan(count, members)
    levels = blocks.bit_length() - 1
    square = shape(members, members)
    ensembles, cotangents, transforms = (
        pltpu.with_memory_space_constraint(value, pltpu.HBM)
        for value in (ensembles, cotangents, transforms)
    )

    def exchange(value, axis, size, bit):
        return lax.ppermute(value, axis, [(at, at ^ bit) for at in range(size)])

    def around(value):
        return [
            lax.ppermute(value, "space", [(at, (at + 2 * d) % lanes) for at in range(lanes)])
            for d in range(1, chips)
        ]

    steps_shape = shape(2, count_steps(count) * members, members, kind=BF16)
    buffers = [shape(last - first, members, cells, kind=BF16) for first, last in plan.pieces] * 2
    suffixes, total, steps, *loaded = call(
        functools.partial(chain_kernel, plan),
        [shape(count * members, members), square, steps_shape] + buffers,
        [HBM] * 3, [VMEM] * (3 + len(buffers)),
        [pltpu.VMEM((count, members, members), F32), pltpu.VMEM((count * members, members), F32),
         pltpu.SemaphoreType.DMA] + [pltpu.SemaphoreType.DMA((len(plan.groups),))] * 2,
        4, "transform_chain",
    )(transforms, ensembles, cotangents)
    parts = list(zip(loaded[:PIECES], loaded[PIECES:]))

    later = before = jnp.eye(members, dtype=F32)
    grams, uppers, befores = [], [], []
    done = suffixes
    for level in range(levels):
        other = exchange(total, "tm", blocks, 1 << level)
        if level < PIECES - 1:
            first, last = plan.first_group[level : level + 2]
            width = plan.lanes(last).start - plan.lanes(first).start
            sums = call(
                functools.partial(gram_kernel, plan, level),
                [shape(members, width), square],
                [VMEM] * 3 + [ANY], [VMEM] * 2, [], 1.5, f"gram_{level}",
            )(*parts[level], suffixes, done)
            grams += sums
            done = sums[1]
        befores.append(before)
        if level < levels - 1:
            total, later, before, upper = call(
                functools.partial(join_kernel, level),
                [square] * 4, [VMEM] * 4 + [ANY], [VMEM] * 4, [], 0.3, f"join_{level}",
            )(total, other, later, before, done)
            uppers.append(upper)
            done = later
    gram, offset = call(
        functools.partial(gram_kernel, plan, PIECES - 1),
        [shape(members, plan.width), square],
        [VMEM] * (3 + len(grams)) + [ANY], [VMEM] * 2, [], 1.5, "gram_last",
    )(*parts[-1], suffixes, *grams, done)
    offset_core = exchange(offset, "space", lanes, 1)

    size = plan.stack * members
    ens_factors, cot_factors, follow = call(
        functools.partial(carry_kernel, plan, levels - 1),
        [shape(len(plan.groups), size, size, kind=BF16)] * 2
        + [shape(2, count * members, members, kind=BF16)],
        [VMEM] * 3 + [ANY], [VMEM] * 3, [], 1.5, "carries",
    )(suffixes, later, other, offset)

    def add(values, after, name, through):
        number = len(values)
        return call(
            functools.partial(sum_kernel, number),
            [shape(*values[0].shape), shape(*through.shape)],
            [VMEM] * number + [ANY] * 2, [VMEM, ANY], [], 0.1, name, aliases={number + 1: 1},
        )(*values, after, through)

    offset, gram = add([offset, offset_core], follow, "chip_offset", gram)
    gram_core = exchange(gram, "space", lanes, 1)
    offsets = [offset] + around(offset)

    def apply(factors, which, pieces, out, after, name):
        first, last = plan.pieces[pieces[0]][0], plan.pieces[pieces[-1]][1]
        number = 2 * sum(len(plan.piece_groups[piece]) for piece in pieces)
        return call(
            functools.partial(apply_kernel, plan, pieces),
            [shape(count, members, cells, kind=BF16), shape(8, 128)],
            [VMEM] * (1 + len(pieces)) + [ANY] + [HBM] * len(out), [HBM, VMEM],
            [pltpu.VMEM((last - first, members, cells), BF16),
             pltpu.SemaphoreType.DMA((number,))],
            1.5, name, aliases={2 + len(pieces): 0} if out else None,
        )(factors, *(parts[piece][which] for piece in pieces), after, *out)

    later_pieces = tuple(range(1, PIECES))
    smoothed, done = apply(ens_factors, 0, (0,), (), offset, "smoothed_0")
    own, gram_core = add(offsets, done, "own_offset", gram_core)
    gram = gram + gram_core
    grams = [gram] + around(gram)
    carry = jnp.zeros((members, members), F32)
    for level in range(levels):
        other = exchange(own, "tm", blocks, 1 << level)
        if level == 0:
            smoothed, done = apply(ens_factors, 0, later_pieces, (smoothed,), own, "smoothed_1")
        if level == 1:
            ensemble_grad, done = apply(cot_factors, 1, (0,), (), own, "ensemble_grad_0")
        if level == 2:
            ensemble_grad, done = apply(
                cot_factors, 1, later_pieces, (ensemble_grad,), own, "ensemble_grad_1"
            )
        if level < levels - 1:
            own, carry = call(
                functools.partial(pass_kernel, level),
                [square] * 2, [VMEM] * 5 + [ANY], [VMEM] * 2, [], 0.3, f"pass_{level}",
            )(own, other, carry, uppers[level], befores[level], done)
    transform_grad = call(
        functools.partial(final_kernel, plan, levels - 1, scale, chips),
        shape(count, members, members),
        [VMEM] * (chips + 5) + [ANY], HBM,
        [pltpu.VMEM((count, members, members), F32), pltpu.SemaphoreType.DMA((count,))],
        2, "transform_grad",
    )(*grams, other, carry, befores[-1], follow, steps, done)
    return (smoothed, ensemble_grad, transform_grad)


def solution(mesh):
    return jax.shard_map(
        shards,
        mesh=mesh,
        in_specs=(P("tm", None, "space"), P("tm", None, "space"), P("tm", None, None)),
        out_specs=(P("tm", None, "space"), P("tm", None, "space"), P("tm", None, None)),
        check_vma=False,
    )
```

```python
import functools
import math

import jax
import jax.numpy as jnp
from jax import lax
from jax.experimental import pallas as pl
from jax.experimental.pallas import tpu as pltpu
from jax.sharding import PartitionSpec as P

F32 = jnp.float32
BF16 = jnp.bfloat16
VMEM = pl.BlockSpec(memory_space=pltpu.VMEM)
HBM = pl.BlockSpec(memory_space=pltpu.HBM)
ANY = pl.BlockSpec(memory_space=pl.ANY)
DEPTH = 256
PIECES = 3
NORMAL = (((1,), (0,)), ((), ()))
ROWS = (((1,), (1,)), ((), ()))


def split(value):
    high = value.astype(BF16)
    return high, (value - high.astype(F32)).astype(BF16)


def mul(left, right, dims=NORMAL):
    return lax.dot_general(left, right, dims, preferred_element_type=F32)


def mul_pairs(left, right, dims=NORMAL):
    return mul(left[0], right[0], dims) + (
        mul(left[0], right[1], dims) + mul(left[1], right[0], dims)
    )


def mul_exact(left, right, dims=NORMAL):
    return mul_pairs(split(left), split(right), dims)


def product_of(factors):
    while len(factors) > 1:
        joined = [mul_exact(*factors[at : at + 2]) for at in range(0, len(factors) - 1, 2)]
        factors = joined + factors[len(joined) * 2 :]
    return factors[0]


def suffix_scan(ref, count, members, stop):
    width = 1
    while width < stop:
        for start in range(0, count, 2 * width):
            middle = start + width
            if middle < count:
                rows = slice(start * members, middle * members)
                ref[rows] = mul_exact(ref[rows], ref[middle * members : (middle + 1) * members])
        width *= 2


class Plan:
    def __init__(self, count, members):
        self.count, self.members = count, members
        self.stack = DEPTH // members
        self.groups = [
            (start, min(start + self.stack, count)) for start in range(0, count, self.stack)
        ]
        bounds = [len(self.groups) * at // PIECES for at in range(PIECES + 1)]
        self.piece_groups = [self.groups[a:b] for a, b in zip(bounds, bounds[1:])]
        self.pieces = [(part[0][0], part[-1][1]) for part in self.piece_groups]
        self.first_group = bounds[:-1]
        self.widths = [-(-(stop - start) * members // 128) * 128 for start, stop in self.groups]
        self.width = sum(self.widths)

    def lanes(self, at):
        start = sum(self.widths[:at])
        return slice(start, start + self.widths[at])

    def rows(self, first, last):
        return slice(first * self.members, last * self.members)


def on_blocks(members, size):
    rows = lax.broadcasted_iota(jnp.int32, (size, size), 0) // members
    columns = lax.broadcasted_iota(jnp.int32, (size, size), 1) // members
    return rows == columns


def loads(plan, piece, values, buffer, sems):
    base = plan.pieces[piece][0]
    copies = [
        pltpu.make_async_copy(values.at[start:stop], buffer.at[start - base : stop - base], sems.at[at])
        for at, (start, stop) in enumerate(plan.piece_groups[piece])
    ]
    for copy in copies:
        copy.start()
    return copies


def chain_kernel(
    plan, transforms, ensembles, cotangents, suffixes, total, kept, ens, cot, sem, ens_sem, cot_sem
):
    count, members = plan.count, plan.members
    read = pltpu.make_async_copy(transforms, kept, sem)
    read.start()
    read.wait()
    more = loads(plan, 0, ensembles, ens, ens_sem) + loads(plan, 0, cotangents, cot, cot_sem)
    for at in range(count):
        suffixes[plan.rows(at, at + 1)] = kept[at]
    suffix_scan(suffixes, count, members, count)
    total[...] = suffixes[plan.rows(0, 1)]
    for copy in more:
        copy.wait()


def windows_kernel(plan, kept, _, steps, runs):
    count = plan.count
    for at in range(count - 1):
        runs[plan.rows(at + 1, at + 2)] = kept[at].T
    number = 0
    width = 1
    while width < count:
        for middle in range(width, count, 2 * width):
            size = min(width, count - middle)
            for side, part in enumerate(split(runs[plan.rows(middle, middle + size)])):
                steps[side, plan.rows(number, number + size)] = part
            number += size
        for start in range(2 * width, count, 2 * width):
            if start + width < count:
                rows = plan.rows(start + width, min(start + 2 * width, count))
                runs[rows] = mul_exact(runs[rows], runs[plan.rows(start + width - 1, start + width)])
        width *= 2


def count_steps(count):
    total = 0
    width = 1
    while width < count:
        total += sum(min(width, count - middle) for middle in range(width, count, 2 * width))
        width *= 2
    return total


def core_index():
    return lax.rem(lax.axis_index("space"), 2)


def gram_of(plan, piece, cot, ens, suffixes, whole, ready=lambda: None):
    members = plan.members
    base = plan.pieces[piece][0]
    offset = jnp.zeros((members, members), F32)
    for at, (start, stop) in enumerate(plan.piece_groups[piece]):
        ready()
        size = (stop - start) * members
        stacked = [ref[start - base : stop - base].reshape(size, ref.shape[2]) for ref in (cot, ens)]
        wide = jnp.where(on_blocks(members, size), mul(*stacked, ROWS), 0.0)
        gram = wide[:members]
        for i in range(1, stop - start):
            gram = gram + wide[i * members : (i + 1) * members]
        offset = offset + mul_exact(gram, suffixes[plan.rows(start, stop)])
        lanes = plan.lanes(plan.first_group[piece] + at)
        width = lanes.stop - lanes.start
        whole[:, lanes] = jnp.pad(gram, ((0, 0), (0, width - size)))
    return offset


def early_gram_kernel(plan, ensembles, cotangents, suffixes, ens, cot, whole, offset, *refs):
    buffers, sems = refs[: 2 * (PIECES - 1)], refs[2 * (PIECES - 1) :]
    copies = []
    for piece in range(1, PIECES):
        pair = buffers[2 * piece - 2 : 2 * piece]
        own = sems[2 * piece - 2 : 2 * piece]
        copies.append(list(zip(
            loads(plan, piece, ensembles, pair[0], own[0]),
            loads(plan, piece, cotangents, pair[1], own[1]),
        )))
    total = gram_of(plan, 0, cot, ens, suffixes, whole)
    for piece in range(1, PIECES - 1):
        waiting = iter(copies[piece - 1])

        def ready():
            for copy in next(waiting):
                copy.wait()

        ens, cot = buffers[2 * piece - 2 : 2 * piece]
        total = total + gram_of(plan, piece, cot, ens, suffixes, whole, ready)
    offset[...] = total
    for pair in copies[-1]:
        for copy in pair:
            copy.wait()


def late_gram_kernel(
    plan, ens, cot, suffixes, early, offset, _,
    gram_kept, gram_sent, offset_kept, offset_sent, whole, offsets,
):
    members = plan.members
    whole[:, : early.shape[1]] = early[...]
    offsets[...] = offset[...] + gram_of(plan, PIECES - 1, cot, ens, suffixes, whole)
    half = members // 2
    core = lax.rem(lax.axis_index("space"), 2)
    mine, other = pl.ds(core * half, half), pl.ds((1 - core) * half, half)
    gram_kept[...] = whole[mine]
    gram_sent[...] = whole[other]
    offset_kept[...] = offsets[mine]
    offset_sent[...] = offsets[other]


def upper_half(level):
    return lax.rem(lax.axis_index("tm") // (1 << level), 2) == 1


def join_kernel(level, total, other, later, before, _, new_total, new_later, new_before, upper_total):
    upper = upper_half(level)
    left = jnp.where(upper, other[...], total[...])
    right = jnp.where(upper, total[...], other[...])
    new_total[...] = mul_exact(left, right)
    upper_total[...] = right
    new_later[...] = jnp.where(upper, later[...], mul_exact(later[...], other[...]))
    new_before[...] = jnp.where(upper, mul_exact(other[...], before[...]), before[...])


def sum_kernel(number, out, *refs):
    total = refs[0][...]
    for ref in refs[1:number]:
        total = total + ref[...]
    refs[out][...] = total


def pass_kernel(level, last, own, other, carry, upper_total, before, *refs):
    new_own, new_carry = refs[2:4] if last else refs[1:3]
    upper = upper_half(level)
    left = jnp.where(upper, other[...], own[...])
    right = jnp.where(upper, own[...], other[...])
    new_own[...] = mul_exact(left, upper_total[...]) + right
    new_carry[...] = carry[...] + jnp.where(upper, mul_exact(left, before[...]), 0.0)


def last_pass_kernel(level, other, carry, before, _, new_carry):
    added = mul_exact(other[...], before[...])
    new_carry[...] = carry[...] + jnp.where(upper_half(level), added, 0.0)


def carry_kernel(plan, level, suffixes, later, other, _, ens_factors, cot_factors, follow):
    count, members = plan.count, plan.members
    entering = later[...]
    entering = jnp.where(upper_half(level), entering, mul_exact(entering, other[...]))
    mask = on_blocks(members, plan.stack * members)
    repeated = split(jnp.concatenate([entering] * plan.stack, axis=1))
    for at, (start, stop) in enumerate(plan.groups):
        size = (stop - start) * members
        wide = mul_pairs(split(suffixes[plan.rows(start, stop)]), repeated)
        part = jnp.where(mask[:size, :size], wide[:, :size], 0.0)
        cot_factors[at, :size, :size] = part.astype(BF16)
        ens_factors[at, :size, :size] = part.T.astype(BF16)
        first = max(start - 1, 0)
        kept = wide[(first + 1 - start) * members :, :members]
        for side, value in enumerate(split(kept)):
            follow[side, plan.rows(first, stop - 1)] = value
    for side, value in enumerate(split(entering)):
        follow[side, plan.rows(count - 1, count)] = value


def apply_kernel(plan, pieces, factors, *refs):
    out, marker, out_buf, out_sem = refs[-4:]
    members = plan.members
    marker[...] = jnp.zeros_like(marker)
    base = plan.pieces[pieces[0]][0]
    chunk = out_buf.shape[2] // 2
    writes = []
    for values, piece in zip(refs, pieces):
        first = plan.pieces[piece][0]
        for at, (start, stop) in enumerate(plan.piece_groups[piece]):
            size = (stop - start) * members
            for side in range(2):
                columns = slice(side * chunk, (side + 1) * chunk)
                stacked = values[start - first : stop - first, :, columns].reshape(size, chunk)
                result = mul(factors[plan.first_group[piece] + at, :size, :size], stacked)
                out_buf[start - base : stop - base, :, columns] = result.astype(BF16).reshape(
                    stop - start, members, chunk
                )
                copy = pltpu.make_async_copy(
                    out_buf.at[start - base : stop - base, :, columns],
                    out.at[start:stop, :, columns],
                    out_sem.at[len(writes)],
                )
                copy.start()
                writes.append(copy)
    for copy in writes:
        copy.wait()


def final_kernel(
    plan, scale, gram_mine, gram_other, carry_mine, carry_other, follow, steps, _, out, buffer, sems
):
    count, members = plan.count, plan.members
    first = lax.rem(lax.axis_index("space"), 2) == 0

    def whole(mine, other):
        return jnp.concatenate([jnp.where(first, mine, other), jnp.where(first, other, mine)], axis=0)

    totals = []
    for at, (start, stop) in enumerate(plan.groups):
        lanes = plan.lanes(at)
        tall = whole(gram_mine[:, lanes], gram_other[:, lanes]).T
        for i in range(stop - start):
            totals.append(tall[i * members : (i + 1) * members])
    totals[0] = totals[0] + whole(carry_mine[...], carry_other[...]).T
    number = 0
    width = 1
    while width < count:
        for start in range(width, count, 2 * width):
            size = min(width, count - start)
            rows = plan.rows(number, number + size)
            added = mul_pairs((steps[0, rows], steps[1, rows]), split(totals[start - 1]))
            for at in range(size):
                totals[start + at] = totals[start + at] + added[at * members : (at + 1) * members]
            number += size
        width *= 2
    copies = []
    for at in range(count):
        rows = plan.rows(at, at + 1)
        buffer[at] = mul_pairs(split(totals[at]), (follow[0, rows], follow[1, rows]), ROWS) * scale
        copy = pltpu.make_async_copy(buffer.at[at], out.at[at], sems.at[at])
        copy.start()
        copies.append(copy)
    for copy in copies:
        copy.wait()


def call(kernel, outs, ins, out_specs, scratch, micros, name, limit=16, aliases=None):
    return pl.pallas_call(
        kernel,
        out_shape=outs,
        in_specs=ins,
        out_specs=out_specs,
        scratch_shapes=scratch,
        input_output_aliases=aliases or {},
        compiler_params=pltpu.CompilerParams(vmem_limit_bytes=limit << 20),
        cost_estimate=pl.CostEstimate(
            flops=0, bytes_accessed=int(micros * 3.6e6), transcendentals=0
        ),
        name=name,
    )


def shape(*dims, kind=F32):
    return jax.ShapeDtypeStruct(dims, kind)


def shards(ensembles, cotangents, transforms):
    count, members, cells = ensembles.shape
    blocks, lanes = lax.axis_size("tm"), lax.axis_size("space")
    chips = lanes // 2
    scale = 1.0 / math.sqrt(cells * lanes * count * blocks)
    plan = Plan(count, members)
    levels = blocks.bit_length() - 1
    square = shape(members, members)
    ensembles, cotangents, transforms = (
        pltpu.with_memory_space_constraint(value, pltpu.HBM)
        for value in (ensembles, cotangents, transforms)
    )

    def exchange(value, axis, size, bit):
        return lax.ppermute(value, axis, [(at, at ^ bit) for at in range(size)])

    def around(value):
        return [
            lax.ppermute(value, "space", [(at, (at + 2 * d) % lanes) for at in range(lanes)])
            for d in range(1, chips)
        ]

    def piece_shape(piece):
        first, last = plan.pieces[piece]
        return shape(last - first, members, cells, kind=BF16)

    def piece_sems(piece):
        return [pltpu.SemaphoreType.DMA((len(plan.piece_groups[piece]),))] * 2

    suffixes, total, kept, *first_part = call(
        functools.partial(chain_kernel, plan),
        [shape(count * members, members), square, shape(count, members, members)] + [piece_shape(0)] * 2,
        [HBM] * 3, [VMEM] * 5, [pltpu.SemaphoreType.DMA] + piece_sems(0), 3.5, "transform_chain",
    )(transforms, ensembles, cotangents)

    half = members // 2
    later = before = jnp.eye(members, dtype=F32)
    uppers, befores = [], []

    def join(level, total, other, later, before, after):
        befores.append(before)
        *new, upper = call(
            functools.partial(join_kernel, level),
            [square] * 4, [VMEM] * 4 + [ANY], [VMEM] * 4, [], 0.3, f"join_{level}",
        )(total, other, later, before, after)
        uppers.append(upper)
        return new

    def add(values, after, name, *through):
        number = len(values)
        return call(
            functools.partial(sum_kernel, number, number + 1 + len(through)),
            [shape(*values[0].shape)] + [shape(*value.shape) for value in through],
            [VMEM] * number + [ANY] * (1 + len(through)), [VMEM] + [ANY] * len(through), [], 0.1, name,
            aliases={number + 1 + at: 1 + at for at in range(len(through))},
        )(*values, after, *through)

    other = exchange(total, "tm", blocks, 1)
    early_width = plan.lanes(plan.first_group[-1]).start
    early, offset, *loaded = call(
        functools.partial(early_gram_kernel, plan),
        [shape(members, early_width), square]
        + [piece_shape(piece) for piece in range(1, PIECES) for _ in range(2)],
        [HBM] * 2 + [VMEM] * 3, [VMEM] * (2 * PIECES),
        [sem for piece in range(1, PIECES) for sem in piece_sems(piece)], 3, "early_gram",
    )(ensembles, cotangents, suffixes, *first_part)
    parts = [first_part] + [loaded[at : at + 2] for at in range(0, len(loaded), 2)]
    total, later, before = join(0, total, other, later, before, offset)

    other = exchange(total, "tm", blocks, 2)
    gram, gram_sent, offset, offset_sent = call(
        functools.partial(late_gram_kernel, plan),
        [shape(half, plan.width)] * 2 + [shape(half, members)] * 2,
        [VMEM] * 5 + [ANY], [VMEM] * 4,
        [pltpu.VMEM((members, plan.width), F32), pltpu.VMEM((members, members), F32)],
        1.2, "late_gram",
    )(*parts[-1], suffixes, early, offset, total)
    offset_core = exchange(offset_sent, "space", lanes, 1)
    for level in range(1, levels - 1):
        total, later, before = join(level, total, other, later, before, offset)
        other = exchange(total, "tm", blocks, 2 << level)
    befores.append(before)

    offset, gram_sent = add([offset, offset_core], total, "chip_offset", gram_sent)
    gram_core = exchange(gram_sent, "space", lanes, 1)
    offsets = [offset] + around(offset)
    steps = call(
        functools.partial(windows_kernel, plan),
        shape(2, count_steps(count) * members, members, kind=BF16), [VMEM, ANY], VMEM,
        [pltpu.VMEM((count * members, members), F32)], 1.5, "windows",
    )(kept, offset)
    own, gram_core, other = add(offsets, steps, "own_offset", gram_core, other)

    other_own = exchange(own, "tm", blocks, 1)
    gram = gram + gram_core
    grams = around(gram)
    size = plan.stack * members
    ens_factors, cot_factors, follow = call(
        functools.partial(carry_kernel, plan, levels - 1),
        [shape(len(plan.groups), size, size, kind=BF16)] * 2
        + [shape(2, count * members, members, kind=BF16)],
        [VMEM] * 3 + [ANY], [VMEM] * 3, [], 1.0, "carries",
    )(suffixes, later, other, own)

    def apply(factors, which, pieces, out, after, name):
        first, last = plan.pieces[pieces[0]][0], plan.pieces[pieces[-1]][1]
        number = 2 * sum(len(plan.piece_groups[piece]) for piece in pieces)
        return call(
            functools.partial(apply_kernel, plan, pieces),
            [shape(count, members, cells, kind=BF16), shape(8, 128)],
            [VMEM] * (1 + len(pieces)) + [ANY] + [HBM] * len(out), [HBM, VMEM],
            [pltpu.VMEM((last - first, members, cells), BF16), pltpu.SemaphoreType.DMA((number,))],
            1.8, name, aliases={2 + len(pieces): 0} if out else None,
        )(factors, *(parts[piece][which] for piece in pieces), after, *out)

    front, rear = tuple(range(PIECES - 1)), (PIECES - 1,)
    smoothed, done = apply(ens_factors, 0, front, (), follow, "smoothed_0")
    carry = jnp.zeros((half, members), F32)
    for level in range(levels - 1):
        last = level == levels - 2
        own, carry, *rest = call(
            functools.partial(pass_kernel, level, last),
            [shape(half, members)] * 2 + [shape(half, plan.width)] * last,
            [VMEM] * 5 + [ANY] * (1 + last), [VMEM] * 2 + [ANY] * last, [], 0.3, f"pass_{level}",
            aliases={6: 2} if last else None,
        )(own, other_own, carry, uppers[level], befores[level], done, *grams[:last])
        other_own = exchange(own, "tm", blocks, 2 << level)
        if level == 0:
            smoothed, done = apply(ens_factors, 0, rear, (smoothed,), own, "smoothed_1")
        if level == 1:
            ensemble_grad, done = apply(cot_factors, 1, front, (), own, "ensemble_grad_0")
    grams[0] = rest[0]
    for part in grams:
        gram = gram + part
    gram_other = exchange(gram, "space", lanes, 1)
    carry = call(
        functools.partial(last_pass_kernel, levels - 1),
        shape(half, members), [VMEM] * 3 + [ANY], VMEM, [], 0.2, "pass_last",
    )(other_own, carry, befores[-1], done)
    carry_other = exchange(carry, "space", lanes, 1)
    ensemble_grad, done = apply(cot_factors, 1, rear, (ensemble_grad,), carry, "ensemble_grad_1")
    transform_grad = call(
        functools.partial(final_kernel, plan, scale),
        shape(count, members, members),
        [VMEM] * 6 + [ANY], HBM,
        [pltpu.VMEM((count, members, members), F32), pltpu.SemaphoreType.DMA((count,))],
        2.5, "transform_grad",
    )(gram, gram_other, carry, carry_other, follow, steps, done)
    return (smoothed, ensemble_grad, transform_grad)


def solution(mesh):
    return jax.shard_map(
        shards,
        mesh=mesh,
        in_specs=(P("tm", None, "space"), P("tm", None, "space"), P("tm", None, None)),
        out_specs=(P("tm", None, "space"), P("tm", None, "space"), P("tm", None, None)),
        check_vma=False,
    )
```

```python
import functools
import math

import jax
import jax.numpy as jnp
from jax import lax
from jax.experimental import pallas as pl
from jax.experimental.pallas import tpu as pltpu
from jax.sharding import PartitionSpec as P

F32 = jnp.float32
BF16 = jnp.bfloat16
VMEM = pl.BlockSpec(memory_space=pltpu.VMEM)
HBM = pl.BlockSpec(memory_space=pltpu.HBM)
ANY = pl.BlockSpec(memory_space=pl.ANY)
DEPTH = 256
PIECES = 3
NORMAL = (((1,), (0,)), ((), ()))
ROWS = (((1,), (1,)), ((), ()))


def split(value):
    high = value.astype(BF16)
    return high, (value - high.astype(F32)).astype(BF16)


def mul(left, right, dims=NORMAL):
    return lax.dot_general(left, right, dims, preferred_element_type=F32)


def mul_pairs(left, right, dims=NORMAL):
    return mul(left[0], right[0], dims) + (
        mul(left[0], right[1], dims) + mul(left[1], right[0], dims)
    )


def mul_exact(left, right, dims=NORMAL):
    return mul_pairs(split(left), split(right), dims)


def product_of(factors):
    while len(factors) > 1:
        joined = [mul_exact(*factors[at : at + 2]) for at in range(0, len(factors) - 1, 2)]
        factors = joined + factors[len(joined) * 2 :]
    return factors[0]


def suffix_scan(ref, count, members, stop):
    width = 1
    while width < stop:
        for start in range(0, count, 2 * width):
            middle = start + width
            if middle < count:
                rows = slice(start * members, middle * members)
                ref[rows] = mul_exact(ref[rows], ref[middle * members : (middle + 1) * members])
        width *= 2


class Plan:
    def __init__(self, count, members):
        self.count, self.members = count, members
        self.stack = DEPTH // members
        self.groups = [
            (start, min(start + self.stack, count)) for start in range(0, count, self.stack)
        ]
        bounds = [len(self.groups) * at // PIECES for at in range(PIECES + 1)]
        self.piece_groups = [self.groups[a:b] for a, b in zip(bounds, bounds[1:])]
        self.pieces = [(part[0][0], part[-1][1]) for part in self.piece_groups]
        self.first_group = bounds[:-1]
        self.widths = [-(-(stop - start) * members // 128) * 128 for start, stop in self.groups]
        self.width = sum(self.widths)

    def lanes(self, at):
        start = sum(self.widths[:at])
        return slice(start, start + self.widths[at])

    def rows(self, first, last):
        return slice(first * self.members, last * self.members)


def on_blocks(members, size):
    rows = lax.broadcasted_iota(jnp.int32, (size, size), 0) // members
    columns = lax.broadcasted_iota(jnp.int32, (size, size), 1) // members
    return rows == columns


def loads(plan, piece, values, buffer, sems):
    base = plan.pieces[piece][0]
    copies = [
        pltpu.make_async_copy(values.at[start:stop], buffer.at[start - base : stop - base], sems.at[at])
        for at, (start, stop) in enumerate(plan.piece_groups[piece])
    ]
    for copy in copies:
        copy.start()
    return copies


def chain_kernel(
    plan, transforms, ensembles, cotangents, suffixes, total, kept, ens, cot, sem, ens_sem, cot_sem
):
    count, members = plan.count, plan.members
    read = pltpu.make_async_copy(transforms, kept, sem)
    read.start()
    read.wait()
    more = loads(plan, 0, ensembles, ens, ens_sem) + loads(plan, 0, cotangents, cot, cot_sem)
    for at in range(count):
        suffixes[plan.rows(at, at + 1)] = kept[at]
    suffix_scan(suffixes, count, members, count)
    total[...] = suffixes[plan.rows(0, 1)]
    for copy in more:
        copy.wait()


def windows_kernel(plan, kept, _, steps, runs):
    count = plan.count
    for at in range(count - 1):
        runs[plan.rows(at + 1, at + 2)] = kept[at].T
    number = 0
    width = 1
    while width < count:
        for middle in range(width, count, 2 * width):
            size = min(width, count - middle)
            for side, part in enumerate(split(runs[plan.rows(middle, middle + size)])):
                steps[side, plan.rows(number, number + size)] = part
            number += size
        for start in range(2 * width, count, 2 * width):
            if start + width < count:
                rows = plan.rows(start + width, min(start + 2 * width, count))
                runs[rows] = mul_exact(runs[rows], runs[plan.rows(start + width - 1, start + width)])
        width *= 2


def count_steps(count):
    total = 0
    width = 1
    while width < count:
        total += sum(min(width, count - middle) for middle in range(width, count, 2 * width))
        width *= 2
    return total


def core_index():
    return lax.rem(lax.axis_index("space"), 2)


def gram_of(plan, piece, cot, ens, suffixes, whole, ready=lambda: None):
    members = plan.members
    base = plan.pieces[piece][0]
    offset = jnp.zeros((members, members), F32)
    for at, (start, stop) in enumerate(plan.piece_groups[piece]):
        ready()
        size = (stop - start) * members
        stacked = [ref[start - base : stop - base].reshape(size, ref.shape[2]) for ref in (cot, ens)]
        wide = jnp.where(on_blocks(members, size), mul(*stacked, ROWS), 0.0)
        gram = wide[:members]
        for i in range(1, stop - start):
            gram = gram + wide[i * members : (i + 1) * members]
        offset = offset + mul_exact(gram, suffixes[plan.rows(start, stop)])
        lanes = plan.lanes(plan.first_group[piece] + at)
        width = lanes.stop - lanes.start
        whole[:, lanes] = jnp.pad(gram, ((0, 0), (0, width - size)))
    return offset


def early_gram_kernel(plan, ensembles, cotangents, suffixes, ens, cot, whole, offset, *refs):
    buffers, sems = refs[: 2 * (PIECES - 1)], refs[2 * (PIECES - 1) :]
    copies = []
    for piece in range(1, PIECES):
        pair = buffers[2 * piece - 2 : 2 * piece]
        own = sems[2 * piece - 2 : 2 * piece]
        copies.append(list(zip(
            loads(plan, piece, ensembles, pair[0], own[0]),
            loads(plan, piece, cotangents, pair[1], own[1]),
        )))
    total = gram_of(plan, 0, cot, ens, suffixes, whole)
    for piece in range(1, PIECES - 1):
        waiting = iter(copies[piece - 1])

        def ready():
            for copy in next(waiting):
                copy.wait()

        ens, cot = buffers[2 * piece - 2 : 2 * piece]
        total = total + gram_of(plan, piece, cot, ens, suffixes, whole, ready)
    offset[...] = total
    for pair in copies[-1]:
        for copy in pair:
            copy.wait()


def late_gram_kernel(plan, ens, cot, suffixes, early, offset, _, grams, offsets):
    grams[:, : early.shape[1]] = early[...]
    offsets[...] = offset[...] + gram_of(plan, PIECES - 1, cot, ens, suffixes, grams)


def chip_kernel(mine, other, _, __, offset, ___):
    offset[...] = mine[...] + other[...]


def upper_half(level):
    return lax.rem(lax.axis_index("tm") // (1 << level), 2) == 1


def join_kernel(level, total, other, later, before, _, new_total, new_later, new_before, upper_total):
    upper = upper_half(level)
    left = jnp.where(upper, other[...], total[...])
    right = jnp.where(upper, total[...], other[...])
    new_total[...] = mul_exact(left, right)
    upper_total[...] = right
    new_later[...] = jnp.where(upper, later[...], mul_exact(later[...], other[...]))
    new_before[...] = jnp.where(upper, mul_exact(other[...], before[...]), before[...])


def pass_kernel(level, own, other, carry, upper_total, before, *refs):
    new_own, new_carry = refs[len(refs) // 2 : len(refs) // 2 + 2] if len(refs) > 3 else refs[1:]
    upper = upper_half(level)
    left = jnp.where(upper, other[...], own[...])
    right = jnp.where(upper, own[...], other[...])
    new_own[...] = mul_exact(left, upper_total[...]) + right
    new_carry[...] = carry[...] + jnp.where(upper, mul_exact(left, before[...]), 0.0)


def last_pass_kernel(level, other, carry, before, _, __, new_carry, ___):
    added = mul_exact(other[...], before[...])
    new_carry[...] = carry[...] + jnp.where(upper_half(level), added, 0.0)


def enter_kernel(level, number, later, other, *refs):
    values, (_, __, entering, own, ___) = refs[:number], refs[number:]
    joined = mul_exact(later[...], other[...])
    entering[...] = jnp.where(upper_half(level), later[...], joined)
    total = values[0][...]
    for ref in values[1:]:
        total = total + ref[...]
    own[...] = total


def carry_kernel(plan, suffixes, mine, other, _, ens_factors, cot_factors, follow):
    count, members = plan.count, plan.members
    entering = jnp.where(lax.rem(lax.axis_index("space"), 2) == 1, mine[...], other[...])
    mask = on_blocks(members, plan.stack * members)
    repeated = split(jnp.concatenate([entering] * plan.stack, axis=1))
    for at, (start, stop) in enumerate(plan.groups):
        size = (stop - start) * members
        wide = mul_pairs(split(suffixes[plan.rows(start, stop)]), repeated)
        part = jnp.where(mask[:size, :size], wide[:, :size], 0.0)
        cot_factors[at, :size, :size] = part.astype(BF16)
        ens_factors[at, :size, :size] = part.T.astype(BF16)
        first = max(start - 1, 0)
        kept = wide[(first + 1 - start) * members :, :members]
        for side, value in enumerate(split(kept)):
            follow[side, plan.rows(first, stop - 1)] = value
    for side, value in enumerate(split(entering)):
        follow[side, plan.rows(count - 1, count)] = value


def apply_kernel(plan, pieces, factors, *refs):
    out, marker, out_buf, out_sem = refs[-4:]
    members = plan.members
    marker[...] = jnp.zeros_like(marker)
    base = plan.pieces[pieces[0]][0]
    chunk = out_buf.shape[2] // 2
    writes = []
    for values, piece in zip(refs, pieces):
        first = plan.pieces[piece][0]
        for at, (start, stop) in enumerate(plan.piece_groups[piece]):
            size = (stop - start) * members
            for side in range(2):
                columns = slice(side * chunk, (side + 1) * chunk)
                stacked = values[start - first : stop - first, :, columns].reshape(size, chunk)
                result = mul(factors[plan.first_group[piece] + at, :size, :size], stacked)
                out_buf[start - base : stop - base, :, columns] = result.astype(BF16).reshape(
                    stop - start, members, chunk
                )
                copy = pltpu.make_async_copy(
                    out_buf.at[start - base : stop - base, :, columns],
                    out.at[start:stop, :, columns],
                    out_sem.at[len(writes)],
                )
                copy.start()
                writes.append(copy)
    for copy in writes:
        copy.wait()


def final_kernel(
    plan, scale, gram_mine, gram_other, carry_mine, carry_other, follow, steps, _, out, buffer, sems
):
    count, members = plan.count, plan.members
    first = lax.rem(lax.axis_index("space"), 2) == 0
    carry = jnp.where(first, carry_other[...], carry_mine[...])

    totals = []
    for at, (start, stop) in enumerate(plan.groups):
        lanes = plan.lanes(at)
        tall = jnp.where(first, gram_mine[:, lanes], gram_other[:, lanes]).T
        for i in range(stop - start):
            totals.append(tall[i * members : (i + 1) * members])
    totals[0] = totals[0] + carry.T
    number = 0
    width = 1
    while width < count:
        for start in range(width, count, 2 * width):
            size = min(width, count - start)
            rows = plan.rows(number, number + size)
            added = mul_pairs((steps[0, rows], steps[1, rows]), split(totals[start - 1]))
            for at in range(size):
                totals[start + at] = totals[start + at] + added[at * members : (at + 1) * members]
            number += size
        width *= 2
    copies = []
    for at in range(count):
        rows = plan.rows(at, at + 1)
        buffer[at] = mul_pairs(split(totals[at]), (follow[0, rows], follow[1, rows]), ROWS) * scale
        copy = pltpu.make_async_copy(buffer.at[at], out.at[at], sems.at[at])
        copy.start()
        copies.append(copy)
    for copy in copies:
        copy.wait()


def call(kernel, outs, ins, out_specs, scratch, micros, name, limit=16, aliases=None):
    return pl.pallas_call(
        kernel,
        out_shape=outs,
        in_specs=ins,
        out_specs=out_specs,
        scratch_shapes=scratch,
        input_output_aliases=aliases or {},
        compiler_params=pltpu.CompilerParams(vmem_limit_bytes=limit << 20),
        cost_estimate=pl.CostEstimate(
            flops=0, bytes_accessed=int(micros * 3.6e6), transcendentals=0
        ),
        name=name,
    )


def shape(*dims, kind=F32):
    return jax.ShapeDtypeStruct(dims, kind)


def shards(ensembles, cotangents, transforms):
    count, members, cells = ensembles.shape
    blocks, lanes = lax.axis_size("tm"), lax.axis_size("space")
    chips = lanes // 2
    scale = 1.0 / math.sqrt(cells * lanes * count * blocks)
    plan = Plan(count, members)
    levels = blocks.bit_length() - 1
    square = shape(members, members)
    ensembles, cotangents, transforms = (
        pltpu.with_memory_space_constraint(value, pltpu.HBM)
        for value in (ensembles, cotangents, transforms)
    )

    def send(value, target, core):
        pairs = []
        for at in range(blocks * lanes):
            block, lane = divmod(at, lanes)
            if lane % 2 in core:
                block, lane = target(block, lane)
                pairs.append((at, block * lanes + lane))
        return lax.ppermute(value, ("tm", "space"), pairs)

    def exchange(value, bit):
        return send(value, lambda block, lane: (block ^ bit, lane), (1,))

    def hand_over(value, *core):
        return send(value, lambda block, lane: (block, lane ^ 1), core)

    def around(value, *core):
        return [
            send(value, lambda block, lane: (block, (lane + 2 * d) % lanes), core)
            for d in range(1, chips)
        ]

    def piece_shape(piece):
        first, last = plan.pieces[piece]
        return shape(last - first, members, cells, kind=BF16)

    def piece_sems(piece):
        return [pltpu.SemaphoreType.DMA((len(plan.piece_groups[piece]),))] * 2

    suffixes, total, kept, *first_part = call(
        functools.partial(chain_kernel, plan),
        [shape(count * members, members), square, shape(count, members, members)] + [piece_shape(0)] * 2,
        [HBM] * 3, [VMEM] * 5, [pltpu.SemaphoreType.DMA] + piece_sems(0), 3.5, "transform_chain",
    )(transforms, ensembles, cotangents)

    wide = shape(members, plan.width)
    later = before = jnp.eye(members, dtype=F32)
    uppers, befores = [], []

    def join(level, total, other, later, before, after):
        befores.append(before)
        *new, upper = call(
            functools.partial(join_kernel, level),
            [square] * 4, [VMEM] * 4 + [ANY], [VMEM] * 4, [], 3, f"join_{level}",
        )(total, other, later, before, after)
        uppers.append(upper)
        return new

    other = exchange(total, 1)
    early_width = plan.lanes(plan.first_group[-1]).start
    early, offset, *loaded = call(
        functools.partial(early_gram_kernel, plan),
        [shape(members, early_width), square]
        + [piece_shape(piece) for piece in range(1, PIECES) for _ in range(2)],
        [HBM] * 2 + [VMEM] * 3, [VMEM] * (2 * PIECES),
        [sem for piece in range(1, PIECES) for sem in piece_sems(piece)], 3, "early_gram",
    )(ensembles, cotangents, suffixes, *first_part)
    parts = [first_part] + [loaded[at : at + 2] for at in range(0, len(loaded), 2)]
    total, later, before = join(0, total, other, later, before, offset)

    other = exchange(total, 2)
    gram, offset = call(
        functools.partial(late_gram_kernel, plan),
        [wide, square], [VMEM] * 5 + [ANY], [VMEM] * 2, [], 1.2, "late_gram",
    )(*parts[-1], suffixes, early, offset, total)
    offset_core = hand_over(offset, 0)
    for level in range(1, levels - 1):
        total, later, before = join(level, total, other, later, before, gram)
        other = exchange(total, 2 << level)
    befores.append(before)
    offset, gram = call(
        chip_kernel, [square, wide], [VMEM] * 2 + [ANY] * 2, [VMEM, ANY], [], 0.2, "chip_offset",
        aliases={3: 1},
    )(offset, offset_core, total, gram)
    gram_core = hand_over(gram, 1)
    offsets = [offset] + around(offset, 1)

    steps = call(
        functools.partial(windows_kernel, plan),
        shape(2, count_steps(count) * members, members, kind=BF16), [VMEM, ANY], VMEM,
        [pltpu.VMEM((count * members, members), F32)], 10, "windows",
    )(kept, offset)
    entering, own, gram_core = call(
        functools.partial(enter_kernel, levels - 1, chips),
        [square] * 2 + [wide], [VMEM] * (2 + chips) + [ANY] * 2, [VMEM] * 2 + [ANY], [], 0.2,
        "entering", aliases={3 + chips: 2},
    )(later, other, *offsets, steps, gram_core)
    other_own = exchange(own, 1)
    gram = gram + gram_core
    grams = around(gram, 0)
    entering_core = hand_over(entering, 1)
    size = plan.stack * members
    ens_factors, cot_factors, follow = call(
        functools.partial(carry_kernel, plan),
        [shape(len(plan.groups), size, size, kind=BF16)] * 2
        + [shape(2, count * members, members, kind=BF16)],
        [VMEM] * 3 + [ANY], [VMEM] * 3, [], 0.1, "carries",
    )(suffixes, entering, entering_core, own)

    def apply(factors, which, pieces, out, after, name, micros):
        first, last = plan.pieces[pieces[0]][0], plan.pieces[pieces[-1]][1]
        number = 2 * sum(len(plan.piece_groups[piece]) for piece in pieces)
        return call(
            functools.partial(apply_kernel, plan, pieces),
            [shape(count, members, cells, kind=BF16), shape(8, 128)],
            [VMEM] * (1 + len(pieces)) + [ANY] + [HBM] * len(out), [HBM, VMEM],
            [pltpu.VMEM((last - first, members, cells), BF16), pltpu.SemaphoreType.DMA((number,))],
            micros, name, aliases={2 + len(pieces): 0} if out else None,
        )(factors, *(parts[piece][which] for piece in pieces), after, *out)

    front, rear = tuple(range(PIECES - 1)), (PIECES - 1,)
    smoothed, done = apply(ens_factors, 0, rear, (), follow, "smoothed_0", 0.1)
    carry = jnp.zeros((members, members), F32)
    for level in range(levels - 1):
        waits = level > 0
        own, carry, *rest = call(
            functools.partial(pass_kernel, level),
            [square] * 2 + [wide] * waits,
            [VMEM] * 5 + [ANY] * (1 + waits), [VMEM] * 2 + [ANY] * waits, [], 0.3, f"pass_{level}",
            aliases={6: 2} if waits else None,
        )(own, other_own, carry, uppers[level], befores[level], done, *grams[:waits])
        grams[:waits] = rest
        other_own = exchange(own, 2 << level)
        if level == 0:
            smoothed, done = apply(ens_factors, 0, front, (smoothed,), own, "smoothed_1", 2.4)
        if level == 1:
            ensemble_grad, done = apply(cot_factors, 1, front, (), own, "ensemble_grad_0", 2.4)
    carry, grams[0] = call(
        functools.partial(last_pass_kernel, levels - 1),
        [square, wide], [VMEM] * 3 + [ANY] * 2, [VMEM, ANY], [], 0.2, "pass_last",
        aliases={4: 1},
    )(other_own, carry, befores[-1], done, grams[0])
    for part in grams:
        gram = gram + part
    gram_other = hand_over(gram, 0)
    carry_other = hand_over(carry, 1)
    ensemble_grad, done = apply(cot_factors, 1, rear, (ensemble_grad,), carry, "ensemble_grad_1", 1.4)
    transform_grad = call(
        functools.partial(final_kernel, plan, scale),
        shape(count, members, members),
        [VMEM] * 6 + [ANY], HBM,
        [pltpu.VMEM((count, members, members), F32), pltpu.SemaphoreType.DMA((count,))],
        2.5, "transform_grad",
    )(gram, gram_other, carry, carry_other, follow, steps, done)
    return (smoothed, ensemble_grad, transform_grad)


def solution(mesh):
    return jax.shard_map(
        shards,
        mesh=mesh,
        in_specs=(P("tm", None, "space"), P("tm", None, "space"), P("tm", None, None)),
        out_specs=(P("tm", None, "space"), P("tm", None, "space"), P("tm", None, None)),
        check_vma=False,
    )
```

```python
import functools
import math

import jax
import jax.numpy as jnp
from jax import lax
from jax.experimental import pallas as pl
from jax.experimental.pallas import tpu as pltpu
from jax.sharding import PartitionSpec as P

F32 = jnp.float32
BF16 = jnp.bfloat16
VMEM = pl.BlockSpec(memory_space=pltpu.VMEM)
HBM = pl.BlockSpec(memory_space=pltpu.HBM)
ANY = pl.BlockSpec(memory_space=pl.ANY)
DEPTH = 256
PIECES = 3
NORMAL = (((1,), (0,)), ((), ()))
ROWS = (((1,), (1,)), ((), ()))


def split(value):
    high = value.astype(BF16)
    return high, (value - high.astype(F32)).astype(BF16)


def mul(left, right, dims=NORMAL):
    return lax.dot_general(left, right, dims, preferred_element_type=F32)


def mul_pairs(left, right, dims=NORMAL):
    return mul(left[0], right[0], dims) + (
        mul(left[0], right[1], dims) + mul(left[1], right[0], dims)
    )


def mul_exact(left, right, dims=NORMAL):
    return mul_pairs(split(left), split(right), dims)


def product_of(factors):
    while len(factors) > 1:
        joined = [mul_exact(*factors[at : at + 2]) for at in range(0, len(factors) - 1, 2)]
        factors = joined + factors[len(joined) * 2 :]
    return factors[0]


def suffix_scan(ref, count, members, stop):
    width = 1
    while width < stop:
        for start in range(0, count, 2 * width):
            middle = start + width
            if middle < count:
                rows = slice(start * members, middle * members)
                ref[rows] = mul_exact(ref[rows], ref[middle * members : (middle + 1) * members])
        width *= 2


class Plan:
    def __init__(self, count, members):
        self.count, self.members = count, members
        self.stack = DEPTH // members
        self.groups = [
            (start, min(start + self.stack, count)) for start in range(0, count, self.stack)
        ]
        bounds = [len(self.groups) * at // PIECES for at in range(PIECES + 1)]
        self.piece_groups = [self.groups[a:b] for a, b in zip(bounds, bounds[1:])]
        self.pieces = [(part[0][0], part[-1][1]) for part in self.piece_groups]
        self.first_group = bounds[:-1]
        self.widths = [-(-(stop - start) * members // 128) * 128 for start, stop in self.groups]
        self.width = sum(self.widths)

    def lanes(self, at):
        start = sum(self.widths[:at])
        return slice(start, start + self.widths[at])

    def rows(self, first, last):
        return slice(first * self.members, last * self.members)


def on_blocks(members, size):
    rows = lax.broadcasted_iota(jnp.int32, (size, size), 0) // members
    columns = lax.broadcasted_iota(jnp.int32, (size, size), 1) // members
    return rows == columns


def loads(plan, piece, values, buffer, sems):
    base = plan.pieces[piece][0]
    copies = [
        pltpu.make_async_copy(values.at[start:stop], buffer.at[start - base : stop - base], sems.at[at])
        for at, (start, stop) in enumerate(plan.piece_groups[piece])
    ]
    for copy in copies:
        copy.start()
    return copies


def chain_kernel(
    plan, transforms, ensembles, cotangents, suffixes, total, kept, ens, cot, sem, ens_sem, cot_sem
):
    count, members = plan.count, plan.members
    read = pltpu.make_async_copy(transforms, kept, sem)
    read.start()
    read.wait()
    more = loads(plan, 0, ensembles, ens, ens_sem) + loads(plan, 0, cotangents, cot, cot_sem)
    for at in range(count):
        suffixes[plan.rows(at, at + 1)] = kept[at]
    suffix_scan(suffixes, count, members, count)
    total[...] = suffixes[plan.rows(0, 1)]
    for copy in more:
        copy.wait()


def windows_kernel(plan, kept, _, steps, runs):
    count = plan.count
    for at in range(count - 1):
        runs[plan.rows(at + 1, at + 2)] = kept[at].T
    number = 0
    width = 1
    while width < count:
        for middle in range(width, count, 2 * width):
            size = min(width, count - middle)
            for side, part in enumerate(split(runs[plan.rows(middle, middle + size)])):
                steps[side, plan.rows(number, number + size)] = part
            number += size
        for start in range(2 * width, count, 2 * width):
            if start + width < count:
                rows = plan.rows(start + width, min(start + 2 * width, count))
                runs[rows] = mul_exact(runs[rows], runs[plan.rows(start + width - 1, start + width)])
        width *= 2


def count_steps(count):
    total = 0
    width = 1
    while width < count:
        total += sum(min(width, count - middle) for middle in range(width, count, 2 * width))
        width *= 2
    return total


def core_index():
    return lax.rem(lax.axis_index("space"), 2)


def gram_of(plan, piece, cot, ens, suffixes, whole, ready=lambda: None):
    members = plan.members
    base = plan.pieces[piece][0]
    offset = jnp.zeros((members, members), F32)
    for at, (start, stop) in enumerate(plan.piece_groups[piece]):
        ready()
        size = (stop - start) * members
        stacked = [ref[start - base : stop - base].reshape(size, ref.shape[2]) for ref in (cot, ens)]
        wide = jnp.where(on_blocks(members, size), mul(*stacked, ROWS), 0.0)
        gram = wide[:members]
        for i in range(1, stop - start):
            gram = gram + wide[i * members : (i + 1) * members]
        offset = offset + mul_exact(gram, suffixes[plan.rows(start, stop)])
        lanes = plan.lanes(plan.first_group[piece] + at)
        width = lanes.stop - lanes.start
        whole[:, lanes] = jnp.pad(gram, ((0, 0), (0, width - size)))
    return offset


def early_gram_kernel(plan, ensembles, cotangents, suffixes, ens, cot, whole, offset, *refs):
    buffers, sems = refs[: 2 * (PIECES - 1)], refs[2 * (PIECES - 1) :]
    copies = []
    for piece in range(1, PIECES):
        pair = buffers[2 * piece - 2 : 2 * piece]
        own = sems[2 * piece - 2 : 2 * piece]
        copies.append(list(zip(
            loads(plan, piece, ensembles, pair[0], own[0]),
            loads(plan, piece, cotangents, pair[1], own[1]),
        )))
    total = gram_of(plan, 0, cot, ens, suffixes, whole)
    for piece in range(1, PIECES - 1):
        waiting = iter(copies[piece - 1])

        def ready():
            for copy in next(waiting):
                copy.wait()

        ens, cot = buffers[2 * piece - 2 : 2 * piece]
        total = total + gram_of(plan, piece, cot, ens, suffixes, whole, ready)
    offset[...] = total
    for pair in copies[-1]:
        for copy in pair:
            copy.wait()


def late_gram_kernel(plan, ens, cot, suffixes, early, offset, _, grams, offsets):
    grams[:, : early.shape[1]] = early[...]
    offsets[...] = offset[...] + gram_of(plan, PIECES - 1, cot, ens, suffixes, grams)


def chip_kernel(mine, other, _, __, offset, ___):
    offset[...] = mine[...] + other[...]


def upper_half(level):
    return lax.rem(lax.axis_index("tm") // (1 << level), 2) == 1


def join_kernel(level, total, other, later, before, _, new_total, new_later, new_before, upper_total):
    upper = upper_half(level)
    left = jnp.where(upper, other[...], total[...])
    right = jnp.where(upper, total[...], other[...])
    new_total[...] = mul_exact(left, right)
    upper_total[...] = right
    new_later[...] = jnp.where(upper, later[...], mul_exact(later[...], other[...]))
    new_before[...] = jnp.where(upper, mul_exact(other[...], before[...]), before[...])


def pass_kernel(level, own, other, carry, upper_total, before, *refs):
    new_own, new_carry = refs[len(refs) // 2 : len(refs) // 2 + 2] if len(refs) > 3 else refs[1:]
    upper = upper_half(level)
    left = jnp.where(upper, other[...], own[...])
    right = jnp.where(upper, own[...], other[...])
    new_own[...] = mul_exact(left, upper_total[...]) + right
    new_carry[...] = carry[...] + jnp.where(upper, mul_exact(left, before[...]), 0.0)


def last_pass_kernel(level, other, carry, before, _, __, new_carry, ___):
    added = mul_exact(other[...], before[...])
    new_carry[...] = carry[...] + jnp.where(upper_half(level), added, 0.0)


def enter_kernel(level, number, later, other, *refs):
    values, (_, __, entering, own, ___) = refs[:number], refs[number:]
    joined = mul_exact(later[...], other[...])
    entering[...] = jnp.where(upper_half(level), later[...], joined)
    total = values[0][...]
    for ref in values[1:]:
        total = total + ref[...]
    own[...] = total


def carry_kernel(plan, suffixes, mine, other, _, ens_factors, cot_factors, follow):
    count, members = plan.count, plan.members
    entering = jnp.where(lax.rem(lax.axis_index("space"), 2) == 1, mine[...], other[...])
    mask = on_blocks(members, plan.stack * members)
    repeated = split(jnp.concatenate([entering] * plan.stack, axis=1))
    for at, (start, stop) in enumerate(plan.groups):
        size = (stop - start) * members
        wide = mul_pairs(split(suffixes[plan.rows(start, stop)]), repeated)
        part = jnp.where(mask[:size, :size], wide[:, :size], 0.0)
        cot_factors[at, :size, :size] = part.astype(BF16)
        ens_factors[at, :size, :size] = part.T.astype(BF16)
        first = max(start - 1, 0)
        kept = wide[(first + 1 - start) * members :, :members]
        for side, value in enumerate(split(kept)):
            follow[side, plan.rows(first, stop - 1)] = value
    for side, value in enumerate(split(entering)):
        follow[side, plan.rows(count - 1, count)] = value


def apply_kernel(plan, pieces, factors, *refs):
    out, marker, out_buf, out_sem = refs[-4:]
    members = plan.members
    marker[...] = jnp.zeros_like(marker)
    base = plan.pieces[pieces[0]][0]
    chunk = out_buf.shape[2] // 2
    writes = []
    for values, piece in zip(refs, pieces):
        first = plan.pieces[piece][0]
        for at, (start, stop) in enumerate(plan.piece_groups[piece]):
            size = (stop - start) * members
            for side in range(2):
                columns = slice(side * chunk, (side + 1) * chunk)
                stacked = values[start - first : stop - first, :, columns].reshape(size, chunk)
                result = mul(factors[plan.first_group[piece] + at, :size, :size], stacked)
                out_buf[start - base : stop - base, :, columns] = result.astype(BF16).reshape(
                    stop - start, members, chunk
                )
                copy = pltpu.make_async_copy(
                    out_buf.at[start - base : stop - base, :, columns],
                    out.at[start:stop, :, columns],
                    out_sem.at[len(writes)],
                )
                copy.start()
                writes.append(copy)
    for copy in writes:
        copy.wait()


def final_kernel(
    plan, scale, gram_mine, gram_other, carry_mine, carry_other, follow, steps, _, out, buffer, sems
):
    count, members = plan.count, plan.members
    first = lax.rem(lax.axis_index("space"), 2) == 0
    carry = jnp.where(first, carry_other[...], carry_mine[...])

    totals = []
    for at, (start, stop) in enumerate(plan.groups):
        lanes = plan.lanes(at)
        tall = jnp.where(first, gram_mine[:, lanes], gram_other[:, lanes]).T
        for i in range(stop - start):
            totals.append(tall[i * members : (i + 1) * members])
    totals[0] = totals[0] + carry.T
    number = 0
    width = 1
    while width < count:
        for start in range(width, count, 2 * width):
            size = min(width, count - start)
            rows = plan.rows(number, number + size)
            added = mul_pairs((steps[0, rows], steps[1, rows]), split(totals[start - 1]))
            for at in range(size):
                totals[start + at] = totals[start + at] + added[at * members : (at + 1) * members]
            number += size
        width *= 2
    copies = []
    for at in range(count):
        rows = plan.rows(at, at + 1)
        buffer[at] = mul_pairs(split(totals[at]), (follow[0, rows], follow[1, rows]), ROWS) * scale
        copy = pltpu.make_async_copy(buffer.at[at], out.at[at], sems.at[at])
        copy.start()
        copies.append(copy)
    for copy in copies:
        copy.wait()


def call(kernel, outs, ins, out_specs, scratch, micros, name, limit=16, aliases=None):
    return pl.pallas_call(
        kernel,
        out_shape=outs,
        in_specs=ins,
        out_specs=out_specs,
        scratch_shapes=scratch,
        input_output_aliases=aliases or {},
        compiler_params=pltpu.CompilerParams(vmem_limit_bytes=limit << 20),
        cost_estimate=pl.CostEstimate(
            flops=0, bytes_accessed=int(micros * 3.6e6), transcendentals=0
        ),
        name=name,
    )


def shape(*dims, kind=F32):
    return jax.ShapeDtypeStruct(dims, kind)


def shards(ensembles, cotangents, transforms):
    count, members, cells = ensembles.shape
    blocks, lanes = lax.axis_size("tm"), lax.axis_size("space")
    chips = lanes // 2
    scale = 1.0 / math.sqrt(cells * lanes * count * blocks)
    plan = Plan(count, members)
    levels = blocks.bit_length() - 1
    square = shape(members, members)
    ensembles, cotangents, transforms = (
        pltpu.with_memory_space_constraint(value, pltpu.HBM)
        for value in (ensembles, cotangents, transforms)
    )

    def send(value, target, core):
        pairs = []
        for at in range(blocks * lanes):
            block, lane = divmod(at, lanes)
            if lane % 2 in core:
                block, lane = target(block, lane)
            pairs.append((at, block * lanes + lane))
        return lax.ppermute(value, ("tm", "space"), pairs)

    def exchange(value, bit):
        return send(value, lambda block, lane: (block ^ bit, lane), (1,))

    def hand_over(value):
        return send(value, lambda block, lane: (block, lane ^ 1), (0, 1))

    def around(value, *core):
        return [
            send(value, lambda block, lane: (block, (lane + 2 * d) % lanes), core)
            for d in range(1, chips)
        ]

    def piece_shape(piece):
        first, last = plan.pieces[piece]
        return shape(last - first, members, cells, kind=BF16)

    def piece_sems(piece):
        return [pltpu.SemaphoreType.DMA((len(plan.piece_groups[piece]),))] * 2

    suffixes, total, kept, *first_part = call(
        functools.partial(chain_kernel, plan),
        [shape(count * members, members), square, shape(count, members, members)] + [piece_shape(0)] * 2,
        [HBM] * 3, [VMEM] * 5, [pltpu.SemaphoreType.DMA] + piece_sems(0), 3.5, "transform_chain",
    )(transforms, ensembles, cotangents)

    wide = shape(members, plan.width)
    later = before = jnp.eye(members, dtype=F32)
    uppers, befores = [], []

    def join(level, total, other, later, before, after):
        befores.append(before)
        *new, upper = call(
            functools.partial(join_kernel, level),
            [square] * 4, [VMEM] * 4 + [ANY], [VMEM] * 4, [], 3, f"join_{level}",
        )(total, other, later, before, after)
        uppers.append(upper)
        return new

    other = exchange(total, 1)
    early_width = plan.lanes(plan.first_group[-1]).start
    early, offset, *loaded = call(
        functools.partial(early_gram_kernel, plan),
        [shape(members, early_width), square]
        + [piece_shape(piece) for piece in range(1, PIECES) for _ in range(2)],
        [HBM] * 2 + [VMEM] * 3, [VMEM] * (2 * PIECES),
        [sem for piece in range(1, PIECES) for sem in piece_sems(piece)], 3, "early_gram",
    )(ensembles, cotangents, suffixes, *first_part)
    parts = [first_part] + [loaded[at : at + 2] for at in range(0, len(loaded), 2)]
    total, later, before = join(0, total, other, later, before, offset)

    other = exchange(total, 2)
    gram, offset = call(
        functools.partial(late_gram_kernel, plan),
        [wide, square], [VMEM] * 5 + [ANY], [VMEM] * 2, [], 1.2, "late_gram",
    )(*parts[-1], suffixes, early, offset, total)
    offset_core = hand_over(offset)
    for level in range(1, levels - 1):
        total, later, before = join(level, total, other, later, before, gram)
        other = exchange(total, 2 << level)
    befores.append(before)
    offset, gram = call(
        chip_kernel, [square, wide], [VMEM] * 2 + [ANY] * 2, [VMEM, ANY], [], 0.2, "chip_offset",
        aliases={3: 1},
    )(offset, offset_core, total, gram)
    gram_core = hand_over(gram)
    offsets = [offset] + around(offset, 1)

    steps = call(
        functools.partial(windows_kernel, plan),
        shape(2, count_steps(count) * members, members, kind=BF16), [VMEM, ANY], VMEM,
        [pltpu.VMEM((count * members, members), F32)], 10, "windows",
    )(kept, offset)
    entering, own, gram_core = call(
        functools.partial(enter_kernel, levels - 1, chips),
        [square] * 2 + [wide], [VMEM] * (2 + chips) + [ANY] * 2, [VMEM] * 2 + [ANY], [], 0.2,
        "entering", aliases={3 + chips: 2},
    )(later, other, *offsets, steps, gram_core)
    other_own = exchange(own, 1)
    gram = gram + gram_core
    grams = around(gram, 0)
    entering_core = hand_over(entering)
    size = plan.stack * members
    ens_factors, cot_factors, follow = call(
        functools.partial(carry_kernel, plan),
        [shape(len(plan.groups), size, size, kind=BF16)] * 2
        + [shape(2, count * members, members, kind=BF16)],
        [VMEM] * 3 + [ANY], [VMEM] * 3, [], 0.1, "carries",
    )(suffixes, entering, entering_core, own)

    def apply(factors, which, pieces, out, after, name, micros):
        first, last = plan.pieces[pieces[0]][0], plan.pieces[pieces[-1]][1]
        number = 2 * sum(len(plan.piece_groups[piece]) for piece in pieces)
        return call(
            functools.partial(apply_kernel, plan, pieces),
            [shape(count, members, cells, kind=BF16), shape(8, 128)],
            [VMEM] * (1 + len(pieces)) + [ANY] + [HBM] * len(out), [HBM, VMEM],
            [pltpu.VMEM((last - first, members, cells), BF16), pltpu.SemaphoreType.DMA((number,))],
            micros, name, aliases={2 + len(pieces): 0} if out else None,
        )(factors, *(parts[piece][which] for piece in pieces), after, *out)

    front, rear = tuple(range(PIECES - 1)), (PIECES - 1,)
    smoothed, done = apply(ens_factors, 0, rear, (), follow, "smoothed_0", 0.1)
    carry = jnp.zeros((members, members), F32)
    for level in range(levels - 1):
        waits = level > 0
        own, carry, *rest = call(
            functools.partial(pass_kernel, level),
            [square] * 2 + [wide] * waits,
            [VMEM] * 5 + [ANY] * (1 + waits), [VMEM] * 2 + [ANY] * waits, [], 0.3, f"pass_{level}",
            aliases={6: 2} if waits else None,
        )(own, other_own, carry, uppers[level], befores[level], done, *grams[:waits])
        grams[:waits] = rest
        other_own = exchange(own, 2 << level)
        if level == 0:
            smoothed, done = apply(ens_factors, 0, front, (smoothed,), own, "smoothed_1", 2.4)
        if level == 1:
            ensemble_grad, done = apply(cot_factors, 1, front, (), own, "ensemble_grad_0", 2.4)
    carry, grams[0] = call(
        functools.partial(last_pass_kernel, levels - 1),
        [square, wide], [VMEM] * 3 + [ANY] * 2, [VMEM, ANY], [], 0.2, "pass_last",
        aliases={4: 1},
    )(other_own, carry, befores[-1], done, grams[0])
    for part in grams:
        gram = gram + part
    gram_other = hand_over(gram)
    carry_other = hand_over(carry)
    ensemble_grad, done = apply(cot_factors, 1, rear, (ensemble_grad,), carry, "ensemble_grad_1", 1.4)
    transform_grad = call(
        functools.partial(final_kernel, plan, scale),
        shape(count, members, members),
        [VMEM] * 6 + [ANY], HBM,
        [pltpu.VMEM((count, members, members), F32), pltpu.SemaphoreType.DMA((count,))],
        2.5, "transform_grad",
    )(gram, gram_other, carry, carry_other, follow, steps, done)
    return (smoothed, ensemble_grad, transform_grad)


def solution(mesh):
    return jax.shard_map(
        shards,
        mesh=mesh,
        in_specs=(P("tm", None, "space"), P("tm", None, "space"), P("tm", None, None)),
        out_specs=(P("tm", None, "space"), P("tm", None, "space"), P("tm", None, None)),
        check_vma=False,
    )
```

```python
import functools
import math

import jax
import jax.numpy as jnp
from jax import lax
from jax.experimental import pallas as pl
from jax.experimental.pallas import tpu as pltpu
from jax.sharding import PartitionSpec as P

F32 = jnp.float32
BF16 = jnp.bfloat16
VMEM = pl.BlockSpec(memory_space=pltpu.VMEM)
HBM = pl.BlockSpec(memory_space=pltpu.HBM)
ANY = pl.BlockSpec(memory_space=pl.ANY)
DEPTH = 256
PIECES = 3
NORMAL = (((1,), (0,)), ((), ()))
ROWS = (((1,), (1,)), ((), ()))


def split(value):
    high = value.astype(BF16)
    return high, (value - high.astype(F32)).astype(BF16)


def mul(left, right, dims=NORMAL):
    return lax.dot_general(left, right, dims, preferred_element_type=F32)


def mul_pairs(left, right, dims=NORMAL):
    return mul(left[0], right[0], dims) + (
        mul(left[0], right[1], dims) + mul(left[1], right[0], dims)
    )


def mul_exact(left, right, dims=NORMAL):
    return mul_pairs(split(left), split(right), dims)


def product_of(factors):
    while len(factors) > 1:
        joined = [mul_exact(*factors[at : at + 2]) for at in range(0, len(factors) - 1, 2)]
        factors = joined + factors[len(joined) * 2 :]
    return factors[0]


def suffix_scan(ref, count, members, stop):
    width = 1
    while width < stop:
        for start in range(0, count, 2 * width):
            middle = start + width
            if middle < count:
                rows = slice(start * members, middle * members)
                ref[rows] = mul_exact(ref[rows], ref[middle * members : (middle + 1) * members])
        width *= 2


class Plan:
    def __init__(self, count, members):
        self.count, self.members = count, members
        self.stack = DEPTH // members
        self.groups = [
            (start, min(start + self.stack, count)) for start in range(0, count, self.stack)
        ]
        bounds = [len(self.groups) * at // PIECES for at in range(PIECES + 1)]
        self.piece_groups = [self.groups[a:b] for a, b in zip(bounds, bounds[1:])]
        self.pieces = [(part[0][0], part[-1][1]) for part in self.piece_groups]
        self.first_group = bounds[:-1]
        self.widths = [-(-(stop - start) * members // 128) * 128 for start, stop in self.groups]
        self.width = sum(self.widths)

    def lanes(self, at):
        start = sum(self.widths[:at])
        return slice(start, start + self.widths[at])

    def rows(self, first, last):
        return slice(first * self.members, last * self.members)


def on_blocks(members, size):
    rows = lax.broadcasted_iota(jnp.int32, (size, size), 0) // members
    columns = lax.broadcasted_iota(jnp.int32, (size, size), 1) // members
    return rows == columns


def loads(plan, piece, values, buffer, sems):
    base = plan.pieces[piece][0]
    copies = [
        pltpu.make_async_copy(values.at[start:stop], buffer.at[start - base : stop - base], sems.at[at])
        for at, (start, stop) in enumerate(plan.piece_groups[piece])
    ]
    for copy in copies:
        copy.start()
    return copies


def chain_kernel(
    plan, transforms, ensembles, cotangents, suffixes, total, kept, ens, cot, sem, ens_sem, cot_sem
):
    count, members = plan.count, plan.members
    read = pltpu.make_async_copy(transforms, kept, sem)
    read.start()
    read.wait()
    more = loads(plan, 0, ensembles, ens, ens_sem) + loads(plan, 0, cotangents, cot, cot_sem)
    for at in range(count):
        suffixes[plan.rows(at, at + 1)] = kept[at]
    suffix_scan(suffixes, count, members, count)
    total[...] = suffixes[plan.rows(0, 1)]
    for copy in more:
        copy.wait()


def windows_kernel(plan, kept, _, steps, runs):
    count = plan.count
    for at in range(count - 1):
        runs[plan.rows(at + 1, at + 2)] = kept[at].T
    number = 0
    width = 1
    while width < count:
        for middle in range(width, count, 2 * width):
            size = min(width, count - middle)
            for side, part in enumerate(split(runs[plan.rows(middle, middle + size)])):
                steps[side, plan.rows(number, number + size)] = part
            number += size
        for start in range(2 * width, count, 2 * width):
            if start + width < count:
                rows = plan.rows(start + width, min(start + 2 * width, count))
                runs[rows] = mul_exact(runs[rows], runs[plan.rows(start + width - 1, start + width)])
        width *= 2


def count_steps(count):
    total = 0
    width = 1
    while width < count:
        total += sum(min(width, count - middle) for middle in range(width, count, 2 * width))
        width *= 2
    return total


def core_index():
    return lax.rem(lax.axis_index("space"), 2)


def gram_of(plan, piece, cot, ens, suffixes, whole, ready=lambda: None):
    members = plan.members
    base = plan.pieces[piece][0]
    offset = jnp.zeros((members, members), F32)
    for at, (start, stop) in enumerate(plan.piece_groups[piece]):
        ready()
        size = (stop - start) * members
        stacked = [ref[start - base : stop - base].reshape(size, ref.shape[2]) for ref in (cot, ens)]
        wide = jnp.where(on_blocks(members, size), mul(*stacked, ROWS), 0.0)
        gram = wide[:members]
        for i in range(1, stop - start):
            gram = gram + wide[i * members : (i + 1) * members]
        offset = offset + mul_exact(gram, suffixes[plan.rows(start, stop)])
        lanes = plan.lanes(plan.first_group[piece] + at)
        width = lanes.stop - lanes.start
        whole[:, lanes] = jnp.pad(gram, ((0, 0), (0, width - size)))
    return offset


def early_gram_kernel(plan, ensembles, cotangents, suffixes, ens, cot, whole, offset, *refs):
    buffers, sems = refs[: 2 * (PIECES - 1)], refs[2 * (PIECES - 1) :]
    copies = []
    for piece in range(1, PIECES):
        pair = buffers[2 * piece - 2 : 2 * piece]
        own = sems[2 * piece - 2 : 2 * piece]
        copies.append(list(zip(
            loads(plan, piece, ensembles, pair[0], own[0]),
            loads(plan, piece, cotangents, pair[1], own[1]),
        )))
    total = gram_of(plan, 0, cot, ens, suffixes, whole)
    for piece in range(1, PIECES - 1):
        waiting = iter(copies[piece - 1])

        def ready():
            for copy in next(waiting):
                copy.wait()

        ens, cot = buffers[2 * piece - 2 : 2 * piece]
        total = total + gram_of(plan, piece, cot, ens, suffixes, whole, ready)
    offset[...] = total
    for pair in copies[-1]:
        for copy in pair:
            copy.wait()


def late_gram_kernel(plan, ens, cot, suffixes, early, offset, _, kept, sent, offsets, whole):
    whole[:, : early.shape[1]] = early[...]
    offsets[...] = offset[...] + gram_of(plan, PIECES - 1, cot, ens, suffixes, whole)
    half = plan.members // 2
    core = lax.rem(lax.axis_index("space"), 2)
    kept[...] = whole[pl.ds(core * half, half)]
    sent[...] = whole[pl.ds((1 - core) * half, half)]


def sum_kernel(left, right, _, total):
    total[...] = left[...] + right[...]


def chip_kernel(mine, other, _, __, offset, ___):
    offset[...] = mine[...] + other[...]


def upper_half(level):
    return lax.rem(lax.axis_index("tm") // (1 << level), 2) == 1


def join_kernel(level, total, other, later, before, _, new_total, new_later, new_before, upper_total):
    upper = upper_half(level)
    left = jnp.where(upper, other[...], total[...])
    right = jnp.where(upper, total[...], other[...])
    new_total[...] = mul_exact(left, right)
    upper_total[...] = right
    new_later[...] = jnp.where(upper, later[...], mul_exact(later[...], other[...]))
    new_before[...] = jnp.where(upper, mul_exact(other[...], before[...]), before[...])


def pass_kernel(level, own, other, carry, upper_total, before, _, new_own, new_carry):
    upper = upper_half(level)
    left = jnp.where(upper, other[...], own[...])
    right = jnp.where(upper, own[...], other[...])
    new_own[...] = mul_exact(left, upper_total[...]) + right
    new_carry[...] = carry[...] + jnp.where(upper, mul_exact(left, before[...]), 0.0)


def last_pass_kernel(level, other, carry, before, _, __, new_carry, ___):
    added = mul_exact(other[...], before[...])
    new_carry[...] = carry[...] + jnp.where(upper_half(level), added, 0.0)


def enter_kernel(level, number, later, other, *refs):
    values, (_, entering, own) = refs[:number], refs[number:]
    joined = mul_exact(later[...], other[...])
    entering[...] = jnp.where(upper_half(level), later[...], joined)
    total = values[0][...]
    for ref in values[1:]:
        total = total + ref[...]
    own[...] = total


def carry_kernel(plan, suffixes, mine, other, _, ens_factors, cot_factors, follow):
    count, members = plan.count, plan.members
    entering = jnp.where(lax.rem(lax.axis_index("space"), 2) == 1, mine[...], other[...])
    mask = on_blocks(members, plan.stack * members)
    repeated = split(jnp.concatenate([entering] * plan.stack, axis=1))
    for at, (start, stop) in enumerate(plan.groups):
        size = (stop - start) * members
        wide = mul_pairs(split(suffixes[plan.rows(start, stop)]), repeated)
        part = jnp.where(mask[:size, :size], wide[:, :size], 0.0)
        cot_factors[at, :size, :size] = part.astype(BF16)
        ens_factors[at, :size, :size] = part.T.astype(BF16)
        first = max(start - 1, 0)
        kept = wide[(first + 1 - start) * members :, :members]
        for side, value in enumerate(split(kept)):
            follow[side, plan.rows(first, stop - 1)] = value
    for side, value in enumerate(split(entering)):
        follow[side, plan.rows(count - 1, count)] = value


def apply_kernel(plan, pieces, factors, *refs):
    out, marker, out_buf, out_sem = refs[-4:]
    members = plan.members
    marker[...] = jnp.zeros_like(marker)
    base = plan.pieces[pieces[0]][0]
    chunk = out_buf.shape[2] // 2
    writes = []
    for values, piece in zip(refs, pieces):
        first = plan.pieces[piece][0]
        for at, (start, stop) in enumerate(plan.piece_groups[piece]):
            size = (stop - start) * members
            for side in range(2):
                columns = slice(side * chunk, (side + 1) * chunk)
                stacked = values[start - first : stop - first, :, columns].reshape(size, chunk)
                result = mul(factors[plan.first_group[piece] + at, :size, :size], stacked)
                out_buf[start - base : stop - base, :, columns] = result.astype(BF16).reshape(
                    stop - start, members, chunk
                )
                copy = pltpu.make_async_copy(
                    out_buf.at[start - base : stop - base, :, columns],
                    out.at[start:stop, :, columns],
                    out_sem.at[len(writes)],
                )
                copy.start()
                writes.append(copy)
    for copy in writes:
        copy.wait()


def final_kernel(
    plan, scale, gram_mine, gram_other, carry_mine, carry_other, follow, steps, _, out, buffer, sems
):
    count, members = plan.count, plan.members
    first = lax.rem(lax.axis_index("space"), 2) == 0
    carry = jnp.where(first, carry_other[...], carry_mine[...])

    totals = []
    for at, (start, stop) in enumerate(plan.groups):
        mine, other = gram_mine[:, plan.lanes(at)], gram_other[:, plan.lanes(at)]
        halves = [jnp.where(first, mine, other), jnp.where(first, other, mine)]
        tall = jnp.concatenate(halves, axis=0).T
        for i in range(stop - start):
            totals.append(tall[i * members : (i + 1) * members])
    totals[0] = totals[0] + carry.T
    number = 0
    width = 1
    while width < count:
        for start in range(width, count, 2 * width):
            size = min(width, count - start)
            rows = plan.rows(number, number + size)
            added = mul_pairs((steps[0, rows], steps[1, rows]), split(totals[start - 1]))
            for at in range(size):
                totals[start + at] = totals[start + at] + added[at * members : (at + 1) * members]
            number += size
        width *= 2
    copies = []
    for at in range(count):
        rows = plan.rows(at, at + 1)
        buffer[at] = mul_pairs(split(totals[at]), (follow[0, rows], follow[1, rows]), ROWS) * scale
        copy = pltpu.make_async_copy(buffer.at[at], out.at[at], sems.at[at])
        copy.start()
        copies.append(copy)
    for copy in copies:
        copy.wait()


def call(kernel, outs, ins, out_specs, scratch, micros, name, limit=16, aliases=None):
    return pl.pallas_call(
        kernel,
        out_shape=outs,
        in_specs=ins,
        out_specs=out_specs,
        scratch_shapes=scratch,
        input_output_aliases=aliases or {},
        compiler_params=pltpu.CompilerParams(vmem_limit_bytes=limit << 20),
        cost_estimate=pl.CostEstimate(
            flops=0, bytes_accessed=int(micros * 3.6e6), transcendentals=0
        ),
        name=name,
    )


def shape(*dims, kind=F32):
    return jax.ShapeDtypeStruct(dims, kind)


def shards(ensembles, cotangents, transforms):
    count, members, cells = ensembles.shape
    blocks, lanes = lax.axis_size("tm"), lax.axis_size("space")
    chips = lanes // 2
    scale = 1.0 / math.sqrt(cells * lanes * count * blocks)
    plan = Plan(count, members)
    levels = blocks.bit_length() - 1
    square = shape(members, members)
    ensembles, cotangents, transforms = (
        pltpu.with_memory_space_constraint(value, pltpu.HBM)
        for value in (ensembles, cotangents, transforms)
    )

    def send(value, *targets):
        pairs = []
        for at in range(blocks * lanes):
            block, lane = divmod(at, lanes)
            block, lane = targets[lane % 2](block, lane)
            pairs.append((at, block * lanes + lane))
        return lax.ppermute(value, ("tm", "space"), pairs)

    def along_tm(bit):
        return lambda block, lane: (block ^ bit, lane)

    def along_space(distance):
        return lambda block, lane: (block, (lane + distance) % lanes)

    def exchange(value, bit):
        return send(value, along_space(2), along_tm(bit))

    def hand_over(value):
        return send(value, along_space(1), along_space(lanes - 1))

    def piece_shape(piece):
        first, last = plan.pieces[piece]
        return shape(last - first, members, cells, kind=BF16)

    def piece_sems(piece):
        return [pltpu.SemaphoreType.DMA((len(plan.piece_groups[piece]),))] * 2

    suffixes, total, kept, *first_part = call(
        functools.partial(chain_kernel, plan),
        [shape(count * members, members), square, shape(count, members, members)] + [piece_shape(0)] * 2,
        [HBM] * 3, [VMEM] * 5, [pltpu.SemaphoreType.DMA] + piece_sems(0), 3.5, "transform_chain",
    )(transforms, ensembles, cotangents)

    wide = shape(members // 2, plan.width)
    later = before = jnp.eye(members, dtype=F32)
    uppers, befores = [], []

    def join(level, total, other, later, before, after):
        befores.append(before)
        *new, upper = call(
            functools.partial(join_kernel, level),
            [square] * 4, [VMEM] * 4 + [ANY], [VMEM] * 4, [], 3, f"join_{level}",
        )(total, other, later, before, after)
        uppers.append(upper)
        return new

    other = exchange(total, 1)
    early_width = plan.lanes(plan.first_group[-1]).start
    early, offset, *loaded = call(
        functools.partial(early_gram_kernel, plan),
        [shape(members, early_width), square]
        + [piece_shape(piece) for piece in range(1, PIECES) for _ in range(2)],
        [HBM] * 2 + [VMEM] * 3, [VMEM] * (2 * PIECES),
        [sem for piece in range(1, PIECES) for sem in piece_sems(piece)], 3, "early_gram",
    )(ensembles, cotangents, suffixes, *first_part)
    parts = [first_part] + [loaded[at : at + 2] for at in range(0, len(loaded), 2)]
    total, later, before = join(0, total, other, later, before, offset)

    other = exchange(total, 2)
    gram, gram_sent, offset = call(
        functools.partial(late_gram_kernel, plan),
        [wide, wide, square], [VMEM] * 5 + [ANY], [VMEM] * 3,
        [pltpu.VMEM((members, plan.width), F32)], 1.2, "late_gram",
    )(*parts[-1], suffixes, early, offset, total)
    offset_core = hand_over(offset)
    for level in range(1, levels - 1):
        total, later, before = join(level, total, other, later, before, gram)
        other = exchange(total, 2 << level)
    befores.append(before)
    offset, gram_sent = call(
        chip_kernel, [square, wide], [VMEM] * 2 + [ANY] * 2, [VMEM, ANY], [], 0.2, "chip_offset",
        aliases={3: 1},
    )(offset, offset_core, total, gram_sent)
    gram_core = hand_over(gram_sent)
    offsets = [offset] + [send(offset, along_tm(1), along_space(2 * d)) for d in range(1, chips)]

    steps = call(
        functools.partial(windows_kernel, plan),
        shape(2, count_steps(count) * members, members, kind=BF16), [VMEM, ANY], VMEM,
        [pltpu.VMEM((count * members, members), F32)], 10, "windows",
    )(kept, offset)
    entering, own = call(
        functools.partial(enter_kernel, levels - 1, chips),
        [square] * 2, [VMEM] * (2 + chips) + [ANY], [VMEM] * 2, [], 0.2, "entering",
    )(later, other, *offsets, steps)
    gram = call(
        sum_kernel, wide, [VMEM] * 2 + [ANY], VMEM, [], 0.1, "chip_gram",
    )(gram, gram_core, own)
    grams = [send(gram, *[along_space(2 * d)] * 2) for d in range(1, chips)]
    other_own = exchange(own, 1)
    entering_core = hand_over(entering)
    size = plan.stack * members
    ens_factors, cot_factors, follow = call(
        functools.partial(carry_kernel, plan),
        [shape(len(plan.groups), size, size, kind=BF16)] * 2
        + [shape(2, count * members, members, kind=BF16)],
        [VMEM] * 3 + [ANY], [VMEM] * 3, [], 0.1, "carries",
    )(suffixes, entering, entering_core, own)
    def apply(factors, which, pieces, out, after, name, micros):
        first, last = plan.pieces[pieces[0]][0], plan.pieces[pieces[-1]][1]
        number = 2 * sum(len(plan.piece_groups[piece]) for piece in pieces)
        return call(
            functools.partial(apply_kernel, plan, pieces),
            [shape(count, members, cells, kind=BF16), shape(8, 128)],
            [VMEM] * (1 + len(pieces)) + [ANY] + [HBM] * len(out), [HBM, VMEM],
            [pltpu.VMEM((last - first, members, cells), BF16), pltpu.SemaphoreType.DMA((number,))],
            micros, name, aliases={2 + len(pieces): 0} if out else None,
        )(factors, *(parts[piece][which] for piece in pieces), after, *out)

    front, rear = tuple(range(PIECES - 1)), (PIECES - 1,)
    smoothed, done = apply(ens_factors, 0, rear, (), follow, "smoothed_0", 0.1)
    carry = jnp.zeros((members, members), F32)
    for level in range(levels - 1):
        own, carry = call(
            functools.partial(pass_kernel, level),
            [square] * 2, [VMEM] * 5 + [ANY], [VMEM] * 2, [], 0.3, f"pass_{level}",
        )(own, other_own, carry, uppers[level], befores[level], done)
        other_own = exchange(own, 2 << level)
        if level == 0:
            smoothed, done = apply(ens_factors, 0, front, (smoothed,), own, "smoothed_1", 2.4)
        if level == 1:
            ensemble_grad, done = apply(cot_factors, 1, front, (), own, "ensemble_grad_0", 2.4)
    carry, grams[0] = call(
        functools.partial(last_pass_kernel, levels - 1),
        [square, wide], [VMEM] * 3 + [ANY] * 2, [VMEM, ANY], [], 0.2, "pass_last",
        aliases={4: 1},
    )(other_own, carry, befores[-1], done, grams[0])
    for part in grams:
        gram = gram + part
    gram_other = hand_over(gram)
    carry_other = hand_over(carry)
    ensemble_grad, done = apply(cot_factors, 1, rear, (ensemble_grad,), carry, "ensemble_grad_1", 1.4)
    transform_grad = call(
        functools.partial(final_kernel, plan, scale),
        shape(count, members, members),
        [VMEM] * 6 + [ANY], HBM,
        [pltpu.VMEM((count, members, members), F32), pltpu.SemaphoreType.DMA((count,))],
        2.5, "transform_grad",
    )(gram, gram_other, carry, carry_other, follow, steps, done)
    return (smoothed, ensemble_grad, transform_grad)


def solution(mesh):
    return jax.shard_map(
        shards,
        mesh=mesh,
        in_specs=(P("tm", None, "space"), P("tm", None, "space"), P("tm", None, None)),
        out_specs=(P("tm", None, "space"), P("tm", None, "space"), P("tm", None, None)),
        check_vma=False,
    )
```

```python
import functools
import math

import jax
import jax.numpy as jnp
from jax import lax
from jax.experimental import pallas as pl
from jax.experimental.pallas import tpu as pltpu
from jax.sharding import PartitionSpec as P

F32 = jnp.float32
BF16 = jnp.bfloat16
VMEM = pl.BlockSpec(memory_space=pltpu.VMEM)
HBM = pl.BlockSpec(memory_space=pltpu.HBM)
ANY = pl.BlockSpec(memory_space=pl.ANY)
DEPTH = 256
PIECES = 3
NORMAL = (((1,), (0,)), ((), ()))
ROWS = (((1,), (1,)), ((), ()))


def split(value):
    high = value.astype(BF16)
    return high, (value - high.astype(F32)).astype(BF16)


def mul(left, right, dims=NORMAL):
    return lax.dot_general(left, right, dims, preferred_element_type=F32)


def mul_pairs(left, right, dims=NORMAL):
    return mul(left[0], right[0], dims) + (
        mul(left[0], right[1], dims) + mul(left[1], right[0], dims)
    )


def mul_exact(left, right, dims=NORMAL):
    return mul_pairs(split(left), split(right), dims)


def product_of(factors):
    while len(factors) > 1:
        joined = [mul_exact(*factors[at : at + 2]) for at in range(0, len(factors) - 1, 2)]
        factors = joined + factors[len(joined) * 2 :]
    return factors[0]


def suffix_scan(ref, count, members, stop):
    width = 1
    while width < stop:
        for start in range(0, count, 2 * width):
            middle = start + width
            if middle < count:
                rows = slice(start * members, middle * members)
                ref[rows] = mul_exact(ref[rows], ref[middle * members : (middle + 1) * members])
        width *= 2


class Plan:
    def __init__(self, count, members):
        self.count, self.members = count, members
        self.stack = DEPTH // members
        self.groups = [
            (start, min(start + self.stack, count)) for start in range(0, count, self.stack)
        ]
        bounds = [len(self.groups) * at // PIECES for at in range(PIECES + 1)]
        self.piece_groups = [self.groups[a:b] for a, b in zip(bounds, bounds[1:])]
        self.pieces = [(part[0][0], part[-1][1]) for part in self.piece_groups]
        self.first_group = bounds[:-1]
        self.widths = [-(-(stop - start) * members // 128) * 128 for start, stop in self.groups]
        self.width = sum(self.widths)

    def lanes(self, at):
        start = sum(self.widths[:at])
        return slice(start, start + self.widths[at])

    def rows(self, first, last):
        return slice(first * self.members, last * self.members)


def eye(members):
    rows = lax.broadcasted_iota(jnp.int32, (members, members), 0)
    columns = lax.broadcasted_iota(jnp.int32, (members, members), 1)
    return (rows == columns).astype(F32)


def on_blocks(members, size):
    rows = lax.broadcasted_iota(jnp.int32, (size, size), 0) // members
    columns = lax.broadcasted_iota(jnp.int32, (size, size), 1) // members
    return rows == columns


def loads(plan, piece, values, buffer, sems):
    base = plan.pieces[piece][0]
    copies = [
        pltpu.make_async_copy(values.at[start:stop], buffer.at[start - base : stop - base], sems.at[at])
        for at, (start, stop) in enumerate(plan.piece_groups[piece])
    ]
    for copy in copies:
        copy.start()
    return copies


def chain_kernel(
    plan, transforms, ensembles, cotangents, suffixes, total, kept, ens, cot, sem, ens_sem, cot_sem
):
    count, members = plan.count, plan.members
    read = pltpu.make_async_copy(transforms, kept, sem)
    read.start()
    read.wait()
    more = loads(plan, 0, ensembles, ens, ens_sem) + loads(plan, 0, cotangents, cot, cot_sem)
    for at in range(count):
        suffixes[plan.rows(at, at + 1)] = kept[at]
    suffix_scan(suffixes, count, members, count)
    total[...] = suffixes[plan.rows(0, 1)]
    for copy in more:
        copy.wait()


def windows_kernel(plan, kept, _, steps, runs):
    count = plan.count
    for at in range(count - 1):
        runs[plan.rows(at + 1, at + 2)] = kept[at].T
    number = 0
    width = 1
    while width < count:
        for middle in range(width, count, 2 * width):
            size = min(width, count - middle)
            for side, part in enumerate(split(runs[plan.rows(middle, middle + size)])):
                steps[side, plan.rows(number, number + size)] = part
            number += size
        for start in range(2 * width, count, 2 * width):
            if start + width < count:
                rows = plan.rows(start + width, min(start + 2 * width, count))
                runs[rows] = mul_exact(runs[rows], runs[plan.rows(start + width - 1, start + width)])
        width *= 2


def count_steps(count):
    total = 0
    width = 1
    while width < count:
        total += sum(min(width, count - middle) for middle in range(width, count, 2 * width))
        width *= 2
    return total


def core_index():
    return lax.rem(lax.axis_index("space"), 2)


def gram_of(plan, piece, cot, ens, suffixes, whole, ready=lambda: None):
    members = plan.members
    base = plan.pieces[piece][0]
    offset = jnp.zeros((members, members), F32)
    for at, (start, stop) in enumerate(plan.piece_groups[piece]):
        ready()
        size = (stop - start) * members
        stacked = [ref[start - base : stop - base].reshape(size, ref.shape[2]) for ref in (cot, ens)]
        wide = jnp.where(on_blocks(members, size), mul(*stacked, ROWS), 0.0)
        gram = wide[:members]
        for i in range(1, stop - start):
            gram = gram + wide[i * members : (i + 1) * members]
        offset = offset + mul_exact(gram, suffixes[plan.rows(start, stop)])
        lanes = plan.lanes(plan.first_group[piece] + at)
        width = lanes.stop - lanes.start
        whole[:, lanes] = jnp.pad(gram, ((0, 0), (0, width - size)))
    return offset


def early_gram_kernel(plan, ensembles, cotangents, suffixes, ens, cot, whole, offset, *refs):
    buffers, sems = refs[: 2 * (PIECES - 1)], refs[2 * (PIECES - 1) :]
    copies = []
    for piece in range(1, PIECES):
        pair = buffers[2 * piece - 2 : 2 * piece]
        own = sems[2 * piece - 2 : 2 * piece]
        copies.append(list(zip(
            loads(plan, piece, ensembles, pair[0], own[0]),
            loads(plan, piece, cotangents, pair[1], own[1]),
        )))
    total = gram_of(plan, 0, cot, ens, suffixes, whole)
    for piece in range(1, PIECES - 1):
        waiting = iter(copies[piece - 1])

        def ready():
            for copy in next(waiting):
                copy.wait()

        ens, cot = buffers[2 * piece - 2 : 2 * piece]
        total = total + gram_of(plan, piece, cot, ens, suffixes, whole, ready)
    offset[...] = total
    for pair in copies[-1]:
        for copy in pair:
            copy.wait()


def late_gram_kernel(plan, ens, cot, suffixes, early, offset, _, grams, offsets):
    grams[:, : early.shape[1]] = early[...]
    offsets[...] = offset[...] + gram_of(plan, PIECES - 1, cot, ens, suffixes, grams)


def sum_kernel(number, through, *refs):
    total = refs[0][...]
    for ref in refs[1:number]:
        total = total + ref[...]
    refs[number + 1 + through][...] = total


def upper_half(level):
    return lax.rem(lax.axis_index("tm") // (1 << level), 2) == 1


def join_kernel(level, total, other, later, before, _, new_total, new_later, new_before, upper_total):
    upper = upper_half(level)
    left = jnp.where(upper, other[...], total[...])
    right = jnp.where(upper, total[...], other[...])
    new_total[...] = mul_exact(left, right)
    upper_total[...] = right
    new_later[...] = jnp.where(upper, later[...], mul_exact(later[...], other[...]))
    new_before[...] = jnp.where(upper, mul_exact(other[...], before[...]), before[...])


def pass_kernel(level, own, other, carry, upper_total, before, _, new_own, new_carry):
    upper = upper_half(level)
    left = jnp.where(upper, other[...], own[...])
    right = jnp.where(upper, own[...], other[...])
    new_own[...] = mul_exact(left, upper_total[...]) + right
    new_carry[...] = carry[...] + jnp.where(upper, mul_exact(left, before[...]), 0.0)


def enter_kernel(level, total, later, before, near, far, cross, entering, upper_total, new_before):
    place = lax.rem(lax.axis_index("tm") // (1 << level), 4)
    unit = eye(total.shape[0])
    odd = lax.rem(place, 2) == 1
    first = jnp.where(odd, cross[...], near[...])
    second = far[...]
    joined = mul_exact(later[...], jnp.where(place == 3, unit, first))
    rest = jnp.where(place == 0, mul_exact(second, cross[...]), jnp.where(place == 1, second, unit))
    entering[...] = mul_exact(joined, rest)
    upper_total[...] = jnp.where(odd, total[...], near[...])
    new_before[...] = jnp.where(odd, mul_exact(near[...], before[...]), before[...])


def carry_kernel(plan, suffixes, later, _, ens_factors, cot_factors, follow):
    count, members = plan.count, plan.members
    entering = later[...]
    mask = on_blocks(members, plan.stack * members)
    repeated = split(jnp.concatenate([entering] * plan.stack, axis=1))
    for at, (start, stop) in enumerate(plan.groups):
        size = (stop - start) * members
        wide = mul_pairs(split(suffixes[plan.rows(start, stop)]), repeated)
        part = jnp.where(mask[:size, :size], wide[:, :size], 0.0)
        cot_factors[at, :size, :size] = part.astype(BF16)
        ens_factors[at, :size, :size] = part.T.astype(BF16)
        first = max(start - 1, 0)
        kept = wide[(first + 1 - start) * members :, :members]
        for side, value in enumerate(split(kept)):
            follow[side, plan.rows(first, stop - 1)] = value
    for side, value in enumerate(split(entering)):
        follow[side, plan.rows(count - 1, count)] = value


def apply_kernel(plan, pieces, factors, *refs):
    out, marker, out_buf, out_sem = refs[-4:]
    members = plan.members
    marker[...] = jnp.zeros_like(marker)
    base = plan.pieces[pieces[0]][0]
    chunk = out_buf.shape[2] // 2
    writes = []
    for values, piece in zip(refs, pieces):
        first = plan.pieces[piece][0]
        for at, (start, stop) in enumerate(plan.piece_groups[piece]):
            size = (stop - start) * members
            for side in range(2):
                columns = slice(side * chunk, (side + 1) * chunk)
                stacked = values[start - first : stop - first, :, columns].reshape(size, chunk)
                result = mul(factors[plan.first_group[piece] + at, :size, :size], stacked)
                out_buf[start - base : stop - base, :, columns] = result.astype(BF16).reshape(
                    stop - start, members, chunk
                )
                copy = pltpu.make_async_copy(
                    out_buf.at[start - base : stop - base, :, columns],
                    out.at[start:stop, :, columns],
                    out_sem.at[len(writes)],
                )
                copy.start()
                writes.append(copy)
    for copy in writes:
        copy.wait()


def final_kernel(plan, level, scale, number, *refs):
    messages = refs[:number]
    other, carry, before, follow, steps, _, out, buffer, sems = refs[number:]
    count, members = plan.count, plan.members
    added = mul_exact(other[...], before[...])
    carry = carry[...] + jnp.where(upper_half(level), added, 0.0)
    totals = []
    for at, (start, stop) in enumerate(plan.groups):
        wide = messages[0][:, plan.lanes(at)]
        for ref in messages[1:]:
            wide = wide + ref[:, plan.lanes(at)]
        tall = wide.T
        for i in range(stop - start):
            totals.append(tall[i * members : (i + 1) * members])
    totals[0] = totals[0] + carry.T
    number = 0
    width = 1
    while width < count:
        for start in range(width, count, 2 * width):
            size = min(width, count - start)
            rows = plan.rows(number, number + size)
            added = mul_pairs((steps[0, rows], steps[1, rows]), split(totals[start - 1]))
            for at in range(size):
                totals[start + at] = totals[start + at] + added[at * members : (at + 1) * members]
            number += size
        width *= 2
    copies = []
    for at in range(count):
        rows = plan.rows(at, at + 1)
        buffer[at] = mul_pairs(split(totals[at]), (follow[0, rows], follow[1, rows]), ROWS) * scale
        copy = pltpu.make_async_copy(buffer.at[at], out.at[at], sems.at[at])
        copy.start()
        copies.append(copy)
    for copy in copies:
        copy.wait()


def call(kernel, outs, ins, out_specs, scratch, micros, name, limit=16, aliases=None):
    return pl.pallas_call(
        kernel,
        out_shape=outs,
        in_specs=ins,
        out_specs=out_specs,
        scratch_shapes=scratch,
        input_output_aliases=aliases or {},
        compiler_params=pltpu.CompilerParams(vmem_limit_bytes=limit << 20),
        cost_estimate=pl.CostEstimate(
            flops=0, bytes_accessed=int(micros * 3.6e6), transcendentals=0
        ),
        name=name,
    )


def shape(*dims, kind=F32):
    return jax.ShapeDtypeStruct(dims, kind)


def shards(ensembles, cotangents, transforms):
    count, members, cells = ensembles.shape
    blocks, lanes = lax.axis_size("tm"), lax.axis_size("space")
    chips = lanes // 2
    scale = 1.0 / math.sqrt(cells * lanes * count * blocks)
    plan = Plan(count, members)
    levels = blocks.bit_length() - 1
    square = shape(members, members)
    ensembles, cotangents, transforms = (
        pltpu.with_memory_space_constraint(value, pltpu.HBM)
        for value in (ensembles, cotangents, transforms)
    )

    def exchange(value, bit):
        return lax.ppermute(value, "tm", [(at, at ^ bit) for at in range(blocks)])

    def swap_cores(value):
        return lax.ppermute(value, "space", [(at, at ^ 1) for at in range(lanes)])

    def around(value):
        return [
            lax.ppermute(value, "space", [(at, (at + 2 * d) % lanes) for at in range(lanes)])
            for d in range(1, chips)
        ]

    def piece_shape(piece):
        first, last = plan.pieces[piece]
        return shape(last - first, members, cells, kind=BF16)

    def piece_sems(piece):
        return [pltpu.SemaphoreType.DMA((len(plan.piece_groups[piece]),))] * 2

    suffixes, total, kept, *first_part = call(
        functools.partial(chain_kernel, plan),
        [shape(count * members, members), square, shape(count, members, members)] + [piece_shape(0)] * 2,
        [HBM] * 3, [VMEM] * 5, [pltpu.SemaphoreType.DMA] + piece_sems(0), 3.5, "transform_chain",
    )(transforms, ensembles, cotangents)

    wide = shape(members, plan.width)
    later = before = jnp.eye(members, dtype=F32)
    uppers, befores = [], []

    def join(level, total, other, later, before, after):
        befores.append(before)
        *new, upper = call(
            functools.partial(join_kernel, level),
            [square] * 4, [VMEM] * 4 + [ANY], [VMEM] * 4, [], 0.3, f"join_{level}",
        )(total, other, later, before, after)
        uppers.append(upper)
        return new

    def add(values, after, name, *through):
        number = len(values)
        return call(
            functools.partial(sum_kernel, number, len(through)),
            [shape(*values[0].shape)] + [shape(*value.shape) for value in through],
            [VMEM] * number + [ANY] * (1 + len(through)), [VMEM] + [ANY] * len(through), [], 0.1, name,
            aliases={number + 1 + at: 1 + at for at in range(len(through))},
        )(*values, after, *through)

    other = exchange(total, 1)
    early_width = plan.lanes(plan.first_group[-1]).start
    early, offset, *loaded = call(
        functools.partial(early_gram_kernel, plan),
        [shape(members, early_width), square]
        + [piece_shape(piece) for piece in range(1, PIECES) for _ in range(2)],
        [HBM] * 2 + [VMEM] * 3, [VMEM] * (2 * PIECES),
        [sem for piece in range(1, PIECES) for sem in piece_sems(piece)], 3, "early_gram",
    )(ensembles, cotangents, suffixes, *first_part)
    parts = [first_part] + [loaded[at : at + 2] for at in range(0, len(loaded), 2)]
    total, later, before = join(0, total, other, later, before, offset)
    for level in range(1, levels - 2):
        other = exchange(total, 1 << level)
        total, later, before = join(level, total, other, later, before, total)

    others = [exchange(total, bit << (levels - 2)) for bit in (1, 2, 3)]
    gram, offset = call(
        functools.partial(late_gram_kernel, plan),
        [wide, square], [VMEM] * 5 + [ANY], [VMEM] * 2, [], 1.2, "late_gram",
    )(*parts[-1], suffixes, early, offset, total)
    offset_core = swap_cores(offset)
    befores.append(before)
    entering, upper, before = call(
        functools.partial(enter_kernel, levels - 2),
        [square] * 3, [VMEM] * 6, [VMEM] * 3, [], 0.4, "entering",
    )(total, later, before, *others)
    uppers.append(upper)
    befores.append(before)
    offset, gram = add([offset, offset_core], entering, "chip_offset", gram)
    gram_core = swap_cores(gram)
    offsets = [offset] + around(offset)

    steps = call(
        functools.partial(windows_kernel, plan),
        shape(2, count_steps(count) * members, members, kind=BF16), [VMEM, ANY], VMEM,
        [pltpu.VMEM((count * members, members), F32)], 1.0, "windows",
    )(kept, offset)
    size = plan.stack * members
    ens_factors, cot_factors, follow = call(
        functools.partial(carry_kernel, plan),
        [shape(len(plan.groups), size, size, kind=BF16)] * 2
        + [shape(2, count * members, members, kind=BF16)],
        [VMEM] * 2 + [ANY], [VMEM] * 3, [], 0.9, "carries",
    )(suffixes, entering, steps)

    def apply(factors, which, pieces, out, after, name, micros):
        first, last = plan.pieces[pieces[0]][0], plan.pieces[pieces[-1]][1]
        number = 2 * sum(len(plan.piece_groups[piece]) for piece in pieces)
        return call(
            functools.partial(apply_kernel, plan, pieces),
            [shape(count, members, cells, kind=BF16), shape(8, 128)],
            [VMEM] * (1 + len(pieces)) + [ANY] + [HBM] * len(out), [HBM, VMEM],
            [pltpu.VMEM((last - first, members, cells), BF16), pltpu.SemaphoreType.DMA((number,))],
            micros, name, aliases={2 + len(pieces): 0} if out else None,
        )(factors, *(parts[piece][which] for piece in pieces), after, *out)

    front, rear = tuple(range(PIECES - 1)), (PIECES - 1,)
    smoothed, done = apply(ens_factors, 0, rear, (), follow, "smoothed_0", 1.4)
    own, gram_core = add(offsets, done, "own_offset", gram_core)
    gram = gram + gram_core
    grams = [gram] + around(gram)
    carry = jnp.zeros((members, members), F32)
    for level in range(levels):
        other = exchange(own, 1 << level)
        if level == 0:
            smoothed, done = apply(ens_factors, 0, front, (smoothed,), own, "smoothed_1", 2.3)
        if level == 1:
            ensemble_grad, done = apply(cot_factors, 1, front, (), own, "ensemble_grad_0", 2.3)
        if level == levels - 1:
            ensemble_grad, done = apply(cot_factors, 1, rear, (ensemble_grad,), own, "ensemble_grad_1", 1.4)
        if level < levels - 1:
            own, carry = call(
                functools.partial(pass_kernel, level),
                [square] * 2, [VMEM] * 5 + [ANY], [VMEM] * 2, [], 0.3, f"pass_{level}",
            )(own, other, carry, uppers[level], befores[level], done)
    transform_grad = call(
        functools.partial(final_kernel, plan, levels - 1, scale, chips),
        shape(count, members, members),
        [VMEM] * (chips + 5) + [ANY], HBM,
        [pltpu.VMEM((count, members, members), F32), pltpu.SemaphoreType.DMA((count,))],
        2.5, "transform_grad",
    )(*grams, other, carry, befores[-1], follow, steps, done)
    return (smoothed, ensemble_grad, transform_grad)


def solution(mesh):
    return jax.shard_map(
        shards,
        mesh=mesh,
        in_specs=(P("tm", None, "space"), P("tm", None, "space"), P("tm", None, None)),
        out_specs=(P("tm", None, "space"), P("tm", None, "space"), P("tm", None, None)),
        check_vma=False,
    )
```

```python
import functools
import math

import jax
import jax.numpy as jnp
from jax import lax
from jax.experimental import pallas as pl
from jax.experimental.pallas import tpu as pltpu
from jax.sharding import PartitionSpec as P

F32 = jnp.float32
BF16 = jnp.bfloat16
VMEM = pl.BlockSpec(memory_space=pltpu.VMEM)
HBM = pl.BlockSpec(memory_space=pltpu.HBM)
ANY = pl.BlockSpec(memory_space=pl.ANY)
DEPTH = 256
PIECES = 3
NORMAL = (((1,), (0,)), ((), ()))
ROWS = (((1,), (1,)), ((), ()))


def split(value):
    high = value.astype(BF16)
    return high, (value - high.astype(F32)).astype(BF16)


def mul(left, right, dims=NORMAL):
    return lax.dot_general(left, right, dims, preferred_element_type=F32)


def mul_pairs(left, right, dims=NORMAL):
    return mul(left[0], right[0], dims) + (
        mul(left[0], right[1], dims) + mul(left[1], right[0], dims)
    )


def mul_exact(left, right, dims=NORMAL):
    return mul_pairs(split(left), split(right), dims)


def product_of(factors):
    while len(factors) > 1:
        joined = [mul_exact(*factors[at : at + 2]) for at in range(0, len(factors) - 1, 2)]
        factors = joined + factors[len(joined) * 2 :]
    return factors[0]


def suffix_scan(ref, count, members, stop):
    width = 1
    while width < stop:
        for start in range(0, count, 2 * width):
            middle = start + width
            if middle < count:
                rows = slice(start * members, middle * members)
                ref[rows] = mul_exact(ref[rows], ref[middle * members : (middle + 1) * members])
        width *= 2


class Plan:
    def __init__(self, count, members):
        self.count, self.members = count, members
        self.stack = DEPTH // members
        self.groups = [
            (start, min(start + self.stack, count)) for start in range(0, count, self.stack)
        ]
        bounds = [len(self.groups) * at // PIECES for at in range(PIECES + 1)]
        self.piece_groups = [self.groups[a:b] for a, b in zip(bounds, bounds[1:])]
        self.pieces = [(part[0][0], part[-1][1]) for part in self.piece_groups]
        self.first_group = bounds[:-1]
        self.widths = [-(-(stop - start) * members // 128) * 128 for start, stop in self.groups]
        self.width = sum(self.widths)

    def lanes(self, at):
        start = sum(self.widths[:at])
        return slice(start, start + self.widths[at])

    def rows(self, first, last):
        return slice(first * self.members, last * self.members)


def eye(members):
    rows = lax.broadcasted_iota(jnp.int32, (members, members), 0)
    columns = lax.broadcasted_iota(jnp.int32, (members, members), 1)
    return (rows == columns).astype(F32)


def on_blocks(members, size):
    rows = lax.broadcasted_iota(jnp.int32, (size, size), 0) // members
    columns = lax.broadcasted_iota(jnp.int32, (size, size), 1) // members
    return rows == columns


def loads(plan, piece, values, buffer, sems):
    base = plan.pieces[piece][0]
    copies = [
        pltpu.make_async_copy(values.at[start:stop], buffer.at[start - base : stop - base], sems.at[at])
        for at, (start, stop) in enumerate(plan.piece_groups[piece])
    ]
    for copy in copies:
        copy.start()
    return copies


def chain_kernel(
    plan, transforms, ensembles, cotangents, suffixes, total, kept, ens, cot, sem, ens_sem, cot_sem
):
    count, members = plan.count, plan.members
    read = pltpu.make_async_copy(transforms, kept, sem)
    read.start()
    read.wait()
    more = loads(plan, 0, ensembles, ens, ens_sem) + loads(plan, 0, cotangents, cot, cot_sem)
    for at in range(count):
        suffixes[plan.rows(at, at + 1)] = kept[at]
    suffix_scan(suffixes, count, members, count)
    total[...] = suffixes[plan.rows(0, 1)]
    for copy in more:
        copy.wait()


def windows_kernel(plan, kept, _, steps, runs):
    count = plan.count
    for at in range(count - 1):
        runs[plan.rows(at + 1, at + 2)] = kept[at].T
    number = 0
    width = 1
    while width < count:
        for middle in range(width, count, 2 * width):
            size = min(width, count - middle)
            for side, part in enumerate(split(runs[plan.rows(middle, middle + size)])):
                steps[side, plan.rows(number, number + size)] = part
            number += size
        for start in range(2 * width, count, 2 * width):
            if start + width < count:
                rows = plan.rows(start + width, min(start + 2 * width, count))
                runs[rows] = mul_exact(runs[rows], runs[plan.rows(start + width - 1, start + width)])
        width *= 2


def count_steps(count):
    total = 0
    width = 1
    while width < count:
        total += sum(min(width, count - middle) for middle in range(width, count, 2 * width))
        width *= 2
    return total


def core_index():
    return lax.rem(lax.axis_index("space"), 2)


def gram_of(plan, piece, cot, ens, suffixes, whole, ready=lambda: None):
    members = plan.members
    base = plan.pieces[piece][0]
    offset = jnp.zeros((members, members), F32)
    for at, (start, stop) in enumerate(plan.piece_groups[piece]):
        ready()
        size = (stop - start) * members
        stacked = [ref[start - base : stop - base].reshape(size, ref.shape[2]) for ref in (cot, ens)]
        wide = jnp.where(on_blocks(members, size), mul(*stacked, ROWS), 0.0)
        gram = wide[:members]
        for i in range(1, stop - start):
            gram = gram + wide[i * members : (i + 1) * members]
        offset = offset + mul_exact(gram, suffixes[plan.rows(start, stop)])
        lanes = plan.lanes(plan.first_group[piece] + at)
        width = lanes.stop - lanes.start
        whole[:, lanes] = jnp.pad(gram, ((0, 0), (0, width - size)))
    return offset


def early_gram_kernel(plan, ensembles, cotangents, suffixes, ens, cot, whole, offset, *refs):
    buffers, sems = refs[: 2 * (PIECES - 1)], refs[2 * (PIECES - 1) :]
    copies = []
    for piece in range(1, PIECES):
        pair = buffers[2 * piece - 2 : 2 * piece]
        own = sems[2 * piece - 2 : 2 * piece]
        copies.append(list(zip(
            loads(plan, piece, ensembles, pair[0], own[0]),
            loads(plan, piece, cotangents, pair[1], own[1]),
        )))
    total = gram_of(plan, 0, cot, ens, suffixes, whole)
    for piece in range(1, PIECES - 1):
        waiting = iter(copies[piece - 1])

        def ready():
            for copy in next(waiting):
                copy.wait()

        ens, cot = buffers[2 * piece - 2 : 2 * piece]
        total = total + gram_of(plan, piece, cot, ens, suffixes, whole, ready)
    offset[...] = total
    for pair in copies[-1]:
        for copy in pair:
            copy.wait()


def late_gram_kernel(plan, ens, cot, suffixes, early, offset, _, grams, offsets):
    grams[:, : early.shape[1]] = early[...]
    offsets[...] = offset[...] + gram_of(plan, PIECES - 1, cot, ens, suffixes, grams)


def sum_kernel(number, through, *refs):
    total = refs[0][...]
    for ref in refs[1:number]:
        total = total + ref[...]
    refs[number + 1 + through][...] = total


def enter_kernel(blocks, products, entering, windows):
    members = entering.shape[0]
    mine = lax.axis_index("tm")
    unit = eye(members)
    factors = [products[at] for at in range(blocks)]
    entering[...] = product_of([jnp.where(at > mine, factors[at], unit) for at in range(1, blocks)])
    for at in range(1, blocks):
        windows[(at - 1) * members : at * members] = jnp.where(at < mine, factors[at], unit)
    suffix_scan(windows, blocks - 1, members, blocks - 1)


def carry_kernel(plan, suffixes, later, _, ens_factors, cot_factors, follow):
    count, members = plan.count, plan.members
    entering = later[...]
    mask = on_blocks(members, plan.stack * members)
    repeated = split(jnp.concatenate([entering] * plan.stack, axis=1))
    for at, (start, stop) in enumerate(plan.groups):
        size = (stop - start) * members
        wide = mul_pairs(split(suffixes[plan.rows(start, stop)]), repeated)
        part = jnp.where(mask[:size, :size], wide[:, :size], 0.0)
        cot_factors[at, :size, :size] = part.astype(BF16)
        ens_factors[at, :size, :size] = part.T.astype(BF16)
        first = max(start - 1, 0)
        kept = wide[(first + 1 - start) * members :, :members]
        for side, value in enumerate(split(kept)):
            follow[side, plan.rows(first, stop - 1)] = value
    for side, value in enumerate(split(entering)):
        follow[side, plan.rows(count - 1, count)] = value


def apply_kernel(plan, pieces, factors, *refs):
    out, marker, out_buf, out_sem = refs[-4:]
    members = plan.members
    marker[...] = jnp.zeros_like(marker)
    base = plan.pieces[pieces[0]][0]
    chunk = out_buf.shape[2] // 2
    writes = []
    for values, piece in zip(refs, pieces):
        first = plan.pieces[piece][0]
        for at, (start, stop) in enumerate(plan.piece_groups[piece]):
            size = (stop - start) * members
            for side in range(2):
                columns = slice(side * chunk, (side + 1) * chunk)
                stacked = values[start - first : stop - first, :, columns].reshape(size, chunk)
                result = mul(factors[plan.first_group[piece] + at, :size, :size], stacked)
                out_buf[start - base : stop - base, :, columns] = result.astype(BF16).reshape(
                    stop - start, members, chunk
                )
                copy = pltpu.make_async_copy(
                    out_buf.at[start - base : stop - base, :, columns],
                    out.at[start:stop, :, columns],
                    out_sem.at[len(writes)],
                )
                copy.start()
                writes.append(copy)
    for copy in writes:
        copy.wait()


def final_kernel(plan, blocks, scale, number, *refs):
    messages = refs[:number]
    offsets, windows, follow, steps, _, out, buffer, sems = refs[number:]
    count, members = plan.count, plan.members
    mine = lax.axis_index("tm")
    carry = jnp.zeros((members, members), F32)
    for at in range(blocks - 1):
        window = windows[at * members : (at + 1) * members]
        carry = carry + mul_exact(jnp.where(at < mine, offsets[at], 0.0), window)
    totals = []
    for at, (start, stop) in enumerate(plan.groups):
        wide = messages[0][:, plan.lanes(at)]
        for ref in messages[1:]:
            wide = wide + ref[:, plan.lanes(at)]
        tall = wide.T
        for i in range(stop - start):
            totals.append(tall[i * members : (i + 1) * members])
    totals[0] = totals[0] + carry.T
    number = 0
    width = 1
    while width < count:
        for start in range(width, count, 2 * width):
            size = min(width, count - start)
            rows = plan.rows(number, number + size)
            added = mul_pairs((steps[0, rows], steps[1, rows]), split(totals[start - 1]))
            for at in range(size):
                totals[start + at] = totals[start + at] + added[at * members : (at + 1) * members]
            number += size
        width *= 2
    copies = []
    for at in range(count):
        rows = plan.rows(at, at + 1)
        buffer[at] = mul_pairs(split(totals[at]), (follow[0, rows], follow[1, rows]), ROWS) * scale
        copy = pltpu.make_async_copy(buffer.at[at], out.at[at], sems.at[at])
        copy.start()
        copies.append(copy)
    for copy in copies:
        copy.wait()


def call(kernel, outs, ins, out_specs, scratch, micros, name, limit=16, aliases=None):
    return pl.pallas_call(
        kernel,
        out_shape=outs,
        in_specs=ins,
        out_specs=out_specs,
        scratch_shapes=scratch,
        input_output_aliases=aliases or {},
        compiler_params=pltpu.CompilerParams(vmem_limit_bytes=limit << 20),
        cost_estimate=pl.CostEstimate(
            flops=0, bytes_accessed=int(micros * 3.6e6), transcendentals=0
        ),
        name=name,
    )


def shape(*dims, kind=F32):
    return jax.ShapeDtypeStruct(dims, kind)


def shards(ensembles, cotangents, transforms):
    count, members, cells = ensembles.shape
    blocks, lanes = lax.axis_size("tm"), lax.axis_size("space")
    chips = lanes // 2
    scale = 1.0 / math.sqrt(cells * lanes * count * blocks)
    plan = Plan(count, members)
    square = shape(members, members)
    ensembles, cotangents, transforms = (
        pltpu.with_memory_space_constraint(value, pltpu.HBM)
        for value in (ensembles, cotangents, transforms)
    )

    def to_all(value):
        copies = jnp.broadcast_to(value[None], (blocks,) + value.shape)
        return lax.all_to_all(copies, "tm", 0, 0)

    def swap_cores(value):
        return lax.ppermute(value, "space", [(at, at ^ 1) for at in range(lanes)])

    def around(value):
        return [
            lax.ppermute(value, "space", [(at, (at + 2 * d) % lanes) for at in range(lanes)])
            for d in range(1, chips)
        ]

    def piece_shape(piece):
        first, last = plan.pieces[piece]
        return shape(last - first, members, cells, kind=BF16)

    def piece_sems(piece):
        return [pltpu.SemaphoreType.DMA((len(plan.piece_groups[piece]),))] * 2

    suffixes, total, kept, *first_part = call(
        functools.partial(chain_kernel, plan),
        [shape(count * members, members), square, shape(count, members, members)] + [piece_shape(0)] * 2,
        [HBM] * 3, [VMEM] * 5, [pltpu.SemaphoreType.DMA] + piece_sems(0), 3.5, "transform_chain",
    )(transforms, ensembles, cotangents)

    wide = shape(members, plan.width)
    def add(values, after, name, *through):
        number = len(values)
        return call(
            functools.partial(sum_kernel, number, len(through)),
            [shape(*values[0].shape)] + [shape(*value.shape) for value in through],
            [VMEM] * number + [ANY] * (1 + len(through)), [VMEM] + [ANY] * len(through), [], 0.1, name,
            aliases={number + 1 + at: 1 + at for at in range(len(through))},
        )(*values, after, *through)

    products = to_all(total)
    early_width = plan.lanes(plan.first_group[-1]).start
    early, offset, *loaded = call(
        functools.partial(early_gram_kernel, plan),
        [shape(members, early_width), square]
        + [piece_shape(piece) for piece in range(1, PIECES) for _ in range(2)],
        [HBM] * 2 + [VMEM] * 3, [VMEM] * (2 * PIECES),
        [sem for piece in range(1, PIECES) for sem in piece_sems(piece)], 3, "early_gram",
    )(ensembles, cotangents, suffixes, *first_part)
    parts = [first_part] + [loaded[at : at + 2] for at in range(0, len(loaded), 2)]
    gram, offset = call(
        functools.partial(late_gram_kernel, plan),
        [wide, square], [VMEM] * 5 + [ANY], [VMEM] * 2, [], 1.2, "late_gram",
    )(*parts[-1], suffixes, early, offset, offset)
    offset_core = swap_cores(offset)
    offset, gram = add([offset, offset_core], offset, "chip_offset", gram)
    gram_core = swap_cores(gram)
    offsets = [offset] + around(offset)
    entering, windows = call(
        functools.partial(enter_kernel, blocks),
        [square, shape((blocks - 1) * members, members)], [VMEM], [VMEM] * 2, [], 0.8, "entering",
    )(products)

    steps = call(
        functools.partial(windows_kernel, plan),
        shape(2, count_steps(count) * members, members, kind=BF16), [VMEM, ANY], VMEM,
        [pltpu.VMEM((count * members, members), F32)], 1.0, "windows",
    )(kept, offset)
    size = plan.stack * members
    ens_factors, cot_factors, follow = call(
        functools.partial(carry_kernel, plan),
        [shape(len(plan.groups), size, size, kind=BF16)] * 2
        + [shape(2, count * members, members, kind=BF16)],
        [VMEM] * 2 + [ANY], [VMEM] * 3, [], 0.9, "carries",
    )(suffixes, entering, steps)

    def apply(factors, which, pieces, out, after, name, micros):
        first, last = plan.pieces[pieces[0]][0], plan.pieces[pieces[-1]][1]
        number = 2 * sum(len(plan.piece_groups[piece]) for piece in pieces)
        return call(
            functools.partial(apply_kernel, plan, pieces),
            [shape(count, members, cells, kind=BF16), shape(8, 128)],
            [VMEM] * (1 + len(pieces)) + [ANY] + [HBM] * len(out), [HBM, VMEM],
            [pltpu.VMEM((last - first, members, cells), BF16), pltpu.SemaphoreType.DMA((number,))],
            micros, name, aliases={2 + len(pieces): 0} if out else None,
        )(factors, *(parts[piece][which] for piece in pieces), after, *out)

    front, rear = tuple(range(PIECES - 1)), (PIECES - 1,)
    smoothed, done = apply(ens_factors, 0, rear, (), follow, "smoothed_0", 1.4)
    own, gram_core = add(offsets, done, "own_offset", gram_core)
    gram = gram + gram_core
    grams = [gram] + around(gram)
    offsets = to_all(own)
    smoothed, done = apply(ens_factors, 0, front, (smoothed,), own, "smoothed_1", 2.3)
    ensemble_grad, done = apply(cot_factors, 1, tuple(range(PIECES)), (), done, "ensemble_grad", 2.8)
    transform_grad = call(
        functools.partial(final_kernel, plan, blocks, scale, chips),
        shape(count, members, members),
        [VMEM] * (chips + 4) + [ANY], HBM,
        [pltpu.VMEM((count, members, members), F32), pltpu.SemaphoreType.DMA((count,))],
        2.5, "transform_grad",
    )(*grams, offsets, windows, follow, steps, done)
    return (smoothed, ensemble_grad, transform_grad)


def solution(mesh):
    return jax.shard_map(
        shards,
        mesh=mesh,
        in_specs=(P("tm", None, "space"), P("tm", None, "space"), P("tm", None, None)),
        out_specs=(P("tm", None, "space"), P("tm", None, "space"), P("tm", None, None)),
        check_vma=False,
    )
```

```python
import functools
import math

import jax
import jax.numpy as jnp
from jax import lax
from jax.experimental import pallas as pl
from jax.experimental.pallas import tpu as pltpu
from jax.sharding import PartitionSpec as P

F32 = jnp.float32
BF16 = jnp.bfloat16
VMEM = pl.BlockSpec(memory_space=pltpu.VMEM)
HBM = pl.BlockSpec(memory_space=pltpu.HBM)
ANY = pl.BlockSpec(memory_space=pl.ANY)
DEPTH = 256
PIECES = 3
NORMAL = (((1,), (0,)), ((), ()))
ROWS = (((1,), (1,)), ((), ()))


def split(value):
    high = value.astype(BF16)
    return high, (value - high.astype(F32)).astype(BF16)


def mul(left, right, dims=NORMAL):
    return lax.dot_general(left, right, dims, preferred_element_type=F32)


def mul_pairs(left, right, dims=NORMAL):
    return mul(left[0], right[0], dims) + (
        mul(left[0], right[1], dims) + mul(left[1], right[0], dims)
    )


def mul_exact(left, right, dims=NORMAL):
    return mul_pairs(split(left), split(right), dims)


def product_of(factors):
    while len(factors) > 1:
        joined = [mul_exact(*factors[at : at + 2]) for at in range(0, len(factors) - 1, 2)]
        factors = joined + factors[len(joined) * 2 :]
    return factors[0]


def suffix_scan(ref, count, members, stop):
    width = 1
    while width < stop:
        for start in range(0, count, 2 * width):
            middle = start + width
            if middle < count:
                rows = slice(start * members, middle * members)
                ref[rows] = mul_exact(ref[rows], ref[middle * members : (middle + 1) * members])
        width *= 2


class Plan:
    def __init__(self, count, members):
        self.count, self.members = count, members
        self.stack = DEPTH // members
        self.groups = [
            (start, min(start + self.stack, count)) for start in range(0, count, self.stack)
        ]
        bounds = [len(self.groups) * at // PIECES for at in range(PIECES + 1)]
        self.piece_groups = [self.groups[a:b] for a, b in zip(bounds, bounds[1:])]
        self.pieces = [(part[0][0], part[-1][1]) for part in self.piece_groups]
        self.first_group = bounds[:-1]
        self.widths = [-(-(stop - start) * members // 128) * 128 for start, stop in self.groups]
        self.width = sum(self.widths)

    def lanes(self, at):
        start = sum(self.widths[:at])
        return slice(start, start + self.widths[at])

    def rows(self, first, last):
        return slice(first * self.members, last * self.members)


def on_blocks(members, size):
    rows = lax.broadcasted_iota(jnp.int32, (size, size), 0) // members
    columns = lax.broadcasted_iota(jnp.int32, (size, size), 1) // members
    return rows == columns


def loads(plan, piece, values, buffer, sems):
    base = plan.pieces[piece][0]
    copies = [
        pltpu.make_async_copy(values.at[start:stop], buffer.at[start - base : stop - base], sems.at[at])
        for at, (start, stop) in enumerate(plan.piece_groups[piece])
    ]
    for copy in copies:
        copy.start()
    return copies


def chain_kernel(
    plan, transforms, ensembles, cotangents, suffixes, total, kept, ens, cot, sem, ens_sem, cot_sem
):
    count, members = plan.count, plan.members
    read = pltpu.make_async_copy(transforms, kept, sem)
    read.start()
    read.wait()
    more = loads(plan, 0, ensembles, ens, ens_sem) + loads(plan, 0, cotangents, cot, cot_sem)
    for at in range(count):
        suffixes[plan.rows(at, at + 1)] = kept[at]
    suffix_scan(suffixes, count, members, count)
    total[...] = suffixes[plan.rows(0, 1)]
    for copy in more:
        copy.wait()


def windows_kernel(plan, kept, _, steps, runs):
    count = plan.count
    for at in range(count - 1):
        runs[plan.rows(at + 1, at + 2)] = kept[at].T
    number = 0
    width = 1
    while width < count:
        for middle in range(width, count, 2 * width):
            size = min(width, count - middle)
            for side, part in enumerate(split(runs[plan.rows(middle, middle + size)])):
                steps[side, plan.rows(number, number + size)] = part
            number += size
        for start in range(2 * width, count, 2 * width):
            if start + width < count:
                rows = plan.rows(start + width, min(start + 2 * width, count))
                runs[rows] = mul_exact(runs[rows], runs[plan.rows(start + width - 1, start + width)])
        width *= 2


def count_steps(count):
    total = 0
    width = 1
    while width < count:
        total += sum(min(width, count - middle) for middle in range(width, count, 2 * width))
        width *= 2
    return total


def core_index():
    return lax.rem(lax.axis_index("space"), 2)


def gram_of(plan, piece, cot, ens, suffixes, whole, ready=lambda: None):
    members = plan.members
    base = plan.pieces[piece][0]
    offset = jnp.zeros((members, members), F32)
    for at, (start, stop) in enumerate(plan.piece_groups[piece]):
        ready()
        size = (stop - start) * members
        stacked = [ref[start - base : stop - base].reshape(size, ref.shape[2]) for ref in (cot, ens)]
        wide = jnp.where(on_blocks(members, size), mul(*stacked, ROWS), 0.0)
        gram = wide[:members]
        for i in range(1, stop - start):
            gram = gram + wide[i * members : (i + 1) * members]
        offset = offset + mul_exact(gram, suffixes[plan.rows(start, stop)])
        lanes = plan.lanes(plan.first_group[piece] + at)
        width = lanes.stop - lanes.start
        whole[:, lanes] = jnp.pad(gram, ((0, 0), (0, width - size)))
    return offset


def early_gram_kernel(plan, ensembles, cotangents, suffixes, ens, cot, whole, offset, *refs):
    buffers, sems = refs[: 2 * (PIECES - 1)], refs[2 * (PIECES - 1) :]
    copies = []
    for piece in range(1, PIECES):
        pair = buffers[2 * piece - 2 : 2 * piece]
        own = sems[2 * piece - 2 : 2 * piece]
        copies.append(list(zip(
            loads(plan, piece, ensembles, pair[0], own[0]),
            loads(plan, piece, cotangents, pair[1], own[1]),
        )))
    total = gram_of(plan, 0, cot, ens, suffixes, whole)
    for piece in range(1, PIECES - 1):
        waiting = iter(copies[piece - 1])

        def ready():
            for copy in next(waiting):
                copy.wait()

        ens, cot = buffers[2 * piece - 2 : 2 * piece]
        total = total + gram_of(plan, piece, cot, ens, suffixes, whole, ready)
    offset[...] = total
    for pair in copies[-1]:
        for copy in pair:
            copy.wait()


def late_gram_kernel(plan, ens, cot, suffixes, early, offset, _, kept, sent, offsets, whole):
    whole[:, : early.shape[1]] = early[...]
    offsets[...] = offset[...] + gram_of(plan, PIECES - 1, cot, ens, suffixes, whole)
    half = plan.members // 2
    core = lax.rem(lax.axis_index("space"), 2)
    kept[...] = whole[pl.ds(core * half, half)]
    sent[...] = whole[pl.ds((1 - core) * half, half)]


def upper_half(level):
    return lax.rem(lax.axis_index("tm") // (1 << level), 2) == 1


def join_kernel(level, total, other, later, before, _, new_total, new_later, new_before, upper_total):
    upper = upper_half(level)
    left = jnp.where(upper, other[...], total[...])
    right = jnp.where(upper, total[...], other[...])
    new_total[...] = mul_exact(left, right)
    upper_total[...] = right
    new_later[...] = jnp.where(upper, later[...], mul_exact(later[...], other[...]))
    new_before[...] = jnp.where(upper, mul_exact(other[...], before[...]), before[...])


def sum_kernel(left, right, _, __, total, ___):
    total[...] = left[...] + right[...]


def pass_kernel(level, own, other, carry, upper_total, before, _, *refs):
    new_own, new_carry = refs[len(refs) // 2 - 1 : len(refs) // 2 + 1]
    upper = upper_half(level)
    left = jnp.where(upper, other[...], own[...])
    right = jnp.where(upper, own[...], other[...])
    new_own[...] = mul_exact(left, upper_total[...]) + right
    new_carry[...] = carry[...] + jnp.where(upper, mul_exact(left, before[...]), 0.0)


def last_pass_kernel(level, other, carry, before, _, new_carry):
    added = mul_exact(other[...], before[...])
    new_carry[...] = carry[...] + jnp.where(upper_half(level), added, 0.0)


def enter_kernel(level, later, other, _, entering):
    joined = mul_exact(later[...], other[...])
    entering[...] = jnp.where(upper_half(level), later[...], joined)


def carry_kernel(plan, suffixes, later, ens_factors, cot_factors, follow):
    count, members = plan.count, plan.members
    entering = later[...]
    mask = on_blocks(members, plan.stack * members)
    repeated = split(jnp.concatenate([entering] * plan.stack, axis=1))
    for at, (start, stop) in enumerate(plan.groups):
        size = (stop - start) * members
        wide = mul_pairs(split(suffixes[plan.rows(start, stop)]), repeated)
        part = jnp.where(mask[:size, :size], wide[:, :size], 0.0)
        cot_factors[at, :size, :size] = part.astype(BF16)
        ens_factors[at, :size, :size] = part.T.astype(BF16)
        first = max(start - 1, 0)
        kept = wide[(first + 1 - start) * members :, :members]
        for side, value in enumerate(split(kept)):
            follow[side, plan.rows(first, stop - 1)] = value
    for side, value in enumerate(split(entering)):
        follow[side, plan.rows(count - 1, count)] = value


def apply_kernel(plan, pieces, factors, *refs):
    out, marker, out_buf, out_sem = refs[-4:]
    members = plan.members
    marker[...] = jnp.zeros_like(marker)
    base = plan.pieces[pieces[0]][0]
    chunk = out_buf.shape[2] // 2
    writes = []
    for values, piece in zip(refs, pieces):
        first = plan.pieces[piece][0]
        for at, (start, stop) in enumerate(plan.piece_groups[piece]):
            size = (stop - start) * members
            for side in range(2):
                columns = slice(side * chunk, (side + 1) * chunk)
                stacked = values[start - first : stop - first, :, columns].reshape(size, chunk)
                result = mul(factors[plan.first_group[piece] + at, :size, :size], stacked)
                out_buf[start - base : stop - base, :, columns] = result.astype(BF16).reshape(
                    stop - start, members, chunk
                )
                copy = pltpu.make_async_copy(
                    out_buf.at[start - base : stop - base, :, columns],
                    out.at[start:stop, :, columns],
                    out_sem.at[len(writes)],
                )
                copy.start()
                writes.append(copy)
    for copy in writes:
        copy.wait()


def final_kernel(plan, scale, gram_mine, gram_other, follow, steps, _, *refs):
    carries, (out, buffer, sems) = refs[:-3], refs[-3:]
    carry = carries[0][...]
    for ref in carries[1:]:
        carry = carry + ref[...]
    count, members = plan.count, plan.members
    first = lax.rem(lax.axis_index("space"), 2) == 0

    def whole(mine, other):
        return jnp.concatenate([jnp.where(first, mine, other), jnp.where(first, other, mine)], axis=0)

    totals = []
    for at, (start, stop) in enumerate(plan.groups):
        lanes = plan.lanes(at)
        tall = whole(gram_mine[:, lanes], gram_other[:, lanes]).T
        for i in range(stop - start):
            totals.append(tall[i * members : (i + 1) * members])
    totals[0] = totals[0] + carry.T
    number = 0
    width = 1
    while width < count:
        for start in range(width, count, 2 * width):
            size = min(width, count - start)
            rows = plan.rows(number, number + size)
            added = mul_pairs((steps[0, rows], steps[1, rows]), split(totals[start - 1]))
            for at in range(size):
                totals[start + at] = totals[start + at] + added[at * members : (at + 1) * members]
            number += size
        width *= 2
    copies = []
    for at in range(count):
        rows = plan.rows(at, at + 1)
        buffer[at] = mul_pairs(split(totals[at]), (follow[0, rows], follow[1, rows]), ROWS) * scale
        copy = pltpu.make_async_copy(buffer.at[at], out.at[at], sems.at[at])
        copy.start()
        copies.append(copy)
    for copy in copies:
        copy.wait()


def call(kernel, outs, ins, out_specs, scratch, micros, name, limit=16, aliases=None):
    return pl.pallas_call(
        kernel,
        out_shape=outs,
        in_specs=ins,
        out_specs=out_specs,
        scratch_shapes=scratch,
        input_output_aliases=aliases or {},
        compiler_params=pltpu.CompilerParams(vmem_limit_bytes=limit << 20),
        cost_estimate=pl.CostEstimate(
            flops=0, bytes_accessed=int(micros * 3.6e6), transcendentals=0
        ),
        name=name,
    )


def shape(*dims, kind=F32):
    return jax.ShapeDtypeStruct(dims, kind)


def shards(ensembles, cotangents, transforms):
    count, members, cells = ensembles.shape
    blocks, lanes = lax.axis_size("tm"), lax.axis_size("space")
    chips = lanes // 2
    scale = 1.0 / math.sqrt(cells * lanes * count * blocks)
    plan = Plan(count, members)
    levels = blocks.bit_length() - 1
    square = shape(members, members)
    ensembles, cotangents, transforms = (
        pltpu.with_memory_space_constraint(value, pltpu.HBM)
        for value in (ensembles, cotangents, transforms)
    )

    def exchange(value, axis, size, bit):
        return lax.ppermute(value, axis, [(at, at ^ bit) for at in range(size)])

    def around(value):
        return [
            lax.ppermute(value, "space", [(at, (at + 2 * d) % lanes) for at in range(lanes)])
            for d in range(1, chips)
        ]

    def piece_shape(piece):
        first, last = plan.pieces[piece]
        return shape(last - first, members, cells, kind=BF16)

    def piece_sems(piece):
        return [pltpu.SemaphoreType.DMA((len(plan.piece_groups[piece]),))] * 2

    suffixes, total, kept, *first_part = call(
        functools.partial(chain_kernel, plan),
        [shape(count * members, members), square, shape(count, members, members)] + [piece_shape(0)] * 2,
        [HBM] * 3, [VMEM] * 5, [pltpu.SemaphoreType.DMA] + piece_sems(0), 3.5, "transform_chain",
    )(transforms, ensembles, cotangents)

    wide = shape(members // 2, plan.width)
    later = before = jnp.eye(members, dtype=F32)
    uppers, befores = [], []

    def join(level, total, other, later, before, after):
        befores.append(before)
        *new, upper = call(
            functools.partial(join_kernel, level),
            [square] * 4, [VMEM] * 4 + [ANY], [VMEM] * 4, [], 0.3, f"join_{level}",
        )(total, other, later, before, after)
        uppers.append(upper)
        return new

    other = exchange(total, "tm", blocks, 1)
    early_width = plan.lanes(plan.first_group[-1]).start
    early, offset, *loaded = call(
        functools.partial(early_gram_kernel, plan),
        [shape(members, early_width), square]
        + [piece_shape(piece) for piece in range(1, PIECES) for _ in range(2)],
        [HBM] * 2 + [VMEM] * 3, [VMEM] * (2 * PIECES),
        [sem for piece in range(1, PIECES) for sem in piece_sems(piece)], 3, "early_gram",
    )(ensembles, cotangents, suffixes, *first_part)
    parts = [first_part] + [loaded[at : at + 2] for at in range(0, len(loaded), 2)]
    total, later, before = join(0, total, other, later, before, offset)

    other = exchange(total, "tm", blocks, 2)
    gram, gram_sent, own = call(
        functools.partial(late_gram_kernel, plan),
        [wide, wide, square], [VMEM] * 5 + [ANY], [VMEM] * 3,
        [pltpu.VMEM((members, plan.width), F32)], 1.2, "late_gram",
    )(*parts[-1], suffixes, early, offset, total)
    other_own = exchange(own, "tm", blocks, 1)
    for level in range(1, levels - 1):
        total, later, before = join(level, total, other, later, before, own)
        other = exchange(total, "tm", blocks, 2 << level)
    befores.append(before)
    steps = call(
        functools.partial(windows_kernel, plan),
        shape(2, count_steps(count) * members, members, kind=BF16), [VMEM, ANY], VMEM,
        [pltpu.VMEM((count * members, members), F32)], 1.0, "windows",
    )(kept, total)

    def pass_on(level, carry, after, *through):
        more = [shape(*value.shape) for value in through]
        return call(
            functools.partial(pass_kernel, level),
            [square] * 2 + more, [VMEM] * 5 + [ANY] * (1 + len(more)), [VMEM] * 2 + [ANY] * len(more),
            [], 0.3, f"pass_{level}", aliases={6 + at: 2 + at for at in range(len(more))},
        )(own, other_own, carry, uppers[level], befores[level], after, *through)

    carry = jnp.zeros((members, members), F32)
    own, carry, gram_sent = pass_on(0, carry, steps, gram_sent)
    other_own = exchange(own, "tm", blocks, 2)
    gram_core = exchange(gram_sent, "space", lanes, 1)
    for level in range(1, levels - 2):
        own, carry = pass_on(level, carry, own)
        other_own = exchange(own, "tm", blocks, 2 << level)
    own, carry, gram_core, other = pass_on(levels - 2, carry, own, gram_core, other)
    other_own = exchange(own, "tm", blocks, blocks // 2)
    gram = gram + gram_core
    grams = around(gram)
    entering = call(
        functools.partial(enter_kernel, levels - 1),
        square, [VMEM] * 2 + [ANY], VMEM, [], 0.2, "entering",
    )(later, other, own)
    size = plan.stack * members
    ens_factors, cot_factors, follow = call(
        functools.partial(carry_kernel, plan),
        [shape(len(plan.groups), size, size, kind=BF16)] * 2
        + [shape(2, count * members, members, kind=BF16)],
        [VMEM] * 2, [VMEM] * 3, [], 0.9, "carries",
    )(suffixes, entering)

    def apply(factors, which, pieces, out, after, name):
        first, last = plan.pieces[pieces[0]][0], plan.pieces[pieces[-1]][1]
        number = 2 * sum(len(plan.piece_groups[piece]) for piece in pieces)
        return call(
            functools.partial(apply_kernel, plan, pieces),
            [shape(count, members, cells, kind=BF16), shape(8, 128)],
            [VMEM] * (1 + len(pieces)) + [ANY] + [HBM] * len(out), [HBM, VMEM],
            [pltpu.VMEM((last - first, members, cells), BF16), pltpu.SemaphoreType.DMA((number,))],
            1.8, name, aliases={2 + len(pieces): 0} if out else None,
        )(factors, *(parts[piece][which] for piece in pieces), after, *out)

    front, rear = tuple(range(PIECES - 1)), (PIECES - 1,)
    smoothed, done = apply(ens_factors, 0, front + rear, (), follow, "smoothed")
    carry = call(
        functools.partial(last_pass_kernel, levels - 1),
        square, [VMEM] * 3 + [ANY], VMEM, [], 0.2, "pass_last",
    )(other_own, carry, befores[-1], done)
    carry_core = exchange(carry, "space", lanes, 1)
    ensemble_grad, done = apply(cot_factors, 1, rear, (), carry, "ensemble_grad_0")
    carry, grams[0] = call(
        sum_kernel, [square, wide], [VMEM] * 2 + [ANY] * 2, [VMEM, ANY], [], 0.1, "chip_carry",
        aliases={3: 1},
    )(carry, carry_core, done, grams[0])
    carries = [carry] + around(carry)
    for part in grams:
        gram = gram + part
    gram_other = exchange(gram, "space", lanes, 1)
    ensemble_grad, done = apply(cot_factors, 1, front, (ensemble_grad,), carry, "ensemble_grad_1")
    transform_grad = call(
        functools.partial(final_kernel, plan, scale),
        shape(count, members, members),
        [VMEM] * 4 + [ANY] + [VMEM] * chips, HBM,
        [pltpu.VMEM((count, members, members), F32), pltpu.SemaphoreType.DMA((count,))],
        2.5, "transform_grad",
    )(gram, gram_other, follow, steps, done, *carries)
    return (smoothed, ensemble_grad, transform_grad)


def solution(mesh):
    return jax.shard_map(
        shards,
        mesh=mesh,
        in_specs=(P("tm", None, "space"), P("tm", None, "space"), P("tm", None, None)),
        out_specs=(P("tm", None, "space"), P("tm", None, "space"), P("tm", None, None)),
        check_vma=False,
    )
```

```python
import functools
import math

import jax
import jax.numpy as jnp
from jax import lax
from jax.experimental import pallas as pl
from jax.experimental.pallas import tpu as pltpu
from jax.sharding import PartitionSpec as P

F32 = jnp.float32
BF16 = jnp.bfloat16
VMEM = pl.BlockSpec(memory_space=pltpu.VMEM)
HBM = pl.BlockSpec(memory_space=pltpu.HBM)
ANY = pl.BlockSpec(memory_space=pl.ANY)
DEPTH = 256
PIECES = 3
NORMAL = (((1,), (0,)), ((), ()))
ROWS = (((1,), (1,)), ((), ()))


def split(value):
    high = value.astype(BF16)
    return high, (value - high.astype(F32)).astype(BF16)


def mul(left, right, dims=NORMAL):
    return lax.dot_general(left, right, dims, preferred_element_type=F32)


def mul_pairs(left, right, dims=NORMAL):
    return mul(left[0], right[0], dims) + (
        mul(left[0], right[1], dims) + mul(left[1], right[0], dims)
    )


def mul_exact(left, right, dims=NORMAL):
    return mul_pairs(split(left), split(right), dims)


def product_of(factors):
    while len(factors) > 1:
        joined = [mul_exact(*factors[at : at + 2]) for at in range(0, len(factors) - 1, 2)]
        factors = joined + factors[len(joined) * 2 :]
    return factors[0]


def suffix_scan(ref, count, members, stop):
    width = 1
    while width < stop:
        for start in range(0, count, 2 * width):
            middle = start + width
            if middle < count:
                rows = slice(start * members, middle * members)
                ref[rows] = mul_exact(ref[rows], ref[middle * members : (middle + 1) * members])
        width *= 2


class Plan:
    def __init__(self, count, members):
        self.count, self.members = count, members
        self.stack = DEPTH // members
        self.groups = [
            (start, min(start + self.stack, count)) for start in range(0, count, self.stack)
        ]
        bounds = [len(self.groups) * at // PIECES for at in range(PIECES + 1)]
        self.piece_groups = [self.groups[a:b] for a, b in zip(bounds, bounds[1:])]
        self.pieces = [(part[0][0], part[-1][1]) for part in self.piece_groups]
        self.first_group = bounds[:-1]
        self.widths = [-(-(stop - start) * members // 128) * 128 for start, stop in self.groups]
        self.width = sum(self.widths)

    def lanes(self, at):
        start = sum(self.widths[:at])
        return slice(start, start + self.widths[at])

    def rows(self, first, last):
        return slice(first * self.members, last * self.members)


def on_blocks(members, size):
    rows = lax.broadcasted_iota(jnp.int32, (size, size), 0) // members
    columns = lax.broadcasted_iota(jnp.int32, (size, size), 1) // members
    return rows == columns


def loads(plan, piece, values, buffer, sems):
    base = plan.pieces[piece][0]
    copies = [
        pltpu.make_async_copy(values.at[start:stop], buffer.at[start - base : stop - base], sems.at[at])
        for at, (start, stop) in enumerate(plan.piece_groups[piece])
    ]
    for copy in copies:
        copy.start()
    return copies


def chain_kernel(
    plan, transforms, ensembles, cotangents, suffixes, total, kept, ens, cot, sem, ens_sem, cot_sem
):
    count, members = plan.count, plan.members
    read = pltpu.make_async_copy(transforms, kept, sem)
    read.start()
    read.wait()
    more = loads(plan, 0, ensembles, ens, ens_sem) + loads(plan, 0, cotangents, cot, cot_sem)
    for at in range(count):
        suffixes[plan.rows(at, at + 1)] = kept[at]
    suffix_scan(suffixes, count, members, count)
    total[...] = suffixes[plan.rows(0, 1)]
    for copy in more:
        copy.wait()


def windows_kernel(plan, kept, _, steps, runs):
    count = plan.count
    for at in range(count - 1):
        runs[plan.rows(at + 1, at + 2)] = kept[at].T
    number = 0
    width = 1
    while width < count:
        for middle in range(width, count, 2 * width):
            size = min(width, count - middle)
            for side, part in enumerate(split(runs[plan.rows(middle, middle + size)])):
                steps[side, plan.rows(number, number + size)] = part
            number += size
        for start in range(2 * width, count, 2 * width):
            if start + width < count:
                rows = plan.rows(start + width, min(start + 2 * width, count))
                runs[rows] = mul_exact(runs[rows], runs[plan.rows(start + width - 1, start + width)])
        width *= 2


def count_steps(count):
    total = 0
    width = 1
    while width < count:
        total += sum(min(width, count - middle) for middle in range(width, count, 2 * width))
        width *= 2
    return total


def core_index():
    return lax.rem(lax.axis_index("space"), 2)


def gram_of(plan, piece, cot, ens, suffixes, whole, ready=lambda: None):
    members = plan.members
    base = plan.pieces[piece][0]
    offset = jnp.zeros((members, members), F32)
    for at, (start, stop) in enumerate(plan.piece_groups[piece]):
        ready()
        size = (stop - start) * members
        stacked = [ref[start - base : stop - base].reshape(size, ref.shape[2]) for ref in (cot, ens)]
        wide = jnp.where(on_blocks(members, size), mul(*stacked, ROWS), 0.0)
        gram = wide[:members]
        for i in range(1, stop - start):
            gram = gram + wide[i * members : (i + 1) * members]
        offset = offset + mul_exact(gram, suffixes[plan.rows(start, stop)])
        lanes = plan.lanes(plan.first_group[piece] + at)
        width = lanes.stop - lanes.start
        whole[:, lanes] = jnp.pad(gram, ((0, 0), (0, width - size)))
    return offset


def early_gram_kernel(plan, ensembles, cotangents, suffixes, ens, cot, whole, offset, *refs):
    buffers, sems = refs[: 2 * (PIECES - 1)], refs[2 * (PIECES - 1) :]
    copies = []
    for piece in range(1, PIECES):
        pair = buffers[2 * piece - 2 : 2 * piece]
        own = sems[2 * piece - 2 : 2 * piece]
        copies.append(list(zip(
            loads(plan, piece, ensembles, pair[0], own[0]),
            loads(plan, piece, cotangents, pair[1], own[1]),
        )))
    total = gram_of(plan, 0, cot, ens, suffixes, whole)
    for piece in range(1, PIECES - 1):
        waiting = iter(copies[piece - 1])

        def ready():
            for copy in next(waiting):
                copy.wait()

        ens, cot = buffers[2 * piece - 2 : 2 * piece]
        total = total + gram_of(plan, piece, cot, ens, suffixes, whole, ready)
    offset[...] = total
    for pair in copies[-1]:
        for copy in pair:
            copy.wait()


def late_gram_kernel(plan, ens, cot, suffixes, early, offset, _, grams, offsets):
    grams[:, : early.shape[1]] = early[...]
    offsets[...] = offset[...] + gram_of(plan, PIECES - 1, cot, ens, suffixes, grams)


def upper_half(level):
    return lax.rem(lax.axis_index("tm") // (1 << level), 2) == 1


def join_kernel(level, total, other, later, before, _, *refs):
    new_total, new_later, new_before, upper_total = refs[len(refs) // 2 - 2 : len(refs) // 2 + 2]
    upper = upper_half(level)
    left = jnp.where(upper, other[...], total[...])
    right = jnp.where(upper, total[...], other[...])
    new_total[...] = mul_exact(left, right)
    upper_total[...] = right
    new_later[...] = jnp.where(upper, later[...], mul_exact(later[...], other[...]))
    new_before[...] = jnp.where(upper, mul_exact(other[...], before[...]), before[...])


def sum_kernel(left, right, _, total):
    total[...] = left[...] + right[...]


def pass_kernel(level, own, other, carry, upper_total, before, _, *refs):
    new_own, new_carry = refs[len(refs) // 2 - 1 : len(refs) // 2 + 1]
    upper = upper_half(level)
    left = jnp.where(upper, other[...], own[...])
    right = jnp.where(upper, own[...], other[...])
    new_own[...] = mul_exact(left, upper_total[...]) + right
    new_carry[...] = carry[...] + jnp.where(upper, mul_exact(left, before[...]), 0.0)


def last_pass_kernel(level, other, carry, before, _, __, new_carry, ___):
    added = mul_exact(other[...], before[...])
    new_carry[...] = carry[...] + jnp.where(upper_half(level), added, 0.0)


def enter_kernel(level, later, other, _, entering):
    joined = mul_exact(later[...], other[...])
    entering[...] = jnp.where(upper_half(level), later[...], joined)


def carry_kernel(plan, suffixes, later, ens_factors, cot_factors, follow):
    count, members = plan.count, plan.members
    entering = later[...]
    mask = on_blocks(members, plan.stack * members)
    repeated = split(jnp.concatenate([entering] * plan.stack, axis=1))
    for at, (start, stop) in enumerate(plan.groups):
        size = (stop - start) * members
        wide = mul_pairs(split(suffixes[plan.rows(start, stop)]), repeated)
        part = jnp.where(mask[:size, :size], wide[:, :size], 0.0)
        cot_factors[at, :size, :size] = part.astype(BF16)
        ens_factors[at, :size, :size] = part.T.astype(BF16)
        first = max(start - 1, 0)
        kept = wide[(first + 1 - start) * members :, :members]
        for side, value in enumerate(split(kept)):
            follow[side, plan.rows(first, stop - 1)] = value
    for side, value in enumerate(split(entering)):
        follow[side, plan.rows(count - 1, count)] = value


def apply_kernel(plan, pieces, factors, *refs):
    out, marker, out_buf, out_sem = refs[-4:]
    members = plan.members
    marker[...] = jnp.zeros_like(marker)
    base = plan.pieces[pieces[0]][0]
    chunk = out_buf.shape[2] // 2
    writes = []
    for values, piece in zip(refs, pieces):
        first = plan.pieces[piece][0]
        for at, (start, stop) in enumerate(plan.piece_groups[piece]):
            size = (stop - start) * members
            for side in range(2):
                columns = slice(side * chunk, (side + 1) * chunk)
                stacked = values[start - first : stop - first, :, columns].reshape(size, chunk)
                result = mul(factors[plan.first_group[piece] + at, :size, :size], stacked)
                out_buf[start - base : stop - base, :, columns] = result.astype(BF16).reshape(
                    stop - start, members, chunk
                )
                copy = pltpu.make_async_copy(
                    out_buf.at[start - base : stop - base, :, columns],
                    out.at[start:stop, :, columns],
                    out_sem.at[len(writes)],
                )
                copy.start()
                writes.append(copy)
    for copy in writes:
        copy.wait()


def final_kernel(plan, scale, gram, gram_core, follow, steps, _, *refs):
    carries, (out, buffer, sems) = refs[:-3], refs[-3:]
    carry = carries[0][...]
    for ref in carries[1:]:
        carry = carry + ref[...]
    count, members = plan.count, plan.members
    totals = []
    for at, (start, stop) in enumerate(plan.groups):
        tall = (gram[:, plan.lanes(at)] + gram_core[:, plan.lanes(at)]).T
        for i in range(stop - start):
            totals.append(tall[i * members : (i + 1) * members])
    totals[0] = totals[0] + carry.T
    number = 0
    width = 1
    while width < count:
        for start in range(width, count, 2 * width):
            size = min(width, count - start)
            rows = plan.rows(number, number + size)
            added = mul_pairs((steps[0, rows], steps[1, rows]), split(totals[start - 1]))
            for at in range(size):
                totals[start + at] = totals[start + at] + added[at * members : (at + 1) * members]
            number += size
        width *= 2
    copies = []
    for at in range(count):
        rows = plan.rows(at, at + 1)
        buffer[at] = mul_pairs(split(totals[at]), (follow[0, rows], follow[1, rows]), ROWS) * scale
        copy = pltpu.make_async_copy(buffer.at[at], out.at[at], sems.at[at])
        copy.start()
        copies.append(copy)
    for copy in copies:
        copy.wait()


def call(kernel, outs, ins, out_specs, scratch, micros, name, limit=16, aliases=None):
    return pl.pallas_call(
        kernel,
        out_shape=outs,
        in_specs=ins,
        out_specs=out_specs,
        scratch_shapes=scratch,
        input_output_aliases=aliases or {},
        compiler_params=pltpu.CompilerParams(vmem_limit_bytes=limit << 20),
        cost_estimate=pl.CostEstimate(
            flops=0, bytes_accessed=int(micros * 3.6e6), transcendentals=0
        ),
        name=name,
    )


def shape(*dims, kind=F32):
    return jax.ShapeDtypeStruct(dims, kind)


def shards(ensembles, cotangents, transforms):
    count, members, cells = ensembles.shape
    blocks, lanes = lax.axis_size("tm"), lax.axis_size("space")
    chips = lanes // 2
    scale = 1.0 / math.sqrt(cells * lanes * count * blocks)
    plan = Plan(count, members)
    levels = blocks.bit_length() - 1
    square = shape(members, members)
    ensembles, cotangents, transforms = (
        pltpu.with_memory_space_constraint(value, pltpu.HBM)
        for value in (ensembles, cotangents, transforms)
    )

    def exchange(value, axis, size, bit):
        return lax.ppermute(value, axis, [(at, at ^ bit) for at in range(size)])

    def around(value):
        return [
            lax.ppermute(value, "space", [(at, (at + 2 * d) % lanes) for at in range(lanes)])
            for d in range(1, chips)
        ]

    def piece_shape(piece):
        first, last = plan.pieces[piece]
        return shape(last - first, members, cells, kind=BF16)

    def piece_sems(piece):
        return [pltpu.SemaphoreType.DMA((len(plan.piece_groups[piece]),))] * 2

    suffixes, total, kept, *first_part = call(
        functools.partial(chain_kernel, plan),
        [shape(count * members, members), square, shape(count, members, members)] + [piece_shape(0)] * 2,
        [HBM] * 3, [VMEM] * 5, [pltpu.SemaphoreType.DMA] + piece_sems(0), 3.5, "transform_chain",
    )(transforms, ensembles, cotangents)

    wide = shape(members, plan.width)
    later = before = jnp.eye(members, dtype=F32)
    uppers, befores = [], []

    def join(level, total, other, later, before, after, *through):
        more = [shape(*value.shape) for value in through]
        befores.append(before)
        total, later, before, upper, *through = call(
            functools.partial(join_kernel, level),
            [square] * 4 + more, [VMEM] * 4 + [ANY] * (1 + len(more)), [VMEM] * 4 + [ANY] * len(more),
            [], 0.3, f"join_{level}", aliases={5 + at: 4 + at for at in range(len(more))},
        )(total, other, later, before, after, *through)
        uppers.append(upper)
        return total, later, before, *through

    other = exchange(total, "tm", blocks, 1)
    early_width = plan.lanes(plan.first_group[-1]).start
    early, offset, *loaded = call(
        functools.partial(early_gram_kernel, plan),
        [shape(members, early_width), square]
        + [piece_shape(piece) for piece in range(1, PIECES) for _ in range(2)],
        [HBM] * 2 + [VMEM] * 3, [VMEM] * (2 * PIECES),
        [sem for piece in range(1, PIECES) for sem in piece_sems(piece)], 3, "early_gram",
    )(ensembles, cotangents, suffixes, *first_part)
    parts = [first_part] + [loaded[at : at + 2] for at in range(0, len(loaded), 2)]
    total, later, before = join(0, total, other, later, before, offset)

    other = exchange(total, "tm", blocks, 2)
    gram, own = call(
        functools.partial(late_gram_kernel, plan),
        [wide, square], [VMEM] * 5 + [ANY], [VMEM] * 2, [], 1.2, "late_gram",
    )(*parts[-1], suffixes, early, offset, total)
    other_own = exchange(own, "tm", blocks, 1)
    for level in range(1, levels - 1):
        total, later, before = join(level, total, other, later, before, own)
        other = exchange(total, "tm", blocks, 2 << level)
    befores.append(before)
    steps = call(
        functools.partial(windows_kernel, plan),
        shape(2, count_steps(count) * members, members, kind=BF16), [VMEM, ANY], VMEM,
        [pltpu.VMEM((count * members, members), F32)], 1.0, "windows",
    )(kept, total)

    def pass_on(level, carry, after, *through):
        more = [shape(*value.shape) for value in through]
        return call(
            functools.partial(pass_kernel, level),
            [square] * 2 + more, [VMEM] * 5 + [ANY] * (1 + len(more)), [VMEM] * 2 + [ANY] * len(more),
            [], 0.3, f"pass_{level}", aliases={6 + at: 2 + at for at in range(len(more))},
        )(own, other_own, carry, uppers[level], befores[level], after, *through)

    carry = jnp.zeros((members, members), F32)
    for level in range(levels - 2):
        if level == levels - 3:
            own, carry, gram, other = pass_on(level, carry, steps, gram, other)
        else:
            own, carry = pass_on(level, carry, steps)
        other_own = exchange(own, "tm", blocks, 2 << level)
    grams = around(gram)
    entering = call(
        functools.partial(enter_kernel, levels - 1),
        square, [VMEM] * 2 + [ANY], VMEM, [], 0.2, "entering",
    )(later, other, own)
    size = plan.stack * members
    ens_factors, cot_factors, follow = call(
        functools.partial(carry_kernel, plan),
        [shape(len(plan.groups), size, size, kind=BF16)] * 2
        + [shape(2, count * members, members, kind=BF16)],
        [VMEM] * 2, [VMEM] * 3, [], 0.9, "carries",
    )(suffixes, entering)
    own, carry = pass_on(levels - 2, carry, follow)
    other_own = exchange(own, "tm", blocks, blocks // 2)

    def apply(factors, which, pieces, out, after, name):
        first, last = plan.pieces[pieces[0]][0], plan.pieces[pieces[-1]][1]
        number = 2 * sum(len(plan.piece_groups[piece]) for piece in pieces)
        return call(
            functools.partial(apply_kernel, plan, pieces),
            [shape(count, members, cells, kind=BF16), shape(8, 128)],
            [VMEM] * (1 + len(pieces)) + [ANY] + [HBM] * len(out), [HBM, VMEM],
            [pltpu.VMEM((last - first, members, cells), BF16), pltpu.SemaphoreType.DMA((number,))],
            1.8, name, aliases={2 + len(pieces): 0} if out else None,
        )(factors, *(parts[piece][which] for piece in pieces), after, *out)

    front, rear = tuple(range(PIECES - 1)), (PIECES - 1,)
    smoothed, done = apply(ens_factors, 0, front + rear, (), own, "smoothed")
    carry, grams[0] = call(
        functools.partial(last_pass_kernel, levels - 1),
        [square, wide], [VMEM] * 3 + [ANY] * 2, [VMEM, ANY], [], 0.2, "pass_last", aliases={4: 1},
    )(other_own, carry, befores[-1], done, grams[0])
    carry_core = exchange(carry, "space", lanes, 1)
    for part in grams:
        gram = gram + part
    gram_core = exchange(gram, "space", lanes, 1)
    ensemble_grad, done = apply(cot_factors, 1, rear, (), carry, "ensemble_grad_0")
    carry = call(
        sum_kernel, square, [VMEM] * 2 + [ANY], VMEM, [], 0.1, "chip_carry",
    )(carry, carry_core, done)
    carries = [carry] + around(carry)
    ensemble_grad, done = apply(cot_factors, 1, front, (ensemble_grad,), carry, "ensemble_grad_1")
    transform_grad = call(
        functools.partial(final_kernel, plan, scale),
        shape(count, members, members),
        [VMEM] * 4 + [ANY] + [VMEM] * chips, HBM,
        [pltpu.VMEM((count, members, members), F32), pltpu.SemaphoreType.DMA((count,))],
        2.5, "transform_grad",
    )(gram, gram_core, follow, steps, done, *carries)
    return (smoothed, ensemble_grad, transform_grad)


def solution(mesh):
    return jax.shard_map(
        shards,
        mesh=mesh,
        in_specs=(P("tm", None, "space"), P("tm", None, "space"), P("tm", None, None)),
        out_specs=(P("tm", None, "space"), P("tm", None, "space"), P("tm", None, None)),
        check_vma=False,
    )
```

```python
import functools
import math

import jax
import jax.numpy as jnp
from jax import lax
from jax.experimental import pallas as pl
from jax.experimental.pallas import tpu as pltpu
from jax.sharding import PartitionSpec as P

F32 = jnp.float32
BF16 = jnp.bfloat16
VMEM = pl.BlockSpec(memory_space=pltpu.VMEM)
HBM = pl.BlockSpec(memory_space=pltpu.HBM)
ANY = pl.BlockSpec(memory_space=pl.ANY)
DEPTH = 256
PIECES = 3
NORMAL = (((1,), (0,)), ((), ()))
ROWS = (((1,), (1,)), ((), ()))


def split(value):
    high = value.astype(BF16)
    return high, (value - high.astype(F32)).astype(BF16)


def mul(left, right, dims=NORMAL):
    return lax.dot_general(left, right, dims, preferred_element_type=F32)


def mul_pairs(left, right, dims=NORMAL):
    return mul(left[0], right[0], dims) + (
        mul(left[0], right[1], dims) + mul(left[1], right[0], dims)
    )


def mul_exact(left, right, dims=NORMAL):
    return mul_pairs(split(left), split(right), dims)


def product_of(factors):
    while len(factors) > 1:
        joined = [mul_exact(*factors[at : at + 2]) for at in range(0, len(factors) - 1, 2)]
        factors = joined + factors[len(joined) * 2 :]
    return factors[0]


def suffix_scan(ref, count, members, stop):
    width = 1
    while width < stop:
        for start in range(0, count, 2 * width):
            middle = start + width
            if middle < count:
                rows = slice(start * members, middle * members)
                ref[rows] = mul_exact(ref[rows], ref[middle * members : (middle + 1) * members])
        width *= 2


class Plan:
    def __init__(self, count, members):
        self.count, self.members = count, members
        self.stack = DEPTH // members
        self.groups = [
            (start, min(start + self.stack, count)) for start in range(0, count, self.stack)
        ]
        bounds = [len(self.groups) * at // PIECES for at in range(PIECES + 1)]
        self.piece_groups = [self.groups[a:b] for a, b in zip(bounds, bounds[1:])]
        self.pieces = [(part[0][0], part[-1][1]) for part in self.piece_groups]
        self.first_group = bounds[:-1]
        self.widths = [-(-(stop - start) * members // 128) * 128 for start, stop in self.groups]
        self.width = sum(self.widths)

    def lanes(self, at):
        start = sum(self.widths[:at])
        return slice(start, start + self.widths[at])

    def rows(self, first, last):
        return slice(first * self.members, last * self.members)


def on_blocks(members, size):
    rows = lax.broadcasted_iota(jnp.int32, (size, size), 0) // members
    columns = lax.broadcasted_iota(jnp.int32, (size, size), 1) // members
    return rows == columns


def loads(plan, piece, values, buffer, sems):
    base = plan.pieces[piece][0]
    copies = [
        pltpu.make_async_copy(values.at[start:stop], buffer.at[start - base : stop - base], sems.at[at])
        for at, (start, stop) in enumerate(plan.piece_groups[piece])
    ]
    for copy in copies:
        copy.start()
    return copies


def chain_kernel(
    plan, transforms, ensembles, cotangents, suffixes, total, kept, ens, cot, sem, ens_sem, cot_sem
):
    count, members = plan.count, plan.members
    read = pltpu.make_async_copy(transforms, kept, sem)
    read.start()
    read.wait()
    more = loads(plan, 0, ensembles, ens, ens_sem) + loads(plan, 0, cotangents, cot, cot_sem)
    for at in range(count):
        suffixes[plan.rows(at, at + 1)] = kept[at]
    suffix_scan(suffixes, count, members, count)
    total[...] = suffixes[plan.rows(0, 1)]
    for copy in more:
        copy.wait()


def windows_kernel(plan, kept, _, steps, runs):
    count = plan.count
    for at in range(count - 1):
        runs[plan.rows(at + 1, at + 2)] = kept[at].T
    number = 0
    width = 1
    while width < count:
        for middle in range(width, count, 2 * width):
            size = min(width, count - middle)
            for side, part in enumerate(split(runs[plan.rows(middle, middle + size)])):
                steps[side, plan.rows(number, number + size)] = part
            number += size
        for start in range(2 * width, count, 2 * width):
            if start + width < count:
                rows = plan.rows(start + width, min(start + 2 * width, count))
                runs[rows] = mul_exact(runs[rows], runs[plan.rows(start + width - 1, start + width)])
        width *= 2


def count_steps(count):
    total = 0
    width = 1
    while width < count:
        total += sum(min(width, count - middle) for middle in range(width, count, 2 * width))
        width *= 2
    return total


def core_index():
    return lax.rem(lax.axis_index("space"), 2)


def gram_of(plan, piece, cot, ens, suffixes, whole, ready=lambda: None):
    members = plan.members
    base = plan.pieces[piece][0]
    offset = jnp.zeros((members, members), F32)
    for at, (start, stop) in enumerate(plan.piece_groups[piece]):
        ready()
        size = (stop - start) * members
        stacked = [ref[start - base : stop - base].reshape(size, ref.shape[2]) for ref in (cot, ens)]
        wide = jnp.where(on_blocks(members, size), mul(*stacked, ROWS), 0.0)
        gram = wide[:members]
        for i in range(1, stop - start):
            gram = gram + wide[i * members : (i + 1) * members]
        offset = offset + mul_exact(gram, suffixes[plan.rows(start, stop)])
        lanes = plan.lanes(plan.first_group[piece] + at)
        width = lanes.stop - lanes.start
        whole[:, lanes] = jnp.pad(gram, ((0, 0), (0, width - size)))
    return offset


def early_gram_kernel(plan, ensembles, cotangents, suffixes, ens, cot, whole, offset, *refs):
    buffers, sems = refs[: 2 * (PIECES - 1)], refs[2 * (PIECES - 1) :]
    copies = []
    for piece in range(1, PIECES):
        pair = buffers[2 * piece - 2 : 2 * piece]
        own = sems[2 * piece - 2 : 2 * piece]
        copies.append(list(zip(
            loads(plan, piece, ensembles, pair[0], own[0]),
            loads(plan, piece, cotangents, pair[1], own[1]),
        )))
    total = gram_of(plan, 0, cot, ens, suffixes, whole)
    for piece in range(1, PIECES - 1):
        waiting = iter(copies[piece - 1])

        def ready():
            for copy in next(waiting):
                copy.wait()

        ens, cot = buffers[2 * piece - 2 : 2 * piece]
        total = total + gram_of(plan, piece, cot, ens, suffixes, whole, ready)
    offset[...] = total
    for pair in copies[-1]:
        for copy in pair:
            copy.wait()


def late_gram_kernel(plan, ens, cot, suffixes, early, offset, _, grams, offsets):
    grams[:, : early.shape[1]] = early[...]
    offsets[...] = offset[...] + gram_of(plan, PIECES - 1, cot, ens, suffixes, grams)


def upper_half(level):
    return lax.rem(lax.axis_index("tm") // (1 << level), 2) == 1


def join_kernel(level, total, other, later, before, _, *refs):
    new_total, new_later, new_before, upper_total = refs[len(refs) // 2 - 2 : len(refs) // 2 + 2]
    upper = upper_half(level)
    left = jnp.where(upper, other[...], total[...])
    right = jnp.where(upper, total[...], other[...])
    new_total[...] = mul_exact(left, right)
    upper_total[...] = right
    new_later[...] = jnp.where(upper, later[...], mul_exact(later[...], other[...]))
    new_before[...] = jnp.where(upper, mul_exact(other[...], before[...]), before[...])


def sum_kernel(left, right, _, total):
    total[...] = left[...] + right[...]


def pass_kernel(level, own, other, carry, upper_total, before, _, *refs):
    new_own, new_carry = refs[len(refs) // 2 - 1 : len(refs) // 2 + 1]
    upper = upper_half(level)
    left = jnp.where(upper, other[...], own[...])
    right = jnp.where(upper, own[...], other[...])
    new_own[...] = mul_exact(left, upper_total[...]) + right
    new_carry[...] = carry[...] + jnp.where(upper, mul_exact(left, before[...]), 0.0)


def last_pass_kernel(level, other, carry, before, _, __, new_carry, ___):
    added = mul_exact(other[...], before[...])
    new_carry[...] = carry[...] + jnp.where(upper_half(level), added, 0.0)


def enter_kernel(level, later, other, _, entering):
    joined = mul_exact(later[...], other[...])
    entering[...] = jnp.where(upper_half(level), later[...], joined)


def carry_kernel(plan, suffixes, later, ens_factors, cot_factors, follow):
    count, members = plan.count, plan.members
    entering = later[...]
    mask = on_blocks(members, plan.stack * members)
    repeated = split(jnp.concatenate([entering] * plan.stack, axis=1))
    for at, (start, stop) in enumerate(plan.groups):
        size = (stop - start) * members
        wide = mul_pairs(split(suffixes[plan.rows(start, stop)]), repeated)
        part = jnp.where(mask[:size, :size], wide[:, :size], 0.0)
        cot_factors[at, :size, :size] = part.astype(BF16)
        ens_factors[at, :size, :size] = part.T.astype(BF16)
        first = max(start - 1, 0)
        kept = wide[(first + 1 - start) * members :, :members]
        for side, value in enumerate(split(kept)):
            follow[side, plan.rows(first, stop - 1)] = value
    for side, value in enumerate(split(entering)):
        follow[side, plan.rows(count - 1, count)] = value


def apply_kernel(plan, pieces, factors, *refs):
    out, marker, out_buf, out_sem = refs[-4:]
    members = plan.members
    marker[...] = jnp.zeros_like(marker)
    base = plan.pieces[pieces[0]][0]
    chunk = out_buf.shape[2] // 2
    writes = []
    for values, piece in zip(refs, pieces):
        first = plan.pieces[piece][0]
        for at, (start, stop) in enumerate(plan.piece_groups[piece]):
            size = (stop - start) * members
            for side in range(2):
                columns = slice(side * chunk, (side + 1) * chunk)
                stacked = values[start - first : stop - first, :, columns].reshape(size, chunk)
                result = mul(factors[plan.first_group[piece] + at, :size, :size], stacked)
                out_buf[start - base : stop - base, :, columns] = result.astype(BF16).reshape(
                    stop - start, members, chunk
                )
                copy = pltpu.make_async_copy(
                    out_buf.at[start - base : stop - base, :, columns],
                    out.at[start:stop, :, columns],
                    out_sem.at[len(writes)],
                )
                copy.start()
                writes.append(copy)
    for copy in writes:
        copy.wait()


def final_kernel(plan, scale, gram, gram_core, follow, steps, _, *refs):
    carries, (out, buffer, sems) = refs[:-3], refs[-3:]
    carry = carries[0][...]
    for ref in carries[1:]:
        carry = carry + ref[...]
    count, members = plan.count, plan.members
    totals = []
    for at, (start, stop) in enumerate(plan.groups):
        tall = (gram[:, plan.lanes(at)] + gram_core[:, plan.lanes(at)]).T
        for i in range(stop - start):
            totals.append(tall[i * members : (i + 1) * members])
    totals[0] = totals[0] + carry.T
    number = 0
    width = 1
    while width < count:
        for start in range(width, count, 2 * width):
            size = min(width, count - start)
            rows = plan.rows(number, number + size)
            added = mul_pairs((steps[0, rows], steps[1, rows]), split(totals[start - 1]))
            for at in range(size):
                totals[start + at] = totals[start + at] + added[at * members : (at + 1) * members]
            number += size
        width *= 2
    copies = []
    for at in range(count):
        rows = plan.rows(at, at + 1)
        buffer[at] = mul_pairs(split(totals[at]), (follow[0, rows], follow[1, rows]), ROWS) * scale
        copy = pltpu.make_async_copy(buffer.at[at], out.at[at], sems.at[at])
        copy.start()
        copies.append(copy)
    for copy in copies:
        copy.wait()


def call(kernel, outs, ins, out_specs, scratch, micros, name, limit=16, aliases=None):
    return pl.pallas_call(
        kernel,
        out_shape=outs,
        in_specs=ins,
        out_specs=out_specs,
        scratch_shapes=scratch,
        input_output_aliases=aliases or {},
        compiler_params=pltpu.CompilerParams(vmem_limit_bytes=limit << 20),
        cost_estimate=pl.CostEstimate(
            flops=int(micros * 1e9), bytes_accessed=int(micros * 3e6), transcendentals=0
        ),
        name=name,
    )


def shape(*dims, kind=F32):
    return jax.ShapeDtypeStruct(dims, kind)


def shards(ensembles, cotangents, transforms):
    count, members, cells = ensembles.shape
    blocks, lanes = lax.axis_size("tm"), lax.axis_size("space")
    chips = lanes // 2
    scale = 1.0 / math.sqrt(cells * lanes * count * blocks)
    plan = Plan(count, members)
    levels = blocks.bit_length() - 1
    square = shape(members, members)
    ensembles, cotangents, transforms = (
        pltpu.with_memory_space_constraint(value, pltpu.HBM)
        for value in (ensembles, cotangents, transforms)
    )

    def exchange(value, axis, size, bit):
        return lax.ppermute(value, axis, [(at, at ^ bit) for at in range(size)])

    def around(value):
        return [
            lax.ppermute(value, "space", [(at, (at + 2 * d) % lanes) for at in range(lanes)])
            for d in range(1, chips)
        ]

    def piece_shape(piece):
        first, last = plan.pieces[piece]
        return shape(last - first, members, cells, kind=BF16)

    def piece_sems(piece):
        return [pltpu.SemaphoreType.DMA((len(plan.piece_groups[piece]),))] * 2

    suffixes, total, kept, *first_part = call(
        functools.partial(chain_kernel, plan),
        [shape(count * members, members), square, shape(count, members, members)] + [piece_shape(0)] * 2,
        [HBM] * 3, [VMEM] * 5, [pltpu.SemaphoreType.DMA] + piece_sems(0), 3.5, "transform_chain",
    )(transforms, ensembles, cotangents)

    wide = shape(members, plan.width)
    later = before = jnp.eye(members, dtype=F32)
    uppers, befores = [], []

    def join(level, total, other, later, before, after, *through):
        more = [shape(*value.shape) for value in through]
        befores.append(before)
        total, later, before, upper, *through = call(
            functools.partial(join_kernel, level),
            [square] * 4 + more, [VMEM] * 4 + [ANY] * (1 + len(more)), [VMEM] * 4 + [ANY] * len(more),
            [], 0.3, f"join_{level}", aliases={5 + at: 4 + at for at in range(len(more))},
        )(total, other, later, before, after, *through)
        uppers.append(upper)
        return total, later, before, *through

    other = exchange(total, "tm", blocks, 1)
    early_width = plan.lanes(plan.first_group[-1]).start
    early, offset, *loaded = call(
        functools.partial(early_gram_kernel, plan),
        [shape(members, early_width), square]
        + [piece_shape(piece) for piece in range(1, PIECES) for _ in range(2)],
        [HBM] * 2 + [VMEM] * 3, [VMEM] * (2 * PIECES),
        [sem for piece in range(1, PIECES) for sem in piece_sems(piece)], 3, "early_gram",
    )(ensembles, cotangents, suffixes, *first_part)
    parts = [first_part] + [loaded[at : at + 2] for at in range(0, len(loaded), 2)]
    total, later, before = join(0, total, other, later, before, offset)

    other = exchange(total, "tm", blocks, 2)
    gram, own = call(
        functools.partial(late_gram_kernel, plan),
        [wide, square], [VMEM] * 5 + [ANY], [VMEM] * 2, [], 1.2, "late_gram",
    )(*parts[-1], suffixes, early, offset, total)
    other_own = exchange(own, "tm", blocks, 1)
    grams = around(gram)
    for level in range(1, levels - 1):
        total, later, before = join(level, total, other, later, before, own)
        other = exchange(total, "tm", blocks, 2 << level)
    befores.append(before)
    steps = call(
        functools.partial(windows_kernel, plan),
        shape(2, count_steps(count) * members, members, kind=BF16), [VMEM, ANY], VMEM,
        [pltpu.VMEM((count * members, members), F32)], 1.0, "windows",
    )(kept, total)

    def pass_on(level, carry, after, *through):
        more = [shape(*value.shape) for value in through]
        return call(
            functools.partial(pass_kernel, level),
            [square] * 2 + more, [VMEM] * 5 + [ANY] * (1 + len(more)), [VMEM] * 2 + [ANY] * len(more),
            [], 0.3, f"pass_{level}", aliases={6 + at: 2 + at for at in range(len(more))},
        )(own, other_own, carry, uppers[level], befores[level], after, *through)

    carry = jnp.zeros((members, members), F32)
    for level in range(levels - 2):
        own, carry = pass_on(level, carry, steps)
        other_own = exchange(own, "tm", blocks, 2 << level)
    entering = call(
        functools.partial(enter_kernel, levels - 1),
        square, [VMEM] * 2 + [ANY], VMEM, [], 0.2, "entering",
    )(later, other, own)
    size = plan.stack * members
    ens_factors, cot_factors, follow = call(
        functools.partial(carry_kernel, plan),
        [shape(len(plan.groups), size, size, kind=BF16)] * 2
        + [shape(2, count * members, members, kind=BF16)],
        [VMEM] * 2, [VMEM] * 3, [], 0.9, "carries",
    )(suffixes, entering)
    own, carry = pass_on(levels - 2, carry, follow)
    other_own = exchange(own, "tm", blocks, blocks // 2)

    def apply(factors, which, pieces, out, after, name):
        first, last = plan.pieces[pieces[0]][0], plan.pieces[pieces[-1]][1]
        number = 2 * sum(len(plan.piece_groups[piece]) for piece in pieces)
        return call(
            functools.partial(apply_kernel, plan, pieces),
            [shape(count, members, cells, kind=BF16), shape(8, 128)],
            [VMEM] * (1 + len(pieces)) + [ANY] + [HBM] * len(out), [HBM, VMEM],
            [pltpu.VMEM((last - first, members, cells), BF16), pltpu.SemaphoreType.DMA((number,))],
            0.15 * (last - first) + 0.6, name, aliases={2 + len(pieces): 0} if out else None,
        )(factors, *(parts[piece][which] for piece in pieces), after, *out)

    front, rear = tuple(range(PIECES - 1)), (PIECES - 1,)
    smoothed, done = apply(ens_factors, 0, front + rear, (), own, "smoothed")
    carry, grams[0] = call(
        functools.partial(last_pass_kernel, levels - 1),
        [square, wide], [VMEM] * 3 + [ANY] * 2, [VMEM, ANY], [], 0.2, "pass_last", aliases={4: 1},
    )(other_own, carry, befores[-1], done, grams[0])
    carry_core = exchange(carry, "space", lanes, 1)
    for part in grams:
        gram = gram + part
    gram_core = exchange(gram, "space", lanes, 1)
    ensemble_grad, done = apply(cot_factors, 1, rear, (), carry, "ensemble_grad_0")
    carry = call(
        sum_kernel, square, [VMEM] * 2 + [ANY], VMEM, [], 0.1, "chip_carry",
    )(carry, carry_core, done)
    carries = [carry] + around(carry)
    ensemble_grad, done = apply(cot_factors, 1, front, (ensemble_grad,), carry, "ensemble_grad_1")
    transform_grad = call(
        functools.partial(final_kernel, plan, scale),
        shape(count, members, members),
        [VMEM] * 4 + [ANY] + [VMEM] * chips, HBM,
        [pltpu.VMEM((count, members, members), F32), pltpu.SemaphoreType.DMA((count,))],
        2.5, "transform_grad",
    )(gram, gram_core, follow, steps, done, *carries)
    return (smoothed, ensemble_grad, transform_grad)


def solution(mesh):
    return jax.shard_map(
        shards,
        mesh=mesh,
        in_specs=(P("tm", None, "space"), P("tm", None, "space"), P("tm", None, None)),
        out_specs=(P("tm", None, "space"), P("tm", None, "space"), P("tm", None, None)),
        check_vma=False,
    )
```

```python
import functools
import math

import jax
import jax.numpy as jnp
from jax import lax
from jax.experimental import pallas as pl
from jax.experimental.pallas import tpu as pltpu
from jax.sharding import PartitionSpec as P

F32 = jnp.float32
BF16 = jnp.bfloat16
VMEM = pl.BlockSpec(memory_space=pltpu.VMEM)
HBM = pl.BlockSpec(memory_space=pltpu.HBM)
ANY = pl.BlockSpec(memory_space=pl.ANY)
DEPTH = 256
PIECES = 3
NORMAL = (((1,), (0,)), ((), ()))
ROWS = (((1,), (1,)), ((), ()))


def split(value):
    high = value.astype(BF16)
    return high, (value - high.astype(F32)).astype(BF16)


def mul(left, right, dims=NORMAL):
    return lax.dot_general(left, right, dims, preferred_element_type=F32)


def mul_pairs(left, right, dims=NORMAL):
    return mul(left[0], right[0], dims) + (
        mul(left[0], right[1], dims) + mul(left[1], right[0], dims)
    )


def mul_exact(left, right, dims=NORMAL):
    return mul_pairs(split(left), split(right), dims)


def product_of(factors):
    while len(factors) > 1:
        joined = [mul_exact(*factors[at : at + 2]) for at in range(0, len(factors) - 1, 2)]
        factors = joined + factors[len(joined) * 2 :]
    return factors[0]


def suffix_scan(ref, count, members, stop):
    width = 1
    while width < stop:
        for start in range(0, count, 2 * width):
            middle = start + width
            if middle < count:
                rows = slice(start * members, middle * members)
                ref[rows] = mul_exact(ref[rows], ref[middle * members : (middle + 1) * members])
        width *= 2


class Plan:
    def __init__(self, count, members):
        self.count, self.members = count, members
        self.stack = DEPTH // members
        self.groups = [
            (start, min(start + self.stack, count)) for start in range(0, count, self.stack)
        ]
        bounds = [len(self.groups) * at // PIECES for at in range(PIECES + 1)]
        self.piece_groups = [self.groups[a:b] for a, b in zip(bounds, bounds[1:])]
        self.pieces = [(part[0][0], part[-1][1]) for part in self.piece_groups]
        self.first_group = bounds[:-1]
        self.widths = [-(-(stop - start) * members // 128) * 128 for start, stop in self.groups]
        self.width = sum(self.widths)

    def lanes(self, at):
        start = sum(self.widths[:at])
        return slice(start, start + self.widths[at])

    def rows(self, first, last):
        return slice(first * self.members, last * self.members)


def on_blocks(members, size):
    rows = lax.broadcasted_iota(jnp.int32, (size, size), 0) // members
    columns = lax.broadcasted_iota(jnp.int32, (size, size), 1) // members
    return rows == columns


def loads(plan, piece, values, buffer, sems):
    base = plan.pieces[piece][0]
    copies = [
        pltpu.make_async_copy(values.at[start:stop], buffer.at[start - base : stop - base], sems.at[at])
        for at, (start, stop) in enumerate(plan.piece_groups[piece])
    ]
    for copy in copies:
        copy.start()
    return copies


def chain_kernel(
    plan, transforms, ensembles, cotangents, suffixes, total, kept, ens, cot, sem, ens_sem, cot_sem
):
    count, members = plan.count, plan.members
    read = pltpu.make_async_copy(transforms, kept, sem)
    read.start()
    read.wait()
    more = loads(plan, 0, ensembles, ens, ens_sem) + loads(plan, 0, cotangents, cot, cot_sem)
    for at in range(count):
        suffixes[plan.rows(at, at + 1)] = kept[at]
    suffix_scan(suffixes, count, members, count)
    total[...] = suffixes[plan.rows(0, 1)]
    for copy in more:
        copy.wait()


def windows_kernel(plan, kept, _, __, steps, ___, runs):
    count = plan.count
    for at in range(count - 1):
        runs[plan.rows(at + 1, at + 2)] = kept[at].T
    number = 0
    width = 1
    while width < count:
        for middle in range(width, count, 2 * width):
            size = min(width, count - middle)
            for side, part in enumerate(split(runs[plan.rows(middle, middle + size)])):
                steps[side, plan.rows(number, number + size)] = part
            number += size
        for start in range(2 * width, count, 2 * width):
            if start + width < count:
                rows = plan.rows(start + width, min(start + 2 * width, count))
                runs[rows] = mul_exact(runs[rows], runs[plan.rows(start + width - 1, start + width)])
        width *= 2


def count_steps(count):
    total = 0
    width = 1
    while width < count:
        total += sum(min(width, count - middle) for middle in range(width, count, 2 * width))
        width *= 2
    return total


def core_index():
    return lax.rem(lax.axis_index("space"), 2)


def gram_of(plan, piece, cot, ens, suffixes, whole, ready=lambda: None):
    members = plan.members
    base = plan.pieces[piece][0]
    offset = jnp.zeros((members, members), F32)
    for at, (start, stop) in enumerate(plan.piece_groups[piece]):
        ready()
        size = (stop - start) * members
        stacked = [ref[start - base : stop - base].reshape(size, ref.shape[2]) for ref in (cot, ens)]
        wide = jnp.where(on_blocks(members, size), mul(*stacked, ROWS), 0.0)
        gram = wide[:members]
        for i in range(1, stop - start):
            gram = gram + wide[i * members : (i + 1) * members]
        offset = offset + mul_exact(gram, suffixes[plan.rows(start, stop)])
        lanes = plan.lanes(plan.first_group[piece] + at)
        width = lanes.stop - lanes.start
        whole[:, lanes] = jnp.pad(gram, ((0, 0), (0, width - size)))
    return offset


def early_gram_kernel(plan, ensembles, cotangents, suffixes, ens, cot, whole, offset, *refs):
    buffers, sems = refs[: 2 * (PIECES - 1)], refs[2 * (PIECES - 1) :]
    copies = []
    for piece in range(1, PIECES):
        pair = buffers[2 * piece - 2 : 2 * piece]
        own = sems[2 * piece - 2 : 2 * piece]
        copies.append(list(zip(
            loads(plan, piece, ensembles, pair[0], own[0]),
            loads(plan, piece, cotangents, pair[1], own[1]),
        )))
    total = gram_of(plan, 0, cot, ens, suffixes, whole)
    for piece in range(1, PIECES - 1):
        waiting = iter(copies[piece - 1])

        def ready():
            for copy in next(waiting):
                copy.wait()

        ens, cot = buffers[2 * piece - 2 : 2 * piece]
        total = total + gram_of(plan, piece, cot, ens, suffixes, whole, ready)
    offset[...] = total
    for pair in copies[-1]:
        for copy in pair:
            copy.wait()


def late_gram_kernel(plan, ens, cot, suffixes, early, offset, _, kept, sent, offsets, whole):
    whole[:, : early.shape[1]] = early[...]
    offsets[...] = offset[...] + gram_of(plan, PIECES - 1, cot, ens, suffixes, whole)
    half = plan.members // 2
    core = lax.rem(lax.axis_index("space"), 2)
    kept[...] = whole[pl.ds(core * half, half)]
    sent[...] = whole[pl.ds((1 - core) * half, half)]


def upper_half(level):
    return lax.rem(lax.axis_index("tm") // (1 << level), 2) == 1


def join_kernel(level, total, other, later, before, _, *refs):
    new_total, new_later, new_before, upper_total = refs[len(refs) // 2 - 2 : len(refs) // 2 + 2]
    upper = upper_half(level)
    left = jnp.where(upper, other[...], total[...])
    right = jnp.where(upper, total[...], other[...])
    new_total[...] = mul_exact(left, right)
    upper_total[...] = right
    new_later[...] = jnp.where(upper, later[...], mul_exact(later[...], other[...]))
    new_before[...] = jnp.where(upper, mul_exact(other[...], before[...]), before[...])


def sum_kernel(left, right, _, total):
    total[...] = left[...] + right[...]


def pass_kernel(level, own, other, carry, upper_total, before, _, *refs):
    new_own, new_carry = refs[len(refs) // 2 - 1 : len(refs) // 2 + 1]
    upper = upper_half(level)
    left = jnp.where(upper, other[...], own[...])
    right = jnp.where(upper, own[...], other[...])
    new_own[...] = mul_exact(left, upper_total[...]) + right
    new_carry[...] = carry[...] + jnp.where(upper, mul_exact(left, before[...]), 0.0)


def last_pass_kernel(level, other, carry, before, _, __, new_carry, ___):
    added = mul_exact(other[...], before[...])
    new_carry[...] = carry[...] + jnp.where(upper_half(level), added, 0.0)


def enter_kernel(level, later, other, _, entering):
    joined = mul_exact(later[...], other[...])
    entering[...] = jnp.where(upper_half(level), later[...], joined)


def carry_kernel(plan, suffixes, later, ens_factors, cot_factors, follow):
    count, members = plan.count, plan.members
    entering = later[...]
    mask = on_blocks(members, plan.stack * members)
    repeated = split(jnp.concatenate([entering] * plan.stack, axis=1))
    for at, (start, stop) in enumerate(plan.groups):
        size = (stop - start) * members
        wide = mul_pairs(split(suffixes[plan.rows(start, stop)]), repeated)
        part = jnp.where(mask[:size, :size], wide[:, :size], 0.0)
        cot_factors[at, :size, :size] = part.astype(BF16)
        ens_factors[at, :size, :size] = part.T.astype(BF16)
        first = max(start - 1, 0)
        kept = wide[(first + 1 - start) * members :, :members]
        for side, value in enumerate(split(kept)):
            follow[side, plan.rows(first, stop - 1)] = value
    for side, value in enumerate(split(entering)):
        follow[side, plan.rows(count - 1, count)] = value


def apply_kernel(plan, pieces, factors, *refs):
    out, marker, out_buf, out_sem = refs[-4:]
    members = plan.members
    marker[...] = jnp.zeros_like(marker)
    base = plan.pieces[pieces[0]][0]
    chunk = out_buf.shape[2] // 2
    writes = []
    for values, piece in zip(refs, pieces):
        first = plan.pieces[piece][0]
        for at, (start, stop) in enumerate(plan.piece_groups[piece]):
            size = (stop - start) * members
            for side in range(2):
                columns = slice(side * chunk, (side + 1) * chunk)
                stacked = values[start - first : stop - first, :, columns].reshape(size, chunk)
                result = mul(factors[plan.first_group[piece] + at, :size, :size], stacked)
                out_buf[start - base : stop - base, :, columns] = result.astype(BF16).reshape(
                    stop - start, members, chunk
                )
                copy = pltpu.make_async_copy(
                    out_buf.at[start - base : stop - base, :, columns],
                    out.at[start:stop, :, columns],
                    out_sem.at[len(writes)],
                )
                copy.start()
                writes.append(copy)
    for copy in writes:
        copy.wait()


def final_kernel(plan, scale, gram, gram_core, follow, steps, _, *refs):
    carries, (out, buffer, sems) = refs[:-3], refs[-3:]
    carry = carries[0][...]
    for ref in carries[1:]:
        carry = carry + ref[...]
    count, members = plan.count, plan.members
    totals = []
    first = lax.rem(lax.axis_index("space"), 2) == 0
    for at, (start, stop) in enumerate(plan.groups):
        mine, other = gram[:, plan.lanes(at)], gram_core[:, plan.lanes(at)]
        halves = [jnp.where(first, mine, other), jnp.where(first, other, mine)]
        tall = jnp.concatenate(halves, axis=0).T
        for i in range(stop - start):
            totals.append(tall[i * members : (i + 1) * members])
    totals[0] = totals[0] + carry.T
    number = 0
    width = 1
    while width < count:
        for start in range(width, count, 2 * width):
            size = min(width, count - start)
            rows = plan.rows(number, number + size)
            added = mul_pairs((steps[0, rows], steps[1, rows]), split(totals[start - 1]))
            for at in range(size):
                totals[start + at] = totals[start + at] + added[at * members : (at + 1) * members]
            number += size
        width *= 2
    copies = []
    for at in range(count):
        rows = plan.rows(at, at + 1)
        buffer[at] = mul_pairs(split(totals[at]), (follow[0, rows], follow[1, rows]), ROWS) * scale
        copy = pltpu.make_async_copy(buffer.at[at], out.at[at], sems.at[at])
        copy.start()
        copies.append(copy)
    for copy in copies:
        copy.wait()


def call(kernel, outs, ins, out_specs, scratch, micros, name, limit=16, aliases=None):
    return pl.pallas_call(
        kernel,
        out_shape=outs,
        in_specs=ins,
        out_specs=out_specs,
        scratch_shapes=scratch,
        input_output_aliases=aliases or {},
        compiler_params=pltpu.CompilerParams(vmem_limit_bytes=limit << 20),
        cost_estimate=pl.CostEstimate(
            flops=int(micros * 1e9), bytes_accessed=int(micros * 3e6), transcendentals=0
        ),
        name=name,
    )


def shape(*dims, kind=F32):
    return jax.ShapeDtypeStruct(dims, kind)


def shards(ensembles, cotangents, transforms):
    count, members, cells = ensembles.shape
    blocks, lanes = lax.axis_size("tm"), lax.axis_size("space")
    chips = lanes // 2
    scale = 1.0 / math.sqrt(cells * lanes * count * blocks)
    plan = Plan(count, members)
    levels = blocks.bit_length() - 1
    square = shape(members, members)
    ensembles, cotangents, transforms = (
        pltpu.with_memory_space_constraint(value, pltpu.HBM)
        for value in (ensembles, cotangents, transforms)
    )

    def exchange(value, axis, size, bit):
        return lax.ppermute(value, axis, [(at, at ^ bit) for at in range(size)])

    def around(value):
        return [
            lax.ppermute(value, "space", [(at, (at + 2 * d) % lanes) for at in range(lanes)])
            for d in range(1, chips)
        ]

    def piece_shape(piece):
        first, last = plan.pieces[piece]
        return shape(last - first, members, cells, kind=BF16)

    def piece_sems(piece):
        return [pltpu.SemaphoreType.DMA((len(plan.piece_groups[piece]),))] * 2

    suffixes, total, kept, *first_part = call(
        functools.partial(chain_kernel, plan),
        [shape(count * members, members), square, shape(count, members, members)] + [piece_shape(0)] * 2,
        [HBM] * 3, [VMEM] * 5, [pltpu.SemaphoreType.DMA] + piece_sems(0), 3.5, "transform_chain",
    )(transforms, ensembles, cotangents)

    wide = shape(members // 2, plan.width)
    later = before = jnp.eye(members, dtype=F32)
    uppers, befores = [], []

    def join(level, total, other, later, before, after, *through):
        more = [shape(*value.shape) for value in through]
        befores.append(before)
        total, later, before, upper, *through = call(
            functools.partial(join_kernel, level),
            [square] * 4 + more, [VMEM] * 4 + [ANY] * (1 + len(more)), [VMEM] * 4 + [ANY] * len(more),
            [], 3, f"join_{level}", aliases={5 + at: 4 + at for at in range(len(more))},
        )(total, other, later, before, after, *through)
        uppers.append(upper)
        return total, later, before, *through

    other = exchange(total, "tm", blocks, 1)
    early_width = plan.lanes(plan.first_group[-1]).start
    early, offset, *loaded = call(
        functools.partial(early_gram_kernel, plan),
        [shape(members, early_width), square]
        + [piece_shape(piece) for piece in range(1, PIECES) for _ in range(2)],
        [HBM] * 2 + [VMEM] * 3, [VMEM] * (2 * PIECES),
        [sem for piece in range(1, PIECES) for sem in piece_sems(piece)], 3, "early_gram",
    )(ensembles, cotangents, suffixes, *first_part)
    parts = [first_part] + [loaded[at : at + 2] for at in range(0, len(loaded), 2)]
    total, later, before = join(0, total, other, later, before, offset)

    other = exchange(total, "tm", blocks, 2)
    gram, gram_sent, own = call(
        functools.partial(late_gram_kernel, plan),
        [wide, wide, square], [VMEM] * 5 + [ANY], [VMEM] * 3,
        [pltpu.VMEM((members, plan.width), F32)], 1.2, "late_gram",
    )(*parts[-1], suffixes, early, offset, total)
    other_own = exchange(own, "tm", blocks, 1)
    gram_core = exchange(gram_sent, "space", lanes, 1)
    for level in range(1, levels - 1):
        total, later, before = join(level, total, other, later, before, own)
        other = exchange(total, "tm", blocks, 2 << level)
    befores.append(before)

    def pass_on(level, carry, after, *through):
        more = [shape(*value.shape) for value in through]
        return call(
            functools.partial(pass_kernel, level),
            [square] * 2 + more, [VMEM] * 5 + [ANY] * (1 + len(more)), [VMEM] * 2 + [ANY] * len(more),
            [], 3, f"pass_{level}", aliases={6 + at: 2 + at for at in range(len(more))},
        )(own, other_own, carry, uppers[level], befores[level], after, *through)

    carry = jnp.zeros((members, members), F32)
    for level in range(levels - 2):
        own, carry = pass_on(level, carry, total)
        other_own = exchange(own, "tm", blocks, 2 << level)
    steps, gram_core = call(
        functools.partial(windows_kernel, plan),
        [shape(2, count_steps(count) * members, members, kind=BF16), wide],
        [VMEM, ANY, ANY], [VMEM, ANY], [pltpu.VMEM((count * members, members), F32)], 1.0, "windows",
        aliases={2: 1},
    )(kept, own, gram_core)
    gram = gram + gram_core
    grams = around(gram)
    entering = call(
        functools.partial(enter_kernel, levels - 1),
        square, [VMEM] * 2 + [ANY], VMEM, [], 0.2, "entering",
    )(later, other, steps)
    size = plan.stack * members
    ens_factors, cot_factors, follow = call(
        functools.partial(carry_kernel, plan),
        [shape(len(plan.groups), size, size, kind=BF16)] * 2
        + [shape(2, count * members, members, kind=BF16)],
        [VMEM] * 2, [VMEM] * 3, [], 0.9, "carries",
    )(suffixes, entering)
    own, carry = pass_on(levels - 2, carry, follow)
    other_own = exchange(own, "tm", blocks, blocks // 2)

    def apply(factors, which, pieces, out, after, name):
        first, last = plan.pieces[pieces[0]][0], plan.pieces[pieces[-1]][1]
        number = 2 * sum(len(plan.piece_groups[piece]) for piece in pieces)
        return call(
            functools.partial(apply_kernel, plan, pieces),
            [shape(count, members, cells, kind=BF16), shape(8, 128)],
            [VMEM] * (1 + len(pieces)) + [ANY] + [HBM] * len(out), [HBM, VMEM],
            [pltpu.VMEM((last - first, members, cells), BF16), pltpu.SemaphoreType.DMA((number,))],
            0.15 * (last - first) + 0.6, name, aliases={2 + len(pieces): 0} if out else None,
        )(factors, *(parts[piece][which] for piece in pieces), after, *out)

    front, rear = tuple(range(PIECES - 1)), (PIECES - 1,)
    smoothed, done = apply(ens_factors, 0, front + rear, (), own, "smoothed")
    carry, grams[0] = call(
        functools.partial(last_pass_kernel, levels - 1),
        [square, wide], [VMEM] * 3 + [ANY] * 2, [VMEM, ANY], [], 0.2, "pass_last", aliases={4: 1},
    )(other_own, carry, befores[-1], done, grams[0])
    carry_core = exchange(carry, "space", lanes, 1)
    for part in grams:
        gram = gram + part
    gram_core = exchange(gram, "space", lanes, 1)
    ensemble_grad, done = apply(cot_factors, 1, rear, (), carry, "ensemble_grad_0")
    carry = call(
        sum_kernel, square, [VMEM] * 2 + [ANY], VMEM, [], 0.1, "chip_carry",
    )(carry, carry_core, done)
    carries = [carry] + around(carry)
    ensemble_grad, done = apply(cot_factors, 1, front, (ensemble_grad,), carry, "ensemble_grad_1")
    transform_grad = call(
        functools.partial(final_kernel, plan, scale),
        shape(count, members, members),
        [VMEM] * 4 + [ANY] + [VMEM] * chips, HBM,
        [pltpu.VMEM((count, members, members), F32), pltpu.SemaphoreType.DMA((count,))],
        2.5, "transform_grad",
    )(gram, gram_core, follow, steps, done, *carries)
    return (smoothed, ensemble_grad, transform_grad)


def solution(mesh):
    return jax.shard_map(
        shards,
        mesh=mesh,
        in_specs=(P("tm", None, "space"), P("tm", None, "space"), P("tm", None, None)),
        out_specs=(P("tm", None, "space"), P("tm", None, "space"), P("tm", None, None)),
        check_vma=False,
    )
```

```python
import functools
import math

import jax
import jax.numpy as jnp
from jax import lax
from jax.experimental import pallas as pl
from jax.experimental.pallas import tpu as pltpu
from jax.sharding import PartitionSpec as P

F32 = jnp.float32
BF16 = jnp.bfloat16
VMEM = pl.BlockSpec(memory_space=pltpu.VMEM)
HBM = pl.BlockSpec(memory_space=pltpu.HBM)
ANY = pl.BlockSpec(memory_space=pl.ANY)
DEPTH = 256
PIECES = 3
NORMAL = (((1,), (0,)), ((), ()))
ROWS = (((1,), (1,)), ((), ()))


def split(value):
    high = value.astype(BF16)
    return high, (value - high.astype(F32)).astype(BF16)


def mul(left, right, dims=NORMAL):
    return lax.dot_general(left, right, dims, preferred_element_type=F32)


def mul_pairs(left, right, dims=NORMAL):
    return mul(left[0], right[0], dims) + (
        mul(left[0], right[1], dims) + mul(left[1], right[0], dims)
    )


def mul_exact(left, right, dims=NORMAL):
    return mul_pairs(split(left), split(right), dims)


def product_of(factors):
    while len(factors) > 1:
        joined = [mul_exact(*factors[at : at + 2]) for at in range(0, len(factors) - 1, 2)]
        factors = joined + factors[len(joined) * 2 :]
    return factors[0]


def suffix_scan(ref, count, members, stop):
    width = 1
    while width < stop:
        for start in range(0, count, 2 * width):
            middle = start + width
            if middle < count:
                rows = slice(start * members, middle * members)
                ref[rows] = mul_exact(ref[rows], ref[middle * members : (middle + 1) * members])
        width *= 2


class Plan:
    def __init__(self, count, members):
        self.count, self.members = count, members
        self.stack = DEPTH // members
        self.groups = [
            (start, min(start + self.stack, count)) for start in range(0, count, self.stack)
        ]
        bounds = [len(self.groups) * at // PIECES for at in range(PIECES + 1)]
        self.piece_groups = [self.groups[a:b] for a, b in zip(bounds, bounds[1:])]
        self.pieces = [(part[0][0], part[-1][1]) for part in self.piece_groups]
        self.first_group = bounds[:-1]
        self.widths = [-(-(stop - start) * members // 128) * 128 for start, stop in self.groups]
        self.width = sum(self.widths)

    def lanes(self, at):
        start = sum(self.widths[:at])
        return slice(start, start + self.widths[at])

    def rows(self, first, last):
        return slice(first * self.members, last * self.members)


def on_blocks(members, size):
    rows = lax.broadcasted_iota(jnp.int32, (size, size), 0) // members
    columns = lax.broadcasted_iota(jnp.int32, (size, size), 1) // members
    return rows == columns


def loads(plan, piece, values, buffer, sems):
    base = plan.pieces[piece][0]
    copies = [
        pltpu.make_async_copy(values.at[start:stop], buffer.at[start - base : stop - base], sems.at[at])
        for at, (start, stop) in enumerate(plan.piece_groups[piece])
    ]
    for copy in copies:
        copy.start()
    return copies


def chain_kernel(
    plan, transforms, ensembles, cotangents, suffixes, total, kept, ens, cot, sem, ens_sem, cot_sem
):
    count, members = plan.count, plan.members
    read = pltpu.make_async_copy(transforms, kept, sem)
    read.start()
    read.wait()
    more = loads(plan, 0, ensembles, ens, ens_sem) + loads(plan, 0, cotangents, cot, cot_sem)
    for at in range(count):
        suffixes[plan.rows(at, at + 1)] = kept[at]
    suffix_scan(suffixes, count, members, count)
    total[...] = suffixes[plan.rows(0, 1)]
    for copy in more:
        copy.wait()


def windows_kernel(plan, kept, _, steps, runs):
    count = plan.count
    for at in range(count - 1):
        runs[plan.rows(at + 1, at + 2)] = kept[at].T
    number = 0
    width = 1
    while width < count:
        for middle in range(width, count, 2 * width):
            size = min(width, count - middle)
            for side, part in enumerate(split(runs[plan.rows(middle, middle + size)])):
                steps[side, plan.rows(number, number + size)] = part
            number += size
        for start in range(2 * width, count, 2 * width):
            if start + width < count:
                rows = plan.rows(start + width, min(start + 2 * width, count))
                runs[rows] = mul_exact(runs[rows], runs[plan.rows(start + width - 1, start + width)])
        width *= 2


def count_steps(count):
    total = 0
    width = 1
    while width < count:
        total += sum(min(width, count - middle) for middle in range(width, count, 2 * width))
        width *= 2
    return total


def core_index():
    return lax.rem(lax.axis_index("space"), 2)


def gram_of(plan, piece, cot, ens, suffixes, whole, ready=lambda: None):
    members = plan.members
    base = plan.pieces[piece][0]
    offset = jnp.zeros((members, members), F32)
    for at, (start, stop) in enumerate(plan.piece_groups[piece]):
        ready()
        size = (stop - start) * members
        stacked = [ref[start - base : stop - base].reshape(size, ref.shape[2]) for ref in (cot, ens)]
        wide = jnp.where(on_blocks(members, size), mul(*stacked, ROWS), 0.0)
        gram = wide[:members]
        for i in range(1, stop - start):
            gram = gram + wide[i * members : (i + 1) * members]
        offset = offset + mul_exact(gram, suffixes[plan.rows(start, stop)])
        lanes = plan.lanes(plan.first_group[piece] + at)
        width = lanes.stop - lanes.start
        whole[:, lanes] = jnp.pad(gram, ((0, 0), (0, width - size)))
    return offset


def early_gram_kernel(plan, ensembles, cotangents, suffixes, ens, cot, whole, offset, *refs):
    buffers, sems = refs[: 2 * (PIECES - 1)], refs[2 * (PIECES - 1) :]
    copies = []
    for piece in range(1, PIECES):
        pair = buffers[2 * piece - 2 : 2 * piece]
        own = sems[2 * piece - 2 : 2 * piece]
        copies.append(list(zip(
            loads(plan, piece, ensembles, pair[0], own[0]),
            loads(plan, piece, cotangents, pair[1], own[1]),
        )))
    total = gram_of(plan, 0, cot, ens, suffixes, whole)
    for piece in range(1, PIECES - 1):
        waiting = iter(copies[piece - 1])

        def ready():
            for copy in next(waiting):
                copy.wait()

        ens, cot = buffers[2 * piece - 2 : 2 * piece]
        total = total + gram_of(plan, piece, cot, ens, suffixes, whole, ready)
    offset[...] = total
    for pair in copies[-1]:
        for copy in pair:
            copy.wait()


def late_gram_kernel(plan, ens, cot, suffixes, early, offset, _, kept, sent, offsets, whole):
    whole[:, : early.shape[1]] = early[...]
    offsets[...] = offset[...] + gram_of(plan, PIECES - 1, cot, ens, suffixes, whole)
    half = plan.members // 2
    core = lax.rem(lax.axis_index("space"), 2)
    kept[...] = whole[pl.ds(core * half, half)]
    sent[...] = whole[pl.ds((1 - core) * half, half)]


def upper_half(level):
    return lax.rem(lax.axis_index("tm") // (1 << level), 2) == 1


def join_kernel(level, total, other, later, before, _, *refs):
    new_total, new_later, new_before, upper_total = refs[len(refs) // 2 - 2 : len(refs) // 2 + 2]
    upper = upper_half(level)
    left = jnp.where(upper, other[...], total[...])
    right = jnp.where(upper, total[...], other[...])
    new_total[...] = mul_exact(left, right)
    upper_total[...] = right
    new_later[...] = jnp.where(upper, later[...], mul_exact(later[...], other[...]))
    new_before[...] = jnp.where(upper, mul_exact(other[...], before[...]), before[...])


def sum_kernel(left, right, _, total):
    total[...] = left[...] + right[...]


def pass_kernel(level, own, other, carry, upper_total, before, _, *refs):
    new_own, new_carry = refs[len(refs) // 2 - 1 : len(refs) // 2 + 1]
    upper = upper_half(level)
    left = jnp.where(upper, other[...], own[...])
    right = jnp.where(upper, own[...], other[...])
    new_own[...] = mul_exact(left, upper_total[...]) + right
    new_carry[...] = carry[...] + jnp.where(upper, mul_exact(left, before[...]), 0.0)


def last_pass_kernel(level, other, carry, before, _, __, new_carry, ___):
    added = mul_exact(other[...], before[...])
    new_carry[...] = carry[...] + jnp.where(upper_half(level), added, 0.0)


def enter_kernel(level, later, other, _, entering):
    joined = mul_exact(later[...], other[...])
    entering[...] = jnp.where(upper_half(level), later[...], joined)


def carry_kernel(plan, suffixes, later, _, ens_factors, cot_factors, follow):
    count, members = plan.count, plan.members
    entering = later[...]
    mask = on_blocks(members, plan.stack * members)
    repeated = split(jnp.concatenate([entering] * plan.stack, axis=1))
    for at, (start, stop) in enumerate(plan.groups):
        size = (stop - start) * members
        wide = mul_pairs(split(suffixes[plan.rows(start, stop)]), repeated)
        part = jnp.where(mask[:size, :size], wide[:, :size], 0.0)
        cot_factors[at, :size, :size] = part.astype(BF16)
        ens_factors[at, :size, :size] = part.T.astype(BF16)
        first = max(start - 1, 0)
        kept = wide[(first + 1 - start) * members :, :members]
        for side, value in enumerate(split(kept)):
            follow[side, plan.rows(first, stop - 1)] = value
    for side, value in enumerate(split(entering)):
        follow[side, plan.rows(count - 1, count)] = value


def apply_kernel(plan, factors, *refs):
    out, marker, out_buf, out_sem = refs[-4:]
    members = plan.members
    marker[...] = jnp.zeros_like(marker)
    chunk = out_buf.shape[2] // 2
    writes = []
    for piece, values in enumerate(refs[:PIECES]):
        first = plan.pieces[piece][0]
        for at, (start, stop) in enumerate(plan.piece_groups[piece]):
            size = (stop - start) * members
            for side in range(2):
                columns = slice(side * chunk, (side + 1) * chunk)
                stacked = values[start - first : stop - first, :, columns].reshape(size, chunk)
                result = mul(factors[plan.first_group[piece] + at, :size, :size], stacked)
                out_buf[start:stop, :, columns] = result.astype(BF16).reshape(
                    stop - start, members, chunk
                )
                copy = pltpu.make_async_copy(
                    out_buf.at[start:stop, :, columns],
                    out.at[start:stop, :, columns],
                    out_sem.at[len(writes)],
                )
                copy.start()
                writes.append(copy)
    for copy in writes:
        copy.wait()


def final_kernel(plan, scale, gram, gram_core, follow, steps, _, *refs):
    carries, (out, buffer, sems) = refs[:-3], refs[-3:]
    carry = carries[0][...]
    for ref in carries[1:]:
        carry = carry + ref[...]
    count, members = plan.count, plan.members
    totals = []
    first = lax.rem(lax.axis_index("space"), 2) == 0
    for at, (start, stop) in enumerate(plan.groups):
        mine, other = gram[:, plan.lanes(at)], gram_core[:, plan.lanes(at)]
        halves = [jnp.where(first, mine, other), jnp.where(first, other, mine)]
        tall = jnp.concatenate(halves, axis=0).T
        for i in range(stop - start):
            totals.append(tall[i * members : (i + 1) * members])
    totals[0] = totals[0] + carry.T
    number = 0
    width = 1
    while width < count:
        for start in range(width, count, 2 * width):
            size = min(width, count - start)
            rows = plan.rows(number, number + size)
            added = mul_pairs((steps[0, rows], steps[1, rows]), split(totals[start - 1]))
            for at in range(size):
                totals[start + at] = totals[start + at] + added[at * members : (at + 1) * members]
            number += size
        width *= 2
    copies = []
    for at in range(count):
        rows = plan.rows(at, at + 1)
        buffer[at] = mul_pairs(split(totals[at]), (follow[0, rows], follow[1, rows]), ROWS) * scale
        copy = pltpu.make_async_copy(buffer.at[at], out.at[at], sems.at[at])
        copy.start()
        copies.append(copy)
    for copy in copies:
        copy.wait()


def call(kernel, outs, ins, out_specs, scratch, micros, name, limit=16, aliases=None):
    return pl.pallas_call(
        kernel,
        out_shape=outs,
        in_specs=ins,
        out_specs=out_specs,
        scratch_shapes=scratch,
        input_output_aliases=aliases or {},
        compiler_params=pltpu.CompilerParams(vmem_limit_bytes=limit << 20),
        cost_estimate=pl.CostEstimate(
            flops=int(micros * 1e9), bytes_accessed=int(micros * 3e6), transcendentals=0
        ),
        name=name,
    )


def shape(*dims, kind=F32):
    return jax.ShapeDtypeStruct(dims, kind)


def shards(ensembles, cotangents, transforms):
    count, members, cells = ensembles.shape
    blocks, lanes = lax.axis_size("tm"), lax.axis_size("space")
    chips = lanes // 2
    scale = 1.0 / math.sqrt(cells * lanes * count * blocks)
    plan = Plan(count, members)
    levels = blocks.bit_length() - 1
    square = shape(members, members)
    ensembles, cotangents, transforms = (
        pltpu.with_memory_space_constraint(value, pltpu.HBM)
        for value in (ensembles, cotangents, transforms)
    )

    def exchange(value, axis, size, bit):
        return lax.ppermute(value, axis, [(at, at ^ bit) for at in range(size)])

    def around(value):
        return [
            lax.ppermute(value, "space", [(at, (at + 2 * d) % lanes) for at in range(lanes)])
            for d in range(1, chips)
        ]

    def piece_shape(piece):
        first, last = plan.pieces[piece]
        return shape(last - first, members, cells, kind=BF16)

    def piece_sems(piece):
        return [pltpu.SemaphoreType.DMA((len(plan.piece_groups[piece]),))] * 2

    suffixes, total, kept, *first_part = call(
        functools.partial(chain_kernel, plan),
        [shape(count * members, members), square, shape(count, members, members)] + [piece_shape(0)] * 2,
        [HBM] * 3, [VMEM] * 5, [pltpu.SemaphoreType.DMA] + piece_sems(0), 3.5, "transform_chain",
    )(transforms, ensembles, cotangents)

    wide = shape(members // 2, plan.width)
    later = before = jnp.eye(members, dtype=F32)
    uppers, befores = [], []

    def join(level, total, other, later, before, after, *through):
        more = [shape(*value.shape) for value in through]
        befores.append(before)
        total, later, before, upper, *through = call(
            functools.partial(join_kernel, level),
            [square] * 4 + more, [VMEM] * 4 + [ANY] * (1 + len(more)), [VMEM] * 4 + [ANY] * len(more),
            [], 3, f"join_{level}", aliases={5 + at: 4 + at for at in range(len(more))},
        )(total, other, later, before, after, *through)
        uppers.append(upper)
        return total, later, before, *through

    other = exchange(total, "tm", blocks, 1)
    early_width = plan.lanes(plan.first_group[-1]).start
    early, offset, *loaded = call(
        functools.partial(early_gram_kernel, plan),
        [shape(members, early_width), square]
        + [piece_shape(piece) for piece in range(1, PIECES) for _ in range(2)],
        [HBM] * 2 + [VMEM] * 3, [VMEM] * (2 * PIECES),
        [sem for piece in range(1, PIECES) for sem in piece_sems(piece)], 3, "early_gram",
    )(ensembles, cotangents, suffixes, *first_part)
    parts = [first_part] + [loaded[at : at + 2] for at in range(0, len(loaded), 2)]
    total, later, before = join(0, total, other, later, before, offset)

    other = exchange(total, "tm", blocks, 2)
    gram, gram_sent, own = call(
        functools.partial(late_gram_kernel, plan),
        [wide, wide, square], [VMEM] * 5 + [ANY], [VMEM] * 3,
        [pltpu.VMEM((members, plan.width), F32)], 1.2, "late_gram",
    )(*parts[-1], suffixes, early, offset, total)
    other_own = exchange(own, "tm", blocks, 1)
    gram_core = exchange(gram_sent, "space", lanes, 1)
    for level in range(1, levels - 1):
        total, later, before = join(level, total, other, later, before, own)
        other = exchange(total, "tm", blocks, 2 << level)
    befores.append(before)

    def pass_on(level, carry, after, *through):
        more = [shape(*value.shape) for value in through]
        return call(
            functools.partial(pass_kernel, level),
            [square] * 2 + more, [VMEM] * 5 + [ANY] * (1 + len(more)), [VMEM] * 2 + [ANY] * len(more),
            [], 3, f"pass_{level}", aliases={6 + at: 2 + at for at in range(len(more))},
        )(own, other_own, carry, uppers[level], befores[level], after, *through)

    carry = jnp.zeros((members, members), F32)
    for level in range(levels - 2):
        own, carry = pass_on(level, carry, total)
        other_own = exchange(own, "tm", blocks, 2 << level)
    gram = call(sum_kernel, wide, [VMEM] * 2 + [ANY], VMEM, [], 0.1, "chip_gram")(gram, gram_core, own)
    grams = around(gram)
    entering = call(
        functools.partial(enter_kernel, levels - 1),
        square, [VMEM] * 2 + [ANY], VMEM, [], 0.2, "entering",
    )(later, other, gram)
    own, carry = pass_on(levels - 2, carry, entering)
    other_own = exchange(own, "tm", blocks, blocks // 2)
    size = plan.stack * members
    ens_factors, cot_factors, follow = call(
        functools.partial(carry_kernel, plan),
        [shape(len(plan.groups), size, size, kind=BF16)] * 2
        + [shape(2, count * members, members, kind=BF16)],
        [VMEM] * 2 + [ANY], [VMEM] * 3, [], 0.9, "carries",
    )(suffixes, entering, own)
    def apply(factors, which, after, name):
        return call(
            functools.partial(apply_kernel, plan),
            [shape(count, members, cells, kind=BF16), shape(8, 128)],
            [VMEM] * (1 + PIECES) + [ANY], [HBM, VMEM],
            [pltpu.VMEM((count, members, cells), BF16),
             pltpu.SemaphoreType.DMA((2 * len(plan.groups),))],
            2.7, name,
        )(factors, *(part[which] for part in parts), after)

    smoothed, done = apply(ens_factors, 0, follow, "smoothed")
    carry, grams[0] = call(
        functools.partial(last_pass_kernel, levels - 1),
        [square, wide], [VMEM] * 3 + [ANY] * 2, [VMEM, ANY], [], 0.2, "pass_last", aliases={4: 1},
    )(other_own, carry, befores[-1], done, grams[0])
    carry_core = exchange(carry, "space", lanes, 1)
    for part in grams:
        gram = gram + part
    gram_core = exchange(gram, "space", lanes, 1)
    steps = call(
        functools.partial(windows_kernel, plan),
        shape(2, count_steps(count) * members, members, kind=BF16), [VMEM, ANY], VMEM,
        [pltpu.VMEM((count * members, members), F32)], 1.0, "windows",
    )(kept, carry)
    carry = call(
        sum_kernel, square, [VMEM] * 2 + [ANY], VMEM, [], 0.1, "chip_carry",
    )(carry, carry_core, steps)
    carries = [carry] + around(carry)
    ensemble_grad, done = apply(cot_factors, 1, carry, "ensemble_grad")
    transform_grad = call(
        functools.partial(final_kernel, plan, scale),
        shape(count, members, members),
        [VMEM] * 4 + [ANY] + [VMEM] * chips, HBM,
        [pltpu.VMEM((count, members, members), F32), pltpu.SemaphoreType.DMA((count,))],
        2.5, "transform_grad",
    )(gram, gram_core, follow, steps, done, *carries)
    return (smoothed, ensemble_grad, transform_grad)


def solution(mesh):
    return jax.shard_map(
        shards,
        mesh=mesh,
        in_specs=(P("tm", None, "space"), P("tm", None, "space"), P("tm", None, None)),
        out_specs=(P("tm", None, "space"), P("tm", None, "space"), P("tm", None, None)),
        check_vma=False,
    )
```

```python
import functools
import math

import jax
import jax.numpy as jnp
from jax import lax
from jax.experimental import pallas as pl
from jax.experimental.pallas import tpu as pltpu
from jax.sharding import PartitionSpec as P

F32 = jnp.float32
BF16 = jnp.bfloat16
VMEM = pl.BlockSpec(memory_space=pltpu.VMEM)
HBM = pl.BlockSpec(memory_space=pltpu.HBM)
ANY = pl.BlockSpec(memory_space=pl.ANY)
DEPTH = 256
PIECES = 2
NORMAL = (((1,), (0,)), ((), ()))
ROWS = (((1,), (1,)), ((), ()))


def split(value):
    high = value.astype(BF16)
    return high, (value - high.astype(F32)).astype(BF16)


def mul(left, right, dims=NORMAL):
    return lax.dot_general(left, right, dims, preferred_element_type=F32)


def mul_pairs(left, right, dims=NORMAL):
    return mul(left[0], right[0], dims) + (
        mul(left[0], right[1], dims) + mul(left[1], right[0], dims)
    )


def mul_exact(left, right, dims=NORMAL):
    return mul_pairs(split(left), split(right), dims)


def product_of(factors):
    while len(factors) > 1:
        joined = [mul_exact(*factors[at : at + 2]) for at in range(0, len(factors) - 1, 2)]
        factors = joined + factors[len(joined) * 2 :]
    return factors[0]


def suffix_scan(ref, count, members, stop):
    width = 1
    while width < stop:
        for start in range(0, count, 2 * width):
            middle = start + width
            if middle < count:
                rows = slice(start * members, middle * members)
                ref[rows] = mul_exact(ref[rows], ref[middle * members : (middle + 1) * members])
        width *= 2


class Plan:
    def __init__(self, count, members):
        self.count, self.members = count, members
        self.stack = DEPTH // members
        self.groups = [
            (start, min(start + self.stack, count)) for start in range(0, count, self.stack)
        ]
        bounds = [len(self.groups) * at // PIECES for at in range(PIECES + 1)]
        self.piece_groups = [self.groups[a:b] for a, b in zip(bounds, bounds[1:])]
        self.pieces = [(part[0][0], part[-1][1]) for part in self.piece_groups]
        self.first_group = bounds[:-1]
        self.widths = [-(-(stop - start) * members // 128) * 128 for start, stop in self.groups]
        self.width = sum(self.widths)

    def lanes(self, at):
        start = sum(self.widths[:at])
        return slice(start, start + self.widths[at])

    def rows(self, first, last):
        return slice(first * self.members, last * self.members)


def on_blocks(members, size):
    rows = lax.broadcasted_iota(jnp.int32, (size, size), 0) // members
    columns = lax.broadcasted_iota(jnp.int32, (size, size), 1) // members
    return rows == columns


def loads(plan, piece, values, buffer, sems, which=slice(None)):
    base = plan.pieces[piece][0]
    copies = [
        pltpu.make_async_copy(values.at[start:stop], buffer.at[start - base : stop - base], sems.at[at])
        for at, (start, stop) in enumerate(plan.piece_groups[piece])
    ][which]
    for copy in copies:
        copy.start()
    return copies


def chain_kernel(
    plan, transforms, ensembles, cotangents, suffixes, total, kept, ens, cot, sem, ens_sem, cot_sem
):
    count, members = plan.count, plan.members
    read = pltpu.make_async_copy(transforms, kept, sem)
    read.start()
    more = loads(plan, 0, ensembles, ens, ens_sem, slice(1))
    more += loads(plan, 0, cotangents, cot, cot_sem, slice(1))
    read.wait()
    more += loads(plan, 0, ensembles, ens, ens_sem, slice(1, None))
    more += loads(plan, 0, cotangents, cot, cot_sem, slice(1, None))
    for at in range(count):
        suffixes[plan.rows(at, at + 1)] = kept[at]
    suffix_scan(suffixes, count, members, count)
    total[...] = suffixes[plan.rows(0, 1)]
    for copy in more:
        copy.wait()


def windows_kernel(plan, kept, _, steps, runs):
    count = plan.count
    for at in range(count - 1):
        runs[plan.rows(at + 1, at + 2)] = kept[at].T
    number = 0
    width = 1
    while width < count:
        for middle in range(width, count, 2 * width):
            size = min(width, count - middle)
            for side, part in enumerate(split(runs[plan.rows(middle, middle + size)])):
                steps[side, plan.rows(number, number + size)] = part
            number += size
        for start in range(2 * width, count, 2 * width):
            if start + width < count:
                rows = plan.rows(start + width, min(start + 2 * width, count))
                runs[rows] = mul_exact(runs[rows], runs[plan.rows(start + width - 1, start + width)])
        width *= 2


def count_steps(count):
    total = 0
    width = 1
    while width < count:
        total += sum(min(width, count - middle) for middle in range(width, count, 2 * width))
        width *= 2
    return total


def core_index():
    return lax.rem(lax.axis_index("space"), 2)


def gram_of(plan, piece, cot, ens, suffixes, whole, ready=lambda: None):
    members = plan.members
    base = plan.pieces[piece][0]
    offset = jnp.zeros((members, members), F32)
    for at, (start, stop) in enumerate(plan.piece_groups[piece]):
        ready()
        size = (stop - start) * members
        stacked = [ref[start - base : stop - base].reshape(size, ref.shape[2]) for ref in (cot, ens)]
        wide = jnp.where(on_blocks(members, size), mul(*stacked, ROWS), 0.0)
        gram = wide[:members]
        for i in range(1, stop - start):
            gram = gram + wide[i * members : (i + 1) * members]
        offset = offset + mul_exact(gram, suffixes[plan.rows(start, stop)])
        lanes = plan.lanes(plan.first_group[piece] + at)
        width = lanes.stop - lanes.start
        whole[:, lanes] = jnp.pad(gram, ((0, 0), (0, width - size)))
    return offset


def gram_kernel(
    plan, ensembles, cotangents, suffixes, ens, cot,
    kept, sent, offsets, next_ens, next_cot, whole, ens_sem, cot_sem,
):
    waiting = iter(list(zip(
        loads(plan, 1, ensembles, next_ens, ens_sem), loads(plan, 1, cotangents, next_cot, cot_sem)
    )))

    def ready():
        for copy in next(waiting):
            copy.wait()

    total = gram_of(plan, 0, cot, ens, suffixes, whole)
    offsets[...] = total + gram_of(plan, 1, next_cot, next_ens, suffixes, whole, ready)
    half = plan.members // 2
    core = lax.rem(lax.axis_index("space"), 2)
    kept[...] = whole[pl.ds(core * half, half)]
    sent[...] = whole[pl.ds((1 - core) * half, half)]


def upper_half(level):
    return lax.rem(lax.axis_index("tm") // (1 << level), 2) == 1


def join_kernel(level, total, other, later, before, _, *refs):
    new_total, new_later, new_before, upper_total = refs[len(refs) // 2 - 2 : len(refs) // 2 + 2]
    upper = upper_half(level)
    left = jnp.where(upper, other[...], total[...])
    right = jnp.where(upper, total[...], other[...])
    new_total[...] = mul_exact(left, right)
    upper_total[...] = right
    new_later[...] = jnp.where(upper, later[...], mul_exact(later[...], other[...]))
    new_before[...] = jnp.where(upper, mul_exact(other[...], before[...]), before[...])


def sum_kernel(left, right, _, total):
    total[...] = left[...] + right[...]


def pass_kernel(level, own, other, carry, upper_total, before, _, *refs):
    new_own, new_carry = refs[len(refs) // 2 - 1 : len(refs) // 2 + 1]
    upper = upper_half(level)
    left = jnp.where(upper, other[...], own[...])
    right = jnp.where(upper, own[...], other[...])
    new_own[...] = mul_exact(left, upper_total[...]) + right
    new_carry[...] = carry[...] + jnp.where(upper, mul_exact(left, before[...]), 0.0)


def last_pass_kernel(level, other, carry, before, _, __, new_carry, ___):
    added = mul_exact(other[...], before[...])
    new_carry[...] = carry[...] + jnp.where(upper_half(level), added, 0.0)


def enter_kernel(level, later, other, _, entering):
    joined = mul_exact(later[...], other[...])
    entering[...] = jnp.where(upper_half(level), later[...], joined)


def carry_kernel(plan, suffixes, later, _, ens_factors, cot_factors, follow):
    count, members = plan.count, plan.members
    entering = later[...]
    mask = on_blocks(members, plan.stack * members)
    repeated = split(jnp.concatenate([entering] * plan.stack, axis=1))
    for at, (start, stop) in enumerate(plan.groups):
        size = (stop - start) * members
        wide = mul_pairs(split(suffixes[plan.rows(start, stop)]), repeated)
        part = jnp.where(mask[:size, :size], wide[:, :size], 0.0)
        cot_factors[at, :size, :size] = part.astype(BF16)
        ens_factors[at, :size, :size] = part.T.astype(BF16)
        first = max(start - 1, 0)
        kept = wide[(first + 1 - start) * members :, :members]
        for side, value in enumerate(split(kept)):
            follow[side, plan.rows(first, stop - 1)] = value
    for side, value in enumerate(split(entering)):
        follow[side, plan.rows(count - 1, count)] = value


def apply_kernel(plan, factors, *refs):
    out, marker, out_buf, out_sem = refs[-4:]
    members = plan.members
    marker[...] = jnp.zeros_like(marker)
    chunk = out_buf.shape[2] // 2
    writes = []
    for piece, values in enumerate(refs[:PIECES]):
        first = plan.pieces[piece][0]
        for at, (start, stop) in enumerate(plan.piece_groups[piece]):
            size = (stop - start) * members
            for side in range(2):
                columns = slice(side * chunk, (side + 1) * chunk)
                stacked = values[start - first : stop - first, :, columns].reshape(size, chunk)
                result = mul(factors[plan.first_group[piece] + at, :size, :size], stacked)
                out_buf[start:stop, :, columns] = result.astype(BF16).reshape(
                    stop - start, members, chunk
                )
                copy = pltpu.make_async_copy(
                    out_buf.at[start:stop, :, columns],
                    out.at[start:stop, :, columns],
                    out_sem.at[len(writes)],
                )
                copy.start()
                writes.append(copy)
    for copy in writes:
        copy.wait()


def final_kernel(plan, scale, gram, gram_core, follow, steps, _, *refs):
    carries, (out, buffer, sems) = refs[:-3], refs[-3:]
    carry = carries[0][...]
    for ref in carries[1:]:
        carry = carry + ref[...]
    count, members = plan.count, plan.members
    totals = []
    first = lax.rem(lax.axis_index("space"), 2) == 0
    for at, (start, stop) in enumerate(plan.groups):
        mine, other = gram[:, plan.lanes(at)], gram_core[:, plan.lanes(at)]
        halves = [jnp.where(first, mine, other), jnp.where(first, other, mine)]
        tall = jnp.concatenate(halves, axis=0).T
        for i in range(stop - start):
            totals.append(tall[i * members : (i + 1) * members])
    totals[0] = totals[0] + carry.T
    number = 0
    width = 1
    while width < count:
        for start in range(width, count, 2 * width):
            size = min(width, count - start)
            rows = plan.rows(number, number + size)
            added = mul_pairs((steps[0, rows], steps[1, rows]), split(totals[start - 1]))
            for at in range(size):
                totals[start + at] = totals[start + at] + added[at * members : (at + 1) * members]
            number += size
        width *= 2
    copies = []
    for at in range(count):
        rows = plan.rows(at, at + 1)
        buffer[at] = mul_pairs(split(totals[at]), (follow[0, rows], follow[1, rows]), ROWS) * scale
        copy = pltpu.make_async_copy(buffer.at[at], out.at[at], sems.at[at])
        copy.start()
        copies.append(copy)
    for copy in copies:
        copy.wait()


def call(kernel, outs, ins, out_specs, scratch, micros, name, limit=16, aliases=None):
    return pl.pallas_call(
        kernel,
        out_shape=outs,
        in_specs=ins,
        out_specs=out_specs,
        scratch_shapes=scratch,
        input_output_aliases=aliases or {},
        compiler_params=pltpu.CompilerParams(vmem_limit_bytes=limit << 20),
        cost_estimate=pl.CostEstimate(
            flops=int(micros * 1e9), bytes_accessed=int(micros * 3e6), transcendentals=0
        ),
        name=name,
    )


def shape(*dims, kind=F32):
    return jax.ShapeDtypeStruct(dims, kind)


def shards(ensembles, cotangents, transforms):
    count, members, cells = ensembles.shape
    blocks, lanes = lax.axis_size("tm"), lax.axis_size("space")
    chips = lanes // 2
    scale = 1.0 / math.sqrt(cells * lanes * count * blocks)
    plan = Plan(count, members)
    levels = blocks.bit_length() - 1
    square = shape(members, members)
    ensembles, cotangents, transforms = (
        pltpu.with_memory_space_constraint(value, pltpu.HBM)
        for value in (ensembles, cotangents, transforms)
    )

    def exchange(value, axis, size, bit):
        return lax.ppermute(value, axis, [(at, at ^ bit) for at in range(size)])

    def around(value):
        return [
            lax.ppermute(value, "space", [(at, (at + 2 * d) % lanes) for at in range(lanes)])
            for d in range(1, chips)
        ]

    def piece_shape(piece):
        first, last = plan.pieces[piece]
        return shape(last - first, members, cells, kind=BF16)

    def piece_sems(piece):
        return [pltpu.SemaphoreType.DMA((len(plan.piece_groups[piece]),))] * 2

    suffixes, total, kept, *first_part = call(
        functools.partial(chain_kernel, plan),
        [shape(count * members, members), square, shape(count, members, members)] + [piece_shape(0)] * 2,
        [HBM] * 3, [VMEM] * 5, [pltpu.SemaphoreType.DMA] + piece_sems(0), 3.5, "transform_chain",
    )(transforms, ensembles, cotangents)

    wide = shape(members // 2, plan.width)
    later = before = jnp.eye(members, dtype=F32)
    uppers, befores = [], []

    def join(level, total, other, later, before, after, *through):
        more = [shape(*value.shape) for value in through]
        befores.append(before)
        total, later, before, upper, *through = call(
            functools.partial(join_kernel, level),
            [square] * 4 + more, [VMEM] * 4 + [ANY] * (1 + len(more)), [VMEM] * 4 + [ANY] * len(more),
            [], 3, f"join_{level}", aliases={5 + at: 4 + at for at in range(len(more))},
        )(total, other, later, before, after, *through)
        uppers.append(upper)
        return total, later, before, *through

    other = exchange(total, "tm", blocks, 1)
    gram, gram_sent, own, *second_part = call(
        functools.partial(gram_kernel, plan),
        [wide, wide, square] + [piece_shape(1)] * 2,
        [HBM] * 2 + [VMEM] * 3, [VMEM] * 5,
        [pltpu.VMEM((members, plan.width), F32)] + piece_sems(1), 4.5, "gram",
    )(ensembles, cotangents, suffixes, *first_part)
    parts = [first_part, second_part]
    other_own = exchange(own, "tm", blocks, 1)
    gram_core = exchange(gram_sent, "space", lanes, 1)
    total, later, before = join(0, total, other, later, before, own)
    other = exchange(total, "tm", blocks, 2)
    gram = call(sum_kernel, wide, [VMEM] * 2 + [ANY], VMEM, [], 0.1, "chip_gram")(gram, gram_core, total)
    grams = around(gram)

    def pass_on(level, carry, after, *through):
        more = [shape(*value.shape) for value in through]
        return call(
            functools.partial(pass_kernel, level),
            [square] * 2 + more, [VMEM] * 5 + [ANY] * (1 + len(more)), [VMEM] * 2 + [ANY] * len(more),
            [], 3, f"pass_{level}", aliases={6 + at: 2 + at for at in range(len(more))},
        )(own, other_own, carry, uppers[level], befores[level], after, *through)

    carry = jnp.zeros((members, members), F32)
    after = gram
    for level in range(levels - 2):
        own, carry = pass_on(level, carry, after)
        other_own = exchange(own, "tm", blocks, 2 << level)
        total, later, before = join(level + 1, total, other, later, before, own)
        other = exchange(total, "tm", blocks, 4 << level)
        after = total
    befores.append(before)
    own, carry = pass_on(levels - 2, carry, total)
    other_own = exchange(own, "tm", blocks, blocks // 2)
    entering = call(
        functools.partial(enter_kernel, levels - 1),
        square, [VMEM] * 2 + [ANY], VMEM, [], 0.2, "entering",
    )(later, other, own)
    size = plan.stack * members
    ens_factors, cot_factors, follow = call(
        functools.partial(carry_kernel, plan),
        [shape(len(plan.groups), size, size, kind=BF16)] * 2
        + [shape(2, count * members, members, kind=BF16)],
        [VMEM] * 2 + [ANY], [VMEM] * 3, [], 0.9, "carries",
    )(suffixes, entering, own)
    def apply(factors, which, after, name):
        return call(
            functools.partial(apply_kernel, plan),
            [shape(count, members, cells, kind=BF16), shape(8, 128)],
            [VMEM] * (1 + PIECES) + [ANY], [HBM, VMEM],
            [pltpu.VMEM((count, members, cells), BF16),
             pltpu.SemaphoreType.DMA((2 * len(plan.groups),))],
            0.5, name,
        )(factors, *(part[which] for part in parts), after)

    smoothed, done = apply(ens_factors, 0, follow, "smoothed")
    carry, grams[0] = call(
        functools.partial(last_pass_kernel, levels - 1),
        [square, wide], [VMEM] * 3 + [ANY] * 2, [VMEM, ANY], [], 0.2, "pass_last", aliases={4: 1},
    )(other_own, carry, befores[-1], done, grams[0])
    carry_core = exchange(carry, "space", lanes, 1)
    for part in grams:
        gram = gram + part
    gram_core = exchange(gram, "space", lanes, 1)
    steps = call(
        functools.partial(windows_kernel, plan),
        shape(2, count_steps(count) * members, members, kind=BF16), [VMEM, ANY], VMEM,
        [pltpu.VMEM((count * members, members), F32)], 1.0, "windows",
    )(kept, carry)
    carry = call(
        sum_kernel, square, [VMEM] * 2 + [ANY], VMEM, [], 0.1, "chip_carry",
    )(carry, carry_core, steps)
    carries = [carry] + around(carry)
    ensemble_grad, done = apply(cot_factors, 1, carry, "ensemble_grad")
    transform_grad = call(
        functools.partial(final_kernel, plan, scale),
        shape(count, members, members),
        [VMEM] * 4 + [ANY] + [VMEM] * chips, HBM,
        [pltpu.VMEM((count, members, members), F32), pltpu.SemaphoreType.DMA((count,))],
        2.5, "transform_grad",
    )(gram, gram_core, follow, steps, done, *carries)
    return (smoothed, ensemble_grad, transform_grad)


def solution(mesh):
    return jax.shard_map(
        shards,
        mesh=mesh,
        in_specs=(P("tm", None, "space"), P("tm", None, "space"), P("tm", None, None)),
        out_specs=(P("tm", None, "space"), P("tm", None, "space"), P("tm", None, None)),
        check_vma=False,
    )
```

```python
import functools
import math

import jax
import jax.numpy as jnp
from jax import lax
from jax.experimental import pallas as pl
from jax.experimental.pallas import tpu as pltpu
from jax.sharding import PartitionSpec as P

F32 = jnp.float32
BF16 = jnp.bfloat16
VMEM = pl.BlockSpec(memory_space=pltpu.VMEM)
HBM = pl.BlockSpec(memory_space=pltpu.HBM)
ANY = pl.BlockSpec(memory_space=pl.ANY)
DEPTH = 256
PIECES = 2
NORMAL = (((1,), (0,)), ((), ()))
ROWS = (((1,), (1,)), ((), ()))


def split(value):
    high = value.astype(BF16)
    return high, (value - high.astype(F32)).astype(BF16)


def mul(left, right, dims=NORMAL):
    return lax.dot_general(left, right, dims, preferred_element_type=F32)


def mul_pairs(left, right, dims=NORMAL):
    return mul(left[0], right[0], dims) + (
        mul(left[0], right[1], dims) + mul(left[1], right[0], dims)
    )


def mul_exact(left, right, dims=NORMAL):
    return mul_pairs(split(left), split(right), dims)


def product_of(factors):
    while len(factors) > 1:
        joined = [mul_exact(*factors[at : at + 2]) for at in range(0, len(factors) - 1, 2)]
        factors = joined + factors[len(joined) * 2 :]
    return factors[0]


def suffix_scan(ref, count, members, stop):
    width = 1
    while width < stop:
        for start in range(0, count, 2 * width):
            middle = start + width
            if middle < count:
                rows = slice(start * members, middle * members)
                ref[rows] = mul_exact(ref[rows], ref[middle * members : (middle + 1) * members])
        width *= 2


class Plan:
    def __init__(self, count, members):
        self.count, self.members = count, members
        self.stack = DEPTH // members
        self.groups = [
            (start, min(start + self.stack, count)) for start in range(0, count, self.stack)
        ]
        bounds = [len(self.groups) * at // PIECES for at in range(PIECES + 1)]
        self.piece_groups = [self.groups[a:b] for a, b in zip(bounds, bounds[1:])]
        self.pieces = [(part[0][0], part[-1][1]) for part in self.piece_groups]
        self.first_group = bounds[:-1]
        self.widths = [-(-(stop - start) * members // 128) * 128 for start, stop in self.groups]
        self.width = sum(self.widths)

    def lanes(self, at):
        start = sum(self.widths[:at])
        return slice(start, start + self.widths[at])

    def rows(self, first, last):
        return slice(first * self.members, last * self.members)


def on_blocks(members, size):
    rows = lax.broadcasted_iota(jnp.int32, (size, size), 0) // members
    columns = lax.broadcasted_iota(jnp.int32, (size, size), 1) // members
    return rows == columns


def loads(plan, piece, values, buffer, sems, which=slice(None)):
    base = plan.pieces[piece][0]
    copies = [
        pltpu.make_async_copy(values.at[start:stop], buffer.at[start - base : stop - base], sems.at[at])
        for at, (start, stop) in enumerate(plan.piece_groups[piece])
    ][which]
    for copy in copies:
        copy.start()
    return copies


def chain_kernel(
    plan, transforms, ensembles, cotangents, suffixes, total, kept, ens, cot, sem, ens_sem, cot_sem
):
    count, members = plan.count, plan.members
    read = pltpu.make_async_copy(transforms, kept, sem)
    read.start()
    more = loads(plan, 0, ensembles, ens, ens_sem, slice(1))
    more += loads(plan, 0, cotangents, cot, cot_sem, slice(1))
    read.wait()
    more += loads(plan, 0, ensembles, ens, ens_sem, slice(1, None))
    more += loads(plan, 0, cotangents, cot, cot_sem, slice(1, None))
    for at in range(count):
        suffixes[plan.rows(at, at + 1)] = kept[at]
    suffix_scan(suffixes, count, members, count)
    total[...] = suffixes[plan.rows(0, 1)]
    for copy in more:
        copy.wait()


def windows_kernel(plan, kept, _, steps, prefixes, runs):
    count = plan.count
    for at in range(count - 1):
        runs[plan.rows(at + 1, at + 2)] = kept[at].T
    number = 0
    width = 1
    while width < count:
        for middle in range(width, count, 2 * width):
            size = min(width, count - middle)
            for side, part in enumerate(split(runs[plan.rows(middle, middle + size)])):
                steps[side, plan.rows(number, number + size)] = part
            number += size
        for start in range(0, count, 2 * width):
            if start + width < count and (start or width > 1):
                rows = plan.rows(start + width, min(start + 2 * width, count))
                runs[rows] = mul_exact(runs[rows], runs[plan.rows(start + width - 1, start + width)])
        width *= 2
    for side, part in enumerate(split(runs[plan.rows(1, count)])):
        prefixes[side] = part


def count_steps(count):
    total = 0
    width = 1
    while width < count:
        total += sum(min(width, count - middle) for middle in range(width, count, 2 * width))
        width *= 2
    return total


def core_index():
    return lax.rem(lax.axis_index("space"), 2)


def gram_of(plan, piece, cot, ens, suffixes, whole, ready=lambda: None):
    members = plan.members
    base = plan.pieces[piece][0]
    offset = jnp.zeros((members, members), F32)
    for at, (start, stop) in enumerate(plan.piece_groups[piece]):
        ready()
        size = (stop - start) * members
        stacked = [ref[start - base : stop - base].reshape(size, ref.shape[2]) for ref in (cot, ens)]
        wide = jnp.where(on_blocks(members, size), mul(*stacked, ROWS), 0.0)
        gram = wide[:members]
        for i in range(1, stop - start):
            gram = gram + wide[i * members : (i + 1) * members]
        offset = offset + mul_exact(gram, suffixes[plan.rows(start, stop)])
        lanes = plan.lanes(plan.first_group[piece] + at)
        width = lanes.stop - lanes.start
        whole[:, lanes] = jnp.pad(gram, ((0, 0), (0, width - size)))
    return offset


def gram_kernel(
    plan, ensembles, cotangents, suffixes, ens, cot,
    kept, sent, offsets, next_ens, next_cot, whole, ens_sem, cot_sem,
):
    waiting = iter(list(zip(
        loads(plan, 1, ensembles, next_ens, ens_sem), loads(plan, 1, cotangents, next_cot, cot_sem)
    )))

    def ready():
        for copy in next(waiting):
            copy.wait()

    total = gram_of(plan, 0, cot, ens, suffixes, whole)
    offsets[...] = total + gram_of(plan, 1, next_cot, next_ens, suffixes, whole, ready)
    half = plan.members // 2
    core = lax.rem(lax.axis_index("space"), 2)
    kept[...] = whole[pl.ds(core * half, half)]
    sent[...] = whole[pl.ds((1 - core) * half, half)]


def upper_half(level):
    return lax.rem(lax.axis_index("tm") // (1 << level), 2) == 1


def join_kernel(level, total, other, later, before, _, *refs):
    new_total, new_later, new_before, upper_total = refs[len(refs) // 2 - 2 : len(refs) // 2 + 2]
    upper = upper_half(level)
    left = jnp.where(upper, other[...], total[...])
    right = jnp.where(upper, total[...], other[...])
    new_total[...] = mul_exact(left, right)
    upper_total[...] = right
    new_later[...] = jnp.where(upper, later[...], mul_exact(later[...], other[...]))
    new_before[...] = jnp.where(upper, mul_exact(other[...], before[...]), before[...])


def sum_kernel(left, right, _, total):
    total[...] = left[...] + right[...]


def pass_kernel(level, own, other, carry, upper_total, before, _, new_own, new_carry):
    upper = upper_half(level)
    left = jnp.where(upper, other[...], own[...])
    right = jnp.where(upper, own[...], other[...])
    new_own[...] = mul_exact(left, upper_total[...]) + right
    new_carry[...] = carry[...] + jnp.where(upper, mul_exact(left, before[...]), 0.0)


def last_pass_kernel(
    level, own, other, carry, upper_total, before, total, _, __, message, new_carry, ___
):
    pass_kernel(level, own, other, carry, upper_total, before, _, message, new_carry)
    message[...] = jnp.where(upper_half(level + 1), total[...], message[...])


def enter_kernel(level, later, carry, before, message, _, entering, new_carry):
    upper = upper_half(level)
    joined = mul_exact(later[...], message[...])
    added = mul_exact(message[...], before[...])
    entering[...] = jnp.where(upper, later[...], joined)
    new_carry[...] = carry[...] + jnp.where(upper, added, 0.0)


def carry_kernel(plan, suffixes, later, _, ens_factors, cot_factors, follow):
    count, members = plan.count, plan.members
    entering = later[...]
    mask = on_blocks(members, plan.stack * members)
    repeated = split(jnp.concatenate([entering] * plan.stack, axis=1))
    for at, (start, stop) in enumerate(plan.groups):
        size = (stop - start) * members
        wide = mul_pairs(split(suffixes[plan.rows(start, stop)]), repeated)
        part = jnp.where(mask[:size, :size], wide[:, :size], 0.0)
        cot_factors[at, :size, :size] = part.astype(BF16)
        ens_factors[at, :size, :size] = part.T.astype(BF16)
        first = max(start - 1, 0)
        kept = wide[(first + 1 - start) * members :, :members]
        for side, value in enumerate(split(kept)):
            follow[side, plan.rows(first, stop - 1)] = value
    for side, value in enumerate(split(entering)):
        follow[side, plan.rows(count - 1, count)] = value


def apply_kernel(plan, factors, *refs):
    out, marker, out_buf, out_sem = refs[-4:]
    members = plan.members
    marker[...] = jnp.zeros_like(marker)
    chunk = out_buf.shape[2] // 2
    writes = []
    for piece, values in enumerate(refs[:PIECES]):
        first = plan.pieces[piece][0]
        for at, (start, stop) in enumerate(plan.piece_groups[piece]):
            size = (stop - start) * members
            for side in range(2):
                columns = slice(side * chunk, (side + 1) * chunk)
                stacked = values[start - first : stop - first, :, columns].reshape(size, chunk)
                result = mul(factors[plan.first_group[piece] + at, :size, :size], stacked)
                out_buf[start:stop, :, columns] = result.astype(BF16).reshape(
                    stop - start, members, chunk
                )
                copy = pltpu.make_async_copy(
                    out_buf.at[start:stop, :, columns],
                    out.at[start:stop, :, columns],
                    out_sem.at[len(writes)],
                )
                copy.start()
                writes.append(copy)
    for copy in writes:
        copy.wait()


def scan_kernel(plan, gram, gram_core, steps, out):
    count, members = plan.count, plan.members
    first = lax.rem(lax.axis_index("space"), 2) == 0
    totals = []
    for at, (start, stop) in enumerate(plan.groups):
        mine, other = gram[:, plan.lanes(at)], gram_core[:, plan.lanes(at)]
        halves = [jnp.where(first, mine, other), jnp.where(first, other, mine)]
        tall = jnp.concatenate(halves, axis=0).T
        for i in range(stop - start):
            totals.append(tall[i * members : (i + 1) * members])
    number = 0
    width = 1
    while width < count:
        for start in range(width, count, 2 * width):
            size = min(width, count - start)
            rows = plan.rows(number, number + size)
            added = mul_pairs((steps[0, rows], steps[1, rows]), split(totals[start - 1]))
            for at in range(size):
                totals[start + at] = totals[start + at] + added[at * members : (at + 1) * members]
            number += size
        width *= 2
    for at in range(count):
        out[at] = totals[at]


def final_kernel(plan, scale, totals, prefixes, follow, _, *refs):
    carries, (out, buffer, sems) = refs[:-3], refs[-3:]
    count, members = plan.count, plan.members
    carry = carries[0][...]
    for ref in carries[1:]:
        carry = carry + ref[...]
    carry = carry.T
    added = mul_pairs((prefixes[0], prefixes[1]), split(carry))
    copies = []
    for at in range(count):
        rows = plan.rows(at, at + 1)
        total = totals[at] + (added[plan.rows(at - 1, at)] if at else carry)
        buffer[at] = mul_pairs(split(total), (follow[0, rows], follow[1, rows]), ROWS) * scale
        copy = pltpu.make_async_copy(buffer.at[at], out.at[at], sems.at[at])
        copy.start()
        copies.append(copy)
    for copy in copies:
        copy.wait()


def call(kernel, outs, ins, out_specs, scratch, micros, name, limit=16, aliases=None):
    return pl.pallas_call(
        kernel,
        out_shape=outs,
        in_specs=ins,
        out_specs=out_specs,
        scratch_shapes=scratch,
        input_output_aliases=aliases or {},
        compiler_params=pltpu.CompilerParams(vmem_limit_bytes=limit << 20),
        cost_estimate=pl.CostEstimate(
            flops=int(micros * 1e9), bytes_accessed=int(micros * 3e6), transcendentals=0
        ),
        name=name,
    )


def shape(*dims, kind=F32):
    return jax.ShapeDtypeStruct(dims, kind)


def shards(ensembles, cotangents, transforms):
    count, members, cells = ensembles.shape
    blocks, lanes = lax.axis_size("tm"), lax.axis_size("space")
    chips = lanes // 2
    scale = 1.0 / math.sqrt(cells * lanes * count * blocks)
    plan = Plan(count, members)
    levels = blocks.bit_length() - 1
    square = shape(members, members)
    ensembles, cotangents, transforms = (
        pltpu.with_memory_space_constraint(value, pltpu.HBM)
        for value in (ensembles, cotangents, transforms)
    )

    def exchange(value, axis, size, bit):
        return lax.ppermute(value, axis, [(at, at ^ bit) for at in range(size)])

    def around(value):
        return [
            lax.ppermute(value, "space", [(at, (at + 2 * d) % lanes) for at in range(lanes)])
            for d in range(1, chips)
        ]

    def piece_shape(piece):
        first, last = plan.pieces[piece]
        return shape(last - first, members, cells, kind=BF16)

    def piece_sems(piece):
        return [pltpu.SemaphoreType.DMA((len(plan.piece_groups[piece]),))] * 2

    suffixes, total, kept, *first_part = call(
        functools.partial(chain_kernel, plan),
        [shape(count * members, members), square, shape(count, members, members)] + [piece_shape(0)] * 2,
        [HBM] * 3, [VMEM] * 5, [pltpu.SemaphoreType.DMA] + piece_sems(0), 3.5, "transform_chain",
    )(transforms, ensembles, cotangents)

    wide = shape(members // 2, plan.width)
    later = before = jnp.eye(members, dtype=F32)
    uppers, befores = [], []

    def join(level, total, other, later, before, after, *through):
        more = [shape(*value.shape) for value in through]
        befores.append(before)
        total, later, before, upper, *through = call(
            functools.partial(join_kernel, level),
            [square] * 4 + more, [VMEM] * 4 + [ANY] * (1 + len(more)), [VMEM] * 4 + [ANY] * len(more),
            [], 3, f"join_{level}", aliases={5 + at: 4 + at for at in range(len(more))},
        )(total, other, later, before, after, *through)
        uppers.append(upper)
        return total, later, before, *through

    other = exchange(total, "tm", blocks, 1)
    gram, gram_sent, own, *second_part = call(
        functools.partial(gram_kernel, plan),
        [wide, wide, square] + [piece_shape(1)] * 2,
        [HBM] * 2 + [VMEM] * 3, [VMEM] * 5,
        [pltpu.VMEM((members, plan.width), F32)] + piece_sems(1), 4.5, "gram",
    )(ensembles, cotangents, suffixes, *first_part)
    parts = [first_part, second_part]
    other_own = exchange(own, "tm", blocks, 1)
    gram_core = exchange(gram_sent, "space", lanes, 1)
    total, later, before = join(0, total, other, later, before, own)
    other = exchange(total, "tm", blocks, 2)
    gram = call(sum_kernel, wide, [VMEM] * 2 + [ANY], VMEM, [], 0.1, "chip_gram")(gram, gram_core, total)
    grams = around(gram)

    carry = jnp.zeros((members, members), F32)
    after = gram
    for level in range(levels - 2):
        own, carry = call(
            functools.partial(pass_kernel, level),
            [square] * 2, [VMEM] * 5 + [ANY], [VMEM] * 2, [], 3, f"pass_{level}",
        )(own, other_own, carry, uppers[level], befores[level], after)
        other_own = exchange(own, "tm", blocks, 2 << level)
        total, later, before = join(level + 1, total, other, later, before, own)
        if level < levels - 3:
            other = exchange(total, "tm", blocks, 4 << level)
        after = total
    befores.append(before)
    level = levels - 2
    message, carry, grams[0] = call(
        functools.partial(last_pass_kernel, level),
        [square] * 2 + [wide], [VMEM] * 6 + [ANY] * 2, [VMEM] * 2 + [ANY], [], 3, f"pass_{level}",
        aliases={7: 2},
    )(own, other_own, carry, uppers[level], befores[level], total, total, grams[0])
    message_other = exchange(message, "tm", blocks, blocks // 2)
    for part in grams:
        gram = gram + part
    gram_core = exchange(gram, "space", lanes, 1)
    steps, prefixes = call(
        functools.partial(windows_kernel, plan),
        [shape(2, count_steps(count) * members, members, kind=BF16),
         shape(2, (count - 1) * members, members, kind=BF16)],
        [VMEM, ANY], [VMEM] * 2,
        [pltpu.VMEM((count * members, members), F32)], 1.3, "windows",
    )(kept, message)
    totals = call(
        functools.partial(scan_kernel, plan),
        shape(count, members, members), [VMEM] * 3, VMEM, [], 1.2, "scan",
    )(gram, gram_core, steps)
    entering, carry = call(
        functools.partial(enter_kernel, levels - 1),
        [square] * 2, [VMEM] * 4 + [ANY], [VMEM] * 2, [], 0.3, "entering",
    )(later, carry, befores[-1], message_other, totals)
    carry_core = exchange(carry, "space", lanes, 1)
    size = plan.stack * members
    ens_factors, cot_factors, follow = call(
        functools.partial(carry_kernel, plan),
        [shape(len(plan.groups), size, size, kind=BF16)] * 2
        + [shape(2, count * members, members, kind=BF16)],
        [VMEM] * 2 + [ANY], [VMEM] * 3, [], 0.9, "carries",
    )(suffixes, entering, carry)
    def apply(factors, which, after, name):
        return call(
            functools.partial(apply_kernel, plan),
            [shape(count, members, cells, kind=BF16), shape(8, 128)],
            [VMEM] * (1 + PIECES) + [ANY], [HBM, VMEM],
            [pltpu.VMEM((count, members, cells), BF16),
             pltpu.SemaphoreType.DMA((2 * len(plan.groups),))],
            0.5, name,
        )(factors, *(part[which] for part in parts), after)

    carry = call(
        sum_kernel, square, [VMEM] * 2 + [ANY], VMEM, [], 0.1, "chip_carry",
    )(carry, carry_core, follow)
    carries = [carry] + around(carry)
    smoothed, done = apply(ens_factors, 0, carry, "smoothed")
    ensemble_grad, done = apply(cot_factors, 1, done, "ensemble_grad")
    transform_grad = call(
        functools.partial(final_kernel, plan, scale),
        shape(count, members, members),
        [VMEM] * 3 + [ANY] + [VMEM] * chips, HBM,
        [pltpu.VMEM((count, members, members), F32), pltpu.SemaphoreType.DMA((count,))],
        1.5, "transform_grad",
    )(totals, prefixes, follow, done, *carries)
    return (smoothed, ensemble_grad, transform_grad)


def solution(mesh):
    return jax.shard_map(
        shards,
        mesh=mesh,
        in_specs=(P("tm", None, "space"), P("tm", None, "space"), P("tm", None, None)),
        out_specs=(P("tm", None, "space"), P("tm", None, "space"), P("tm", None, None)),
        check_vma=False,
    )
```

```python
import functools
import math

import jax
import jax.numpy as jnp
from jax import lax
from jax.experimental import pallas as pl
from jax.experimental.pallas import tpu as pltpu
from jax.sharding import PartitionSpec as P

F32 = jnp.float32
BF16 = jnp.bfloat16
VMEM = pl.BlockSpec(memory_space=pltpu.VMEM)
HBM = pl.BlockSpec(memory_space=pltpu.HBM)
ANY = pl.BlockSpec(memory_space=pl.ANY)
DEPTH = 256
PIECES = 2
NORMAL = (((1,), (0,)), ((), ()))
ROWS = (((1,), (1,)), ((), ()))


def split(value):
    high = value.astype(BF16)
    return high, (value - high.astype(F32)).astype(BF16)


def mul(left, right, dims=NORMAL):
    return lax.dot_general(left, right, dims, preferred_element_type=F32)


def mul_pairs(left, right, dims=NORMAL):
    return mul(left[0], right[0], dims) + (
        mul(left[0], right[1], dims) + mul(left[1], right[0], dims)
    )


def mul_exact(left, right, dims=NORMAL):
    return mul_pairs(split(left), split(right), dims)


def product_of(factors):
    while len(factors) > 1:
        joined = [mul_exact(*factors[at : at + 2]) for at in range(0, len(factors) - 1, 2)]
        factors = joined + factors[len(joined) * 2 :]
    return factors[0]


def suffix_scan(ref, count, members, stop):
    width = 1
    while width < stop:
        for start in range(0, count, 2 * width):
            middle = start + width
            if middle < count:
                rows = slice(start * members, middle * members)
                ref[rows] = mul_exact(ref[rows], ref[middle * members : (middle + 1) * members])
        width *= 2


class Plan:
    def __init__(self, count, members):
        self.count, self.members = count, members
        self.stack = DEPTH // members
        self.groups = [
            (start, min(start + self.stack, count)) for start in range(0, count, self.stack)
        ]
        bounds = [0, len(self.groups) // 3, len(self.groups)]
        self.piece_groups = [self.groups[a:b] for a, b in zip(bounds, bounds[1:])]
        self.pieces = [(part[0][0], part[-1][1]) for part in self.piece_groups]
        self.first_group = bounds[:-1]
        self.widths = [-(-(stop - start) * members // 128) * 128 for start, stop in self.groups]
        self.width = sum(self.widths)

    def lanes(self, at):
        start = sum(self.widths[:at])
        return slice(start, start + self.widths[at])

    def rows(self, first, last):
        return slice(first * self.members, last * self.members)


def packing(members):
    spare = 128 - members
    strips = -(-members // spare)
    rest = members // (strips + 1) // 8 * 8
    return spare, strips, rest, members - rest


def pack(value):
    members = value.shape[0]
    spare, strips, rest, rows = packing(members)
    side = [value[rows:, at * spare : (at + 1) * spare] for at in range(strips)]
    side = [jnp.pad(part, ((0, 0), (0, spare - part.shape[1]))) for part in side]
    side.append(jnp.zeros((rows - strips * rest, spare), value.dtype))
    return jnp.concatenate([value[:rows], jnp.concatenate(side, axis=0)], axis=1)


def unpack(value, members):
    spare, strips, rest, rows = packing(members)
    side = [value[at * rest : (at + 1) * rest, members:] for at in range(strips)]
    last = jnp.concatenate(side, axis=1)[:, :members]
    return jnp.concatenate([value[:, :members], last], axis=0)


def on_blocks(members, size):
    rows = lax.broadcasted_iota(jnp.int32, (size, size), 0) // members
    columns = lax.broadcasted_iota(jnp.int32, (size, size), 1) // members
    return rows == columns


def loads(plan, piece, values, buffer, sems, which=slice(None)):
    base = plan.pieces[piece][0]
    copies = [
        pltpu.make_async_copy(values.at[start:stop], buffer.at[start - base : stop - base], sems.at[at])
        for at, (start, stop) in enumerate(plan.piece_groups[piece])
    ][which]
    for copy in copies:
        copy.start()
    return copies


def chain_kernel(
    plan, transforms, ensembles, cotangents, suffixes, total, kept, ens, cot, sem, ens_sem, cot_sem
):
    count, members = plan.count, plan.members
    read = pltpu.make_async_copy(transforms, kept, sem)
    read.start()
    more = loads(plan, 0, ensembles, ens, ens_sem, slice(1))
    more += loads(plan, 0, cotangents, cot, cot_sem, slice(1))
    read.wait()
    more += loads(plan, 0, ensembles, ens, ens_sem, slice(1, None))
    more += loads(plan, 0, cotangents, cot, cot_sem, slice(1, None))
    for at in range(count):
        suffixes[plan.rows(at, at + 1)] = kept[at]
    suffix_scan(suffixes, count, members, count)
    total[...] = suffixes[plan.rows(0, 1)]
    for copy in more:
        copy.wait()


def windows_kernel(plan, kept, _, steps, runs):
    count = plan.count
    for at in range(count - 1):
        runs[plan.rows(at + 1, at + 2)] = kept[at].T
    number = 0
    width = 1
    while width < count:
        for middle in range(width, count, 2 * width):
            size = min(width, count - middle)
            for side, part in enumerate(split(runs[plan.rows(middle, middle + size)])):
                steps[side, plan.rows(number, number + size)] = part
            number += size
        for start in range(2 * width, count, 2 * width):
            if start + width < count:
                rows = plan.rows(start + width, min(start + 2 * width, count))
                runs[rows] = mul_exact(runs[rows], runs[plan.rows(start + width - 1, start + width)])
        width *= 2


def count_steps(count):
    total = 0
    width = 1
    while width < count:
        total += sum(min(width, count - middle) for middle in range(width, count, 2 * width))
        width *= 2
    return total


def core_index():
    return lax.rem(lax.axis_index("space"), 2)


def gram_of(plan, piece, cot, ens, suffixes, whole, ready=lambda: None):
    members = plan.members
    base = plan.pieces[piece][0]
    offset = jnp.zeros((members, members), F32)
    for at, (start, stop) in enumerate(plan.piece_groups[piece]):
        ready()
        size = (stop - start) * members
        stacked = [ref[start - base : stop - base].reshape(size, ref.shape[2]) for ref in (cot, ens)]
        wide = jnp.where(on_blocks(members, size), mul(*stacked, ROWS), 0.0)
        gram = wide[:members]
        for i in range(1, stop - start):
            gram = gram + wide[i * members : (i + 1) * members]
        offset = offset + mul_exact(gram, suffixes[plan.rows(start, stop)])
        lanes = plan.lanes(plan.first_group[piece] + at)
        width = lanes.stop - lanes.start
        whole[:, lanes] = jnp.pad(gram, ((0, 0), (0, width - size)))
    return offset


def gram_kernel(
    plan, ensembles, cotangents, suffixes, ens, cot,
    kept, sent, offsets, next_ens, next_cot, whole, ens_sem, cot_sem,
):
    waiting = iter(list(zip(
        loads(plan, 1, ensembles, next_ens, ens_sem), loads(plan, 1, cotangents, next_cot, cot_sem)
    )))

    def ready():
        for copy in next(waiting):
            copy.wait()

    total = gram_of(plan, 0, cot, ens, suffixes, whole)
    offsets[...] = total + gram_of(plan, 1, next_cot, next_ens, suffixes, whole, ready)
    half = plan.members // 2
    core = lax.rem(lax.axis_index("space"), 2)
    kept[...] = whole[pl.ds(core * half, half)]
    sent[...] = whole[pl.ds((1 - core) * half, half)]


def upper_half(level):
    return lax.rem(lax.axis_index("tm") // (1 << level), 2) == 1


def join_kernel(level, last, total, other, later, before, _, new_total, new_later, new_before, upper_total):
    upper = upper_half(level)
    left = jnp.where(upper, other[...], total[...])
    right = jnp.where(upper, total[...], other[...])
    joined = mul_exact(left, right)
    new_total[...] = pack(joined) if last else joined
    upper_total[...] = right
    new_later[...] = jnp.where(upper, later[...], mul_exact(later[...], other[...]))
    new_before[...] = jnp.where(upper, mul_exact(other[...], before[...]), before[...])


def sum_kernel(left, right, _, total):
    total[...] = left[...] + right[...]


def pass_kernel(level, last, own, other, carry, upper_total, before, _, new_own, new_carry):
    upper = upper_half(level)
    left = jnp.where(upper, other[...], own[...])
    right = jnp.where(upper, own[...], other[...])
    passed = mul_exact(left, upper_total[...]) + right
    new_own[...] = pack(passed) if last else passed
    new_carry[...] = carry[...] + jnp.where(upper, mul_exact(left, before[...]), 0.0)


def last_pass_kernel(level, other, carry, before, _, __, new_carry, ___):
    added = mul_exact(unpack(other[...], before.shape[0]), before[...])
    new_carry[...] = carry[...] + jnp.where(upper_half(level), added, 0.0)


def enter_kernel(level, later, other, _, entering):
    joined = mul_exact(later[...], unpack(other[...], later.shape[0]))
    entering[...] = jnp.where(upper_half(level), later[...], joined)


def carry_kernel(plan, suffixes, later, _, ens_factors, cot_factors, follow):
    count, members = plan.count, plan.members
    entering = later[...]
    mask = on_blocks(members, plan.stack * members)
    repeated = split(jnp.concatenate([entering] * plan.stack, axis=1))
    for at, (start, stop) in enumerate(plan.groups):
        size = (stop - start) * members
        wide = mul_pairs(split(suffixes[plan.rows(start, stop)]), repeated)
        part = jnp.where(mask[:size, :size], wide[:, :size], 0.0)
        cot_factors[at, :size, :size] = part.astype(BF16)
        ens_factors[at, :size, :size] = part.T.astype(BF16)
        first = max(start - 1, 0)
        kept = wide[(first + 1 - start) * members :, :members]
        for side, value in enumerate(split(kept)):
            follow[side, plan.rows(first, stop - 1)] = value
    for side, value in enumerate(split(entering)):
        follow[side, plan.rows(count - 1, count)] = value


def apply_kernel(plan, factors, *refs):
    out, marker, out_buf, out_sem = refs[-4:]
    members = plan.members
    marker[...] = jnp.zeros_like(marker)
    chunk = out_buf.shape[2] // 2
    writes = []
    for piece, values in enumerate(refs[:PIECES]):
        first = plan.pieces[piece][0]
        for at, (start, stop) in enumerate(plan.piece_groups[piece]):
            size = (stop - start) * members
            for side in range(2):
                columns = slice(side * chunk, (side + 1) * chunk)
                stacked = values[start - first : stop - first, :, columns].reshape(size, chunk)
                result = mul(factors[plan.first_group[piece] + at, :size, :size], stacked)
                out_buf[start:stop, :, columns] = result.astype(BF16).reshape(
                    stop - start, members, chunk
                )
                copy = pltpu.make_async_copy(
                    out_buf.at[start:stop, :, columns],
                    out.at[start:stop, :, columns],
                    out_sem.at[len(writes)],
                )
                copy.start()
                writes.append(copy)
    for copy in writes:
        copy.wait()


def final_kernel(plan, scale, gram, gram_core, follow, steps, _, *refs):
    carries, (out, buffer, sems) = refs[:-3], refs[-3:]
    carry = carries[0][...]
    for ref in carries[1:]:
        carry = carry + ref[...]
    count, members = plan.count, plan.members
    totals = []
    first = lax.rem(lax.axis_index("space"), 2) == 0
    for at, (start, stop) in enumerate(plan.groups):
        mine, other = gram[:, plan.lanes(at)], gram_core[:, plan.lanes(at)]
        halves = [jnp.where(first, mine, other), jnp.where(first, other, mine)]
        tall = jnp.concatenate(halves, axis=0).T
        for i in range(stop - start):
            totals.append(tall[i * members : (i + 1) * members])
    totals[0] = totals[0] + carry.T
    number = 0
    width = 1
    while width < count:
        for start in range(width, count, 2 * width):
            size = min(width, count - start)
            rows = plan.rows(number, number + size)
            added = mul_pairs((steps[0, rows], steps[1, rows]), split(totals[start - 1]))
            for at in range(size):
                totals[start + at] = totals[start + at] + added[at * members : (at + 1) * members]
            number += size
        width *= 2
    copies = []
    for at in range(count):
        rows = plan.rows(at, at + 1)
        buffer[at] = mul_pairs(split(totals[at]), (follow[0, rows], follow[1, rows]), ROWS) * scale
        copy = pltpu.make_async_copy(buffer.at[at], out.at[at], sems.at[at])
        copy.start()
        copies.append(copy)
    for copy in copies:
        copy.wait()


def call(kernel, outs, ins, out_specs, scratch, micros, name, limit=16, aliases=None):
    return pl.pallas_call(
        kernel,
        out_shape=outs,
        in_specs=ins,
        out_specs=out_specs,
        scratch_shapes=scratch,
        input_output_aliases=aliases or {},
        compiler_params=pltpu.CompilerParams(vmem_limit_bytes=limit << 20),
        cost_estimate=pl.CostEstimate(
            flops=int(micros * 1e9), bytes_accessed=int(micros * 3e6), transcendentals=0
        ),
        name=name,
    )


def shape(*dims, kind=F32):
    return jax.ShapeDtypeStruct(dims, kind)


def shards(ensembles, cotangents, transforms):
    count, members, cells = ensembles.shape
    blocks, lanes = lax.axis_size("tm"), lax.axis_size("space")
    chips = lanes // 2
    scale = 1.0 / math.sqrt(cells * lanes * count * blocks)
    plan = Plan(count, members)
    levels = blocks.bit_length() - 1
    square = shape(members, members)
    ensembles, cotangents, transforms = (
        pltpu.with_memory_space_constraint(value, pltpu.HBM)
        for value in (ensembles, cotangents, transforms)
    )

    def exchange(value, axis, size, bit):
        return lax.ppermute(value, axis, [(at, at ^ bit) for at in range(size)])

    def around(value):
        return [
            lax.ppermute(value, "space", [(at, (at + 2 * d) % lanes) for at in range(lanes)])
            for d in range(1, chips)
        ]

    def piece_shape(piece):
        first, last = plan.pieces[piece]
        return shape(last - first, members, cells, kind=BF16)

    def piece_sems(piece):
        return [pltpu.SemaphoreType.DMA((len(plan.piece_groups[piece]),))] * 2

    suffixes, total, kept, *first_part = call(
        functools.partial(chain_kernel, plan),
        [shape(count * members, members), square, shape(count, members, members)] + [piece_shape(0)] * 2,
        [HBM] * 3, [VMEM] * 5, [pltpu.SemaphoreType.DMA] + piece_sems(0), 3.5, "transform_chain",
    )(transforms, ensembles, cotangents)

    wide = shape(members // 2, plan.width)
    later = before = jnp.eye(members, dtype=F32)
    uppers, befores = [], []

    packed = shape(packing(members)[3], 128)

    def join(level, total, other, later, before, after):
        befores.append(before)
        last = level == levels - 2
        total, later, before, upper = call(
            functools.partial(join_kernel, level, last),
            [packed if last else square] + [square] * 3, [VMEM] * 4 + [ANY], [VMEM] * 4,
            [], 3, f"join_{level}",
        )(total, other, later, before, after)
        uppers.append(upper)
        return total, later, before

    other = exchange(total, "tm", blocks, 1)
    gram, gram_sent, own, *second_part = call(
        functools.partial(gram_kernel, plan),
        [wide, wide, square] + [piece_shape(1)] * 2,
        [HBM] * 2 + [VMEM] * 3, [VMEM] * 5,
        [pltpu.VMEM((members, plan.width), F32)] + piece_sems(1), 4.5, "gram",
    )(ensembles, cotangents, suffixes, *first_part)
    parts = [first_part, second_part]
    other_own = exchange(own, "tm", blocks, 1)
    gram_core = exchange(gram_sent, "space", lanes, 1)
    total, later, before = join(0, total, other, later, before, own)
    other = exchange(total, "tm", blocks, 2)
    gram = call(sum_kernel, wide, [VMEM] * 2 + [ANY], VMEM, [], 0.1, "chip_gram")(gram, gram_core, total)
    grams = around(gram)

    def pass_on(level, carry, after):
        last = level == levels - 2
        return call(
            functools.partial(pass_kernel, level, last),
            [packed if last else square, square], [VMEM] * 5 + [ANY], [VMEM] * 2, [], 3, f"pass_{level}",
        )(own, other_own, carry, uppers[level], befores[level], after)

    carry = jnp.zeros((members, members), F32)
    after = gram
    for level in range(levels - 2):
        own, carry = pass_on(level, carry, after)
        other_own = exchange(own, "tm", blocks, 2 << level)
        total, later, before = join(level + 1, total, other, later, before, own)
        other = exchange(total, "tm", blocks, 4 << level)
        after = total
    befores.append(before)
    own, carry = pass_on(levels - 2, carry, total)
    other_own = exchange(own, "tm", blocks, blocks // 2)
    entering = call(
        functools.partial(enter_kernel, levels - 1),
        square, [VMEM] * 2 + [ANY], VMEM, [], 0.2, "entering",
    )(later, other, own)
    size = plan.stack * members
    ens_factors, cot_factors, follow = call(
        functools.partial(carry_kernel, plan),
        [shape(len(plan.groups), size, size, kind=BF16)] * 2
        + [shape(2, count * members, members, kind=BF16)],
        [VMEM] * 2 + [ANY], [VMEM] * 3, [], 0.9, "carries",
    )(suffixes, entering, own)
    def apply(factors, which, after, name):
        return call(
            functools.partial(apply_kernel, plan),
            [shape(count, members, cells, kind=BF16), shape(8, 128)],
            [VMEM] * (1 + PIECES) + [ANY], [HBM, VMEM],
            [pltpu.VMEM((count, members, cells), BF16),
             pltpu.SemaphoreType.DMA((2 * len(plan.groups),))],
            0.5, name,
        )(factors, *(part[which] for part in parts), after)

    smoothed, done = apply(ens_factors, 0, follow, "smoothed")
    carry, grams[0] = call(
        functools.partial(last_pass_kernel, levels - 1),
        [square, wide], [VMEM] * 3 + [ANY] * 2, [VMEM, ANY], [], 0.2, "pass_last", aliases={4: 1},
    )(other_own, carry, befores[-1], done, grams[0])
    carry_core = exchange(carry, "space", lanes, 1)
    for part in grams:
        gram = gram + part
    gram_core = exchange(gram, "space", lanes, 1)
    steps = call(
        functools.partial(windows_kernel, plan),
        shape(2, count_steps(count) * members, members, kind=BF16), [VMEM, ANY], VMEM,
        [pltpu.VMEM((count * members, members), F32)], 1.0, "windows",
    )(kept, carry)
    carry = call(
        sum_kernel, square, [VMEM] * 2 + [ANY], VMEM, [], 0.1, "chip_carry",
    )(carry, carry_core, steps)
    carries = [carry] + around(carry)
    ensemble_grad, done = apply(cot_factors, 1, carry, "ensemble_grad")
    transform_grad = call(
        functools.partial(final_kernel, plan, scale),
        shape(count, members, members),
        [VMEM] * 4 + [ANY] + [VMEM] * chips, HBM,
        [pltpu.VMEM((count, members, members), F32), pltpu.SemaphoreType.DMA((count,))],
        2.5, "transform_grad",
    )(gram, gram_core, follow, steps, done, *carries)
    return (smoothed, ensemble_grad, transform_grad)


def solution(mesh):
    return jax.shard_map(
        shards,
        mesh=mesh,
        in_specs=(P("tm", None, "space"), P("tm", None, "space"), P("tm", None, None)),
        out_specs=(P("tm", None, "space"), P("tm", None, "space"), P("tm", None, None)),
        check_vma=False,
    )
```

```python
import functools
import math

import jax
import jax.numpy as jnp
from jax import lax
from jax.experimental import pallas as pl
from jax.experimental.pallas import tpu as pltpu
from jax.sharding import PartitionSpec as P

F32 = jnp.float32
BF16 = jnp.bfloat16
VMEM = pl.BlockSpec(memory_space=pltpu.VMEM)
HBM = pl.BlockSpec(memory_space=pltpu.HBM)
ANY = pl.BlockSpec(memory_space=pl.ANY)
DEPTH = 256
PIECES = 2
NORMAL = (((1,), (0,)), ((), ()))
ROWS = (((1,), (1,)), ((), ()))


def split(value):
    high = value.astype(BF16)
    return high, (value - high.astype(F32)).astype(BF16)


def mul(left, right, dims=NORMAL):
    return lax.dot_general(left, right, dims, preferred_element_type=F32)


def mul_pairs(left, right, dims=NORMAL):
    rows = left[0].shape[0]
    both = mul(jnp.concatenate(left, axis=0), right[0], dims)
    return both[:rows] + (both[rows:] + mul(left[0], right[1], dims))


def mul_exact(left, right, dims=NORMAL):
    return mul_pairs(split(left), split(right), dims)


def product_of(factors):
    while len(factors) > 1:
        joined = [mul_exact(*factors[at : at + 2]) for at in range(0, len(factors) - 1, 2)]
        factors = joined + factors[len(joined) * 2 :]
    return factors[0]


def suffix_scan(ref, count, members, stop):
    width = 1
    while width < stop:
        for start in range(0, count, 2 * width):
            middle = start + width
            if middle < count:
                rows = slice(start * members, middle * members)
                ref[rows] = mul_exact(ref[rows], ref[middle * members : (middle + 1) * members])
        width *= 2


class Plan:
    def __init__(self, count, members):
        self.count, self.members = count, members
        self.stack = DEPTH // members
        self.groups = [
            (start, min(start + self.stack, count)) for start in range(0, count, self.stack)
        ]
        bounds = [0, len(self.groups) // 3, len(self.groups)]
        self.piece_groups = [self.groups[a:b] for a, b in zip(bounds, bounds[1:])]
        self.pieces = [(part[0][0], part[-1][1]) for part in self.piece_groups]
        self.first_group = bounds[:-1]
        self.widths = [-(-(stop - start) * members // 128) * 128 for start, stop in self.groups]
        self.width = sum(self.widths)

    def lanes(self, at):
        start = sum(self.widths[:at])
        return slice(start, start + self.widths[at])

    def rows(self, first, last):
        return slice(first * self.members, last * self.members)


def packing(members):
    spare = 128 - members
    strips = -(-members // spare)
    rest = members // (strips + 1) // 8 * 8
    return spare, strips, rest, members - rest


def pack(value):
    members = value.shape[0]
    spare, strips, rest, rows = packing(members)
    side = [value[rows:, at * spare : (at + 1) * spare] for at in range(strips)]
    side = [jnp.pad(part, ((0, 0), (0, spare - part.shape[1]))) for part in side]
    side.append(jnp.zeros((rows - strips * rest, spare), value.dtype))
    return jnp.concatenate([value[:rows], jnp.concatenate(side, axis=0)], axis=1)


def unpack(value, members):
    spare, strips, rest, rows = packing(members)
    side = [value[at * rest : (at + 1) * rest, members:] for at in range(strips)]
    last = jnp.concatenate(side, axis=1)[:, :members]
    return jnp.concatenate([value[:, :members], last], axis=0)


def on_blocks(members, size):
    rows = lax.broadcasted_iota(jnp.int32, (size, size), 0) // members
    columns = lax.broadcasted_iota(jnp.int32, (size, size), 1) // members
    return rows == columns


def loads(plan, piece, values, buffer, sems, which=slice(None)):
    base = plan.pieces[piece][0]
    copies = [
        pltpu.make_async_copy(values.at[start:stop], buffer.at[start - base : stop - base], sems.at[at])
        for at, (start, stop) in enumerate(plan.piece_groups[piece])
    ][which]
    for copy in copies:
        copy.start()
    return copies


def chain_kernel(
    plan, transforms, ensembles, cotangents, suffixes, total, kept, ens, cot, sem, ens_sem, cot_sem
):
    count, members = plan.count, plan.members
    read = pltpu.make_async_copy(transforms, kept, sem)
    read.start()
    more = loads(plan, 0, ensembles, ens, ens_sem, slice(1))
    more += loads(plan, 0, cotangents, cot, cot_sem, slice(1))
    read.wait()
    more += loads(plan, 0, ensembles, ens, ens_sem, slice(1, None))
    more += loads(plan, 0, cotangents, cot, cot_sem, slice(1, None))
    for at in range(count):
        suffixes[plan.rows(at, at + 1)] = kept[at]
    suffix_scan(suffixes, count, members, count)
    total[...] = suffixes[plan.rows(0, 1)]
    for copy in more:
        copy.wait()


def windows_kernel(plan, kept, _, steps, runs):
    count = plan.count
    for at in range(count - 1):
        runs[plan.rows(at + 1, at + 2)] = kept[at].T
    number = 0
    width = 1
    while width < count:
        for middle in range(width, count, 2 * width):
            size = min(width, count - middle)
            for side, part in enumerate(split(runs[plan.rows(middle, middle + size)])):
                steps[side, plan.rows(number, number + size)] = part
            number += size
        for start in range(2 * width, count, 2 * width):
            if start + width < count:
                rows = plan.rows(start + width, min(start + 2 * width, count))
                runs[rows] = mul_exact(runs[rows], runs[plan.rows(start + width - 1, start + width)])
        width *= 2


def count_steps(count):
    total = 0
    width = 1
    while width < count:
        total += sum(min(width, count - middle) for middle in range(width, count, 2 * width))
        width *= 2
    return total


def core_index():
    return lax.rem(lax.axis_index("space"), 2)


def gram_of(plan, piece, cot, ens, suffixes, whole, ready=lambda: None):
    members = plan.members
    base = plan.pieces[piece][0]
    offset = jnp.zeros((members, members), F32)
    for at, (start, stop) in enumerate(plan.piece_groups[piece]):
        ready()
        size = (stop - start) * members
        stacked = [ref[start - base : stop - base].reshape(size, ref.shape[2]) for ref in (cot, ens)]
        wide = jnp.where(on_blocks(members, size), mul(*stacked, ROWS), 0.0)
        gram = wide[:members]
        for i in range(1, stop - start):
            gram = gram + wide[i * members : (i + 1) * members]
        offset = offset + mul_exact(gram, suffixes[plan.rows(start, stop)])
        lanes = plan.lanes(plan.first_group[piece] + at)
        width = lanes.stop - lanes.start
        whole[:, lanes] = jnp.pad(gram, ((0, 0), (0, width - size)))
    return offset


def gram_kernel(
    plan, ensembles, cotangents, suffixes, ens, cot,
    kept, sent, offsets, next_ens, next_cot, whole, ens_sem, cot_sem,
):
    waiting = iter(list(zip(
        loads(plan, 1, ensembles, next_ens, ens_sem), loads(plan, 1, cotangents, next_cot, cot_sem)
    )))

    def ready():
        for copy in next(waiting):
            copy.wait()

    total = gram_of(plan, 0, cot, ens, suffixes, whole)
    offsets[...] = total + gram_of(plan, 1, next_cot, next_ens, suffixes, whole, ready)
    half = plan.members // 2
    core = lax.rem(lax.axis_index("space"), 2)
    kept[...] = whole[pl.ds(core * half, half)]
    sent[...] = whole[pl.ds((1 - core) * half, half)]


def upper_half(level):
    return lax.rem(lax.axis_index("tm") // (1 << level), 2) == 1


def join_kernel(level, last, total, other, later, before, _, new_total, new_later, new_before, upper_total):
    upper = upper_half(level)
    left = jnp.where(upper, other[...], total[...])
    right = jnp.where(upper, total[...], other[...])
    joined = mul_exact(left, right)
    new_total[...] = pack(joined) if last else joined
    upper_total[...] = right
    new_later[...] = jnp.where(upper, later[...], mul_exact(later[...], other[...]))
    new_before[...] = jnp.where(upper, mul_exact(other[...], before[...]), before[...])


def sum_kernel(left, right, _, total):
    total[...] = left[...] + right[...]


def pass_kernel(level, last, own, other, carry, upper_total, before, _, new_own, new_carry):
    upper = upper_half(level)
    left = jnp.where(upper, other[...], own[...])
    right = jnp.where(upper, own[...], other[...])
    passed = mul_exact(left, upper_total[...]) + right
    new_own[...] = pack(passed) if last else passed
    new_carry[...] = carry[...] + jnp.where(upper, mul_exact(left, before[...]), 0.0)


def last_pass_kernel(level, other, carry, before, _, __, new_carry, ___):
    added = mul_exact(unpack(other[...], before.shape[0]), before[...])
    new_carry[...] = carry[...] + jnp.where(upper_half(level), added, 0.0)


def enter_kernel(level, later, other, _, entering):
    joined = mul_exact(later[...], unpack(other[...], later.shape[0]))
    entering[...] = jnp.where(upper_half(level), later[...], joined)


def carry_kernel(plan, suffixes, later, _, ens_factors, cot_factors, follow):
    count, members = plan.count, plan.members
    entering = later[...]
    mask = on_blocks(members, plan.stack * members)
    repeated = split(jnp.concatenate([entering] * plan.stack, axis=1))
    for at, (start, stop) in enumerate(plan.groups):
        size = (stop - start) * members
        wide = mul_pairs(split(suffixes[plan.rows(start, stop)]), repeated)
        part = jnp.where(mask[:size, :size], wide[:, :size], 0.0)
        cot_factors[at, :size, :size] = part.astype(BF16)
        ens_factors[at, :size, :size] = part.T.astype(BF16)
        first = max(start - 1, 0)
        kept = wide[(first + 1 - start) * members :, :members]
        for side, value in enumerate(split(kept)):
            follow[side, plan.rows(first, stop - 1)] = value
    for side, value in enumerate(split(entering)):
        follow[side, plan.rows(count - 1, count)] = value


def apply_kernel(plan, factors, *refs):
    out, marker, out_buf, out_sem = refs[-4:]
    members = plan.members
    marker[...] = jnp.zeros_like(marker)
    chunk = out_buf.shape[2] // 2
    writes = []
    for piece, values in enumerate(refs[:PIECES]):
        first = plan.pieces[piece][0]
        for at, (start, stop) in enumerate(plan.piece_groups[piece]):
            size = (stop - start) * members
            for side in range(2):
                columns = slice(side * chunk, (side + 1) * chunk)
                stacked = values[start - first : stop - first, :, columns].reshape(size, chunk)
                result = mul(factors[plan.first_group[piece] + at, :size, :size], stacked)
                out_buf[start:stop, :, columns] = result.astype(BF16).reshape(
                    stop - start, members, chunk
                )
                copy = pltpu.make_async_copy(
                    out_buf.at[start:stop, :, columns],
                    out.at[start:stop, :, columns],
                    out_sem.at[len(writes)],
                )
                copy.start()
                writes.append(copy)
    for copy in writes:
        copy.wait()


def final_kernel(plan, scale, gram, gram_core, follow, steps, _, *refs):
    carries, (out, buffer, sems) = refs[:-3], refs[-3:]
    carry = carries[0][...]
    for ref in carries[1:]:
        carry = carry + ref[...]
    count, members = plan.count, plan.members
    totals = []
    first = lax.rem(lax.axis_index("space"), 2) == 0
    for at, (start, stop) in enumerate(plan.groups):
        mine, other = gram[:, plan.lanes(at)], gram_core[:, plan.lanes(at)]
        halves = [jnp.where(first, mine, other), jnp.where(first, other, mine)]
        tall = jnp.concatenate(halves, axis=0).T
        for i in range(stop - start):
            totals.append(tall[i * members : (i + 1) * members])
    totals[0] = totals[0] + carry.T
    number = 0
    width = 1
    while width < count:
        for start in range(width, count, 2 * width):
            size = min(width, count - start)
            rows = plan.rows(number, number + size)
            added = mul_pairs((steps[0, rows], steps[1, rows]), split(totals[start - 1]))
            for at in range(size):
                totals[start + at] = totals[start + at] + added[at * members : (at + 1) * members]
            number += size
        width *= 2
    copies = []
    for at in range(count):
        rows = plan.rows(at, at + 1)
        buffer[at] = mul_pairs(split(totals[at]), (follow[0, rows], follow[1, rows]), ROWS) * scale
        copy = pltpu.make_async_copy(buffer.at[at], out.at[at], sems.at[at])
        copy.start()
        copies.append(copy)
    for copy in copies:
        copy.wait()


def call(kernel, outs, ins, out_specs, scratch, micros, name, limit=16, aliases=None):
    return pl.pallas_call(
        kernel,
        out_shape=outs,
        in_specs=ins,
        out_specs=out_specs,
        scratch_shapes=scratch,
        input_output_aliases=aliases or {},
        compiler_params=pltpu.CompilerParams(vmem_limit_bytes=limit << 20),
        cost_estimate=pl.CostEstimate(
            flops=int(micros * 1e9), bytes_accessed=int(micros * 3e6), transcendentals=0
        ),
        name=name,
    )


def shape(*dims, kind=F32):
    return jax.ShapeDtypeStruct(dims, kind)


def shards(ensembles, cotangents, transforms):
    count, members, cells = ensembles.shape
    blocks, lanes = lax.axis_size("tm"), lax.axis_size("space")
    chips = lanes // 2
    scale = 1.0 / math.sqrt(cells * lanes * count * blocks)
    plan = Plan(count, members)
    levels = blocks.bit_length() - 1
    square = shape(members, members)
    ensembles, cotangents, transforms = (
        pltpu.with_memory_space_constraint(value, pltpu.HBM)
        for value in (ensembles, cotangents, transforms)
    )

    def exchange(value, axis, size, bit):
        return lax.ppermute(value, axis, [(at, at ^ bit) for at in range(size)])

    def around(value):
        return [
            lax.ppermute(value, "space", [(at, (at + 2 * d) % lanes) for at in range(lanes)])
            for d in range(1, chips)
        ]

    def piece_shape(piece):
        first, last = plan.pieces[piece]
        return shape(last - first, members, cells, kind=BF16)

    def piece_sems(piece):
        return [pltpu.SemaphoreType.DMA((len(plan.piece_groups[piece]),))] * 2

    suffixes, total, kept, *first_part = call(
        functools.partial(chain_kernel, plan),
        [shape(count * members, members), square, shape(count, members, members)] + [piece_shape(0)] * 2,
        [HBM] * 3, [VMEM] * 5, [pltpu.SemaphoreType.DMA] + piece_sems(0), 3.5, "transform_chain",
    )(transforms, ensembles, cotangents)

    wide = shape(members // 2, plan.width)
    later = before = jnp.eye(members, dtype=F32)
    uppers, befores = [], []

    packed = shape(packing(members)[3], 128)

    def join(level, total, other, later, before, after):
        befores.append(before)
        last = level == levels - 2
        total, later, before, upper = call(
            functools.partial(join_kernel, level, last),
            [packed if last else square] + [square] * 3, [VMEM] * 4 + [ANY], [VMEM] * 4,
            [], 3, f"join_{level}",
        )(total, other, later, before, after)
        uppers.append(upper)
        return total, later, before

    other = exchange(total, "tm", blocks, 1)
    gram, gram_sent, own, *second_part = call(
        functools.partial(gram_kernel, plan),
        [wide, wide, square] + [piece_shape(1)] * 2,
        [HBM] * 2 + [VMEM] * 3, [VMEM] * 5,
        [pltpu.VMEM((members, plan.width), F32)] + piece_sems(1), 4.5, "gram",
    )(ensembles, cotangents, suffixes, *first_part)
    parts = [first_part, second_part]
    other_own = exchange(own, "tm", blocks, 1)
    gram_core = exchange(gram_sent, "space", lanes, 1)
    total, later, before = join(0, total, other, later, before, own)
    other = exchange(total, "tm", blocks, 2)
    gram = call(sum_kernel, wide, [VMEM] * 2 + [ANY], VMEM, [], 0.1, "chip_gram")(gram, gram_core, total)
    grams = around(gram)

    def pass_on(level, carry, after):
        last = level == levels - 2
        return call(
            functools.partial(pass_kernel, level, last),
            [packed if last else square, square], [VMEM] * 5 + [ANY], [VMEM] * 2, [], 3, f"pass_{level}",
        )(own, other_own, carry, uppers[level], befores[level], after)

    carry = jnp.zeros((members, members), F32)
    after = gram
    for level in range(levels - 2):
        own, carry = pass_on(level, carry, after)
        other_own = exchange(own, "tm", blocks, 2 << level)
        total, later, before = join(level + 1, total, other, later, before, own)
        other = exchange(total, "tm", blocks, 4 << level)
        after = total
    befores.append(before)
    own, carry = pass_on(levels - 2, carry, total)
    other_own = exchange(own, "tm", blocks, blocks // 2)
    entering = call(
        functools.partial(enter_kernel, levels - 1),
        square, [VMEM] * 2 + [ANY], VMEM, [], 0.2, "entering",
    )(later, other, own)
    size = plan.stack * members
    ens_factors, cot_factors, follow = call(
        functools.partial(carry_kernel, plan),
        [shape(len(plan.groups), size, size, kind=BF16)] * 2
        + [shape(2, count * members, members, kind=BF16)],
        [VMEM] * 2 + [ANY], [VMEM] * 3, [], 0.9, "carries",
    )(suffixes, entering, own)
    def apply(factors, which, after, name):
        return call(
            functools.partial(apply_kernel, plan),
            [shape(count, members, cells, kind=BF16), shape(8, 128)],
            [VMEM] * (1 + PIECES) + [ANY], [HBM, VMEM],
            [pltpu.VMEM((count, members, cells), BF16),
             pltpu.SemaphoreType.DMA((2 * len(plan.groups),))],
            0.5, name,
        )(factors, *(part[which] for part in parts), after)

    smoothed, done = apply(ens_factors, 0, follow, "smoothed")
    carry, grams[0] = call(
        functools.partial(last_pass_kernel, levels - 1),
        [square, wide], [VMEM] * 3 + [ANY] * 2, [VMEM, ANY], [], 0.2, "pass_last", aliases={4: 1},
    )(other_own, carry, befores[-1], done, grams[0])
    carry_core = exchange(carry, "space", lanes, 1)
    for part in grams:
        gram = gram + part
    gram_core = exchange(gram, "space", lanes, 1)
    steps = call(
        functools.partial(windows_kernel, plan),
        shape(2, count_steps(count) * members, members, kind=BF16), [VMEM, ANY], VMEM,
        [pltpu.VMEM((count * members, members), F32)], 1.0, "windows",
    )(kept, carry)
    carry = call(
        sum_kernel, square, [VMEM] * 2 + [ANY], VMEM, [], 0.1, "chip_carry",
    )(carry, carry_core, steps)
    carries = [carry] + around(carry)
    ensemble_grad, done = apply(cot_factors, 1, carry, "ensemble_grad")
    transform_grad = call(
        functools.partial(final_kernel, plan, scale),
        shape(count, members, members),
        [VMEM] * 4 + [ANY] + [VMEM] * chips, HBM,
        [pltpu.VMEM((count, members, members), F32), pltpu.SemaphoreType.DMA((count,))],
        2.5, "transform_grad",
    )(gram, gram_core, follow, steps, done, *carries)
    return (smoothed, ensemble_grad, transform_grad)


def solution(mesh):
    return jax.shard_map(
        shards,
        mesh=mesh,
        in_specs=(P("tm", None, "space"), P("tm", None, "space"), P("tm", None, None)),
        out_specs=(P("tm", None, "space"), P("tm", None, "space"), P("tm", None, None)),
        check_vma=False,
    )
```

```python
import functools
import math

import jax
import jax.numpy as jnp
from jax import lax
from jax.experimental import pallas as pl
from jax.experimental.pallas import tpu as pltpu
from jax.sharding import PartitionSpec as P

F32 = jnp.float32
BF16 = jnp.bfloat16
VMEM = pl.BlockSpec(memory_space=pltpu.VMEM)
HBM = pl.BlockSpec(memory_space=pltpu.HBM)
ANY = pl.BlockSpec(memory_space=pl.ANY)
DEPTH = 256
PIECES = 2
NORMAL = (((1,), (0,)), ((), ()))
ROWS = (((1,), (1,)), ((), ()))


def split(value):
    high = value.astype(BF16)
    return high, (value - high.astype(F32)).astype(BF16)


def mul(left, right, dims=NORMAL):
    return lax.dot_general(left, right, dims, preferred_element_type=F32)


def mul_pairs(left, right, dims=NORMAL):
    return mul(left[0], right[0], dims) + (
        mul(left[0], right[1], dims) + mul(left[1], right[0], dims)
    )


def mul_exact(left, right, dims=NORMAL):
    return mul_pairs(split(left), split(right), dims)


def mul_stacked(left, right, dims=NORMAL):
    rows = left[0].shape[0]
    both = mul(jnp.concatenate(left, axis=0), right[0], dims)
    return both[:rows] + (both[rows:] + mul(left[0], right[1], dims))


def mul_small(left, right):
    return mul_stacked(split(left), split(right))


def product_of(factors):
    while len(factors) > 1:
        joined = [mul_exact(*factors[at : at + 2]) for at in range(0, len(factors) - 1, 2)]
        factors = joined + factors[len(joined) * 2 :]
    return factors[0]


def suffix_scan(ref, count, members, stop):
    width = 1
    while width < stop:
        for start in range(0, count, 2 * width):
            middle = start + width
            if middle < count:
                rows = slice(start * members, middle * members)
                ref[rows] = mul_exact(ref[rows], ref[middle * members : (middle + 1) * members])
        width *= 2


class Plan:
    def __init__(self, count, members):
        self.count, self.members = count, members
        self.stack = DEPTH // members
        self.groups = [
            (start, min(start + self.stack, count)) for start in range(0, count, self.stack)
        ]
        bounds = [0, len(self.groups) // 3, len(self.groups)]
        self.piece_groups = [self.groups[a:b] for a, b in zip(bounds, bounds[1:])]
        self.pieces = [(part[0][0], part[-1][1]) for part in self.piece_groups]
        self.first_group = bounds[:-1]
        self.widths = [-(-(stop - start) * members // 128) * 128 for start, stop in self.groups]
        self.width = sum(self.widths)

    def lanes(self, at):
        start = sum(self.widths[:at])
        return slice(start, start + self.widths[at])

    def rows(self, first, last):
        return slice(first * self.members, last * self.members)


def packing(members):
    spare = 128 - members
    strips = -(-members // spare)
    rest = members // (strips + 1) // 8 * 8
    return spare, strips, rest, members - rest


def pack(value):
    members = value.shape[0]
    spare, strips, rest, rows = packing(members)
    side = [value[rows:, at * spare : (at + 1) * spare] for at in range(strips)]
    side = [jnp.pad(part, ((0, 0), (0, spare - part.shape[1]))) for part in side]
    side.append(jnp.zeros((rows - strips * rest, spare), value.dtype))
    return jnp.concatenate([value[:rows], jnp.concatenate(side, axis=0)], axis=1)


def unpack(value, members):
    spare, strips, rest, rows = packing(members)
    side = [value[at * rest : (at + 1) * rest, members:] for at in range(strips)]
    last = jnp.concatenate(side, axis=1)[:, :members]
    return jnp.concatenate([value[:, :members], last], axis=0)


def on_blocks(members, size):
    rows = lax.broadcasted_iota(jnp.int32, (size, size), 0) // members
    columns = lax.broadcasted_iota(jnp.int32, (size, size), 1) // members
    return rows == columns


def loads(plan, piece, values, buffer, sems, which=slice(None)):
    base = plan.pieces[piece][0]
    copies = [
        pltpu.make_async_copy(values.at[start:stop], buffer.at[start - base : stop - base], sems.at[at])
        for at, (start, stop) in enumerate(plan.piece_groups[piece])
    ][which]
    for copy in copies:
        copy.start()
    return copies


def chain_kernel(
    plan, transforms, ensembles, cotangents, suffixes, total, kept, ens, cot, sem, ens_sem, cot_sem
):
    count, members = plan.count, plan.members
    read = pltpu.make_async_copy(transforms, kept, sem)
    read.start()
    more = loads(plan, 0, ensembles, ens, ens_sem, slice(1))
    more += loads(plan, 0, cotangents, cot, cot_sem, slice(1))
    read.wait()
    more += loads(plan, 0, ensembles, ens, ens_sem, slice(1, None))
    more += loads(plan, 0, cotangents, cot, cot_sem, slice(1, None))
    for at in range(count):
        suffixes[plan.rows(at, at + 1)] = kept[at]
    suffix_scan(suffixes, count, members, count // 2)
    middle = suffixes[plan.rows(count // 2, count // 2 + 1)]
    total[...] = mul_exact(suffixes[plan.rows(0, 1)], middle)
    for copy in more:
        copy.wait()


def windows_kernel(plan, kept, _, steps, runs):
    count = plan.count
    for at in range(count - 1):
        runs[plan.rows(at + 1, at + 2)] = kept[at].T
    number = 0
    width = 1
    while width < count:
        for middle in range(width, count, 2 * width):
            size = min(width, count - middle)
            for side, part in enumerate(split(runs[plan.rows(middle, middle + size)])):
                steps[side, plan.rows(number, number + size)] = part
            number += size
        for start in range(2 * width, count, 2 * width):
            if start + width < count:
                rows = plan.rows(start + width, min(start + 2 * width, count))
                runs[rows] = mul_small(runs[rows], runs[plan.rows(start + width - 1, start + width)])
        width *= 2


def count_steps(count):
    total = 0
    width = 1
    while width < count:
        total += sum(min(width, count - middle) for middle in range(width, count, 2 * width))
        width *= 2
    return total


def core_index():
    return lax.rem(lax.axis_index("space"), 2)


def gram_of(plan, piece, cot, ens, suffixes, whole, ready=lambda: None):
    members = plan.members
    base = plan.pieces[piece][0]
    offset = jnp.zeros((members, members), F32)
    for at, (start, stop) in enumerate(plan.piece_groups[piece]):
        ready()
        size = (stop - start) * members
        stacked = [ref[start - base : stop - base].reshape(size, ref.shape[2]) for ref in (cot, ens)]
        wide = jnp.where(on_blocks(members, size), mul(*stacked, ROWS), 0.0)
        gram = wide[:members]
        for i in range(1, stop - start):
            gram = gram + wide[i * members : (i + 1) * members]
        offset = offset + mul_exact(gram, suffixes[plan.rows(start, stop)])
        lanes = plan.lanes(plan.first_group[piece] + at)
        width = lanes.stop - lanes.start
        whole[:, lanes] = jnp.pad(gram, ((0, 0), (0, width - size)))
    return offset


def gram_kernel(
    plan, ensembles, cotangents, halves, ens, cot,
    kept, sent, offsets, suffixes, next_ens, next_cot, whole, ens_sem, cot_sem,
):
    waiting = iter(list(zip(
        loads(plan, 1, ensembles, next_ens, ens_sem), loads(plan, 1, cotangents, next_cot, cot_sem)
    )))

    def ready():
        for copy in next(waiting):
            copy.wait()

    count, middle = plan.count, plan.count // 2
    first, last = plan.rows(0, middle), plan.rows(middle, count)
    suffixes[first] = mul_exact(halves[first], halves[plan.rows(middle, middle + 1)])
    suffixes[last] = halves[last]
    total = gram_of(plan, 0, cot, ens, suffixes, whole)
    offsets[...] = total + gram_of(plan, 1, next_cot, next_ens, suffixes, whole, ready)
    half = plan.members // 2
    core = lax.rem(lax.axis_index("space"), 2)
    kept[...] = whole[pl.ds(core * half, half)]
    sent[...] = whole[pl.ds((1 - core) * half, half)]


def upper_half(level):
    return lax.rem(lax.axis_index("tm") // (1 << level), 2) == 1


def join_kernel(level, last, total, other, later, before, _, new_total, new_later, new_before, upper_total):
    upper = upper_half(level)
    left = jnp.where(upper, other[...], total[...])
    right = jnp.where(upper, total[...], other[...])
    joined = mul_small(left, right)
    new_total[...] = pack(joined) if last else joined
    upper_total[...] = right
    new_later[...] = jnp.where(upper, later[...], mul_small(later[...], other[...]))
    new_before[...] = jnp.where(upper, mul_small(other[...], before[...]), before[...])


def sum_kernel(left, right, _, total):
    total[...] = left[...] + right[...]


def pass_kernel(level, last, own, other, carry, upper_total, before, _, new_own, new_carry):
    upper = upper_half(level)
    left = jnp.where(upper, other[...], own[...])
    right = jnp.where(upper, own[...], other[...])
    passed = mul_small(left, upper_total[...]) + right
    new_own[...] = pack(passed) if last else passed
    new_carry[...] = carry[...] + jnp.where(upper, mul_small(left, before[...]), 0.0)


def last_pass_kernel(level, other, carry, before, _, __, new_carry, ___):
    added = mul_small(unpack(other[...], before.shape[0]), before[...])
    new_carry[...] = carry[...] + jnp.where(upper_half(level), added, 0.0)


def enter_kernel(level, later, other, _, entering):
    joined = mul_small(later[...], unpack(other[...], later.shape[0]))
    entering[...] = jnp.where(upper_half(level), later[...], joined)


def carry_kernel(plan, suffixes, later, _, ens_factors, cot_factors, follow):
    count, members = plan.count, plan.members
    entering = later[...]
    mask = on_blocks(members, plan.stack * members)
    repeated = split(jnp.concatenate([entering] * plan.stack, axis=1))
    for at, (start, stop) in enumerate(plan.groups):
        size = (stop - start) * members
        wide = mul_pairs(split(suffixes[plan.rows(start, stop)]), repeated)
        part = jnp.where(mask[:size, :size], wide[:, :size], 0.0)
        cot_factors[at, :size, :size] = part.astype(BF16)
        ens_factors[at, :size, :size] = part.T.astype(BF16)
        first = max(start - 1, 0)
        kept = wide[(first + 1 - start) * members :, :members]
        for side, value in enumerate(split(kept)):
            follow[side, plan.rows(first, stop - 1)] = value
    for side, value in enumerate(split(entering)):
        follow[side, plan.rows(count - 1, count)] = value


def apply_kernel(plan, factors, *refs):
    out, marker, out_buf, out_sem = refs[-4:]
    members = plan.members
    marker[...] = jnp.zeros_like(marker)
    chunk = out_buf.shape[2] // 2
    writes = []
    for piece, values in enumerate(refs[:PIECES]):
        first = plan.pieces[piece][0]
        for at, (start, stop) in enumerate(plan.piece_groups[piece]):
            size = (stop - start) * members
            for side in range(2):
                columns = slice(side * chunk, (side + 1) * chunk)
                stacked = values[start - first : stop - first, :, columns].reshape(size, chunk)
                result = mul(factors[plan.first_group[piece] + at, :size, :size], stacked)
                out_buf[start:stop, :, columns] = result.astype(BF16).reshape(
                    stop - start, members, chunk
                )
                copy = pltpu.make_async_copy(
                    out_buf.at[start:stop, :, columns],
                    out.at[start:stop, :, columns],
                    out_sem.at[len(writes)],
                )
                copy.start()
                writes.append(copy)
    for copy in writes:
        copy.wait()


def final_kernel(plan, scale, gram, gram_core, follow, steps, _, *refs):
    carries, (out, buffer, sems) = refs[:-3], refs[-3:]
    carry = carries[0][...]
    for ref in carries[1:]:
        carry = carry + ref[...]
    count, members = plan.count, plan.members
    totals = []
    first = lax.rem(lax.axis_index("space"), 2) == 0
    for at, (start, stop) in enumerate(plan.groups):
        mine, other = gram[:, plan.lanes(at)], gram_core[:, plan.lanes(at)]
        halves = [jnp.where(first, mine, other), jnp.where(first, other, mine)]
        tall = jnp.concatenate(halves, axis=0).T
        for i in range(stop - start):
            totals.append(tall[i * members : (i + 1) * members])
    totals[0] = totals[0] + carry.T
    number = 0
    width = 1
    while width < count:
        for start in range(width, count, 2 * width):
            size = min(width, count - start)
            rows = plan.rows(number, number + size)
            added = mul_stacked((steps[0, rows], steps[1, rows]), split(totals[start - 1]))
            for at in range(size):
                totals[start + at] = totals[start + at] + added[at * members : (at + 1) * members]
            number += size
        width *= 2
    copies = []
    for at in range(count):
        rows = plan.rows(at, at + 1)
        buffer[at] = mul_stacked(split(totals[at]), (follow[0, rows], follow[1, rows]), ROWS) * scale
        copy = pltpu.make_async_copy(buffer.at[at], out.at[at], sems.at[at])
        copy.start()
        copies.append(copy)
    for copy in copies:
        copy.wait()


def call(kernel, outs, ins, out_specs, scratch, micros, name, limit=16, aliases=None):
    return pl.pallas_call(
        kernel,
        out_shape=outs,
        in_specs=ins,
        out_specs=out_specs,
        scratch_shapes=scratch,
        input_output_aliases=aliases or {},
        compiler_params=pltpu.CompilerParams(vmem_limit_bytes=limit << 20),
        cost_estimate=pl.CostEstimate(
            flops=int(micros * 1e9), bytes_accessed=int(micros * 3e6), transcendentals=0
        ),
        name=name,
    )


def shape(*dims, kind=F32):
    return jax.ShapeDtypeStruct(dims, kind)


def shards(ensembles, cotangents, transforms):
    count, members, cells = ensembles.shape
    blocks, lanes = lax.axis_size("tm"), lax.axis_size("space")
    chips = lanes // 2
    scale = 1.0 / math.sqrt(cells * lanes * count * blocks)
    plan = Plan(count, members)
    levels = blocks.bit_length() - 1
    square = shape(members, members)
    ensembles, cotangents, transforms = (
        pltpu.with_memory_space_constraint(value, pltpu.HBM)
        for value in (ensembles, cotangents, transforms)
    )

    def exchange(value, axis, size, bit):
        return lax.ppermute(value, axis, [(at, at ^ bit) for at in range(size)])

    def around(value):
        return [
            lax.ppermute(value, "space", [(at, (at + 2 * d) % lanes) for at in range(lanes)])
            for d in range(1, chips)
        ]

    def piece_shape(piece):
        first, last = plan.pieces[piece]
        return shape(last - first, members, cells, kind=BF16)

    def piece_sems(piece):
        return [pltpu.SemaphoreType.DMA((len(plan.piece_groups[piece]),))] * 2

    suffixes, total, kept, *first_part = call(
        functools.partial(chain_kernel, plan),
        [shape(count * members, members), square, shape(count, members, members)] + [piece_shape(0)] * 2,
        [HBM] * 3, [VMEM] * 5, [pltpu.SemaphoreType.DMA] + piece_sems(0), 3.5, "transform_chain",
    )(transforms, ensembles, cotangents)

    wide = shape(members // 2, plan.width)
    later = before = jnp.eye(members, dtype=F32)
    uppers, befores = [], []

    packed = shape(packing(members)[3], 128)

    def join(level, total, other, later, before, after):
        befores.append(before)
        last = level == levels - 2
        total, later, before, upper = call(
            functools.partial(join_kernel, level, last),
            [packed if last else square] + [square] * 3, [VMEM] * 4 + [ANY], [VMEM] * 4,
            [], 3, f"join_{level}",
        )(total, other, later, before, after)
        uppers.append(upper)
        return total, later, before

    other = exchange(total, "tm", blocks, 1)
    gram, gram_sent, own, suffixes, *second_part = call(
        functools.partial(gram_kernel, plan),
        [wide, wide, square, shape(count * members, members)] + [piece_shape(1)] * 2,
        [HBM] * 2 + [VMEM] * 3, [VMEM] * 6,
        [pltpu.VMEM((members, plan.width), F32)] + piece_sems(1), 4.5, "gram",
    )(ensembles, cotangents, suffixes, *first_part)
    parts = [first_part, second_part]
    other_own = exchange(own, "tm", blocks, 1)
    gram_core = exchange(gram_sent, "space", lanes, 1)
    total, later, before = join(0, total, other, later, before, own)
    other = exchange(total, "tm", blocks, 2)
    gram = call(sum_kernel, wide, [VMEM] * 2 + [ANY], VMEM, [], 0.1, "chip_gram")(gram, gram_core, total)
    grams = around(gram)

    def pass_on(level, carry, after):
        last = level == levels - 2
        return call(
            functools.partial(pass_kernel, level, last),
            [packed if last else square, square], [VMEM] * 5 + [ANY], [VMEM] * 2, [], 3, f"pass_{level}",
        )(own, other_own, carry, uppers[level], befores[level], after)

    carry = jnp.zeros((members, members), F32)
    after = gram
    for level in range(levels - 2):
        own, carry = pass_on(level, carry, after)
        other_own = exchange(own, "tm", blocks, 2 << level)
        total, later, before = join(level + 1, total, other, later, before, own)
        other = exchange(total, "tm", blocks, 4 << level)
        after = total
    befores.append(before)
    own, carry = pass_on(levels - 2, carry, total)
    other_own = exchange(own, "tm", blocks, blocks // 2)
    entering = call(
        functools.partial(enter_kernel, levels - 1),
        square, [VMEM] * 2 + [ANY], VMEM, [], 0.2, "entering",
    )(later, other, own)
    size = plan.stack * members
    ens_factors, cot_factors, follow = call(
        functools.partial(carry_kernel, plan),
        [shape(len(plan.groups), size, size, kind=BF16)] * 2
        + [shape(2, count * members, members, kind=BF16)],
        [VMEM] * 2 + [ANY], [VMEM] * 3, [], 0.9, "carries",
    )(suffixes, entering, own)
    def apply(factors, which, after, name):
        return call(
            functools.partial(apply_kernel, plan),
            [shape(count, members, cells, kind=BF16), shape(8, 128)],
            [VMEM] * (1 + PIECES) + [ANY], [HBM, VMEM],
            [pltpu.VMEM((count, members, cells), BF16),
             pltpu.SemaphoreType.DMA((2 * len(plan.groups),))],
            0.5, name,
        )(factors, *(part[which] for part in parts), after)

    smoothed, done = apply(ens_factors, 0, follow, "smoothed")
    carry, grams[0] = call(
        functools.partial(last_pass_kernel, levels - 1),
        [square, wide], [VMEM] * 3 + [ANY] * 2, [VMEM, ANY], [], 0.2, "pass_last", aliases={4: 1},
    )(other_own, carry, befores[-1], done, grams[0])
    carry_core = exchange(carry, "space", lanes, 1)
    for part in grams:
        gram = gram + part
    gram_core = exchange(gram, "space", lanes, 1)
    steps = call(
        functools.partial(windows_kernel, plan),
        shape(2, count_steps(count) * members, members, kind=BF16), [VMEM, ANY], VMEM,
        [pltpu.VMEM((count * members, members), F32)], 1.0, "windows",
    )(kept, carry)
    carry = call(
        sum_kernel, square, [VMEM] * 2 + [ANY], VMEM, [], 0.1, "chip_carry",
    )(carry, carry_core, steps)
    carries = [carry] + around(carry)
    ensemble_grad, done = apply(cot_factors, 1, carry, "ensemble_grad")
    transform_grad = call(
        functools.partial(final_kernel, plan, scale),
        shape(count, members, members),
        [VMEM] * 4 + [ANY] + [VMEM] * chips, HBM,
        [pltpu.VMEM((count, members, members), F32), pltpu.SemaphoreType.DMA((count,))],
        2.5, "transform_grad",
    )(gram, gram_core, follow, steps, done, *carries)
    return (smoothed, ensemble_grad, transform_grad)


def solution(mesh):
    return jax.shard_map(
        shards,
        mesh=mesh,
        in_specs=(P("tm", None, "space"), P("tm", None, "space"), P("tm", None, None)),
        out_specs=(P("tm", None, "space"), P("tm", None, "space"), P("tm", None, None)),
        check_vma=False,
    )
```

```python
import functools
import math

import jax
import jax.numpy as jnp
from jax import lax
from jax.experimental import pallas as pl
from jax.experimental.pallas import tpu as pltpu
from jax.sharding import PartitionSpec as P

F32 = jnp.float32
BF16 = jnp.bfloat16
VMEM = pl.BlockSpec(memory_space=pltpu.VMEM)
HBM = pl.BlockSpec(memory_space=pltpu.HBM)
ANY = pl.BlockSpec(memory_space=pl.ANY)
DEPTH = 256
PIECES = 2
NORMAL = (((1,), (0,)), ((), ()))
ROWS = (((1,), (1,)), ((), ()))


def split(value):
    high = value.astype(BF16)
    return high, (value - high.astype(F32)).astype(BF16)


def mul(left, right, dims=NORMAL):
    return lax.dot_general(left, right, dims, preferred_element_type=F32)


def mul_pairs(left, right, dims=NORMAL):
    return mul(left[0], right[0], dims) + (
        mul(left[0], right[1], dims) + mul(left[1], right[0], dims)
    )


def mul_exact(left, right, dims=NORMAL):
    return mul_pairs(split(left), split(right), dims)


def mul_stacked(left, right, dims=NORMAL):
    rows = left[0].shape[0]
    both = mul(jnp.concatenate(left, axis=0), right[0], dims)
    return both[:rows] + (both[rows:] + mul(left[0], right[1], dims))


def mul_small(left, right):
    return mul_stacked(split(left), split(right))


def product_of(factors):
    while len(factors) > 1:
        joined = [mul_exact(*factors[at : at + 2]) for at in range(0, len(factors) - 1, 2)]
        factors = joined + factors[len(joined) * 2 :]
    return factors[0]


def suffix_scan(ref, count, members, stop):
    width = 1
    while width < stop:
        for start in range(0, count, 2 * width):
            middle = start + width
            if middle < count:
                rows = slice(start * members, middle * members)
                ref[rows] = mul_exact(ref[rows], ref[middle * members : (middle + 1) * members])
        width *= 2


class Plan:
    def __init__(self, count, members):
        self.count, self.members = count, members
        self.stack = DEPTH // members
        self.groups = [
            (start, min(start + self.stack, count)) for start in range(0, count, self.stack)
        ]
        bounds = [0, len(self.groups) // 3, len(self.groups)]
        self.piece_groups = [self.groups[a:b] for a, b in zip(bounds, bounds[1:])]
        self.pieces = [(part[0][0], part[-1][1]) for part in self.piece_groups]
        self.first_group = bounds[:-1]
        self.widths = [-(-(stop - start) * members // 128) * 128 for start, stop in self.groups]
        self.width = sum(self.widths)

    def lanes(self, at):
        start = sum(self.widths[:at])
        return slice(start, start + self.widths[at])

    def rows(self, first, last):
        return slice(first * self.members, last * self.members)


def packing(members):
    spare = 128 - members
    strips = -(-members // spare)
    rest = members // (strips + 1) // 8 * 8
    return spare, strips, rest, members - rest


def pack(value):
    members = value.shape[0]
    spare, strips, rest, rows = packing(members)
    side = [value[rows:, at * spare : (at + 1) * spare] for at in range(strips)]
    side = [jnp.pad(part, ((0, 0), (0, spare - part.shape[1]))) for part in side]
    side.append(jnp.zeros((rows - strips * rest, spare), value.dtype))
    return jnp.concatenate([value[:rows], jnp.concatenate(side, axis=0)], axis=1)


def unpack(value, members):
    spare, strips, rest, rows = packing(members)
    side = [value[at * rest : (at + 1) * rest, members:] for at in range(strips)]
    last = jnp.concatenate(side, axis=1)[:, :members]
    return jnp.concatenate([value[:, :members], last], axis=0)


def on_blocks(members, size):
    rows = lax.broadcasted_iota(jnp.int32, (size, size), 0) // members
    columns = lax.broadcasted_iota(jnp.int32, (size, size), 1) // members
    return rows == columns


def loads(plan, piece, values, buffer, sems, which=slice(None)):
    base = plan.pieces[piece][0]
    copies = [
        pltpu.make_async_copy(values.at[start:stop], buffer.at[start - base : stop - base], sems.at[at])
        for at, (start, stop) in enumerate(plan.piece_groups[piece])
    ][which]
    for copy in copies:
        copy.start()
    return copies


def chain_kernel(
    plan, transforms, ensembles, cotangents, suffixes, total, kept, ens, cot, sem, ens_sem, cot_sem
):
    count, members = plan.count, plan.members
    read = pltpu.make_async_copy(transforms, kept, sem)
    read.start()
    more = loads(plan, 0, ensembles, ens, ens_sem, slice(1))
    more += loads(plan, 0, cotangents, cot, cot_sem, slice(1))
    read.wait()
    more += loads(plan, 0, ensembles, ens, ens_sem, slice(1, None))
    more += loads(plan, 0, cotangents, cot, cot_sem, slice(1, None))
    for at in range(count):
        suffixes[plan.rows(at, at + 1)] = kept[at]
    suffix_scan(suffixes, count, members, count)
    total[...] = suffixes[plan.rows(0, 1)]
    for copy in more:
        copy.wait()


def windows_kernel(plan, kept, _, steps, runs):
    count = plan.count
    for at in range(count - 1):
        runs[plan.rows(at + 1, at + 2)] = kept[at].T
    number = 0
    width = 1
    while width < count:
        for middle in range(width, count, 2 * width):
            size = min(width, count - middle)
            for side, part in enumerate(split(runs[plan.rows(middle, middle + size)])):
                steps[side, plan.rows(number, number + size)] = part
            number += size
        for start in range(2 * width, count, 2 * width):
            if start + width < count:
                rows = plan.rows(start + width, min(start + 2 * width, count))
                runs[rows] = mul_small(runs[rows], runs[plan.rows(start + width - 1, start + width)])
        width *= 2


def count_steps(count):
    total = 0
    width = 1
    while width < count:
        total += sum(min(width, count - middle) for middle in range(width, count, 2 * width))
        width *= 2
    return total


def core_index():
    return lax.rem(lax.axis_index("space"), 2)


def gram_of(plan, piece, cot, ens, suffixes, whole, ready=lambda: None):
    members = plan.members
    base = plan.pieces[piece][0]
    offset = jnp.zeros((members, members), F32)
    for at, (start, stop) in enumerate(plan.piece_groups[piece]):
        ready()
        size = (stop - start) * members
        stacked = [ref[start - base : stop - base].reshape(size, ref.shape[2]) for ref in (cot, ens)]
        wide = jnp.where(on_blocks(members, size), mul(*stacked, ROWS), 0.0)
        gram = wide[:members]
        for i in range(1, stop - start):
            gram = gram + wide[i * members : (i + 1) * members]
        offset = offset + mul_exact(gram, suffixes[plan.rows(start, stop)])
        lanes = plan.lanes(plan.first_group[piece] + at)
        width = lanes.stop - lanes.start
        whole[:, lanes] = jnp.pad(gram, ((0, 0), (0, width - size)))
    return offset


def gram_kernel(
    plan, ensembles, cotangents, suffixes, ens, cot,
    kept, sent, offsets, next_ens, next_cot, whole, ens_sem, cot_sem,
):
    pairs = []
    for at in range(len(plan.piece_groups[1])):
        pairs.append(
            loads(plan, 1, ensembles, next_ens, ens_sem, slice(at, at + 1))
            + loads(plan, 1, cotangents, next_cot, cot_sem, slice(at, at + 1))
        )
    waiting = iter(pairs)

    def ready():
        for copy in next(waiting):
            copy.wait()

    total = gram_of(plan, 0, cot, ens, suffixes, whole)
    offsets[...] = total + gram_of(plan, 1, next_cot, next_ens, suffixes, whole, ready)
    half = plan.members // 2
    core = lax.rem(lax.axis_index("space"), 2)
    kept[...] = whole[pl.ds(core * half, half)]
    sent[...] = whole[pl.ds((1 - core) * half, half)]


def upper_half(level):
    return lax.rem(lax.axis_index("tm") // (1 << level), 2) == 1


def join_kernel(level, last, total, other, later, before, _, new_total, new_later, new_before, upper_total):
    upper = upper_half(level)
    left = jnp.where(upper, other[...], total[...])
    right = jnp.where(upper, total[...], other[...])
    joined = mul_small(left, right)
    new_total[...] = pack(joined) if last else joined
    upper_total[...] = right
    new_later[...] = jnp.where(upper, later[...], mul_small(later[...], other[...]))
    new_before[...] = jnp.where(upper, mul_small(other[...], before[...]), before[...])


def sum_kernel(left, right, _, total):
    total[...] = left[...] + right[...]


def pass_kernel(level, last, own, other, carry, upper_total, before, _, new_own, new_carry):
    upper = upper_half(level)
    left = jnp.where(upper, other[...], own[...])
    right = jnp.where(upper, own[...], other[...])
    passed = mul_small(left, upper_total[...]) + right
    new_own[...] = pack(passed) if last else passed
    new_carry[...] = carry[...] + jnp.where(upper, mul_small(left, before[...]), 0.0)


def last_pass_kernel(level, other, carry, before, _, __, new_carry, ___):
    added = mul_small(unpack(other[...], before.shape[0]), before[...])
    new_carry[...] = carry[...] + jnp.where(upper_half(level), added, 0.0)


def enter_kernel(level, later, other, _, entering):
    joined = mul_small(later[...], unpack(other[...], later.shape[0]))
    entering[...] = jnp.where(upper_half(level), later[...], joined)


def carry_kernel(plan, suffixes, later, _, ens_factors, cot_factors, follow):
    count, members = plan.count, plan.members
    entering = later[...]
    mask = on_blocks(members, plan.stack * members)
    repeated = split(jnp.concatenate([entering] * plan.stack, axis=1))
    for at, (start, stop) in enumerate(plan.groups):
        size = (stop - start) * members
        wide = mul_pairs(split(suffixes[plan.rows(start, stop)]), repeated)
        part = jnp.where(mask[:size, :size], wide[:, :size], 0.0)
        cot_factors[at, :size, :size] = part.astype(BF16)
        ens_factors[at, :size, :size] = part.T.astype(BF16)
        first = max(start - 1, 0)
        kept = wide[(first + 1 - start) * members :, :members]
        for side, value in enumerate(split(kept)):
            follow[side, plan.rows(first, stop - 1)] = value
    for side, value in enumerate(split(entering)):
        follow[side, plan.rows(count - 1, count)] = value


def apply_kernel(plan, factors, *refs):
    out, marker, out_buf, out_sem = refs[-4:]
    members = plan.members
    marker[...] = jnp.zeros_like(marker)
    chunk = out_buf.shape[2] // 2
    writes = []
    for piece, values in enumerate(refs[:PIECES]):
        first = plan.pieces[piece][0]
        for at, (start, stop) in enumerate(plan.piece_groups[piece]):
            size = (stop - start) * members
            for side in range(2):
                columns = slice(side * chunk, (side + 1) * chunk)
                stacked = values[start - first : stop - first, :, columns].reshape(size, chunk)
                result = mul(factors[plan.first_group[piece] + at, :size, :size], stacked)
                out_buf[start:stop, :, columns] = result.astype(BF16).reshape(
                    stop - start, members, chunk
                )
                copy = pltpu.make_async_copy(
                    out_buf.at[start:stop, :, columns],
                    out.at[start:stop, :, columns],
                    out_sem.at[len(writes)],
                )
                copy.start()
                writes.append(copy)
    for copy in writes:
        copy.wait()


def final_kernel(plan, scale, gram, gram_core, follow, steps, _, *refs):
    carries, (out, buffer, sems) = refs[:-3], refs[-3:]
    carry = carries[0][...]
    for ref in carries[1:]:
        carry = carry + ref[...]
    count, members = plan.count, plan.members
    totals = []
    first = lax.rem(lax.axis_index("space"), 2) == 0
    for at, (start, stop) in enumerate(plan.groups):
        mine, other = gram[:, plan.lanes(at)], gram_core[:, plan.lanes(at)]
        halves = [jnp.where(first, mine, other), jnp.where(first, other, mine)]
        tall = jnp.concatenate(halves, axis=0).T
        for i in range(stop - start):
            totals.append(tall[i * members : (i + 1) * members])
    totals[0] = totals[0] + carry.T
    number = 0
    width = 1
    while width < count:
        for start in range(width, count, 2 * width):
            size = min(width, count - start)
            rows = plan.rows(number, number + size)
            added = mul_stacked((steps[0, rows], steps[1, rows]), split(totals[start - 1]))
            for at in range(size):
                totals[start + at] = totals[start + at] + added[at * members : (at + 1) * members]
            number += size
        width *= 2
    copies = []
    for at in range(count):
        rows = plan.rows(at, at + 1)
        buffer[at] = mul_stacked(split(totals[at]), (follow[0, rows], follow[1, rows]), ROWS) * scale
        copy = pltpu.make_async_copy(buffer.at[at], out.at[at], sems.at[at])
        copy.start()
        copies.append(copy)
    for copy in copies:
        copy.wait()


def call(kernel, outs, ins, out_specs, scratch, micros, name, limit=16, aliases=None):
    return pl.pallas_call(
        kernel,
        out_shape=outs,
        in_specs=ins,
        out_specs=out_specs,
        scratch_shapes=scratch,
        input_output_aliases=aliases or {},
        compiler_params=pltpu.CompilerParams(vmem_limit_bytes=limit << 20),
        cost_estimate=pl.CostEstimate(
            flops=int(micros * 1e9), bytes_accessed=int(micros * 3e6), transcendentals=0
        ),
        name=name,
    )


def shape(*dims, kind=F32):
    return jax.ShapeDtypeStruct(dims, kind)


def shards(ensembles, cotangents, transforms):
    count, members, cells = ensembles.shape
    blocks, lanes = lax.axis_size("tm"), lax.axis_size("space")
    chips = lanes // 2
    scale = 1.0 / math.sqrt(cells * lanes * count * blocks)
    plan = Plan(count, members)
    levels = blocks.bit_length() - 1
    square = shape(members, members)
    ensembles, cotangents, transforms = (
        pltpu.with_memory_space_constraint(value, pltpu.HBM)
        for value in (ensembles, cotangents, transforms)
    )

    def exchange(value, axis, size, bit):
        return lax.ppermute(value, axis, [(at, at ^ bit) for at in range(size)])

    def around(value):
        return [
            lax.ppermute(value, "space", [(at, (at + 2 * d) % lanes) for at in range(lanes)])
            for d in range(1, chips)
        ]

    def piece_shape(piece):
        first, last = plan.pieces[piece]
        return shape(last - first, members, cells, kind=BF16)

    def piece_sems(piece):
        return [pltpu.SemaphoreType.DMA((len(plan.piece_groups[piece]),))] * 2

    suffixes, total, kept, *first_part = call(
        functools.partial(chain_kernel, plan),
        [shape(count * members, members), square, shape(count, members, members)] + [piece_shape(0)] * 2,
        [HBM] * 3, [VMEM] * 5, [pltpu.SemaphoreType.DMA] + piece_sems(0), 3.5, "transform_chain",
    )(transforms, ensembles, cotangents)

    wide = shape(members // 2, plan.width)
    later = before = jnp.eye(members, dtype=F32)
    uppers, befores = [], []

    packed = shape(packing(members)[3], 128)

    def join(level, total, other, later, before, after):
        befores.append(before)
        last = level == levels - 2
        total, later, before, upper = call(
            functools.partial(join_kernel, level, last),
            [packed if last else square] + [square] * 3, [VMEM] * 4 + [ANY], [VMEM] * 4,
            [], 3, f"join_{level}",
        )(total, other, later, before, after)
        uppers.append(upper)
        return total, later, before

    other = exchange(total, "tm", blocks, 1)
    gram, gram_sent, own, *second_part = call(
        functools.partial(gram_kernel, plan),
        [wide, wide, square] + [piece_shape(1)] * 2,
        [HBM] * 2 + [VMEM] * 3, [VMEM] * 5,
        [pltpu.VMEM((members, plan.width), F32)] + piece_sems(1), 4.5, "gram",
    )(ensembles, cotangents, suffixes, *first_part)
    parts = [first_part, second_part]
    other_own = exchange(own, "tm", blocks, 1)
    gram_core = exchange(gram_sent, "space", lanes, 1)
    total, later, before = join(0, total, other, later, before, own)
    other = exchange(total, "tm", blocks, 2)
    gram = call(sum_kernel, wide, [VMEM] * 2 + [ANY], VMEM, [], 0.1, "chip_gram")(gram, gram_core, total)
    grams = around(gram)

    def pass_on(level, carry, after):
        last = level == levels - 2
        return call(
            functools.partial(pass_kernel, level, last),
            [packed if last else square, square], [VMEM] * 5 + [ANY], [VMEM] * 2, [], 3, f"pass_{level}",
        )(own, other_own, carry, uppers[level], befores[level], after)

    carry = jnp.zeros((members, members), F32)
    after = gram
    for level in range(levels - 2):
        own, carry = pass_on(level, carry, after)
        other_own = exchange(own, "tm", blocks, 2 << level)
        total, later, before = join(level + 1, total, other, later, before, own)
        other = exchange(total, "tm", blocks, 4 << level)
        after = total
    befores.append(before)
    own, carry = pass_on(levels - 2, carry, total)
    other_own = exchange(own, "tm", blocks, blocks // 2)
    entering = call(
        functools.partial(enter_kernel, levels - 1),
        square, [VMEM] * 2 + [ANY], VMEM, [], 0.2, "entering",
    )(later, other, own)
    size = plan.stack * members
    ens_factors, cot_factors, follow = call(
        functools.partial(carry_kernel, plan),
        [shape(len(plan.groups), size, size, kind=BF16)] * 2
        + [shape(2, count * members, members, kind=BF16)],
        [VMEM] * 2 + [ANY], [VMEM] * 3, [], 0.9, "carries",
    )(suffixes, entering, own)
    def apply(factors, which, after, name):
        return call(
            functools.partial(apply_kernel, plan),
            [shape(count, members, cells, kind=BF16), shape(8, 128)],
            [VMEM] * (1 + PIECES) + [ANY], [HBM, VMEM],
            [pltpu.VMEM((count, members, cells), BF16),
             pltpu.SemaphoreType.DMA((2 * len(plan.groups),))],
            0.5, name,
        )(factors, *(part[which] for part in parts), after)

    smoothed, done = apply(ens_factors, 0, follow, "smoothed")
    carry, grams[0] = call(
        functools.partial(last_pass_kernel, levels - 1),
        [square, wide], [VMEM] * 3 + [ANY] * 2, [VMEM, ANY], [], 0.2, "pass_last", aliases={4: 1},
    )(other_own, carry, befores[-1], done, grams[0])
    carry_core = exchange(carry, "space", lanes, 1)
    for part in grams:
        gram = gram + part
    gram_core = exchange(gram, "space", lanes, 1)
    steps = call(
        functools.partial(windows_kernel, plan),
        shape(2, count_steps(count) * members, members, kind=BF16), [VMEM, ANY], VMEM,
        [pltpu.VMEM((count * members, members), F32)], 1.0, "windows",
    )(kept, carry)
    carry = call(
        sum_kernel, square, [VMEM] * 2 + [ANY], VMEM, [], 0.1, "chip_carry",
    )(carry, carry_core, steps)
    carries = [carry] + around(carry)
    ensemble_grad, done = apply(cot_factors, 1, carry, "ensemble_grad")
    transform_grad = call(
        functools.partial(final_kernel, plan, scale),
        shape(count, members, members),
        [VMEM] * 4 + [ANY] + [VMEM] * chips, HBM,
        [pltpu.VMEM((count, members, members), F32), pltpu.SemaphoreType.DMA((count,))],
        2.5, "transform_grad",
    )(gram, gram_core, follow, steps, done, *carries)
    return (smoothed, ensemble_grad, transform_grad)


def solution(mesh):
    return jax.shard_map(
        shards,
        mesh=mesh,
        in_specs=(P("tm", None, "space"), P("tm", None, "space"), P("tm", None, None)),
        out_specs=(P("tm", None, "space"), P("tm", None, "space"), P("tm", None, None)),
        check_vma=False,
    )
```

```python
import functools
import math

import jax
import jax.numpy as jnp
from jax import lax
from jax.experimental import pallas as pl
from jax.experimental.pallas import tpu as pltpu
from jax.sharding import PartitionSpec as P

F32 = jnp.float32
BF16 = jnp.bfloat16
VMEM = pl.BlockSpec(memory_space=pltpu.VMEM)
HBM = pl.BlockSpec(memory_space=pltpu.HBM)
ANY = pl.BlockSpec(memory_space=pl.ANY)
DEPTH = 256
PIECES = 2
NORMAL = (((1,), (0,)), ((), ()))
ROWS = (((1,), (1,)), ((), ()))


def split(value):
    high = value.astype(BF16)
    return high, (value - high.astype(F32)).astype(BF16)


def mul(left, right, dims=NORMAL):
    return lax.dot_general(left, right, dims, preferred_element_type=F32)


def mul_pairs(left, right, dims=NORMAL):
    return mul(left[0], right[0], dims) + (
        mul(left[0], right[1], dims) + mul(left[1], right[0], dims)
    )


def mul_exact(left, right, dims=NORMAL):
    return mul_pairs(split(left), split(right), dims)


def mul_stacked(left, right, dims=NORMAL):
    rows = left[0].shape[0]
    both = mul(jnp.concatenate(left, axis=0), right[0], dims)
    return both[:rows] + (both[rows:] + mul(left[0], right[1], dims))


def mul_small(left, right):
    return mul_stacked(split(left), split(right))


def product_of(factors):
    while len(factors) > 1:
        joined = [mul_exact(*factors[at : at + 2]) for at in range(0, len(factors) - 1, 2)]
        factors = joined + factors[len(joined) * 2 :]
    return factors[0]


def suffix_scan(ref, count, members, stop):
    width = 1
    while width < stop:
        for start in range(0, count, 2 * width):
            middle = start + width
            if middle < count:
                rows = slice(start * members, middle * members)
                ref[rows] = mul_exact(ref[rows], ref[middle * members : (middle + 1) * members])
        width *= 2


class Plan:
    def __init__(self, count, members):
        self.count, self.members = count, members
        self.stack = DEPTH // members
        self.groups = [
            (start, min(start + self.stack, count)) for start in range(0, count, self.stack)
        ]
        bounds = [0, len(self.groups) // 3, len(self.groups)]
        self.piece_groups = [self.groups[a:b] for a, b in zip(bounds, bounds[1:])]
        self.pieces = [(part[0][0], part[-1][1]) for part in self.piece_groups]
        self.first_group = bounds[:-1]
        self.widths = [-(-(stop - start) * members // 128) * 128 for start, stop in self.groups]
        self.width = sum(self.widths)

    def lanes(self, at):
        start = sum(self.widths[:at])
        return slice(start, start + self.widths[at])

    def rows(self, first, last):
        return slice(first * self.members, last * self.members)


def packing(members):
    spare = 128 - members
    strips = -(-members // spare)
    rest = members // (strips + 1) // 8 * 8
    return spare, strips, rest, members - rest


def pack(value):
    members = value.shape[0]
    spare, strips, rest, rows = packing(members)
    side = [value[rows:, at * spare : (at + 1) * spare] for at in range(strips)]
    side = [jnp.pad(part, ((0, 0), (0, spare - part.shape[1]))) for part in side]
    side.append(jnp.zeros((rows - strips * rest, spare), value.dtype))
    return jnp.concatenate([value[:rows], jnp.concatenate(side, axis=0)], axis=1)


def unpack(value, members):
    spare, strips, rest, rows = packing(members)
    side = [value[at * rest : (at + 1) * rest, members:] for at in range(strips)]
    last = jnp.concatenate(side, axis=1)[:, :members]
    return jnp.concatenate([value[:, :members], last], axis=0)


def on_blocks(members, size):
    rows = lax.broadcasted_iota(jnp.int32, (size, size), 0) // members
    columns = lax.broadcasted_iota(jnp.int32, (size, size), 1) // members
    return rows == columns


def loads(plan, piece, values, buffer, sems, which=slice(None)):
    base = plan.pieces[piece][0]
    copies = [
        pltpu.make_async_copy(values.at[start:stop], buffer.at[start - base : stop - base], sems.at[at])
        for at, (start, stop) in enumerate(plan.piece_groups[piece])
    ][which]
    for copy in copies:
        copy.start()
    return copies


def chain_kernel(
    plan, transforms, ensembles, cotangents, suffixes, total, kept, ens, cot, sem, ens_sem, cot_sem
):
    count, members = plan.count, plan.members
    read = pltpu.make_async_copy(transforms, kept, sem)
    read.start()
    more = loads(plan, 0, ensembles, ens, ens_sem, slice(1))
    more += loads(plan, 0, cotangents, cot, cot_sem, slice(1))
    read.wait()
    more += loads(plan, 0, ensembles, ens, ens_sem, slice(1, None))
    more += loads(plan, 0, cotangents, cot, cot_sem, slice(1, None))
    for at in range(count):
        suffixes[plan.rows(at, at + 1)] = kept[at]
    suffix_scan(suffixes, count, members, count)
    total[...] = suffixes[plan.rows(0, 1)]
    for copy in more:
        copy.wait()


def windows_kernel(plan, kept, _, __, steps, ___, runs):
    count = plan.count
    for at in range(count - 1):
        runs[plan.rows(at + 1, at + 2)] = kept[at].T
    number = 0
    width = 1
    while width < count:
        for middle in range(width, count, 2 * width):
            size = min(width, count - middle)
            for side, part in enumerate(split(runs[plan.rows(middle, middle + size)])):
                steps[side, plan.rows(number, number + size)] = part
            number += size
        for start in range(2 * width, count, 2 * width):
            if start + width < count:
                rows = plan.rows(start + width, min(start + 2 * width, count))
                runs[rows] = mul_small(runs[rows], runs[plan.rows(start + width - 1, start + width)])
        width *= 2


def count_steps(count):
    total = 0
    width = 1
    while width < count:
        total += sum(min(width, count - middle) for middle in range(width, count, 2 * width))
        width *= 2
    return total


def core_index():
    return lax.rem(lax.axis_index("space"), 2)


def gram_of(plan, piece, cot, ens, suffixes, whole, ready=lambda: None):
    members = plan.members
    base = plan.pieces[piece][0]
    offset = jnp.zeros((members, members), F32)
    for at, (start, stop) in enumerate(plan.piece_groups[piece]):
        ready()
        size = (stop - start) * members
        stacked = [ref[start - base : stop - base].reshape(size, ref.shape[2]) for ref in (cot, ens)]
        wide = jnp.where(on_blocks(members, size), mul(*stacked, ROWS), 0.0)
        gram = wide[:members]
        for i in range(1, stop - start):
            gram = gram + wide[i * members : (i + 1) * members]
        offset = offset + mul_exact(gram, suffixes[plan.rows(start, stop)])
        lanes = plan.lanes(plan.first_group[piece] + at)
        width = lanes.stop - lanes.start
        whole[:, lanes] = jnp.pad(gram, ((0, 0), (0, width - size)))
    return offset


def gram_kernel(
    plan, ensembles, cotangents, suffixes, ens, cot,
    kept, sent, offsets, next_ens, next_cot, whole, ens_sem, cot_sem,
):
    pairs = []
    for at in range(len(plan.piece_groups[1])):
        pairs.append(
            loads(plan, 1, ensembles, next_ens, ens_sem, slice(at, at + 1))
            + loads(plan, 1, cotangents, next_cot, cot_sem, slice(at, at + 1))
        )
    waiting = iter(pairs)

    def ready():
        for copy in next(waiting):
            copy.wait()

    total = gram_of(plan, 0, cot, ens, suffixes, whole)
    offsets[...] = total + gram_of(plan, 1, next_cot, next_ens, suffixes, whole, ready)
    half = plan.members // 2
    core = lax.rem(lax.axis_index("space"), 2)
    kept[...] = whole[pl.ds(core * half, half)]
    sent[...] = whole[pl.ds((1 - core) * half, half)]


def upper_half(level):
    return lax.rem(lax.axis_index("tm") // (1 << level), 2) == 1


def join_kernel(level, last, total, other, later, before, _, new_total, new_later, new_before, upper_total):
    upper = upper_half(level)
    left = jnp.where(upper, other[...], total[...])
    right = jnp.where(upper, total[...], other[...])
    joined = mul_small(left, right)
    new_total[...] = pack(joined) if last else joined
    upper_total[...] = right
    new_later[...] = jnp.where(upper, later[...], mul_small(later[...], other[...]))
    new_before[...] = jnp.where(upper, mul_small(other[...], before[...]), before[...])


def sum_kernel(left, right, _, total):
    total[...] = left[...] + right[...]


def pass_kernel(level, last, own, other, carry, upper_total, before, _, new_own, new_carry):
    upper = upper_half(level)
    left = jnp.where(upper, other[...], own[...])
    right = jnp.where(upper, own[...], other[...])
    passed = mul_small(left, upper_total[...]) + right
    new_own[...] = pack(passed) if last else passed
    new_carry[...] = carry[...] + jnp.where(upper, mul_small(left, before[...]), 0.0)


def last_pass_kernel(level, other, carry, before, _, new_carry):
    added = mul_small(unpack(other[...], before.shape[0]), before[...])
    new_carry[...] = carry[...] + jnp.where(upper_half(level), added, 0.0)


def enter_kernel(level, later, other, _, entering):
    joined = mul_small(later[...], unpack(other[...], later.shape[0]))
    entering[...] = jnp.where(upper_half(level), later[...], joined)


def carry_kernel(plan, suffixes, later, _, ens_factors, cot_factors, follow):
    count, members = plan.count, plan.members
    entering = later[...]
    mask = on_blocks(members, plan.stack * members)
    repeated = split(jnp.concatenate([entering] * plan.stack, axis=1))
    for at, (start, stop) in enumerate(plan.groups):
        size = (stop - start) * members
        wide = mul_pairs(split(suffixes[plan.rows(start, stop)]), repeated)
        part = jnp.where(mask[:size, :size], wide[:, :size], 0.0)
        cot_factors[at, :size, :size] = part.astype(BF16)
        ens_factors[at, :size, :size] = part.T.astype(BF16)
        first = max(start - 1, 0)
        kept = wide[(first + 1 - start) * members :, :members]
        for side, value in enumerate(split(kept)):
            follow[side, plan.rows(first, stop - 1)] = value
    for side, value in enumerate(split(entering)):
        follow[side, plan.rows(count - 1, count)] = value


def apply_kernel(plan, factors, *refs):
    out, marker, out_buf, out_sem = refs[-4:]
    members = plan.members
    marker[...] = jnp.zeros_like(marker)
    chunk = out_buf.shape[2] // 2
    writes = []
    for piece, values in enumerate(refs[:PIECES]):
        first = plan.pieces[piece][0]
        for at, (start, stop) in enumerate(plan.piece_groups[piece]):
            size = (stop - start) * members
            for side in range(2):
                columns = slice(side * chunk, (side + 1) * chunk)
                stacked = values[start - first : stop - first, :, columns].reshape(size, chunk)
                result = mul(factors[plan.first_group[piece] + at, :size, :size], stacked)
                out_buf[start:stop, :, columns] = result.astype(BF16).reshape(
                    stop - start, members, chunk
                )
                copy = pltpu.make_async_copy(
                    out_buf.at[start:stop, :, columns],
                    out.at[start:stop, :, columns],
                    out_sem.at[len(writes)],
                )
                copy.start()
                writes.append(copy)
    for copy in writes:
        copy.wait()


def final_kernel(plan, scale, gram, gram_core, follow, steps, _, *refs):
    carries, (out, buffer, sems) = refs[:-3], refs[-3:]
    carry = carries[0][...]
    for ref in carries[1:]:
        carry = carry + ref[...]
    count, members = plan.count, plan.members
    totals = []
    first = lax.rem(lax.axis_index("space"), 2) == 0
    for at, (start, stop) in enumerate(plan.groups):
        mine, other = gram[:, plan.lanes(at)], gram_core[:, plan.lanes(at)]
        halves = [jnp.where(first, mine, other), jnp.where(first, other, mine)]
        tall = jnp.concatenate(halves, axis=0).T
        for i in range(stop - start):
            totals.append(tall[i * members : (i + 1) * members])
    totals[0] = totals[0] + carry.T
    number = 0
    width = 1
    while width < count:
        for start in range(width, count, 2 * width):
            size = min(width, count - start)
            rows = plan.rows(number, number + size)
            added = mul_stacked((steps[0, rows], steps[1, rows]), split(totals[start - 1]))
            for at in range(size):
                totals[start + at] = totals[start + at] + added[at * members : (at + 1) * members]
            number += size
        width *= 2
    copies = []
    for at in range(count):
        rows = plan.rows(at, at + 1)
        buffer[at] = mul_stacked(split(totals[at]), (follow[0, rows], follow[1, rows]), ROWS) * scale
        copy = pltpu.make_async_copy(buffer.at[at], out.at[at], sems.at[at])
        copy.start()
        copies.append(copy)
    for copy in copies:
        copy.wait()


def call(kernel, outs, ins, out_specs, scratch, micros, name, limit=16, aliases=None):
    return pl.pallas_call(
        kernel,
        out_shape=outs,
        in_specs=ins,
        out_specs=out_specs,
        scratch_shapes=scratch,
        input_output_aliases=aliases or {},
        compiler_params=pltpu.CompilerParams(vmem_limit_bytes=limit << 20),
        cost_estimate=pl.CostEstimate(
            flops=int(micros * 1e9), bytes_accessed=int(micros * 3e6), transcendentals=0
        ),
        name=name,
    )


def shape(*dims, kind=F32):
    return jax.ShapeDtypeStruct(dims, kind)


def shards(ensembles, cotangents, transforms):
    count, members, cells = ensembles.shape
    blocks, lanes = lax.axis_size("tm"), lax.axis_size("space")
    chips = lanes // 2
    scale = 1.0 / math.sqrt(cells * lanes * count * blocks)
    plan = Plan(count, members)
    levels = blocks.bit_length() - 1
    square = shape(members, members)
    ensembles, cotangents, transforms = (
        pltpu.with_memory_space_constraint(value, pltpu.HBM)
        for value in (ensembles, cotangents, transforms)
    )

    def exchange(value, axis, size, bit):
        return lax.ppermute(value, axis, [(at, at ^ bit) for at in range(size)])

    def around(value):
        return [
            lax.ppermute(value, "space", [(at, (at + 2 * d) % lanes) for at in range(lanes)])
            for d in range(1, chips)
        ]

    def piece_shape(piece):
        first, last = plan.pieces[piece]
        return shape(last - first, members, cells, kind=BF16)

    def piece_sems(piece):
        return [pltpu.SemaphoreType.DMA((len(plan.piece_groups[piece]),))] * 2

    suffixes, total, kept, *first_part = call(
        functools.partial(chain_kernel, plan),
        [shape(count * members, members), square, shape(count, members, members)] + [piece_shape(0)] * 2,
        [HBM] * 3, [VMEM] * 5, [pltpu.SemaphoreType.DMA] + piece_sems(0), 3.5, "transform_chain",
    )(transforms, ensembles, cotangents)

    wide = shape(members // 2, plan.width)
    later = before = jnp.eye(members, dtype=F32)
    uppers, befores = [], []

    packed = shape(packing(members)[3], 128)

    def join(level, total, other, later, before, after):
        befores.append(before)
        last = level == levels - 2
        total, later, before, upper = call(
            functools.partial(join_kernel, level, last),
            [packed if last else square] + [square] * 3, [VMEM] * 4 + [ANY], [VMEM] * 4,
            [], 3, f"join_{level}",
        )(total, other, later, before, after)
        uppers.append(upper)
        return total, later, before

    other = exchange(total, "tm", blocks, 1)
    gram, gram_sent, own, *second_part = call(
        functools.partial(gram_kernel, plan),
        [wide, wide, square] + [piece_shape(1)] * 2,
        [HBM] * 2 + [VMEM] * 3, [VMEM] * 5,
        [pltpu.VMEM((members, plan.width), F32)] + piece_sems(1), 4.5, "gram",
    )(ensembles, cotangents, suffixes, *first_part)
    parts = [first_part, second_part]
    other_own = exchange(own, "tm", blocks, 1)
    gram_core = exchange(gram_sent, "space", lanes, 1)
    total, later, before = join(0, total, other, later, before, own)
    other = exchange(total, "tm", blocks, 2)
    gram = call(sum_kernel, wide, [VMEM] * 2 + [ANY], VMEM, [], 0.1, "chip_gram")(gram, gram_core, total)
    grams = around(gram)

    def pass_on(level, carry, after):
        last = level == levels - 2
        return call(
            functools.partial(pass_kernel, level, last),
            [packed if last else square, square], [VMEM] * 5 + [ANY], [VMEM] * 2, [], 3, f"pass_{level}",
        )(own, other_own, carry, uppers[level], befores[level], after)

    carry = jnp.zeros((members, members), F32)
    after = gram
    for level in range(levels - 2):
        own, carry = pass_on(level, carry, after)
        other_own = exchange(own, "tm", blocks, 2 << level)
        total, later, before = join(level + 1, total, other, later, before, own)
        other = exchange(total, "tm", blocks, 4 << level)
        after = total
    befores.append(before)
    own, carry = pass_on(levels - 2, carry, total)
    other_own = exchange(own, "tm", blocks, blocks // 2)
    entering = call(
        functools.partial(enter_kernel, levels - 1),
        square, [VMEM] * 2 + [ANY], VMEM, [], 0.2, "entering",
    )(later, other, own)
    size = plan.stack * members
    ens_factors, cot_factors, follow = call(
        functools.partial(carry_kernel, plan),
        [shape(len(plan.groups), size, size, kind=BF16)] * 2
        + [shape(2, count * members, members, kind=BF16)],
        [VMEM] * 2 + [ANY], [VMEM] * 3, [], 0.9, "carries",
    )(suffixes, entering, own)
    def apply(factors, which, after, name, micros):
        return call(
            functools.partial(apply_kernel, plan),
            [shape(count, members, cells, kind=BF16), shape(8, 128)],
            [VMEM] * (1 + PIECES) + [ANY], [HBM, VMEM],
            [pltpu.VMEM((count, members, cells), BF16),
             pltpu.SemaphoreType.DMA((2 * len(plan.groups),))],
            micros, name,
        )(factors, *(part[which] for part in parts), after)

    smoothed, done = apply(ens_factors, 0, follow, "smoothed", 0.5)
    carry = call(
        functools.partial(last_pass_kernel, levels - 1),
        square, [VMEM] * 3 + [ANY], VMEM, [], 0.2, "pass_last",
    )(other_own, carry, befores[-1], done)
    carry_core = exchange(carry, "space", lanes, 1)
    steps, grams[0] = call(
        functools.partial(windows_kernel, plan),
        [shape(2, count_steps(count) * members, members, kind=BF16), wide],
        [VMEM, ANY, ANY], [VMEM, ANY],
        [pltpu.VMEM((count * members, members), F32)], 1.0, "windows", aliases={2: 1},
    )(kept, carry, grams[0])
    for part in grams:
        gram = gram + part
    gram_core = exchange(gram, "space", lanes, 1)
    carry = call(
        sum_kernel, square, [VMEM] * 2 + [ANY], VMEM, [], 0.1, "chip_carry",
    )(carry, carry_core, steps)
    carries = [carry] + around(carry)
    ensemble_grad, done = apply(cot_factors, 1, carry, "ensemble_grad", 5)
    transform_grad = call(
        functools.partial(final_kernel, plan, scale),
        shape(count, members, members),
        [VMEM] * 4 + [ANY] + [VMEM] * chips, HBM,
        [pltpu.VMEM((count, members, members), F32), pltpu.SemaphoreType.DMA((count,))],
        2.5, "transform_grad",
    )(gram, gram_core, follow, steps, done, *carries)
    return (smoothed, ensemble_grad, transform_grad)


def solution(mesh):
    return jax.shard_map(
        shards,
        mesh=mesh,
        in_specs=(P("tm", None, "space"), P("tm", None, "space"), P("tm", None, None)),
        out_specs=(P("tm", None, "space"), P("tm", None, "space"), P("tm", None, None)),
        check_vma=False,
    )
```

```python
import functools
import math

import jax
import jax.numpy as jnp
from jax import lax
from jax.experimental import pallas as pl
from jax.experimental.pallas import tpu as pltpu
from jax.sharding import PartitionSpec as P

F32 = jnp.float32
BF16 = jnp.bfloat16
VMEM = pl.BlockSpec(memory_space=pltpu.VMEM)
HBM = pl.BlockSpec(memory_space=pltpu.HBM)
ANY = pl.BlockSpec(memory_space=pl.ANY)
DEPTH = 256
PIECES = 2
NORMAL = (((1,), (0,)), ((), ()))
ROWS = (((1,), (1,)), ((), ()))


def split(value):
    high = value.astype(BF16)
    return high, (value - high.astype(F32)).astype(BF16)


def mul(left, right, dims=NORMAL):
    return lax.dot_general(left, right, dims, preferred_element_type=F32)


def mul_pairs(left, right, dims=NORMAL):
    return mul(left[0], right[0], dims) + (
        mul(left[0], right[1], dims) + mul(left[1], right[0], dims)
    )


def mul_exact(left, right, dims=NORMAL):
    return mul_pairs(split(left), split(right), dims)


def mul_stacked(left, right, dims=NORMAL):
    rows = left[0].shape[0]
    both = mul(jnp.concatenate(left, axis=0), right[0], dims)
    return both[:rows] + (both[rows:] + mul(left[0], right[1], dims))


def mul_small(left, right):
    return mul_stacked(split(left), split(right))


def product_of(factors):
    while len(factors) > 1:
        joined = [mul_exact(*factors[at : at + 2]) for at in range(0, len(factors) - 1, 2)]
        factors = joined + factors[len(joined) * 2 :]
    return factors[0]


def suffix_scan(ref, count, members, stop):
    width = 1
    while width < stop:
        for start in range(0, count, 2 * width):
            middle = start + width
            if middle < count:
                rows = slice(start * members, middle * members)
                ref[rows] = mul_exact(ref[rows], ref[middle * members : (middle + 1) * members])
        width *= 2


class Plan:
    def __init__(self, count, members):
        self.count, self.members = count, members
        self.stack = DEPTH // members
        self.groups = [
            (start, min(start + self.stack, count)) for start in range(0, count, self.stack)
        ]
        bounds = [0, len(self.groups) // 3, len(self.groups)]
        self.piece_groups = [self.groups[a:b] for a, b in zip(bounds, bounds[1:])]
        self.pieces = [(part[0][0], part[-1][1]) for part in self.piece_groups]
        self.first_group = bounds[:-1]
        self.widths = [-(-(stop - start) * members // 128) * 128 for start, stop in self.groups]
        self.width = sum(self.widths)

    def lanes(self, at):
        start = sum(self.widths[:at])
        return slice(start, start + self.widths[at])

    def rows(self, first, last):
        return slice(first * self.members, last * self.members)


def packing(members):
    spare = 128 - members
    strips = -(-members // spare)
    rest = members // (strips + 1) // 8 * 8
    return spare, strips, rest, members - rest


def pack(value):
    members = value.shape[0]
    spare, strips, rest, rows = packing(members)
    side = [value[rows:, at * spare : (at + 1) * spare] for at in range(strips)]
    side = [jnp.pad(part, ((0, 0), (0, spare - part.shape[1]))) for part in side]
    side.append(jnp.zeros((rows - strips * rest, spare), value.dtype))
    return jnp.concatenate([value[:rows], jnp.concatenate(side, axis=0)], axis=1)


def unpack(value, members):
    spare, strips, rest, rows = packing(members)
    side = [value[at * rest : (at + 1) * rest, members:] for at in range(strips)]
    last = jnp.concatenate(side, axis=1)[:, :members]
    return jnp.concatenate([value[:, :members], last], axis=0)


def on_blocks(members, size):
    rows = lax.broadcasted_iota(jnp.int32, (size, size), 0) // members
    columns = lax.broadcasted_iota(jnp.int32, (size, size), 1) // members
    return rows == columns


def loads(plan, piece, values, buffer, sems, which=slice(None)):
    base = plan.pieces[piece][0]
    copies = [
        pltpu.make_async_copy(values.at[start:stop], buffer.at[start - base : stop - base], sems.at[at])
        for at, (start, stop) in enumerate(plan.piece_groups[piece])
    ][which]
    for copy in copies:
        copy.start()
    return copies


def chain_kernel(
    plan, transforms, ensembles, cotangents, suffixes, total, kept, ens, cot, sem, ens_sem, cot_sem
):
    count, members = plan.count, plan.members
    read = pltpu.make_async_copy(transforms, kept, sem)
    read.start()
    more = loads(plan, 0, ensembles, ens, ens_sem, slice(1))
    more += loads(plan, 0, cotangents, cot, cot_sem, slice(1))
    read.wait()
    more += loads(plan, 0, ensembles, ens, ens_sem, slice(1, None))
    more += loads(plan, 0, cotangents, cot, cot_sem, slice(1, None))
    for at in range(count):
        suffixes[plan.rows(at, at + 1)] = kept[at]
    suffix_scan(suffixes, count, members, count)
    total[...] = suffixes[plan.rows(0, 1)]
    for copy in more:
        copy.wait()


def windows_kernel(plan, kept, _, steps, runs):
    count = plan.count
    for at in range(count - 1):
        runs[plan.rows(at + 1, at + 2)] = kept[at].T
    number = 0
    width = 1
    while width < count:
        for middle in range(width, count, 2 * width):
            size = min(width, count - middle)
            for side, part in enumerate(split(runs[plan.rows(middle, middle + size)])):
                steps[side, plan.rows(number, number + size)] = part
            number += size
        for start in range(2 * width, count, 2 * width):
            if start + width < count:
                rows = plan.rows(start + width, min(start + 2 * width, count))
                runs[rows] = mul_small(runs[rows], runs[plan.rows(start + width - 1, start + width)])
        width *= 2


def count_steps(count):
    total = 0
    width = 1
    while width < count:
        total += sum(min(width, count - middle) for middle in range(width, count, 2 * width))
        width *= 2
    return total


def core_index():
    return lax.rem(lax.axis_index("space"), 2)


def gram_of(plan, piece, cot, ens, suffixes, whole, ready=lambda: None):
    members = plan.members
    base = plan.pieces[piece][0]
    offset = jnp.zeros((members, members), F32)
    for at, (start, stop) in enumerate(plan.piece_groups[piece]):
        ready()
        size = (stop - start) * members
        stacked = [ref[start - base : stop - base].reshape(size, ref.shape[2]) for ref in (cot, ens)]
        wide = jnp.where(on_blocks(members, size), mul(*stacked, ROWS), 0.0)
        gram = wide[:members]
        for i in range(1, stop - start):
            gram = gram + wide[i * members : (i + 1) * members]
        offset = offset + mul_exact(gram, suffixes[plan.rows(start, stop)])
        lanes = plan.lanes(plan.first_group[piece] + at)
        width = lanes.stop - lanes.start
        whole[:, lanes] = jnp.pad(gram, ((0, 0), (0, width - size)))
    return offset


def gram_kernel(
    plan, ensembles, cotangents, suffixes, ens, cot,
    kept, sent, offsets, next_ens, next_cot, whole, ens_sem, cot_sem,
):
    pairs = []
    for at in range(len(plan.piece_groups[1])):
        pairs.append(
            loads(plan, 1, ensembles, next_ens, ens_sem, slice(at, at + 1))
            + loads(plan, 1, cotangents, next_cot, cot_sem, slice(at, at + 1))
        )
    waiting = iter(pairs)

    def ready():
        for copy in next(waiting):
            copy.wait()

    total = gram_of(plan, 0, cot, ens, suffixes, whole)
    offsets[...] = total + gram_of(plan, 1, next_cot, next_ens, suffixes, whole, ready)
    half = plan.members // 2
    core = lax.rem(lax.axis_index("space"), 2)
    kept[...] = whole[pl.ds(core * half, half)]
    sent[...] = whole[pl.ds((1 - core) * half, half)]


def upper_half(level):
    return lax.rem(lax.axis_index("tm") // (1 << level), 2) == 1


def join_kernel(level, last, total, other, later, before, _, new_total, new_later, new_before, upper_total):
    upper = upper_half(level)
    left = jnp.where(upper, other[...], total[...])
    right = jnp.where(upper, total[...], other[...])
    joined = mul_small(left, right)
    new_total[...] = pack(joined) if last else joined
    upper_total[...] = right
    new_later[...] = jnp.where(upper, later[...], mul_small(later[...], other[...]))
    new_before[...] = jnp.where(upper, mul_small(other[...], before[...]), before[...])


def sum_kernel(left, right, _, total):
    total[...] = left[...] + right[...]


def pass_kernel(level, last, own, other, carry, upper_total, before, _, new_own, new_carry):
    upper = upper_half(level)
    left = jnp.where(upper, other[...], own[...])
    right = jnp.where(upper, own[...], other[...])
    passed = mul_small(left, upper_total[...]) + right
    new_own[...] = pack(passed) if last else passed
    new_carry[...] = carry[...] + jnp.where(upper, mul_small(left, before[...]), 0.0)


def last_pass_kernel(level, other, carry, before, _, __, new_carry, ___):
    added = mul_small(unpack(other[...], before.shape[0]), before[...])
    new_carry[...] = carry[...] + jnp.where(upper_half(level), added, 0.0)


def carry_kernel(plan, level, suffixes, later, other, _, ens_factors, cot_factors, follow):
    count, members = plan.count, plan.members
    joined = mul_small(later[...], unpack(other[...], members))
    entering = jnp.where(upper_half(level), later[...], joined)
    mask = on_blocks(members, plan.stack * members)
    repeated = split(jnp.concatenate([entering] * plan.stack, axis=1))
    for at, (start, stop) in enumerate(plan.groups):
        size = (stop - start) * members
        wide = mul_pairs(split(suffixes[plan.rows(start, stop)]), repeated)
        part = jnp.where(mask[:size, :size], wide[:, :size], 0.0)
        cot_factors[at, :size, :size] = part.astype(BF16)
        ens_factors[at, :size, :size] = part.T.astype(BF16)
        first = max(start - 1, 0)
        kept = wide[(first + 1 - start) * members :, :members]
        for side, value in enumerate(split(kept)):
            follow[side, plan.rows(first, stop - 1)] = value
    for side, value in enumerate(split(entering)):
        follow[side, plan.rows(count - 1, count)] = value


def apply_kernel(plan, factors, *refs):
    out, marker, out_buf, out_sem = refs[-4:]
    members = plan.members
    marker[...] = jnp.zeros_like(marker)
    chunk = out_buf.shape[2] // 2
    writes = []
    for piece, values in enumerate(refs[:PIECES]):
        first = plan.pieces[piece][0]
        for at, (start, stop) in enumerate(plan.piece_groups[piece]):
            size = (stop - start) * members
            for side in range(2):
                columns = slice(side * chunk, (side + 1) * chunk)
                stacked = values[start - first : stop - first, :, columns].reshape(size, chunk)
                result = mul(factors[plan.first_group[piece] + at, :size, :size], stacked)
                out_buf[start:stop, :, columns] = result.astype(BF16).reshape(
                    stop - start, members, chunk
                )
                copy = pltpu.make_async_copy(
                    out_buf.at[start:stop, :, columns],
                    out.at[start:stop, :, columns],
                    out_sem.at[len(writes)],
                )
                copy.start()
                writes.append(copy)
    for copy in writes:
        copy.wait()


def final_kernel(plan, scale, gram, gram_core, follow, steps, _, *refs):
    carries, (out, buffer, sems) = refs[:-3], refs[-3:]
    carry = carries[0][...]
    for ref in carries[1:]:
        carry = carry + ref[...]
    count, members = plan.count, plan.members
    totals = []
    first = lax.rem(lax.axis_index("space"), 2) == 0
    for at, (start, stop) in enumerate(plan.groups):
        mine, other = gram[:, plan.lanes(at)], gram_core[:, plan.lanes(at)]
        halves = [jnp.where(first, mine, other), jnp.where(first, other, mine)]
        tall = jnp.concatenate(halves, axis=0).T
        for i in range(stop - start):
            totals.append(tall[i * members : (i + 1) * members])
    totals[0] = totals[0] + carry.T
    number = 0
    width = 1
    while width < count:
        for start in range(width, count, 2 * width):
            size = min(width, count - start)
            rows = plan.rows(number, number + size)
            added = mul_stacked((steps[0, rows], steps[1, rows]), split(totals[start - 1]))
            for at in range(size):
                totals[start + at] = totals[start + at] + added[at * members : (at + 1) * members]
            number += size
        width *= 2
    copies = []
    for at in range(count):
        rows = plan.rows(at, at + 1)
        buffer[at] = mul_stacked(split(totals[at]), (follow[0, rows], follow[1, rows]), ROWS) * scale
        copy = pltpu.make_async_copy(buffer.at[at], out.at[at], sems.at[at])
        copy.start()
        copies.append(copy)
    for copy in copies:
        copy.wait()


def call(kernel, outs, ins, out_specs, scratch, micros, name, limit=16, aliases=None):
    return pl.pallas_call(
        kernel,
        out_shape=outs,
        in_specs=ins,
        out_specs=out_specs,
        scratch_shapes=scratch,
        input_output_aliases=aliases or {},
        compiler_params=pltpu.CompilerParams(vmem_limit_bytes=limit << 20),
        cost_estimate=pl.CostEstimate(
            flops=int(micros * 1e9), bytes_accessed=int(micros * 3e6), transcendentals=0
        ),
        name=name,
    )


def shape(*dims, kind=F32):
    return jax.ShapeDtypeStruct(dims, kind)


def shards(ensembles, cotangents, transforms):
    count, members, cells = ensembles.shape
    blocks, lanes = lax.axis_size("tm"), lax.axis_size("space")
    chips = lanes // 2
    scale = 1.0 / math.sqrt(cells * lanes * count * blocks)
    plan = Plan(count, members)
    levels = blocks.bit_length() - 1
    square = shape(members, members)
    ensembles, cotangents, transforms = (
        pltpu.with_memory_space_constraint(value, pltpu.HBM)
        for value in (ensembles, cotangents, transforms)
    )

    def exchange(value, axis, size, bit):
        return lax.ppermute(value, axis, [(at, at ^ bit) for at in range(size)])

    def around(value):
        return [
            lax.ppermute(value, "space", [(at, (at + 2 * d) % lanes) for at in range(lanes)])
            for d in range(1, chips)
        ]

    def piece_shape(piece):
        first, last = plan.pieces[piece]
        return shape(last - first, members, cells, kind=BF16)

    def piece_sems(piece):
        return [pltpu.SemaphoreType.DMA((len(plan.piece_groups[piece]),))] * 2

    suffixes, total, kept, *first_part = call(
        functools.partial(chain_kernel, plan),
        [shape(count * members, members), square, shape(count, members, members)] + [piece_shape(0)] * 2,
        [HBM] * 3, [VMEM] * 5, [pltpu.SemaphoreType.DMA] + piece_sems(0), 3.5, "transform_chain",
    )(transforms, ensembles, cotangents)

    wide = shape(members // 2, plan.width)
    later = before = jnp.eye(members, dtype=F32)
    uppers, befores = [], []

    packed = shape(packing(members)[3], 128)

    def join(level, total, other, later, before, after):
        befores.append(before)
        last = level == levels - 2
        total, later, before, upper = call(
            functools.partial(join_kernel, level, last),
            [packed if last else square] + [square] * 3, [VMEM] * 4 + [ANY], [VMEM] * 4,
            [], 3, f"join_{level}",
        )(total, other, later, before, after)
        uppers.append(upper)
        return total, later, before

    other = exchange(total, "tm", blocks, 1)
    gram, gram_sent, own, *second_part = call(
        functools.partial(gram_kernel, plan),
        [wide, wide, square] + [piece_shape(1)] * 2,
        [HBM] * 2 + [VMEM] * 3, [VMEM] * 5,
        [pltpu.VMEM((members, plan.width), F32)] + piece_sems(1), 4.5, "gram",
    )(ensembles, cotangents, suffixes, *first_part)
    parts = [first_part, second_part]
    other_own = exchange(own, "tm", blocks, 1)
    gram_core = exchange(gram_sent, "space", lanes, 1)
    total, later, before = join(0, total, other, later, before, own)
    other = exchange(total, "tm", blocks, 2)
    gram = call(sum_kernel, wide, [VMEM] * 2 + [ANY], VMEM, [], 0.1, "chip_gram")(gram, gram_core, total)
    grams = around(gram)

    def pass_on(level, carry, after):
        last = level == levels - 2
        return call(
            functools.partial(pass_kernel, level, last),
            [packed if last else square, square], [VMEM] * 5 + [ANY], [VMEM] * 2, [], 3, f"pass_{level}",
        )(own, other_own, carry, uppers[level], befores[level], after)

    carry = jnp.zeros((members, members), F32)
    after = gram
    for level in range(levels - 2):
        own, carry = pass_on(level, carry, after)
        other_own = exchange(own, "tm", blocks, 2 << level)
        total, later, before = join(level + 1, total, other, later, before, own)
        other = exchange(total, "tm", blocks, 4 << level)
        after = total
    befores.append(before)
    own, carry = pass_on(levels - 2, carry, total)
    other_own = exchange(own, "tm", blocks, blocks // 2)
    size = plan.stack * members
    ens_factors, cot_factors, follow = call(
        functools.partial(carry_kernel, plan, levels - 1),
        [shape(len(plan.groups), size, size, kind=BF16)] * 2
        + [shape(2, count * members, members, kind=BF16)],
        [VMEM] * 3 + [ANY], [VMEM] * 3, [], 0.9, "carries",
    )(suffixes, later, other, own)
    def apply(factors, which, after, name):
        return call(
            functools.partial(apply_kernel, plan),
            [shape(count, members, cells, kind=BF16), shape(8, 128)],
            [VMEM] * (1 + PIECES) + [ANY], [HBM, VMEM],
            [pltpu.VMEM((count, members, cells), BF16),
             pltpu.SemaphoreType.DMA((2 * len(plan.groups),))],
            0.5, name,
        )(factors, *(part[which] for part in parts), after)

    smoothed, done = apply(ens_factors, 0, follow, "smoothed")
    carry, grams[0] = call(
        functools.partial(last_pass_kernel, levels - 1),
        [square, wide], [VMEM] * 3 + [ANY] * 2, [VMEM, ANY], [], 0.2, "pass_last", aliases={4: 1},
    )(other_own, carry, befores[-1], done, grams[0])
    carry_core = exchange(carry, "space", lanes, 1)
    for part in grams:
        gram = gram + part
    gram_core = exchange(gram, "space", lanes, 1)
    steps = call(
        functools.partial(windows_kernel, plan),
        shape(2, count_steps(count) * members, members, kind=BF16), [VMEM, ANY], VMEM,
        [pltpu.VMEM((count * members, members), F32)], 1.0, "windows",
    )(kept, carry)
    carry = call(
        sum_kernel, square, [VMEM] * 2 + [ANY], VMEM, [], 0.1, "chip_carry",
    )(carry, carry_core, steps)
    carries = [carry] + around(carry)
    ensemble_grad, done = apply(cot_factors, 1, carry, "ensemble_grad")
    transform_grad = call(
        functools.partial(final_kernel, plan, scale),
        shape(count, members, members),
        [VMEM] * 4 + [ANY] + [VMEM] * chips, HBM,
        [pltpu.VMEM((count, members, members), F32), pltpu.SemaphoreType.DMA((count,))],
        2.5, "transform_grad",
    )(gram, gram_core, follow, steps, done, *carries)
    return (smoothed, ensemble_grad, transform_grad)


def solution(mesh):
    return jax.shard_map(
        shards,
        mesh=mesh,
        in_specs=(P("tm", None, "space"), P("tm", None, "space"), P("tm", None, None)),
        out_specs=(P("tm", None, "space"), P("tm", None, "space"), P("tm", None, None)),
        check_vma=False,
    )
```

```python
import functools
import math

import jax
import jax.numpy as jnp
from jax import lax
from jax.experimental import pallas as pl
from jax.experimental.pallas import tpu as pltpu
from jax.sharding import PartitionSpec as P

F32 = jnp.float32
BF16 = jnp.bfloat16
VMEM = pl.BlockSpec(memory_space=pltpu.VMEM)
HBM = pl.BlockSpec(memory_space=pltpu.HBM)
ANY = pl.BlockSpec(memory_space=pl.ANY)
DEPTH = 256
PIECES = 2
NORMAL = (((1,), (0,)), ((), ()))
ROWS = (((1,), (1,)), ((), ()))


def split(value):
    high = value.astype(BF16)
    return high, (value - high.astype(F32)).astype(BF16)


def mul(left, right, dims=NORMAL):
    return lax.dot_general(left, right, dims, preferred_element_type=F32)


def mul_pairs(left, right, dims=NORMAL):
    return mul(left[0], right[0], dims) + (
        mul(left[0], right[1], dims) + mul(left[1], right[0], dims)
    )


def mul_exact(left, right, dims=NORMAL):
    return mul_pairs(split(left), split(right), dims)


def mul_stacked(left, right, dims=NORMAL):
    rows = left[0].shape[0]
    both = mul(jnp.concatenate(left, axis=0), right[0], dims)
    return both[:rows] + (both[rows:] + mul(left[0], right[1], dims))


def mul_small(left, right):
    return mul_stacked(split(left), split(right))


def product_of(factors):
    while len(factors) > 1:
        joined = [mul_exact(*factors[at : at + 2]) for at in range(0, len(factors) - 1, 2)]
        factors = joined + factors[len(joined) * 2 :]
    return factors[0]


def suffix_scan(ref, count, members, stop):
    width = 1
    while width < stop:
        for start in range(0, count, 2 * width):
            middle = start + width
            if middle < count:
                rows = slice(start * members, middle * members)
                ref[rows] = mul_exact(ref[rows], ref[middle * members : (middle + 1) * members])
        width *= 2


class Plan:
    def __init__(self, count, members):
        self.count, self.members = count, members
        self.stack = DEPTH // members
        self.groups = [
            (start, min(start + self.stack, count)) for start in range(0, count, self.stack)
        ]
        bounds = [0, len(self.groups) // 3, len(self.groups)]
        self.piece_groups = [self.groups[a:b] for a, b in zip(bounds, bounds[1:])]
        self.pieces = [(part[0][0], part[-1][1]) for part in self.piece_groups]
        self.first_group = bounds[:-1]
        self.widths = [-(-(stop - start) * members // 128) * 128 for start, stop in self.groups]
        self.width = sum(self.widths)

    def lanes(self, at):
        start = sum(self.widths[:at])
        return slice(start, start + self.widths[at])

    def rows(self, first, last):
        return slice(first * self.members, last * self.members)


def packing(members):
    spare = 128 - members
    strips = -(-members // spare)
    rest = members // (strips + 1) // 8 * 8
    return spare, strips, rest, members - rest


def pack(value):
    members = value.shape[0]
    spare, strips, rest, rows = packing(members)
    side = [value[rows:, at * spare : (at + 1) * spare] for at in range(strips)]
    side = [jnp.pad(part, ((0, 0), (0, spare - part.shape[1]))) for part in side]
    side.append(jnp.zeros((rows - strips * rest, spare), value.dtype))
    return jnp.concatenate([value[:rows], jnp.concatenate(side, axis=0)], axis=1)


def unpack(value, members):
    spare, strips, rest, rows = packing(members)
    side = [value[at * rest : (at + 1) * rest, members:] for at in range(strips)]
    last = jnp.concatenate(side, axis=1)[:, :members]
    return jnp.concatenate([value[:, :members], last], axis=0)


def on_blocks(members, size):
    rows = lax.broadcasted_iota(jnp.int32, (size, size), 0) // members
    columns = lax.broadcasted_iota(jnp.int32, (size, size), 1) // members
    return rows == columns


def loads(plan, piece, values, buffer, sems, which=slice(None)):
    base = plan.pieces[piece][0]
    copies = [
        pltpu.make_async_copy(values.at[start:stop], buffer.at[start - base : stop - base], sems.at[at])
        for at, (start, stop) in enumerate(plan.piece_groups[piece])
    ][which]
    for copy in copies:
        copy.start()
    return copies


def chain_kernel(
    plan, transforms, ensembles, cotangents, suffixes, total, kept, ens, cot, sem, ens_sem, cot_sem
):
    count, members = plan.count, plan.members
    read = pltpu.make_async_copy(transforms, kept, sem)
    read.start()
    more = []
    for at in range(len(plan.piece_groups[0])):
        more += loads(plan, 0, ensembles, ens, ens_sem, slice(at, at + 1))
        more += loads(plan, 0, cotangents, cot, cot_sem, slice(at, at + 1))
    read.wait()
    for at in range(count):
        suffixes[plan.rows(at, at + 1)] = kept[at]
    suffix_scan(suffixes, count, members, count)
    total[...] = suffixes[plan.rows(0, 1)]
    for copy in more:
        copy.wait()


def windows_kernel(plan, kept, _, steps, runs):
    count = plan.count
    for at in range(count - 1):
        runs[plan.rows(at + 1, at + 2)] = kept[at].T
    number = 0
    width = 1
    while width < count:
        for middle in range(width, count, 2 * width):
            size = min(width, count - middle)
            for side, part in enumerate(split(runs[plan.rows(middle, middle + size)])):
                steps[side, plan.rows(number, number + size)] = part
            number += size
        for start in range(2 * width, count, 2 * width):
            if start + width < count:
                rows = plan.rows(start + width, min(start + 2 * width, count))
                runs[rows] = mul_small(runs[rows], runs[plan.rows(start + width - 1, start + width)])
        width *= 2


def count_steps(count):
    total = 0
    width = 1
    while width < count:
        total += sum(min(width, count - middle) for middle in range(width, count, 2 * width))
        width *= 2
    return total


def core_index():
    return lax.rem(lax.axis_index("space"), 2)


def gram_of(plan, piece, cot, ens, suffixes, whole, ready=lambda: None):
    members = plan.members
    base = plan.pieces[piece][0]
    offset = jnp.zeros((members, members), F32)
    for at, (start, stop) in enumerate(plan.piece_groups[piece]):
        ready()
        size = (stop - start) * members
        stacked = [ref[start - base : stop - base].reshape(size, ref.shape[2]) for ref in (cot, ens)]
        wide = jnp.where(on_blocks(members, size), mul(*stacked, ROWS), 0.0)
        gram = wide[:members]
        for i in range(1, stop - start):
            gram = gram + wide[i * members : (i + 1) * members]
        offset = offset + mul_exact(gram, suffixes[plan.rows(start, stop)])
        lanes = plan.lanes(plan.first_group[piece] + at)
        width = lanes.stop - lanes.start
        whole[:, lanes] = jnp.pad(gram, ((0, 0), (0, width - size)))
    return offset


def gram_kernel(
    plan, ensembles, cotangents, suffixes, ens, cot,
    kept, sent, offsets, next_ens, next_cot, whole, ens_sem, cot_sem,
):
    pairs = []
    for at in range(len(plan.piece_groups[1])):
        pairs.append(
            loads(plan, 1, ensembles, next_ens, ens_sem, slice(at, at + 1))
            + loads(plan, 1, cotangents, next_cot, cot_sem, slice(at, at + 1))
        )
    waiting = iter(pairs)

    def ready():
        for copy in next(waiting):
            copy.wait()

    total = gram_of(plan, 0, cot, ens, suffixes, whole)
    offsets[...] = total + gram_of(plan, 1, next_cot, next_ens, suffixes, whole, ready)
    half = plan.members // 2
    core = lax.rem(lax.axis_index("space"), 2)
    kept[...] = whole[pl.ds(core * half, half)]
    sent[...] = whole[pl.ds((1 - core) * half, half)]


def upper_half(level):
    return lax.rem(lax.axis_index("tm") // (1 << level), 2) == 1


def join_kernel(level, last, total, other, later, before, _, new_total, new_later, new_before, upper_total):
    upper = upper_half(level)
    left = jnp.where(upper, other[...], total[...])
    right = jnp.where(upper, total[...], other[...])
    joined = mul_small(left, right)
    new_total[...] = pack(joined) if last else joined
    upper_total[...] = right
    new_later[...] = jnp.where(upper, later[...], mul_small(later[...], other[...]))
    new_before[...] = jnp.where(upper, mul_small(other[...], before[...]), before[...])


def sum_kernel(left, right, _, total):
    total[...] = left[...] + right[...]


def pass_kernel(level, last, own, other, carry, upper_total, before, _, new_own, new_carry):
    upper = upper_half(level)
    left = jnp.where(upper, other[...], own[...])
    right = jnp.where(upper, own[...], other[...])
    passed = mul_small(left, upper_total[...]) + right
    new_own[...] = pack(passed) if last else passed
    new_carry[...] = carry[...] + jnp.where(upper, mul_small(left, before[...]), 0.0)


def last_pass_kernel(level, other, carry, before, _, __, new_carry, ___):
    added = mul_small(unpack(other[...], before.shape[0]), before[...])
    new_carry[...] = carry[...] + jnp.where(upper_half(level), added, 0.0)


def enter_kernel(level, later, other, _, entering):
    joined = mul_small(later[...], unpack(other[...], later.shape[0]))
    entering[...] = jnp.where(upper_half(level), later[...], joined)


def carry_kernel(plan, suffixes, later, _, ens_factors, cot_factors, follow):
    count, members = plan.count, plan.members
    entering = later[...]
    mask = on_blocks(members, plan.stack * members)
    repeated = split(jnp.concatenate([entering] * plan.stack, axis=1))
    for at, (start, stop) in enumerate(plan.groups):
        size = (stop - start) * members
        wide = mul_pairs(split(suffixes[plan.rows(start, stop)]), repeated)
        part = jnp.where(mask[:size, :size], wide[:, :size], 0.0)
        cot_factors[at, :size, :size] = part.astype(BF16)
        ens_factors[at, :size, :size] = part.T.astype(BF16)
        first = max(start - 1, 0)
        kept = wide[(first + 1 - start) * members :, :members]
        for side, value in enumerate(split(kept)):
            follow[side, plan.rows(first, stop - 1)] = value
    for side, value in enumerate(split(entering)):
        follow[side, plan.rows(count - 1, count)] = value


def apply_kernel(plan, factors, *refs):
    out, marker, out_buf, out_sem = refs[-4:]
    members = plan.members
    marker[...] = jnp.zeros_like(marker)
    chunk = out_buf.shape[2] // 2
    writes = []
    for piece, values in enumerate(refs[:PIECES]):
        first = plan.pieces[piece][0]
        for at, (start, stop) in enumerate(plan.piece_groups[piece]):
            size = (stop - start) * members
            for side in range(2):
                columns = slice(side * chunk, (side + 1) * chunk)
                stacked = values[start - first : stop - first, :, columns].reshape(size, chunk)
                result = mul(factors[plan.first_group[piece] + at, :size, :size], stacked)
                out_buf[start:stop, :, columns] = result.astype(BF16).reshape(
                    stop - start, members, chunk
                )
                copy = pltpu.make_async_copy(
                    out_buf.at[start:stop, :, columns],
                    out.at[start:stop, :, columns],
                    out_sem.at[len(writes)],
                )
                copy.start()
                writes.append(copy)
    for copy in writes:
        copy.wait()


def final_kernel(plan, scale, gram, gram_core, follow, steps, _, *refs):
    carries, (out, buffer, sems) = refs[:-3], refs[-3:]
    carry = carries[0][...]
    for ref in carries[1:]:
        carry = carry + ref[...]
    count, members = plan.count, plan.members
    totals = []
    first = lax.rem(lax.axis_index("space"), 2) == 0
    for at, (start, stop) in enumerate(plan.groups):
        mine, other = gram[:, plan.lanes(at)], gram_core[:, plan.lanes(at)]
        halves = [jnp.where(first, mine, other), jnp.where(first, other, mine)]
        tall = jnp.concatenate(halves, axis=0).T
        for i in range(stop - start):
            totals.append(tall[i * members : (i + 1) * members])
    totals[0] = totals[0] + carry.T
    number = 0
    width = 1
    while width < count:
        for start in range(width, count, 2 * width):
            size = min(width, count - start)
            rows = plan.rows(number, number + size)
            added = mul_stacked((steps[0, rows], steps[1, rows]), split(totals[start - 1]))
            for at in range(size):
                totals[start + at] = totals[start + at] + added[at * members : (at + 1) * members]
            number += size
        width *= 2
    copies = []
    for at in range(count):
        rows = plan.rows(at, at + 1)
        buffer[at] = mul_stacked(split(totals[at]), (follow[0, rows], follow[1, rows]), ROWS) * scale
        copy = pltpu.make_async_copy(buffer.at[at], out.at[at], sems.at[at])
        copy.start()
        copies.append(copy)
    for copy in copies:
        copy.wait()


def call(kernel, outs, ins, out_specs, scratch, micros, name, limit=16, aliases=None):
    return pl.pallas_call(
        kernel,
        out_shape=outs,
        in_specs=ins,
        out_specs=out_specs,
        scratch_shapes=scratch,
        input_output_aliases=aliases or {},
        compiler_params=pltpu.CompilerParams(vmem_limit_bytes=limit << 20),
        cost_estimate=pl.CostEstimate(
            flops=int(micros * 1e9), bytes_accessed=int(micros * 3e6), transcendentals=0
        ),
        name=name,
    )


def shape(*dims, kind=F32):
    return jax.ShapeDtypeStruct(dims, kind)


def shards(ensembles, cotangents, transforms):
    count, members, cells = ensembles.shape
    blocks, lanes = lax.axis_size("tm"), lax.axis_size("space")
    chips = lanes // 2
    scale = 1.0 / math.sqrt(cells * lanes * count * blocks)
    plan = Plan(count, members)
    levels = blocks.bit_length() - 1
    square = shape(members, members)
    ensembles, cotangents, transforms = (
        pltpu.with_memory_space_constraint(value, pltpu.HBM)
        for value in (ensembles, cotangents, transforms)
    )

    def exchange(value, axis, size, bit):
        return lax.ppermute(value, axis, [(at, at ^ bit) for at in range(size)])

    def around(value):
        return [
            lax.ppermute(value, "space", [(at, (at + 2 * d) % lanes) for at in range(lanes)])
            for d in range(1, chips)
        ]

    def piece_shape(piece):
        first, last = plan.pieces[piece]
        return shape(last - first, members, cells, kind=BF16)

    def piece_sems(piece):
        return [pltpu.SemaphoreType.DMA((len(plan.piece_groups[piece]),))] * 2

    suffixes, total, kept, *first_part = call(
        functools.partial(chain_kernel, plan),
        [shape(count * members, members), square, shape(count, members, members)] + [piece_shape(0)] * 2,
        [HBM] * 3, [VMEM] * 5, [pltpu.SemaphoreType.DMA] + piece_sems(0), 3.5, "transform_chain",
    )(transforms, ensembles, cotangents)

    wide = shape(members // 2, plan.width)
    later = before = jnp.eye(members, dtype=F32)
    uppers, befores = [], []

    packed = shape(packing(members)[3], 128)

    def join(level, total, other, later, before, after):
        befores.append(before)
        last = level == levels - 2
        total, later, before, upper = call(
            functools.partial(join_kernel, level, last),
            [packed if last else square] + [square] * 3, [VMEM] * 4 + [ANY], [VMEM] * 4,
            [], 3, f"join_{level}",
        )(total, other, later, before, after)
        uppers.append(upper)
        return total, later, before

    other = exchange(total, "tm", blocks, 1)
    gram, gram_sent, own, *second_part = call(
        functools.partial(gram_kernel, plan),
        [wide, wide, square] + [piece_shape(1)] * 2,
        [HBM] * 2 + [VMEM] * 3, [VMEM] * 5,
        [pltpu.VMEM((members, plan.width), F32)] + piece_sems(1), 4.5, "gram",
    )(ensembles, cotangents, suffixes, *first_part)
    parts = [first_part, second_part]
    other_own = exchange(own, "tm", blocks, 1)
    gram_core = exchange(gram_sent, "space", lanes, 1)
    total, later, before = join(0, total, other, later, before, own)
    other = exchange(total, "tm", blocks, 2)
    gram = call(sum_kernel, wide, [VMEM] * 2 + [ANY], VMEM, [], 0.1, "chip_gram")(gram, gram_core, total)
    grams = around(gram)

    def pass_on(level, carry, after):
        last = level == levels - 2
        return call(
            functools.partial(pass_kernel, level, last),
            [packed if last else square, square], [VMEM] * 5 + [ANY], [VMEM] * 2, [], 3, f"pass_{level}",
        )(own, other_own, carry, uppers[level], befores[level], after)

    carry = jnp.zeros((members, members), F32)
    after = gram
    for level in range(levels - 2):
        own, carry = pass_on(level, carry, after)
        other_own = exchange(own, "tm", blocks, 2 << level)
        total, later, before = join(level + 1, total, other, later, before, own)
        other = exchange(total, "tm", blocks, 4 << level)
        after = total
    befores.append(before)
    own, carry = pass_on(levels - 2, carry, total)
    other_own = exchange(own, "tm", blocks, blocks // 2)
    entering = call(
        functools.partial(enter_kernel, levels - 1),
        square, [VMEM] * 2 + [ANY], VMEM, [], 0.2, "entering",
    )(later, other, own)
    size = plan.stack * members
    ens_factors, cot_factors, follow = call(
        functools.partial(carry_kernel, plan),
        [shape(len(plan.groups), size, size, kind=BF16)] * 2
        + [shape(2, count * members, members, kind=BF16)],
        [VMEM] * 2 + [ANY], [VMEM] * 3, [], 0.9, "carries",
    )(suffixes, entering, own)
    def apply(factors, which, after, name):
        return call(
            functools.partial(apply_kernel, plan),
            [shape(count, members, cells, kind=BF16), shape(8, 128)],
            [VMEM] * (1 + PIECES) + [ANY], [HBM, VMEM],
            [pltpu.VMEM((count, members, cells), BF16),
             pltpu.SemaphoreType.DMA((2 * len(plan.groups),))],
            0.5, name,
        )(factors, *(part[which] for part in parts), after)

    smoothed, done = apply(ens_factors, 0, follow, "smoothed")
    carry, grams[0] = call(
        functools.partial(last_pass_kernel, levels - 1),
        [square, wide], [VMEM] * 3 + [ANY] * 2, [VMEM, ANY], [], 0.2, "pass_last", aliases={4: 1},
    )(other_own, carry, befores[-1], done, grams[0])
    carry_core = exchange(carry, "space", lanes, 1)
    for part in grams:
        gram = gram + part
    gram_core = exchange(gram, "space", lanes, 1)
    steps = call(
        functools.partial(windows_kernel, plan),
        shape(2, count_steps(count) * members, members, kind=BF16), [VMEM, ANY], VMEM,
        [pltpu.VMEM((count * members, members), F32)], 1.0, "windows",
    )(kept, carry)
    carry = call(
        sum_kernel, square, [VMEM] * 2 + [ANY], VMEM, [], 0.1, "chip_carry",
    )(carry, carry_core, steps)
    carries = [carry] + around(carry)
    ensemble_grad, done = apply(cot_factors, 1, carry, "ensemble_grad")
    transform_grad = call(
        functools.partial(final_kernel, plan, scale),
        shape(count, members, members),
        [VMEM] * 4 + [ANY] + [VMEM] * chips, HBM,
        [pltpu.VMEM((count, members, members), F32), pltpu.SemaphoreType.DMA((count,))],
        2.5, "transform_grad",
    )(gram, gram_core, follow, steps, done, *carries)
    return (smoothed, ensemble_grad, transform_grad)


def solution(mesh):
    return jax.shard_map(
        shards,
        mesh=mesh,
        in_specs=(P("tm", None, "space"), P("tm", None, "space"), P("tm", None, None)),
        out_specs=(P("tm", None, "space"), P("tm", None, "space"), P("tm", None, None)),
        check_vma=False,
    )
```
